32 devices in a mesh: dp: 16 (over z, y, core), seq: 2 (over x).
Axes of the slice: x: 2, y: 2, z: 4, core: 2. Of those that a mesh axis runs over, the one named last changes fastest.
Arguments:
- activations: bfloat16 [16, 1024, 1152], P('dp', 'seq'), may hold values from -6 to 6
- conditioning: bfloat16 [16, 1152], P('dp'), may hold values from -6 to 6
- cotangent: bfloat16 [16, 1024, 1152], P('dp', 'seq'), may hold values from -6 to 6
- w_ada: bfloat16 [7962624], P(('dp', 'seq')), may hold values from -0.1875 to 0.1875
- b_ada: bfloat16 [6912], P(('dp', 'seq')), may hold values from -3 to 3
- w_query: bfloat16 [1327104], P(('dp', 'seq')), may hold values from -0.1875 to 0.1875
- w_key: bfloat16 [1327104], P(('dp', 'seq')), may hold values from -0.1875 to 0.1875
- w_value: bfloat16 [1327104], P(('dp', 'seq')), may hold values from -0.1875 to 0.1875
- w_forget: bfloat16 [18432], P(('dp', 'seq')), may hold values from -0.1875 to 0.1875
- b_forget: bfloat16 [16], replicated, may hold values from -8 to -3
- conv_taps: bfloat16 [11520], P(('dp', 'seq')), may hold values from -2 to 2
- w_out: bfloat16 [1327104], P(('dp', 'seq')), may hold values from -0.1875 to 0.1875
- w_up: bfloat16 [5308416], P(('dp', 'seq')), may hold values from -0.1875 to 0.1875
- w_down: bfloat16 [5308416], P(('dp', 'seq')), may hold values from -0.09375 to 0.09375
Outputs:
- output: bfloat16 [16, 1024, 1152], P('dp', 'seq')
- grad_input: float32 [16, 1024, 1152], P('dp', 'seq')
- grad_ada: float32 [7962624], P(('dp', 'seq'))
- grad_ada_bias: float32 [6912], P(('dp', 'seq'))
- grad_query: float32 [1327104], P(('dp', 'seq'))
- grad_key: float32 [1327104], P(('dp', 'seq'))
- grad_value: float32 [1327104], P(('dp', 'seq'))
- grad_forget: float32 [18432], P(('dp', 'seq'))
- grad_forget_bias: float32 [16], replicated
- grad_conv: float32 [11520], P(('dp', 'seq'))
- grad_out: float32 [1327104], P(('dp', 'seq'))
- grad_up: float32 [5308416], P(('dp', 'seq'))
- grad_down: float32 [5308416], P(('dp', 'seq'))
The draws below stay inside these ranges and needn't reach their ends.
All inputs are finite; a program needn't handle non-finite values.
Results may differ from the reference program's by a relative error of at most 0.022.
The reference program's roundings to bfloat16 on the way count: a program that leaves them out, or rounds other values in their place, can miss the bound.
Values may be sent and summed in bfloat16 or wider, within the bound.
A program may use at most 448 MiB of HBM per device.

```python
import jax
import jax.numpy as jnp
from jax import lax

D = 1152
FF = 4608
HEADS = 16
HEAD_DIM = 72
GRID = 32
GROUP = 64
PATCHES = 1024
IMAGES = 16


def levels(rng, extent, cuts, low, largest):
    gain, own = 1.0, jax.random.fold_in(rng, 6)
    for axis_at, shards_of in cuts:
        heights = jnp.exp(jax.random.uniform(jax.random.fold_in(own, axis_at), (shards_of,), jnp.float32, low / len(cuts), largest / len(cuts)))
        gain = gain * jnp.repeat(heights, extent[axis_at] // shards_of).reshape([-1 if axis == axis_at else 1 for axis in range(len(extent))])
    return gain


def bell_draw(rng, dims, deviation, limit, split=(), held_as=jnp.bfloat16):
    values = deviation * jax.random.normal(rng, dims, jnp.float32)
    if split:
        values = values * levels(rng, dims, split, -0.22, 0.18)
    return jnp.clip(values, -limit, limit).astype(held_as)


def setup_inputs(seed: int = 0) -> dict:
    keys = jax.random.split(jax.random.key(seed), 15)
    activations = bell_draw(keys[0], (IMAGES, PATCHES, D), 1.0, 6.0, ((0, 16), (1, 2)))
    conditioning = bell_draw(keys[1], (IMAGES, D), 1.0, 6.0, ((0, 16),))
    cotangent = bell_draw(keys[2], (IMAGES, PATCHES, D), 1.0, 6.0, ((0, 16), (1, 2)))
    w_ada = bell_draw(keys[3], (6 * D * D,), D ** -0.5, 0.1875, ((0, 32),))
    b_ada = bell_draw(keys[4], (6 * D,), 0.5, 3.0, ((0, 32),))
    w_query = bell_draw(keys[5], (D * D,), D ** -0.5, 0.1875, ((0, 32),))
    w_key = bell_draw(keys[6], (D * D,), D ** -0.5, 0.1875, ((0, 32),))
    w_value = bell_draw(keys[7], (D * D,), D ** -0.5, 0.1875, ((0, 32),))
    w_forget = bell_draw(keys[8], (D * HEADS,), D ** -0.5, 0.1875, ((0, 32),))
    b_forget = jnp.clip(jax.random.uniform(keys[9], (HEADS,), jnp.float32, -8.0, -3.0), -8.0, -3.0).astype(jnp.bfloat16)
    conv_taps = bell_draw(keys[10], (10 * D,), 0.35, 2.0, ((0, 32),))
    w_out = bell_draw(keys[11], (D * D,), D ** -0.5, 0.1875, ((0, 32),))
    w_up = bell_draw(keys[12], (D * FF,), D ** -0.5, 0.1875, ((0, 32),))
    w_down = bell_draw(keys[13], (FF * D,), FF ** -0.5, 0.09375, ((0, 32),))
    return {"activations": activations, "conditioning": conditioning, "cotangent": cotangent, "w_ada": w_ada, "b_ada": b_ada, "w_query": w_query, "w_key": w_key, "w_value": w_value, "w_forget": w_forget, "b_forget": b_forget, "conv_taps": conv_taps, "w_out": w_out, "w_up": w_up, "w_down": w_down}


@jax.custom_vjp
def low(v):
    return lax.optimization_barrier(v.astype(jnp.bfloat16)).astype(jnp.float32)

@jax.custom_vjp
def low_back(v):
    return v

def low_keep(v):
    return (low(v), None)

def low_pass(kept, grad):
    return (grad,)

def back_keep(v):
    return (v, None)

def back_low(kept, grad):
    return (low(grad),)
low.defvjp(low_keep, low_pass)
low_back.defvjp(back_keep, back_low)
epsilon = 1e-06
highest = lax.Precision.HIGHEST

def layer_norm(values, offset, factor):
    center = lax.optimization_barrier(jnp.mean(values, axis=-1, keepdims=True))
    centered = values - center
    spread = lax.optimization_barrier(jnp.mean(centered * centered, axis=-1, keepdims=True))
    return centered * lax.rsqrt(spread + epsilon) * (1.0 + factor) + offset

def head_norm(mixture):
    mean_square = lax.optimization_barrier(jnp.mean(mixture * mixture, axis=-1, keepdims=True))
    return mixture * lax.rsqrt(mean_square + epsilon)

def group_scan(queries, key_rows, values, logdecay, opening):
    length = queries.shape[0]
    blocks_total = length // GROUP
    causal = (jnp.arange(GROUP)[:, None] >= jnp.arange(GROUP)[None, :])[:, :, None]

    def advance(carried, pieces):
        q_part, k_part, v_part, g_part = pieces
        running = jnp.cumsum(g_part, axis=0)
        spread = jnp.where(causal, running[:, None, :] - running[None, :, :], 0.0)
        weight = jnp.where(causal, jnp.exp(spread), 0.0)
        scores = jnp.einsum('the,she->tsh', q_part, k_part, precision=highest) * weight
        within = jnp.einsum('tsh,shf->thf', scores, v_part, precision=highest)
        earlier = jnp.exp(running)[:, :, None] * jnp.einsum('the,hef->thf', q_part, carried, precision=highest)
        remaining = jnp.exp(running[-1][None, :] - running)
        update = jnp.einsum('she,shf->hef', k_part * remaining[:, :, None], v_part, precision=highest)
        return (jnp.exp(running[-1])[:, None, None] * carried + update, within + earlier)
    pieces = tuple((source.reshape((blocks_total, GROUP) + source.shape[1:]) for source in (queries, key_rows, values, logdecay)))
    closing, outputs = lax.scan(jax.checkpoint(advance), opening, pieces)
    return (outputs.reshape(queries.shape), closing)

def depthwise(padded, kernel):
    height = padded.shape[1] - 2
    across = padded.shape[2]
    widened = jnp.pad(padded, ((0, 0), (0, 0), (1, 1), (0, 0)))
    summed = jnp.zeros((padded.shape[0], height, across, padded.shape[3]), jnp.float32)
    for vertical in range(3):
        for lateral in range(3):
            window = widened[:, vertical:vertical + height, lateral:lateral + across]
            summed = summed + kernel[3 * vertical + lateral] * window
    return summed

def image_block(patch_rows, cond_row, params):
    ada_matrix, ada_bias, query_w, key_w, value_w, forget_w, forget_bias, conv_w, out_w, up_w, down_w = params
    cond_act = low(jax.nn.silu(cond_row))
    modulation = jnp.dot(cond_act, ada_matrix, precision=highest) + ada_bias
    pieces = [modulation[position * D:(position + 1) * D] for position in range(6)]
    hidden_one = low(layer_norm(patch_rows, pieces[0], pieces[1]))
    queries = low(low_back(jnp.dot(hidden_one, query_w, precision=highest)))
    key_rows = low(low_back(jnp.dot(hidden_one, key_w, precision=highest)))
    values = low(low_back(jnp.dot(hidden_one, value_w, precision=highest)))
    gate_pre = low_back(jnp.dot(hidden_one, forget_w, precision=highest) + forget_bias)
    logdecay = -jax.nn.softplus(gate_pre)

    def split_heads(matrix):
        return matrix.reshape(PATCHES, HEADS, HEAD_DIM)
    zero_state = jnp.zeros((HEADS, HEAD_DIM, HEAD_DIM), jnp.float32)
    forward_mix, _ = group_scan(split_heads(queries), split_heads(key_rows), split_heads(values), logdecay, zero_state)
    behind, _ = group_scan(jnp.flip(split_heads(queries), 0), jnp.flip(split_heads(key_rows), 0), jnp.flip(split_heads(values), 0), jnp.flip(logdecay, 0), zero_state)
    normed = head_norm(forward_mix + jnp.flip(behind, 0)).reshape(PATCHES, D)
    padded = jnp.pad(values.reshape(1, GRID, GRID, D), ((0, 0), (1, 1), (0, 0), (0, 0)))
    conv_out = depthwise(padded, conv_w[:9]).reshape(PATCHES, D)
    mixed = low(low_back(normed + conv_out + conv_w[9]))
    branch = low_back(jnp.dot(mixed, out_w, precision=highest))
    middle = patch_rows + pieces[2] * branch
    hidden_two = low(layer_norm(middle, pieces[3], pieces[4]))
    up_pre = low_back(jnp.dot(hidden_two, up_w, precision=highest))
    activated = low(jax.nn.gelu(up_pre, approximate=True))
    down_out = low_back(jnp.dot(activated, down_w, precision=highest))
    return middle + pieces[5] * down_out

def reference(activations, conditioning, cotangent, w_ada, b_ada, w_query, w_key, w_value, w_forget, b_forget, conv_taps, w_out, w_up, w_down):

    def widen(source):
        return source.astype(jnp.float32)
    params = (widen(w_ada).reshape(D, 6 * D), widen(b_ada), widen(w_query).reshape(D, D), widen(w_key).reshape(D, D), widen(w_value).reshape(D, D), widen(w_forget).reshape(D, HEADS), widen(b_forget), widen(conv_taps).reshape(10, D), widen(w_out).reshape(D, D), widen(w_up).reshape(D, FF), widen(w_down).reshape(FF, D))
    empty_grads = jax.tree.map(jnp.zeros_like, params)

    def advance(summed, item):
        patch_rows, cond_row, grad_rows = item
        result, pullback = jax.vjp(image_block, widen(patch_rows), widen(cond_row), params)
        grad_rows_in, _, grads = pullback(widen(grad_rows))
        return (jax.tree.map(jnp.add, summed, grads), (result, grad_rows_in))
    summed, (output_wide, grad_input) = lax.scan(advance, empty_grads, (activations, conditioning, cotangent))
    output = output_wide.astype(jnp.bfloat16)
    flattened = [piece.reshape(-1) for piece in summed]
    return (output, grad_input, flattened[0], flattened[1], flattened[2], flattened[3], flattened[4], flattened[5], flattened[6], flattened[7], flattened[8], flattened[9], flattened[10])
```

```python
import functools

import jax
import jax.numpy as jnp
import numpy as np
from jax import lax
from jax.experimental import pallas as pl
from jax.experimental.pallas import tpu as pltpu
from jax.sharding import PartitionSpec as P

GRID = 32
LANES = 128
GROUPS = 32
epsilon = 1e-06
f32 = jnp.float32
bf16 = jnp.bfloat16
VMEM_LIMIT = 56 * 1024 * 1024
FORWARD_PLAN = (
    ("f", 0, 0, 0), ("g", 0, 0, 0), -1, ("f", 1, 0, 0), ("f", 0, 0, 1), ("f", 2, 0, 0), ("g", 2, 0, 0),
    ("g", 1, 0, 0), ("f", 1, 0, 1), ("f", 5, 0, 0), ("f", 2, 0, 1), ("f", 0, 0, 2), ("g", 3, 0, 0), ("f", 0, 0, 3),
    ("f", 1, 0, 2), ("g", 0, 0, 1), ("f", 5, 0, 1), ("f", 2, 0, 2), ("f", 2, 0, 3), ("f", 1, 0, 3), ("g", 4, 0, 0),
    ("g", 5, 0, 0), ("g", 2, 0, 1), ("g", 1, 0, 1), ("f", 5, 0, 2), ("f", 5, 0, 3), ("g", 0, 0, 2), -1,
    ("g", 4, 0, 1), ("g", 5, 0, 1), ("g", 2, 0, 2), ("s", 0, 0, 0), ("s", 0, 0, 1), ("s", 0, 0, 2), ("s", 0, 0, 3),
    ("s", 1, 0, 0), ("g", 1, 0, 2), ("s", 1, 0, 1), -1, ("s", 1, 0, 2), ("s", 1, 0, 3), ("s", 2, 0, 0),
    ("g", 4, 0, 2), ("s", 2, 0, 1), ("s", 2, 0, 2), ("s", 2, 0, 3), ("g", 5, 0, 2), ("s", 3, 0, 0), ("g", 0, 0, 3),
    ("g", 4, 0, 3), ("g", 0, 1, 0), ("s", 3, 0, 1), ("g", 2, 0, 3), ("g", 1, 0, 3), ("g", 2, 1, 0), ("s", 3, 0, 2),
    ("g", 1, 1, 0), ("s", 3, 0, 3), ("g", 5, 0, 3), ("g", 3, 1, 0), ("g", 0, 1, 1), -1, ("g", 4, 1, 0),
    ("g", 5, 1, 0), ("g", 0, 1, 2), ("g", 2, 1, 1), ("g", 1, 1, 1), -1, ("g", 2, 1, 2), ("g", 1, 1, 2), -1,
    ("g", 4, 1, 1), -1, ("g", 5, 1, 1), -1, ("g", 0, 1, 3), -1, -1, ("g", 4, 1, 2), ("g", 5, 1, 2), ("g", 1, 1, 3),
    -1, -1, -1, ("g", 2, 1, 3), ("g", 4, 1, 3), -1, -1, -1, ("g", 5, 1, 3),
)
FEED_PLAN = (
    ("g", 0, 0, 0), -1, -1, ("g", 2, 0, 0), ("g", 1, 0, 0), ("g", 3, 0, 0), ("g", 0, 0, 1), -1, -1, ("g", 0, 0, 2),
    ("g", 4, 0, 0), ("g", 5, 0, 0), ("d", 0, 0, 0), ("g", 2, 0, 1), ("d", 4, 0, 0), -1, ("g", 1, 0, 1),
    ("g", 2, 0, 2), -1, ("g", 0, 0, 3), ("g", 1, 0, 2), ("d", 1, 0, 0), ("d", 2, 0, 0), ("d", 0, 0, 1),
    ("g", 4, 0, 1), -1, -1, ("g", 5, 0, 1), ("g", 2, 0, 3), ("d", 4, 0, 1), ("d", 0, 0, 2), -1, ("g", 1, 0, 3),
    ("g", 4, 0, 2), ("g", 5, 0, 2), ("d", 3, 0, 0), -1, -1, ("d", 4, 0, 2), ("d", 0, 0, 3), ("d", 2, 0, 1),
    ("d", 1, 0, 1), -1, -1, ("g", 4, 0, 3), -1, ("d", 1, 0, 2), ("d", 2, 0, 2), -1, -1, ("g", 5, 0, 3),
    ("d", 2, 0, 3), -1, ("d", 4, 0, 3), ("d", 1, 0, 3), ("d", 3, 0, 1), ("d", 5, 0, 0), -1, -1, -1, -1,
    ("d", 3, 0, 2), -1, -1, -1, -1, ("d", 3, 0, 3), ("d", 5, 0, 1), -1,
)
BACKWARD_PLAN = (
    -1, ("u", 0, 0, 0), ("u", 4, 0, 0), -1, ("u", 0, 0, 1), ("u", 0, 0, 2), ("u", 2, 0, 0), ("u", 1, 0, 0),
    ("u", 4, 0, 1), -1, ("u", 0, 0, 3), ("u", 2, 0, 1), ("u", 1, 0, 1), -1, ("u", 4, 0, 2), ("u", 2, 0, 2),
    ("u", 1, 0, 2), ("u", 3, 0, 0), -1, ("u", 2, 0, 3), ("u", 1, 0, 3), -1, ("u", 4, 0, 3), -1, ("u", 3, 0, 1),
    ("u", 5, 0, 0), -1, -1, ("u", 3, 0, 2), -1, -1, ("u", 3, 0, 3), ("u", 5, 0, 1), -1, -1, -1, -1, -1, -1,
)
FINISH_PLAN = (
    -1, ("a", 0, 0, 0), ("a", 4, 0, 0), -1, -1, ("a", 0, 0, 1), -1, ("g", 0, 0, 0), ("a", 2, 0, 0), ("a", 1, 0, 0),
    ("a", 4, 0, 1), ("s", 0, 0, 0), ("g", 1, 0, 0), ("g", 2, 0, 0), ("g", 0, 0, 1), ("s", 0, 0, 1), ("a", 0, 0, 2),
    ("s", 0, 0, 2), ("s", 0, 0, 3), ("g", 2, 0, 1), ("g", 5, 0, 0), ("g", 1, 0, 1), ("s", 1, 0, 0), ("a", 3, 0, 0),
    ("s", 2, 0, 0), ("s", 1, 0, 1), ("s", 2, 0, 1), ("g", 0, 0, 2), ("a", 1, 0, 1), ("a", 2, 0, 1), ("a", 4, 0, 2),
    ("s", 2, 0, 2), ("s", 2, 0, 3), ("a", 1, 0, 2), ("s", 1, 0, 2), ("g", 1, 0, 2), ("s", 1, 0, 3), ("g", 5, 0, 1),
    ("a", 2, 0, 2), ("g", 2, 0, 2), ("g", 0, 0, 3), ("s", 3, 0, 0), ("a", 0, 0, 3), ("a", 3, 0, 1), ("g", 2, 0, 3),
    ("g", 5, 0, 2), ("g", 1, 0, 3), ("s", 3, 0, 1), ("a", 4, 0, 3), ("a", 2, 0, 3), ("a", 1, 0, 3), ("a", 3, 0, 2),
    ("g", 5, 0, 3), ("s", 3, 0, 2), ("a", 5, 0, 0), ("a", 3, 0, 3), ("a", 5, 0, 1), ("s", 3, 0, 3),
)


def dot(a, b):
    return jnp.dot(a, b, preferred_element_type=f32)


def dot_bt(a, b):
    return lax.dot_general(a, b, (((1,), (1,)), ((), ())), preferred_element_type=f32)


def dot_at(a, b):
    return lax.dot_general(a, b, (((0,), (0,)), ((), ())), preferred_element_type=f32)


def halves(a):
    high = a.astype(bf16)
    return high, (a - high.astype(f32)).astype(bf16)


def spans(width, size=512):
    return [slice(start, min(start + size, width)) for start in range(0, width, size)]


def head_lanes(rows, width, start, head_width):
    head = lax.broadcasted_iota(jnp.int32, (rows, width), 0)
    lane = lax.broadcasted_iota(jnp.int32, (rows, width), 1) + start
    return (lane >= head * head_width) & (lane < (head + 1) * head_width)


def pick_left(rows, slot):
    out = lax.broadcasted_iota(jnp.int32, (4 * GROUPS, 16 * GROUPS), 0)
    src = lax.broadcasted_iota(jnp.int32, (4 * GROUPS, 16 * GROUPS), 1)
    return (src == (out // 4) * 16 + slot * 4 + out % 4).astype(bf16)


def norm_parts(values):
    center = jnp.mean(values, axis=-1, keepdims=True)
    centered = values - center
    spread = jnp.mean(centered * centered, axis=-1, keepdims=True)
    rstd = lax.rsqrt(spread + epsilon)
    return centered * rstd, rstd


def call(kernel, out_shape, name, **kw):
    return pl.pallas_call(
        kernel,
        out_shape=out_shape,
        name=name,
        compiler_params=pltpu.CompilerParams(vmem_limit_bytes=VMEM_LIMIT),
        **kw,
    )


def sds(shape, dtype=f32):
    return jax.ShapeDtypeStruct(shape, dtype)


def first_part(x_ref, mod_ref, perm_ref, wf_ref, bf_ref, xp_ref, gate_ref, run_ref, runt_ref):
    length = x_ref.shape[0]
    normed, _ = norm_parts(x_ref[...].astype(f32))
    hidden = (normed * (1.0 + mod_ref[1:2, :]) + mod_ref[0:1, :]).astype(bf16)
    for cols in spans(x_ref.shape[1]):
        xp_ref[:, cols] = dot(hidden, perm_ref[:, cols]).astype(bf16)

    gate = dot(xp_ref[...], wf_ref[...]) + bf_ref[...]
    gate_ref[...] = gate
    decay = -(jnp.maximum(gate, 0.0) + jnp.log1p(jnp.exp(-jnp.abs(gate))))
    row = lax.broadcasted_iota(jnp.int32, (length, length), 0)
    col = lax.broadcasted_iota(jnp.int32, (length, length), 1)
    tri = (row >= col).astype(bf16)
    high, rest = halves(decay)
    rest32 = decay - high.astype(f32)
    low = (rest32 - rest.astype(f32)).astype(bf16)
    inclusive = dot(tri, high) + dot(tri, rest) + dot(tri, low)
    exclusive = inclusive - decay
    run_ref[0] = inclusive
    run_ref[1] = exclusive
    runt_ref[0] = inclusive.T
    runt_ref[1] = exclusive.T


def project_part(slot, xp_ref, main_ref, left_ref, write):
    pick = pick_left(None, slot)
    main_rows = rows_in(main_ref)

    for cols in spans(xp_ref.shape[1]):
        main = main_ref[..., cols].reshape(main_rows, -1)
        left = dot(pick, left_ref[..., cols].reshape(16 * GROUPS, -1)).astype(bf16)
        write(cols, dot(xp_ref[:, :main_rows], main) + dot(xp_ref[:, main_rows:], left))


def two_terms(scale):
    return jnp.concatenate(halves(scale), axis=1)


def spread_heads(terms, cols, head_width):
    spread = head_lanes(LANES, cols.stop - cols.start, cols.start, head_width).astype(bf16)
    return dot(terms, jnp.concatenate([spread, spread], axis=0))


def head_sums(values, cols, head_width):
    return dot_bt(values, head_lanes(LANES, cols.stop - cols.start, cols.start, head_width).astype(bf16))


def own_block(shape, row_start, lane_start, head_width):
    row = lax.broadcasted_iota(jnp.int32, (shape[0], 1), 0) + row_start
    lane = lax.broadcasted_iota(jnp.int32, (1, shape[1]), 1) + lane_start
    same = None
    for head in range(
        max(row_start, lane_start) // head_width,
        min(row_start + shape[0] - 1, lane_start + shape[1] - 1) // head_width + 1,
    ):
        low, high = head * head_width, (head + 1) * head_width
        both = ((row >= low) & (row < high)) & ((lane >= low) & (lane < high))
        same = both if same is None else same | both
    if same is None:
        return jnp.broadcast_to(row < 0, shape)
    return same


def rows_in(ref):
    return int(np.prod(ref.shape[:-1]))


def near_lanes(cols, width, head_width):
    low = cols.start // head_width * head_width // LANES * LANES
    last = (cols.stop - 1) // head_width
    return slice(low, min(width, -(-(last + 1) * head_width // LANES) * LANES))


def unfolded(ref, way, near, cols, head_width):
    folded = ref[way, near, :]
    return jnp.concatenate([
        jnp.where(own_block(folded.shape, near.start, at, head_width), folded, 0)
        for at in range(cols.start, cols.stop, LANES)
    ], axis=1)


def state_part(head_width, ways, left, right_ref, scale_ref, out_ref):
    width = right_ref.shape[1]
    terms = [two_terms(scale_ref[way]) for way in range(ways)]
    for cols in spans(width, 2 * LANES):
        near = near_lanes(cols, width, head_width)
        mask = own_block((cols.stop - cols.start, near.stop - near.start), cols.start, near.start, head_width)
        for way in range(ways):
            scaled = left(cols).astype(f32) * spread_heads(terms[way], cols, head_width)
            product = jnp.where(mask, dot_at(scaled.astype(bf16), right_ref[:, near]), 0.0)
            total = product[:, :LANES]
            for at in range(LANES, near.stop - near.start, LANES):
                total = total + product[:, at : at + LANES]
            out_ref[way, cols, :] = total.astype(bf16)


def edge_part(source, out):
    for t in range(source.shape[1] // LANES):
        out(t, source[:, t * LANES : (t + 1) * LANES])


def pair_weights(run_ref, runt_ref, head, rows, length):
    count = rows.size
    own = lax.broadcasted_iota(jnp.int32, (count, LANES), 1) == head
    inc_t = jnp.sum(jnp.where(own, run_ref[0, rows, :], 0.0), axis=1, keepdims=True)
    exc_t = jnp.sum(jnp.where(own, run_ref[1, rows, :], 0.0), axis=1, keepdims=True)
    inc_s = runt_ref[0, pl.ds(head, 1), :]
    exc_s = runt_ref[1, pl.ds(head, 1), :]
    weight = jnp.exp(jnp.minimum(inc_t - inc_s, exc_s - exc_t))
    row = lax.broadcasted_iota(jnp.int32, (count, length), 0) + rows.start
    col = lax.broadcasted_iota(jnp.int32, (count, length), 1)
    return jnp.where(row == col, 2.0, weight)


def window_of(head, heads, head_width):
    start = pl.multiple_of(((head * head_width) // LANES - head // (heads - 1)) * LANES, LANES)
    return pl.ds(start, 2 * LANES), start


def own_lanes(rows, start, head, head_width):
    lane = lax.broadcasted_iota(jnp.int32, (rows, 2 * LANES), 1) + start
    return (lane >= head * head_width) & (lane < (head + 1) * head_width)


def row_blocks(length):
    size = min(length, 2 * LANES)
    return [pl.ds(start, size) for start in range(0, length, size)]


def mix_part(head_width, heads, low, high, qkv_ref, run_ref, runt_ref, mix_ref):
    length, width = mix_ref.shape

    @pl.loop(low // 2, high // 2)
    def _(pair):
        for odd in range(2):
            head = pair * 2 + odd
            win, start = window_of(head, heads, head_width)
            mask = own_lanes(length, start, head, head_width)
            keys = jnp.where(mask, qkv_ref[1, :, win], 0)
            vals = jnp.where(mask, qkv_ref[2, :, win], 0)
            for rows in row_blocks(length):
                weight = pair_weights(run_ref, runt_ref, head, rows, length)
                score = dot_bt(qkv_ref[0, rows, win], keys)
                mix_ref[rows, win] += dot((score * weight).astype(bf16), vals)


def fill_padded(pad_ref, rims_ref, middle):
    length = pad_ref.shape[0] - 2 * GRID
    pad_ref[:GRID, :] = rims_ref[0]
    pad_ref[GRID : GRID + length, :] = middle
    pad_ref[GRID + length :, :] = rims_ref[1]


def mixed_part(head_width, ways, qkv_ref, taken_ref, state_ref, taps_ref, vpad, mix_ref, mixed):
    length, width = mix_ref.shape
    place = lax.broadcasted_iota(jnp.int32, (length, LANES), 0) % GRID
    sums = jnp.zeros((length, LANES), f32)
    terms = [two_terms(taken_ref[way]) for way in range(ways)]
    for cols in spans(width, 2 * LANES):
        gained = mix_ref[:, cols]
        near = near_lanes(cols, width, head_width)
        for way in range(ways):
            block = unfolded(state_ref, way, near, cols, head_width)
            gained = gained + spread_heads(terms[way], cols, head_width) * dot(qkv_ref[0, :, near], block)
        mix_ref[:, cols] = gained
        sums = sums + head_sums((gained * gained).astype(bf16), cols, head_width)
    inverse = two_terms(lax.rsqrt(sums * (1.0 / head_width) + epsilon))
    for span in spans(width, 2 * LANES):
        normed = mix_ref[:, span] * spread_heads(inverse, span, head_width)
        for start in range(span.start, span.stop, LANES):
            cols = slice(start, start + LANES)
            conv = jnp.zeros((length, LANES), f32)
            for lateral in range(3):
                column = jnp.zeros((length, LANES), f32)
                for vertical in range(3):
                    tap = taps_ref[3 * vertical + lateral : 3 * vertical + lateral + 1, cols]
                    column = column + tap * vpad[vertical * GRID : vertical * GRID + length, cols].astype(f32)
                if lateral == 0:
                    column = jnp.where(place > 0, pltpu.roll(column, 1, 0), 0.0)
                if lateral == 2:
                    column = jnp.where(place < GRID - 1, pltpu.roll(column, length - 1, 0), 0.0)
                conv = conv + column
            own = normed[:, start - span.start : start - span.start + LANES]
            mixed[:, cols] = (own + (conv + taps_ref[9:10, cols])).astype(bf16)


def permute_part(source, perm_ref, out_ref):
    for cols in spans(perm_ref.shape[1]):
        out_ref[:, cols] = dot(source[...], perm_ref[:, cols]).astype(bf16)


def branch_part(x_ref, mod_ref, mixedp_ref, main_ref, left_ref, branch_ref, middle_ref):
    def write(cols, branch):
        branch_ref[:, cols] = branch.astype(bf16)
        middle_ref[:, cols] = x_ref[:, cols].astype(f32) + mod_ref[2:3, cols] * branch

    project_part(3, mixedp_ref, main_ref, left_ref, write)


def second_hidden(mod_ref, middle_ref, mixed):
    normed, _ = norm_parts(middle_ref[...])
    mixed[...] = (normed * (1.0 + mod_ref[4:5, :]) + mod_ref[3:4, :]).astype(bf16)


def project_kernel(xp_ref, main_ref, left_ref, out_ref):
    def write(cols, value):
        out_ref[0, :, cols] = value.astype(bf16)

    project_part(pl.program_id(0), xp_ref, main_ref, left_ref, write)


def state_kernel(head_width, ways, left_ref, right_ref, scale_ref, edge_ref, out_ref):
    width = right_ref.shape[1]
    state_part(head_width, ways, lambda cols: left_ref[:, cols], right_ref, scale_ref, out_ref)
    for way in range(ways):

        def write(t, value, way=way):
            out_ref[way, width + t * GRID : width + (t + 1) * GRID, :] = value

        edge_part(edge_ref[way], write)


def mix_kernel(head_width, heads, qkv_ref, run_ref, runt_ref, mix_ref):
    mix_ref[...] = jnp.zeros_like(mix_ref)
    mix_part(head_width, heads, 0, heads, qkv_ref, run_ref, runt_ref, mix_ref)


def after_kernel(
    head_width, ways, x_ref, mod_ref, perm_ref, qkv_ref, mix_in_ref, taken_ref, state_ref, rims_ref, taps_ref,
    main_ref, left_ref, mix_ref, mixedp_ref, branch_ref, middle_ref, h2p_ref, vpad, mixed,
):
    mix_ref[...] = mix_in_ref[...]
    fill_padded(vpad, rims_ref, qkv_ref[2])
    mixed_part(head_width, ways, qkv_ref, taken_ref, state_ref, taps_ref, vpad, mix_ref, mixed)
    permute_part(mixed, perm_ref, mixedp_ref)
    branch_part(x_ref, mod_ref, mixedp_ref, main_ref, left_ref, branch_ref, middle_ref)
    second_hidden(mod_ref, middle_ref, mixed)
    permute_part(mixed, perm_ref, h2p_ref)


def gelu_both(v):
    c = np.float32(np.sqrt(2.0 / np.pi))
    square = v * v
    th = jnp.tanh(c * (v + np.float32(0.044715) * (square * v)))
    half = 0.5 * (1.0 + th)
    slope = half + 0.5 * v * (1.0 - th * th) * (c * (1.0 + np.float32(3 * 0.044715) * square))
    return v * half, slope


def feed_kernel(
    h2p_ref, cot_ref, mod_ref, middle_ref, main_ref, left_ref, down_ref,
    out_ref, gh_ref, gup_ref, gleft_ref, gdown_ref, ggate_ref, down_acc, gdi, h2pt, act, actt, gup, left,
):
    j = pl.program_id(0)
    main_rows = main_ref.shape[0] * main_ref.shape[1]
    length, width = h2p_ref.shape

    @pl.when(j == 0)
    def _():
        gdi[...] = (cot_ref[...].astype(f32) * mod_ref[5:6, :]).astype(bf16)
        h2pt[...] = h2p_ref[...].T
        down_acc[...] = jnp.zeros_like(down_acc)
        gh_ref[...] = jnp.zeros_like(gh_ref)
        gleft_ref[...] = jnp.zeros_like(gleft_ref)

    pick = pick_left(None, j)
    left[...] = dot(pick, left_ref[...].reshape(16 * GROUPS, width)).astype(bf16)
    for cols in spans(width):
        main = main_ref[:, :, cols].reshape(main_rows, -1)
        up = dot(h2p_ref[:, :main_rows], main) + dot(h2p_ref[:, main_rows:], left[:, cols])
        value, slope = gelu_both(up)
        value = value.astype(bf16)
        act[:, cols] = value
        actt[cols, :] = value.T
        gup[:, cols] = (dot_bt(gdi[...], down_ref[cols, :]) * slope).astype(bf16)
    for cols in spans(width):
        down_acc[:, cols] += dot(act[...], down_ref[:, cols])
        gdown_ref[:, cols] = dot(actt[...], gdi[:, cols]).astype(bf16)
        gup_ref[:, :, cols] = dot(h2pt[:main_rows, :], gup[:, cols]).astype(bf16).reshape(GROUPS, 32, -1)
        part = dot(h2pt[main_rows:, :], gup[:, cols]).astype(bf16)
        gleft_ref[:, :, cols] += dot_at(pick, part).astype(bf16).reshape(GROUPS, 16, -1)
    gh_ref[:, main_rows:] += dot_bt(gup[...], left[...])
    for cols in spans(main_rows):
        gh_ref[:, cols] += dot_bt(gup[...], main_ref[cols.start // 32 : cols.stop // 32].reshape(-1, width))

    @pl.when(j == pl.num_programs(0) - 1)
    def _():
        out_ref[...] = (middle_ref[...] + mod_ref[5:6, :] * down_acc[...]).astype(bf16)
        ggate_ref[...] = jnp.sum(cot_ref[...].astype(f32) * down_acc[...], axis=0, keepdims=True)


def unpermute(perm_ref, source_ref, out_ref):
    source = source_ref[...].astype(bf16)
    for cols in spans(perm_ref.shape[0]):
        out_ref[:, cols] = dot_bt(source, perm_ref[cols, :])


def norm_back(normed, rstd, factor, grad):
    scaled = grad * (1.0 + factor)
    mean = jnp.mean(scaled, axis=-1, keepdims=True)
    along = jnp.mean(scaled * normed, axis=-1, keepdims=True)
    return (scaled - mean - normed * along) * rstd


def second_part(
    head_width, ghp_ref, perm_ref, middle_ref, mod_ref, cot_ref, branch_ref, mixedp_ref, mix_ref, main_ref, left_ref,
    gmid_ref, gmixed_ref, gmix_ref, gout_ref, gleft_ref, sums_ref, gh, gb, turned,
):
    length, width = middle_ref.shape
    main_rows = rows_in(main_ref)
    unpermute(perm_ref, ghp_ref, gh)
    yield
    normed, rstd = norm_parts(middle_ref[...])
    grad = gh[...]
    sums_ref[0:1, :] = jnp.sum(grad, axis=0, keepdims=True)
    sums_ref[1:2, :] = jnp.sum(grad * normed, axis=0, keepdims=True)
    grad_middle = cot_ref[...].astype(f32) + norm_back(normed, rstd, mod_ref[4:5, :], grad)
    gmid_ref[...] = grad_middle
    sums_ref[2:3, :] = jnp.sum(grad_middle * branch_ref[...].astype(f32), axis=0, keepdims=True)
    sums_ref[3:8, :] = jnp.zeros((5, width), f32)
    gb[...] = (grad_middle * mod_ref[2:3, :]).astype(bf16)
    pick = pick_left(None, 3)
    turned[...] = mixedp_ref[...].T
    yield
    for cols in spans(width):
        gout_ref[..., cols] = dot(turned[:main_rows, :], gb[:, cols]).astype(bf16).reshape(gout_ref.shape[:-1] + (-1,))
        part = dot(turned[main_rows:, :], gb[:, cols]).astype(bf16)
        gleft_ref[..., cols] = dot_at(pick, part).astype(bf16).reshape(gleft_ref.shape[:-1] + (-1,))
    left = dot(pick, left_ref[...].reshape(16 * GROUPS, width)).astype(bf16)
    gh[:, main_rows:] = dot_bt(gb[...], left)
    for cols in spans(main_rows):
        gh[:, cols] = dot_bt(gb[...], main_ref[cols.start // 32 : cols.stop // 32].reshape(-1, width))
    gb[...] = gh[...].astype(bf16)
    yield
    for cols in spans(width):
        gmixed_ref[:, cols] = dot_bt(gb[...], perm_ref[cols, :]).astype(bf16)

    sums = jnp.zeros((length, LANES), f32)
    dots = jnp.zeros((length, LANES), f32)
    for cols in spans(width, 2 * LANES):
        mix = mix_ref[:, cols]
        sums = sums + head_sums((mix * mix).astype(bf16), cols, head_width)
        for term in halves(mix * gmixed_ref[:, cols].astype(f32)):
            dots = dots + head_sums(term, cols, head_width)
    inverse = lax.rsqrt(sums * (1.0 / head_width) + epsilon)
    along = two_terms(dots * (1.0 / head_width) * inverse * inverse * inverse)
    inverse = two_terms(inverse)
    for cols in spans(width, 2 * LANES):
        gmix_ref[:, cols] = (
            gmixed_ref[:, cols].astype(f32) * spread_heads(inverse, cols, head_width)
            - mix_ref[:, cols] * spread_heads(along, cols, head_width)
        ).astype(bf16)
    yield


def second_kernel(head_width, *refs):
    for _ in second_part(head_width, *refs):
        pass


def pairs_part(head_width, heads, low, high, qkv_ref, gmix_ref, run_ref, runt_ref, gq_ref, gk_ref, gv_ref, rows_ref, cols_ref, held):
    length, width = gmix_ref.shape

    @pl.loop(low, high)
    def _(head):
        win, start = window_of(head, heads, head_width)
        mask = own_lanes(length, start, head, head_width)
        queries = jnp.where(mask, qkv_ref[0, :, win], 0)
        keys = jnp.where(mask, qkv_ref[1, :, win], 0)
        vals = jnp.where(mask, qkv_ref[2, :, win], 0)
        grads = jnp.where(mask, gmix_ref[:, win], 0)
        own = lax.broadcasted_iota(jnp.int32, (LANES, LANES), 1) == head
        row = lax.broadcasted_iota(jnp.int32, (LANES, LANES), 0)
        col = lax.broadcasted_iota(jnp.int32, (LANES, LANES), 1)
        columns = [None, None]
        for rows in row_blocks(length):
            weight = pair_weights(run_ref, runt_ref, head, rows, length)
            at = slice(rows.start, rows.start + rows.size)
            score = dot_bt(queries[at], keys) * weight
            grad = dot_bt(grads[at], vals)
            both = score * grad
            held[0, rows, :] = score.astype(bf16)
            held[1, rows, :] = (grad * weight).astype(bf16)
            for step in range(rows.size // LANES):
                first = rows.start + step * LANES
                strip = both[step * LANES : (step + 1) * LANES]
                middle = strip[:, first : first + LANES]
                pieces = [
                    (0, strip[:, :first], jnp.where(row > col, middle, 0.0)),
                    (1, strip[:, first + LANES :], jnp.where(row < col, middle, 0.0)),
                ]
                for way, part, corner in pieces:
                    total = jnp.sum(corner, axis=1, keepdims=True)
                    lines = [jnp.sum(corner, axis=0, keepdims=True)]
                    if first if way == 0 else length - first - LANES:
                        total = total + jnp.sum(part, axis=1, keepdims=True)
                        lines.insert(0 if way == 0 else 1, jnp.sum(part, axis=0, keepdims=True))
                    blank = jnp.zeros((1, length - sum(line.shape[1] for line in lines)), f32)
                    if blank.shape[1]:
                        lines.insert(len(lines) if way == 0 else 0, blank)
                    line = jnp.concatenate(lines, axis=1)
                    columns[way] = line if columns[way] is None else columns[way] + line
                    rows_ref[way, first : first + LANES, :] += jnp.where(own, total, 0.0)
        for way in range(2):
            cols_ref[way, pl.ds(head, 1), :] = columns[way]
        gq_ref[:, win] += dot(held[1], keys)
        gk_ref[:, win] += dot_at(held[1], queries)
        gv_ref[:, win] += dot_at(held[0], grads)


def pairs_kernel(head_width, heads, qkv_ref, gmix_ref, run_ref, runt_ref, gq_ref, gk_ref, gv_ref, rows_ref, cols_ref, held):
    for ref in (gq_ref, gk_ref, gv_ref, rows_ref, cols_ref):
        ref[...] = jnp.zeros_like(ref)
    pairs_part(
        head_width, heads, 0, heads, qkv_ref, gmix_ref, run_ref, runt_ref, gq_ref, gk_ref, gv_ref, rows_ref, cols_ref, held
    )


def carry_part(
    head_width, ways, early, qkv_ref, gmix_ref, gq_in, gk_in, gv_in, rows_ref, cols_ref, taken_ref, given_ref, gate_ref,
    state_ref, leave_ref, through, vpad, gpad, taps_ref, gqkv_ref, ggate_ref, conv_ref, bias_ref,
):
    length, width = gmix_ref.shape
    place = lax.broadcasted_iota(jnp.int32, (length, LANES), 0) % GRID
    taken_sums = [jnp.zeros((length, LANES), f32) for _ in range(ways)]
    given_sums = [jnp.zeros((length, LANES), f32) for _ in range(ways)]
    take_terms = [two_terms(taken_ref[way]) for way in range(ways)]
    give_terms = [two_terms(given_ref[way]) for way in range(ways)]
    for span in spans(width, 2 * LANES):
        near = near_lanes(span, width, head_width)
        gq, gk, gv = gq_in[:, span], gk_in[:, span], gv_in[:, span]
        for way in range(ways):
            take = spread_heads(take_terms[way], span, head_width)
            give = spread_heads(give_terms[way], span, head_width)
            back_q = take * dot_bt(gmix_ref[:, near], unfolded(state_ref, way, span, near, head_width))
            gq = gq + back_q
            for term in halves(qkv_ref[0, :, span].astype(f32) * back_q):
                taken_sums[way] = taken_sums[way] + head_sums(term, span, head_width)
            back_k = give * dot_bt(qkv_ref[2, :, near], unfolded(leave_ref, way, span, near, head_width))
            gk = gk + back_k
            for term in halves(qkv_ref[1, :, span].astype(f32) * back_k):
                given_sums[way] = given_sums[way] + head_sums(term, span, head_width)
            gv = gv + give * dot(qkv_ref[1, :, near], unfolded(leave_ref, way, near, span, head_width))
        gqkv_ref[0, :, span] = gq.astype(bf16)
        gqkv_ref[1, :, span] = gk.astype(bf16)
        for first in range(span.start, span.stop, LANES):
            cols = slice(first, first + LANES)
            grad = gpad[GRID : GRID + length, cols].astype(f32)
            total = gv[:, first - span.start : first - span.start + LANES]
            for lateral in range(3):
                b = lateral - 1
                column = jnp.zeros((length, LANES), f32)
                for vertical in range(3):
                    tap = taps_ref[3 * vertical + lateral : 3 * vertical + lateral + 1, cols]
                    start = (2 - vertical) * GRID
                    column = column + tap * gpad[start : start + length, cols].astype(f32)
                shifted = grad
                if b == -1:
                    column = jnp.where(place < GRID - 1, pltpu.roll(column, length - 1, 0), 0.0)
                    shifted = jnp.where(place < GRID - 1, pltpu.roll(grad, length - 1, 0), 0.0)
                if b == 1:
                    column = jnp.where(place > 0, pltpu.roll(column, 1, 0), 0.0)
                    shifted = jnp.where(place > 0, pltpu.roll(grad, 1, 0), 0.0)
                total = total + column
                for vertical in range(3):
                    window = vpad[vertical * GRID : vertical * GRID + length, cols].astype(f32)
                    conv_ref[3 * vertical + lateral : 3 * vertical + lateral + 1, cols] = jnp.sum(
                        window * shifted, axis=0, keepdims=True
                    )
            conv_ref[9:10, cols] = jnp.sum(grad, axis=0, keepdims=True)
            gqkv_ref[2, :, cols] = total.astype(bf16)
        if span.start // (2 * LANES) in (1, 3) or span.stop == width:
            yield
    conv_ref[10:16, :] = jnp.zeros((6, width), f32)

    row = lax.broadcasted_iota(jnp.int32, (length, length), 0)
    col = lax.broadcasted_iota(jnp.int32, (length, length), 1)
    before = (col < row).astype(bf16)
    upto = (col <= row).astype(bf16)

    def summed(product, matrix, value):
        high, rest = halves(value)
        low = (value - high.astype(f32) - rest.astype(f32)).astype(bf16)
        return product(matrix, high) + product(matrix, rest) + product(matrix, low)

    def columns(way):
        lines = cols_ref[way]
        if lines.shape[0] < LANES:
            lines = jnp.concatenate([lines, jnp.zeros((LANES - lines.shape[0], length), f32)], axis=0)
        return lines.T

    ahead = rows_ref[0] - columns(0)
    behind = rows_ref[1] - columns(1)
    if ways == 2:
        ahead, behind = ahead + taken_sums[0], behind + taken_sums[1]
        given_ahead, given_behind = given_sums
    else:
        ahead = ahead + taken_sums[0] * (1.0 - early)
        behind = behind + taken_sums[0] * early
        given_ahead, given_behind = given_sums[0] * early, given_sums[0] * (1.0 - early)
    grad_decay = (
        summed(dot_at, upto, ahead)
        + summed(dot, before, given_ahead)
        + summed(dot, upto, behind)
        + summed(dot_at, before, given_behind)
        + through
    )
    gate = gate_ref[...]
    small = jnp.exp(-jnp.abs(gate))
    sigmoid = jnp.where(gate >= 0, 1.0, small) / (1.0 + small)
    grad_gate = (-grad_decay * sigmoid).astype(bf16)
    lane = lax.broadcasted_iota(jnp.int32, grad_gate.shape, 1)
    grad_gate = jnp.where(lane < width // head_width, grad_gate.astype(f32), 0.0)
    ggate_ref[...] = grad_gate.astype(bf16)
    bias_ref[...] = jnp.sum(grad_gate, axis=0, keepdims=True)
    yield


def carry_kernel(
    head_width, ways, qkv_ref, gmix_ref, gq_in, gk_in, gv_in, rows_ref, cols_ref, taken_ref, given_ref, gate_ref,
    state_ref, leave_ref, through_ref, early_ref, gmixed_ref, grims_ref, vrims_ref, taps_ref,
    gqkv_ref, ggate_ref, conv_ref, bias_ref, vpad, gpad,
):
    fill_padded(vpad, vrims_ref, qkv_ref[2])
    fill_padded(gpad, grims_ref, gmixed_ref[...])
    for _ in carry_part(
        head_width, ways, early_ref[...], qkv_ref, gmix_ref, gq_in, gk_in, gv_in, rows_ref, cols_ref, taken_ref,
        given_ref, gate_ref, state_ref, leave_ref, through_ref[...], vpad, gpad, taps_ref, gqkv_ref, ggate_ref, conv_ref,
        bias_ref,
    ):
        pass


def projection_grads(slot, turned, grad_ref, gmain_ref, gleft_ref):
    pick = pick_left(None, slot)
    main_rows = rows_in(gmain_ref)
    for cols in spans(grad_ref.shape[1]):
        grad = grad_ref[:, cols]
        gmain_ref[..., cols] = dot(turned[:main_rows, :], grad).astype(bf16).reshape(gmain_ref.shape[:-1] + (-1,))
        part = dot(turned[main_rows:, :], grad).astype(bf16)
        gleft_ref[..., cols] += dot_at(pick, part).astype(bf16).reshape(gleft_ref.shape[:-1] + (-1,))


def projection_back(slot, grad_ref, main_ref, left_ref, gh_ref):
    width = grad_ref.shape[1]
    main_rows = rows_in(main_ref)
    left = dot(pick_left(None, slot), left_ref[...].reshape(16 * GROUPS, width)).astype(bf16)
    gh_ref[:, main_rows:] += dot_bt(grad_ref[...], left)
    for cols in spans(main_rows):
        gh_ref[:, cols] += dot_bt(grad_ref[...], main_ref[cols.start // 32 : cols.stop // 32].reshape(-1, width))


def weights_kernel(
    xp_ref, gqkv_ref, ggate_ref, wf_ref, main_ref, left_ref, gout_left_ref, gmain_ref, gleft_ref, gforget_ref, gh_ref, turned
):
    slot = pl.program_id(0)

    @pl.when(slot == 0)
    def _():
        turned[...] = xp_ref[...].T
        gleft_ref[...] = gout_left_ref[...]
        gh_ref[...] = dot_bt(ggate_ref[...], wf_ref[...])
        gforget_ref[...] = dot(turned[...], ggate_ref[...])

    projection_grads(slot, turned, gqkv_ref.at[0], gmain_ref, gleft_ref)
    projection_back(slot, gqkv_ref.at[0], main_ref, left_ref, gh_ref)


def last_part(ghp_ref, perm_ref, x_ref, mod_ref, gmid_ref, gin_ref, sums_ref, gh):
    unpermute(perm_ref, ghp_ref, gh)
    normed, rstd = norm_parts(x_ref[...].astype(f32))
    grad = gh[...]
    sums_ref[0:1, :] = jnp.sum(grad, axis=0, keepdims=True)
    sums_ref[1:2, :] = jnp.sum(grad * normed, axis=0, keepdims=True)
    gin_ref[...] = gmid_ref[...] + norm_back(normed, rstd, mod_ref[1:2, :], grad)


def ring_place(z):
    return z + (z // 2) * (5 - 2 * z)


class Here:
    def __init__(self):
        row, x = lax.axis_index("dp"), lax.axis_index("seq")
        z, y, core = row // 4, (row // 2) % 2, row % 2
        self.x, self.y, self.z, self.core = x, y, z, core
        self.p = ring_place(z)
        place = lambda z, y, core, x: ((z * 2 + y) * 2 + core, x)
        self.next = place(ring_place((self.p + 1) % 4), y, core, x)
        self.prev = place(ring_place((self.p + 3) % 4), y, core, x)
        self.over_y = place(z, 1 - y, core, x)
        self.over_x = place(z, y, core, 1 - x)
        self.sibling = place(z, y, 1 - core, x)

    def ring_z(self, back):
        return ring_place((self.p + 8 - back) % 4)

    def greet(self):
        barrier = pltpu.get_barrier_semaphore()
        for device in (self.next, self.prev, self.over_y, self.over_x, self.sibling):
            pl.semaphore_signal(barrier, inc=1, device_id=device, device_id_type=pl.DeviceIdType.MESH)
        pl.semaphore_wait(barrier, 5)


def push(source, target, send, recv, device):
    copy = pltpu.make_async_remote_copy(
        src_ref=source, dst_ref=target, send_sem=send, recv_sem=recv, device_id=device,
        device_id_type=pl.DeviceIdType.MESH,
    )
    copy.start()
    return copy


def routes(rows):
    tiles = rows // 16
    third = 2 if tiles >= 8 else 0
    first = -(-(tiles - third) // 2)
    cuts = [0, 16 * first, 16 * (tiles - third), rows]
    return [pl.ds(low, high - low) for low, high in zip(cuts, cuts[1:])]


class Gather:
    def __init__(self, tag, here, ins, outs, sems):
        self.here, self.ins, self.outs, self.sems = here, ins, outs, sems
        self.flights, self.todo, self.own = {}, {}, {}
        for i in range(len(ins)):
            a, b, c = routes(ins[i].shape[0])
            self.todo[tag, 0, i, 0] = (), functools.partial(self.along_z, i, 0)
            for s in range(4):
                if s:
                    self.todo[tag, 0, i, s] = (("z", i, s - 1),), functools.partial(self.along_z, i, s)
                self.todo[tag, 1, i, s] = (("a1", i, s),), functools.partial(self.second, i, s, 0)
                waits = [("a2", i, s)]
                if b.size:
                    self.todo[tag, 2, i, s] = (("b1", i, s),), functools.partial(self.second, i, s, 1)
                    waits.append(("b2", i, s))
                if c.size:
                    waits.append(("cy", i, 0) if s == 0 else ("cz", i, s - 1))
                    self.todo[tag, 4, i, s] = (waits[-1],), functools.partial(self.third, i, s)
                    waits[-1] = ("c", i, s)
                self.todo[tag, 5, i, s] = tuple(waits), functools.partial(self.across, i, s)
            if c.size:
                self.todo[tag, 3, i, 0] = (("cx", i, 0),), functools.partial(self.third_over_y, i)

    def send(self, key, number, source, target, device):
        i, s = key[1:]
        self.flights[key] = push(source, target, self.sems[0].at[number, i, s], self.sems[1].at[number, i, s], device)

    def start(self):
        here = self.here
        for i, block in enumerate(self.ins):
            target = self.outs[i].at[here.z, here.y, here.core, here.x]
            self.own[i] = pltpu.make_async_copy(block, target, self.sems[2].at[i])
            self.own[i].start()

    def run(self, name):
        waits, action = self.todo.pop(name)
        for key in waits:
            if key[0] != "c":
                self.flights[key].wait_recv()
        action()

    def settle(self, i):
        if i in self.own:
            self.own.pop(i).wait()

    def along_z(self, i, s):
        here = self.here
        a, b, c = routes(self.ins[i].shape[0])
        slot = self.outs[i].at[here.ring_z(s), here.y, here.core, here.x]
        held = self.ins[i] if s == 0 else slot
        if s < 3:
            both = pl.ds(0, a.size + b.size)
            self.send(("z", i, s), 0, held.at[both], slot.at[both], here.next)
        self.send(("a1", i, s), 1, held.at[a], slot.at[a], here.over_y)
        if b.size:
            self.send(("b1", i, s), 2, held.at[b], slot.at[b], here.over_x)
        if s == 0 and c.size:
            self.send(("cx", i, 0), 5, held.at[c], slot.at[c], here.over_x)

    def second(self, i, s, half):
        here, out = self.here, self.outs[i]
        a, b, c = routes(self.ins[i].shape[0])
        z = here.ring_z(s)
        if s == 0:
            self.settle(i)
        if half:
            block = out.at[z, here.y, here.core, :, b]
            self.send(("b2", i, s), 4, block, block, here.over_y)
        else:
            block = out.at[z, :, here.core, here.x, a]
            self.send(("a2", i, s), 3, block, block, here.over_x)

    def third_over_y(self, i):
        here = self.here
        c = routes(self.ins[i].shape[0])[2]
        self.settle(i)
        block = self.outs[i].at[here.z, here.y, here.core, :, c]
        self.send(("cy", i, 0), 6, block, block, here.over_y)

    def third(self, i, s):
        here = self.here
        c = routes(self.ins[i].shape[0])[2]
        if s < 3:
            block = self.outs[i].at[here.ring_z(s), :, here.core, :, c]
            self.send(("cz", i, s), 7, block, block, here.next)

    def across(self, i, s):
        here = self.here
        block = self.outs[i].at[here.ring_z(s), :, here.core]
        self.send(("core", i, s), 8, block, block, here.sibling)

    def arrived(self, i, places=range(4)):
        for s in places:
            self.flights["core", i, s].wait_recv()

    def finish(self):
        for copy in self.flights.values():
            copy.wait_send()


def gather_sems(count):
    dma = pltpu.SemaphoreType.DMA
    return [dma((9, count, 4)), dma((9, count, 4)), dma((count,))]


def gathered_shape(block):
    return sds((4, 2, 2, 2) + block.shape, block.dtype)


def add_rows(target, source, lead, low, size):
    chunk = 16

    @pl.loop(0, size // chunk)
    def _(r):
        start = pl.multiple_of(r * chunk, chunk)
        here, there = pl.ds(low + start, chunk), pl.ds(start, chunk)
        for at in lead:
            target[at + (here,)] = target[at + (here,)] + source[at + (there,)]


class Scatter:
    def __init__(self, tag, here, ins, final, scratch):
        (
            self.acc, self.mate, self.one_a, self.one_b, self.two_rows, self.ring_rows, self.ring_c, self.c_y, self.c_x,
            self.send_sem, self.recv_sem, self.load_sem,
        ) = scratch
        self.here, self.ins, self.final = here, ins, final
        self.rows = self.acc.shape[3]
        self.a, self.b, self.c = routes(self.rows)
        self.flights, self.loads, self.todo, self.released = {}, {}, {}, set()
        for k in range(4):
            self.todo[tag, 0, 0, k] = (("core", k),), functools.partial(self.from_sibling, k)
            self.todo[tag, 1, 0, k] = (("a1", k),), functools.partial(self.first_sum, k, 0)
            waits = [("a2", k)]
            if self.b.size:
                self.todo[tag, 2, 0, k] = (("b1", k),), functools.partial(self.first_sum, k, 1)
                waits.append(("b2", k))
            if k:
                waits.append(("z", k - 1))
            self.todo[tag, 3, 0, k] = tuple(waits), functools.partial(self.second_sum, k)
            if self.c.size:
                waits = (("c", k), ("cz", k - 1)) if k else (("c", k),)
                self.todo[tag, 4, 0, k] = waits, functools.partial(self.third_sum, k)
        if self.c.size:
            self.todo[tag, 5, 0, 0] = (("cy", 0),), self.third_over_y
            self.todo[tag, 5, 0, 1] = (("cx", 0), ("own", 0)), self.third_over_x

    def send(self, key, number, source, target, device, piece=0):
        at = (number + piece, key[1])
        self.flights[key] = push(source, target, self.send_sem.at[at], self.recv_sem.at[at], device)

    def pieces(self, k):
        z, low = self.here.ring_z(k + 1), 0
        for number, ref in enumerate(self.ins):
            if len(ref.shape) == 3:
                for y in range(2):
                    yield (
                        number + y, lambda core, y=y: ref.at[pl.ds(8 * z + 4 * y + 2 * core, 2)], lambda slot, y=y: slot.at[y]
                    )
            elif len(ref.shape) == 5:
                yield number, lambda core, ref=ref: ref.at[:, core], lambda slot: slot
            else:
                span = pl.ds(low, ref.shape[4])
                low += ref.shape[4]
                yield (
                    number, lambda core, ref=ref: ref.at[z, :, core], lambda slot, span=span: slot.at[:, :, span]
                )

    def load(self, k):
        for number, source, target in self.pieces(k):
            self.loads[k, number] = pltpu.make_async_copy(
                source(self.here.core), target(self.acc.at[k]), self.load_sem.at[k, number]
            )
            self.loads[k, number].start()

    def to_sibling(self, k):
        for number, source, target in self.pieces(k):
            self.send(
                ("core", k, number), 8, source(1 - self.here.core), target(self.mate.at[k]), self.here.sibling, number
            )

    def offer(self, k):
        self.load(k)
        self.to_sibling(k)

    def release(self, k):
        for number, _, _ in self.pieces(k):
            self.flights["core", k, number].wait_send()
        self.released.add(k)

    def prepare(self):
        for k in range(4):
            self.load(k)

    def start(self):
        for k in range(4):
            self.to_sibling(k)

    def run(self, name):
        waits, action = self.todo.pop(name)
        for key in waits:
            if key[0] == "core":
                for number, _, _ in self.pieces(key[1]):
                    self.loads[key[1], number].wait()
                    self.flights["core", key[1], number].wait_recv()
            elif key[0] not in ("c", "own"):
                self.flights[key].wait_recv()
        action()

    def from_sibling(self, k):
        here, acc = self.here, self.acc.at[k]
        add_rows(acc, self.mate.at[k], [(a, b) for a in range(2) for b in range(2)], 0, self.rows)
        self.send(("a1", k), 0, acc.at[:, 1 - here.x, self.a], self.one_a.at[k], here.over_x)
        if self.b.size:
            self.send(("b1", k), 1, acc.at[1 - here.y, :, self.b], self.one_b.at[k], here.over_y)

    def first_sum(self, k, half):
        here, acc = self.here, self.acc.at[k]
        if half:
            add_rows(acc.at[here.y], self.one_b.at[k], [(0,), (1,)], self.b.start, self.b.size)
            self.send(
                ("b2", k), 3, acc.at[here.y, 1 - here.x, self.b], self.two_rows.at[k, self.b], here.over_x
            )
        else:
            add_rows(acc.at[:, here.x], self.one_a.at[k], [(0,), (1,)], self.a.start, self.a.size)
            self.send(
                ("a2", k), 2, acc.at[1 - here.y, here.x, self.a], self.two_rows.at[k, self.a], here.over_y
            )

    def second_sum(self, k):
        here = self.here
        size = self.a.size + self.b.size
        mine = self.acc.at[k, here.y, here.x]
        add_rows(mine, self.two_rows.at[k], [()], 0, size)
        if k:
            add_rows(mine, self.ring_rows.at[k - 1], [()], 0, size)
        if k < 3:
            self.send(("z", k), 4, mine.at[pl.ds(0, size)], self.ring_rows.at[k], here.next)
        elif not self.c.size:
            self.final(mine)

    def third_sum(self, k):
        here, acc = self.here, self.acc.at[k]
        if k:
            add_rows(acc, self.ring_c.at[k - 1], [(a, b) for a in range(2) for b in range(2)], self.c.start, self.c.size)
        if k < 3:
            self.send(("cz", k), 5, acc.at[:, :, self.c], self.ring_c.at[k], here.next)
        else:
            self.send(("cy", 0), 6, acc.at[1 - here.y, :, self.c], self.c_y, here.over_y)

    def third_over_y(self):
        here, acc = self.here, self.acc.at[3]
        add_rows(acc.at[here.y], self.c_y, [(0,), (1,)], self.c.start, self.c.size)
        self.send(("cx", 0), 7, acc.at[here.y, 1 - here.x, self.c], self.c_x, here.over_x)

    def third_over_x(self):
        mine = self.acc.at[3, self.here.y, self.here.x]
        add_rows(mine, self.c_x, [()], self.c.start, self.c.size)
        self.final(mine)

    def finish(self):
        for key, copy in self.flights.items():
            if key[0] != "core" or key[1] not in self.released:
                copy.wait_send()


def scatter_scratch(block):
    dma = pltpu.SemaphoreType.DMA
    rows, lanes, kind = sum(b.shape[-2] for b in block), block[0].shape[-1], block[0].dtype
    a, b, c = (max(span.size, 16) for span in routes(rows))
    both = sum(span.size for span in routes(rows)[:2])
    return [
        pltpu.VMEM((4, 2, 2, rows, lanes), kind), pltpu.VMEM((4, 2, 2, rows, lanes), kind),
        pltpu.VMEM((4, 2, a, lanes), kind), pltpu.VMEM((4, 2, b, lanes), kind),
        pltpu.VMEM((4, both, lanes), kind), pltpu.VMEM((3, both, lanes), kind),
        pltpu.VMEM((3, 2, 2, c, lanes), kind), pltpu.VMEM((2, c, lanes), kind), pltpu.VMEM((c, lanes), kind),
        dma((11, 4)), dma((11, 4)), dma((4, 3)),
    ]


def in_order(plan, chain, networks):
    pieces = iter(chain)
    for item in plan:
        if item == -1:
            next(pieces)()
        else:
            networks[item[0]].run(item)
    assert next(pieces, None) is None and not any(net.todo for net in networks.values())


def small_rows(cond, forget, taps, place):
    at = lax.rem(place * taps.shape[0], LANES)
    taps = lax.dynamic_update_slice(jnp.zeros((4 * LANES,), bf16), taps, (at,)).reshape(4, LANES)
    cond = cond.reshape(-1, LANES)
    forget = forget.reshape(36, -1)
    return jnp.concatenate([
        jnp.pad(cond, ((0, 16 - cond.shape[0]), (0, 0))), jnp.pad(taps, ((0, 12), (0, 0))),
        jnp.pad(forget, ((0, 12), (0, LANES - forget.shape[1]))),
    ])


def unpack_small(small, taps_share, wf_ref, taps_ref, flat):
    wf_ref[: 32 * GROUPS, :] = small[:, 32:64, :].reshape(32 * GROUPS, LANES)
    wf_ref[32 * GROUPS :, :] = dot(pick_left(None, 0), small[:, 64:80, :].reshape(16 * GROUPS, LANES)).astype(bf16)
    flat[...] = jnp.zeros_like(flat)
    for d in range(GROUPS):
        row = d * taps_share // LANES
        flat[row : row + 4, :] += small[d, 16:32, :].astype(f32)[:4]
    tiles = taps_ref.shape[1] // LANES
    taps_ref[...] = jnp.zeros_like(taps_ref)
    for k in range(10):
        for t in range(tiles):
            taps_ref[k : k + 1, t * LANES : (t + 1) * LANES] = flat[k * tiles + t : k * tiles + t + 1, :]


def pack_rows(sources, wide, left, out):
    for j, (source, first, per_row) in enumerate(sources):
        if first == 0:
            wide[: source.shape[0], :] = source[...].astype(f32)
        for t in range(out.shape[1] // LANES):
            cols = slice(t * LANES, (t + 1) * LANES)
            rows = wide[pl.ds(first + t, 36, stride=per_row), :]
            out[32 * j : 32 * j + 32, cols] = rows[:32].astype(bf16)
            left[4 * j : 4 * j + 4, cols] = rows[32:]
    out[128:144, :] = left[...].astype(bf16)


def fill_permutation(perm_ref):
    width = perm_ref.shape[0]
    at = lax.broadcasted_iota(jnp.int32, (1, width), 1)
    late = at - 32 * GROUPS
    order = jnp.where(late < 0, (at >> 5) * 36 + (at & 31), (late >> 2) * 36 + 32 + (late & 3))
    for rows in spans(width, 2 * LANES):
        row = lax.broadcasted_iota(jnp.int32, (rows.stop - rows.start, width), 0) + rows.start
        perm_ref[rows, :] = (row == order).astype(bf16)


def forward_kernel(
    head_width, heads, taps_share, x_ref, ada_ref, bf_ref, own_s, query_ref, key_ref, value_ref, out_ref, up_ref,
    all_s, all_a, all_u, xp_out, qkv_out, mix_out, mixedp_out, branch_out, middle_out, h2p_out, perm_out,
    mod_ref, wf_ref, taps_ref, gate_ref, run_ref, runt_ref, state_ref, rims_ref, given_ref, taken_ref,
    xp_ref, qkv_ref, mix_ref, mixedp_ref, branch_ref, middle_ref, h2p_ref, perm_ref,
    own_a, own_u, wide, rows_left, small, flat, partial, main, left, outbox, inbox, vpad, mixed, load_sem, swap_sem, *rest,
):
    length, width = x_ref.shape
    tiles = width // LANES
    here = Here()
    lower = here.x == 0
    pack_rows([(ref, 0, tiles) for ref in (query_ref, key_ref, value_ref, out_ref)], wide, rows_left, own_a)
    pack_rows([(up_ref, j * tiles, 4 * tiles) for j in range(4)], wide, rows_left, own_u)
    first = Gather("f", here, (own_s,), (all_s,), rest[:3])
    gather = Gather("g", here, (own_a, own_u), (all_a, all_u), rest[3:6])

    def to_mod(total):
        for k in range(6):
            for t in range(tiles):
                mod_ref[k : k + 1, t * LANES : (t + 1) * LANES] = total[k * tiles + t : k * tiles + t + 1, :]
        mod_ref[6:8, :] = jnp.zeros((2, width), f32)

    scatter = Scatter("s", here, [partial], to_mod, rest[6:])
    stores, loads = [], []

    def fetch(number, source, target):
        copy = pltpu.make_async_copy(source, target, load_sem.at[number])
        copy.start()
        return copy

    def modulation():
        first.arrived(0)
        fetch(5, all_s, small).wait()
        me = ((here.z * 2 + here.y) * 2 + here.core) * 2 + here.x
        row = lax.broadcasted_iota(jnp.int32, (width, LANES), 0)
        lane = lax.broadcasted_iota(jnp.int32, (width, LANES), 1)
        pick = ((row == lane + me * 36) & (lane < 36)).astype(bf16)
        lines = small[...].reshape(GROUPS, 80, LANES)[:, :16, :].astype(f32)
        mine = jnp.zeros((GROUPS, LANES), f32)
        for t in range(tiles):
            cond = lines[:, t, :]
            cond = (cond / (1.0 + jnp.exp(-cond))).astype(bf16)
            mine = mine + dot(cond, pick[t * LANES : (t + 1) * LANES])
        lane = lax.broadcasted_iota(jnp.int32, mine.shape, 1)
        mine = jnp.where(lane == 36, 1.0, mine).astype(bf16)
        for t in range(6 * tiles):
            partial[:, t, :] = dot(mine, ada_ref[:, t * LANES : (t + 1) * LANES])
        partial[:, 6 * tiles :, :] = jnp.zeros((GROUPS, 64 - 6 * tiles, LANES), f32)
        scatter.prepare()
        scatter.start()

    def small_arrays():
        unpack_small(small[...].reshape(GROUPS, 80, LANES), taps_share, wf_ref, taps_ref, flat)

    def norm_one():
        first_part(x_ref, mod_ref, perm_ref, wf_ref, bf_ref, xp_ref, gate_ref, run_ref, runt_ref)
        stores.extend([fetch(6, xp_ref, xp_out), fetch(13, perm_ref, perm_out)])
        total = run_ref[0, length - 1 : length, :]
        given_ref[0] = jnp.where(lower, jnp.exp(total - run_ref[0]), jnp.exp(run_ref[1]))
        taken_ref[0] = jnp.where(lower, jnp.exp(total - run_ref[1]), jnp.exp(run_ref[0]))
        mix_ref[...] = jnp.zeros_like(mix_ref)

    def load(slot):
        loads.append(fetch(slot, all_a.at[:, :, :, :, pl.ds(32 * slot, 32)], main.at[slot % 2]))

    def project(slot):
        if slot == 0:
            gather.arrived(0)
            others = fetch(4, all_a.at[:, :, :, :, pl.ds(128, 16)], left)
            load(0)
            load(1)
            others.wait()
        loads[slot].wait()

        def write(cols, value):
            qkv_ref[slot, :, cols] = value.astype(bf16)

        project_part(slot, xp_ref, main.at[slot % 2], left, write)
        if slot < 2:
            load(slot + 2)
        else:
            stores.append(fetch(7, qkv_ref, qkv_out))

    def states():
        state_part(head_width, 1, lambda cols: qkv_ref[1, :, cols], qkv_ref.at[2], given_ref, outbox)
        edge = pl.multiple_of((1 - here.x) * (length - GRID), GRID)

        def write_edge(t, value):
            outbox[0, width + t * GRID : width + (t + 1) * GRID, :] = value

        edge_part(qkv_ref[2, pl.ds(edge, GRID), :], write_edge)
        stores.append(push(outbox, inbox, swap_sem.at[0], swap_sem.at[1], here.over_x))

    def mix(part):
        mix_part(head_width, heads, part * heads // 4, (part + 1) * heads // 4, qkv_ref, run_ref, runt_ref, mix_ref)

    def mixing():
        swap = stores.pop()
        swap.wait_recv()
        state_ref[0] = inbox[0, :width, :]
        for t in range(tiles):
            cols = slice(t * LANES, (t + 1) * LANES)
            rows = inbox[0, width + t * GRID : width + (t + 1) * GRID, :]
            rims_ref[0, :, cols] = jnp.where(lower, 0, rows).astype(bf16)
            rims_ref[1, :, cols] = jnp.where(lower, rows, 0).astype(bf16)
        fill_padded(vpad, rims_ref, qkv_ref[2])
        mixed_part(head_width, 1, qkv_ref, taken_ref, state_ref, taps_ref, vpad, mix_ref, mixed)
        stores.append(fetch(8, mix_ref, mix_out))
        swap.wait_send()

    def turn():
        permute_part(mixed, perm_ref, mixedp_ref)
        stores.append(fetch(9, mixedp_ref, mixedp_out))

    def branch():
        loads[3].wait()
        branch_part(x_ref, mod_ref, mixedp_ref, main.at[1], left, branch_ref, middle_ref)
        stores.extend([fetch(10, branch_ref, branch_out), fetch(11, middle_ref, middle_out)])

    def norm_two():
        second_hidden(mod_ref, middle_ref, mixed)
        permute_part(mixed, perm_ref, h2p_ref)
        stores.append(fetch(12, h2p_ref, h2p_out))

    chain = [functools.partial(fill_permutation, perm_ref), modulation, small_arrays, norm_one]
    chain += [functools.partial(project, slot) for slot in range(3)] + [states]
    chain += [functools.partial(mix, part) for part in range(4)] + [mixing, turn, branch, norm_two]
    first.start()
    gather.start()
    here.greet()
    in_order(FORWARD_PLAN, chain, {"f": first, "g": gather, "s": scatter})
    gather.arrived(1)
    for network in (first, gather, scatter):
        network.finish()
    for copy in stores:
        copy.wait()


def forward_fused(x, ada, bf, small, shards, heads, taps_share):
    length, width = x.shape
    head_width = width // heads
    message = width + width // LANES * GRID
    anywhere, vm = pl.BlockSpec(memory_space=pl.ANY), pl.BlockSpec(memory_space=pltpu.VMEM)
    rows, wide = (length, width), (length, LANES)
    bulk = (
        sds(rows, bf16), sds((3,) + rows, bf16), sds(rows), sds(rows, bf16), sds(rows, bf16), sds(rows), sds(rows, bf16),
        sds((width, width), bf16),
    )
    kept = (
        sds((8, width)), sds((width, LANES), bf16), sds((16, width)), sds(wide), sds((2,) + wide), sds((2, LANES, length)),
        sds((1, width, LANES), bf16), sds((2, GRID, width), bf16), sds((1,) + wide), sds((1,) + wide),
    )
    partial = sds((GROUPS, 64, LANES))
    own = sds((144, width), bf16)
    dma = pltpu.SemaphoreType.DMA
    out = pl.pallas_call(
        functools.partial(forward_kernel, head_width, heads, taps_share),
        out_shape=tuple(gathered_shape(b) for b in (small, own, own)) + bulk + kept,
        in_specs=[vm] * 9,
        out_specs=(anywhere,) * (3 + len(bulk)) + (vm,) * len(kept),
        scratch_shapes=[pltpu.VMEM(b.shape, b.dtype) for b in bulk] + [
            pltpu.VMEM(own.shape, bf16), pltpu.VMEM(own.shape, bf16), pltpu.VMEM(shards[4].shape, f32),
            pltpu.VMEM((16, width), f32),
            pltpu.VMEM((4, 2, 2, 2) + small.shape, bf16), pltpu.VMEM((96, LANES), f32),
            pltpu.VMEM(partial.shape, f32), pltpu.VMEM((2, 4, 2, 2, 2, 32, width), bf16),
            pltpu.VMEM((4, 2, 2, 2, 16, width), bf16), pltpu.VMEM((1, message, LANES), bf16),
            pltpu.VMEM((1, message, LANES), bf16), pltpu.VMEM((length + 2 * GRID, width), bf16), pltpu.VMEM(rows, bf16),
            dma((14,)), dma((2,)),
        ] + gather_sems(1) + gather_sems(2) + scatter_scratch([partial]),
        compiler_params=pltpu.CompilerParams(collective_id=0, has_side_effects=True, vmem_limit_bytes=VMEM_LIMIT),
        name="forward",
    )(x, ada, bf, small, *shards)
    gathered = [g.reshape((GROUPS,) + g.shape[4:]) for g in out[:3]]
    return gathered, out[3 : 3 + len(bulk)], out[3 + len(bulk) :]


def feed_fused_kernel(
    h2p, cot, mod_ref, flat_d, up_in, middle_in,
    all_d, out_out, gh_out, gup_out, gleft_ref, ggate_ref, down_own,
    gdi, h2pt, act, slope, actt, gup, main, left, left_own, down, down_acc, gh, stage_d, stage_u, own_d, wide, load_sem, *rest,
):
    length, width = h2p.shape
    main_rows = GROUPS * 32
    here = Here()
    gather = Gather("g", here, (own_d,), (all_d,), rest[:3])
    scatter = Scatter("d", here, [stage_d], plain_final(down_own), rest[3:])
    order = [here.ring_z(k + 1) for k in range(4)]

    def fetch(number, source, target):
        copy = pltpu.make_async_copy(source, target, load_sem.at[number])
        copy.start()
        return copy

    def load_up(k, number):
        rows = pl.ds(pl.multiple_of(32 * order[k], 32), 32)
        return fetch(number, up_in.at[:, rows], main.at[k % 2])

    def load_down(k):
        gather.arrived(0, [(k + 1) % 4])
        return fetch(8 + k, all_d.at[order[k]], down.at[k % 2])

    def left_rows(k):
        return dot(pick_left(None, order[k]), left[...].reshape(16 * GROUPS, width)).astype(bf16)

    def start():
        gdi[...] = (cot[...].astype(f32) * mod_ref[5:6, :]).astype(bf16)
        h2pt[...] = h2p[...].T
        gleft_ref[...] = jnp.zeros_like(gleft_ref)
        others.wait()

    def up_step(k):
        loads[k].wait()
        left_own[...] = left_rows(k)
        for cols in spans(width):
            up = dot(h2p[:, :main_rows], main[k % 2, :, :, cols].reshape(main_rows, -1))
            up = up + dot(h2p[:, main_rows:], left_own[:, cols])
            value, rate = gelu_both(up)
            value = value.astype(bf16)
            act[k, :, cols] = value
            actt[cols, :] = value.T
            slope[k, :, cols] = rate.astype(bf16)
        loads.append(load_up(k + 2, k + 2) if k < 2 else load_up(k - 2, k + 2))

    def down_grad(k):
        if k > 0:
            scatter.release(k - 1)
        for cols in spans(width):
            stage_d[:, :, :, :, cols] = dot(actt[...], gdi[:, cols]).astype(bf16).reshape(2, 2, 2, width // 8, -1)
        scatter.offer(k)

    def back_act(k):
        load_down(k).wait()
        rows_of = down[k % 2].reshape(width, width)
        for cols in spans(width):
            gup[:, cols] = (dot_bt(gdi[...], rows_of[cols]) * slope[k, :, cols].astype(f32)).astype(bf16)

    def down_step(k):
        rows_of = down[k % 2].reshape(width, width)
        for cols in spans(width):
            part = dot(act[k], rows_of[:, cols])
            if k == 0:
                down_acc[:, cols] = part
            else:
                down_acc[:, cols] += part
    def back_hidden(k):
        loads[4 + k].wait()
        for cols in spans(main_rows):
            part = dot_bt(gup[...], main[k % 2, cols.start // 32 : cols.stop // 32].reshape(-1, width))
            if k == 0:
                gh[:, cols] = part
            else:
                gh[:, cols] += part
        part = dot_bt(gup[...], left_rows(k))
        if k == 0:
            gh[:, main_rows:] = part
        else:
            gh[:, main_rows:] += part
        if k < 2:
            loads.append(load_up(k + 2, 6 + k))

    def up_grad(k):
        if k > 0:
            stores[k - 1].wait()
        projection_grads(order[k], h2pt, gup, stage_u, gleft_ref)
        rows = pl.ds(pl.multiple_of(32 * order[k], 32), 32)
        stores.append(fetch(13 + k, stage_u, gup_out.at[:, rows]))

    def end():
        keep = fetch(17, gh, gh_out)
        ggate_ref[...] = jnp.sum(cot[...].astype(f32) * down_acc[...], axis=0, keepdims=True)
        keep.wait()
        fetch(18, middle_in, gh).wait()
        for cols in spans(width):
            act[0, :, cols] = (gh[:, cols] + mod_ref[5:6, cols] * down_acc[:, cols]).astype(bf16)
        stores.append(fetch(19, act.at[0], out_out))

    chain = [start]
    for k in range(4):
        chain += [functools.partial(up_step, k), functools.partial(down_grad, k)]
    for k in range(4):
        chain += [functools.partial(step, k) for step in (back_act, down_step, back_hidden, up_grad)]
    others = fetch(12, up_in.at[:, pl.ds(128, 16)], left)
    loads = [load_up(0, 0), load_up(1, 1)]
    stores = []
    wide[...] = flat_d[...].astype(f32)
    for t in range(width // LANES):
        rows = wide[pl.ds(t, own_d.shape[0], stride=width // LANES), :]
        own_d[:, t * LANES : (t + 1) * LANES] = rows.astype(bf16)
    gather.start()
    here.greet()
    in_order(FEED_PLAN, chain + [end], {"d": scatter, "g": gather})
    scatter.finish()
    gather.finish()
    stores[3].wait()
    stores[4].wait()


def feed_fused(h2p, cot, mod, flat_d, up_w, middle):
    length, width = h2p.shape
    anywhere, vm = pl.BlockSpec(memory_space=pl.ANY), pl.BlockSpec(memory_space=pltpu.VMEM)
    rows = (length, width)
    dma = pltpu.SemaphoreType.DMA
    stage = (2, 2, 2, width // 8, width)
    own = sds((width // 8, width), bf16)
    return pl.pallas_call(
        feed_fused_kernel,
        out_shape=(
            gathered_shape(own), sds(rows, bf16), sds(rows), sds((GROUPS, 128, width), bf16),
            sds((GROUPS, 16, width), bf16), sds((1, width)), sds(flat_d.shape),
        ),
        in_specs=[vm] * 4 + [anywhere] * 2,
        out_specs=(anywhere,) * 4 + (vm,) * 3,
        scratch_shapes=[
            pltpu.VMEM(rows, bf16), pltpu.VMEM((width, length), bf16), pltpu.VMEM((4,) + rows, bf16),
            pltpu.VMEM((4,) + rows, bf16), pltpu.VMEM((width, length), bf16), pltpu.VMEM(rows, bf16),
            pltpu.VMEM((2, GROUPS, 32, width), bf16), pltpu.VMEM((GROUPS, 16, width), bf16), pltpu.VMEM((128, width), bf16),
            pltpu.VMEM((2,) + stage, bf16), pltpu.VMEM(rows, f32), pltpu.VMEM(rows, f32), pltpu.VMEM(stage, bf16),
            pltpu.VMEM((GROUPS, 32, width), bf16), pltpu.VMEM(own.shape, bf16), pltpu.VMEM(flat_d.shape, f32), dma((20,)),
        ] + gather_sems(1) + scatter_scratch([sds(stage, bf16)]),
        compiler_params=pltpu.CompilerParams(
            collective_id=1, has_side_effects=True, vmem_limit_bytes=62 * 1024 * 1024
        ),
        name="feed",
    )(h2p, cot, mod, flat_d, up_w, middle)[1:]


def six(array):
    return array.reshape((4, 2, 2, 2) + array.shape[1:])


def flat_rows(out, first, value, per_row):
    for t in range(value.shape[1] // LANES):
        out[pl.ds(first + t, value.shape[0], stride=per_row), :] = value[:, t * LANES : (t + 1) * LANES]


def square_final(outs):
    def final(total):
        value = total[...].astype(f32)
        per_row = value.shape[1] // LANES
        for j, out in enumerate(outs):
            flat_rows(out, 0, value[32 * j : 32 * j + 32], per_row)
            flat_rows(out, 32 * per_row, value[128 + 4 * j : 132 + 4 * j], per_row)

    return final


def columns_final(out):
    def final(total):
        value = total[...].astype(f32)
        tiles = value.shape[1] // LANES
        for j in range(4):
            flat_rows(out, j * tiles, value[32 * j : 32 * j + 32], 4 * tiles)
            flat_rows(out, 32 * 4 * tiles + j * tiles, value[128 + 4 * j : 132 + 4 * j], 4 * tiles)

    return final


def plain_final(out):
    def final(total):
        value = total[...].astype(f32)
        flat_rows(out, 0, value, value.shape[1] // LANES)

    return final


def small_final(out):
    def final(total):
        out[...] = total[...]

    return final


def fill_small(block, gforget, conv, bias, flat, taps_share):
    tiles = conv.shape[1] // LANES
    for k in range(10):
        for t in range(tiles):
            flat[k * tiles + t : k * tiles + t + 1, :] = conv[k : k + 1, t * LANES : (t + 1) * LANES]
    flat[10 * tiles :, :] = jnp.zeros_like(flat[10 * tiles :, :])
    block[:, :32, :] = gforget[: 32 * GROUPS, :].reshape(GROUPS, 32, LANES)
    block[:, 40:, :] = jnp.broadcast_to(bias[...].reshape(1, 1, LANES), (GROUPS, 8, LANES))
    for d in range(GROUPS):
        at = 32 * GROUPS + 4 * d
        block[d, 32:36, :] = gforget[at : at + 4, :]
        row = d * taps_share // LANES
        block[d, 36:40, :] = flat[row : row + 4, :]


def backward_kernel(
    head_width, heads, taps_share,
    mod_ref, run_ref, runt_ref, taken_ref, given_ref, gate_ref, state_ref, vrims_ref, taps_ref,
    ghp_in, perm_in, middle_in, cot_in, branch_in, mixedp_in, mix_in, weight_in, qkv_in, xp_in, gup_in, gupl_in,
    gmid_out, gqkv_out, gmain_out, gout_out, small_out, gleft_ref, ggate_ref, sums_ref, up_ref,
    pool, perm, gmixed, gmix, gb, turned, main, left, qkv, gqkv, held, vpad, gpad, pair_rows, pair_cols,
    outbox, inbox, rims, leave, conv_ref, bias_ref, gforget_ref, flat, small, fetch_sem, swap_sem, *scratch,
):
    length, width = gmix.shape
    here = Here()
    lower = here.x == 0
    scatter = Scatter("u", here, [gup_in, gupl_in], columns_final(up_ref), scratch)
    scatter.prepare()

    def fetch(number, source, target):
        copy = pltpu.make_async_copy(source, target, fetch_sem.at[number])
        copy.start()
        return copy

    first = [
        fetch(0, ghp_in, pool.at[0]), fetch(1, perm_in, perm), fetch(2, middle_in, pool.at[1]), fetch(3, cot_in, qkv.at[0]),
        fetch(4, branch_in, qkv.at[1]), fetch(5, mixedp_in, qkv.at[2]),
        fetch(6, weight_in.at[:, pl.ds(96, 32)], main.at[0]), fetch(7, weight_in.at[:, pl.ds(128, 16)], left),
        fetch(8, mix_in, pool.at[2]),
    ]
    second = second_part(
        head_width, pool.at[0], perm, pool.at[1], mod_ref, qkv.at[0], qkv.at[1], qkv.at[2], pool.at[2], main.at[0], left,
        pool.at[1], gmixed, gmix, main.at[1], gleft_ref, sums_ref, pool.at[3], gb, turned,
    )
    gq, gk, gv = pool.at[0], pool.at[2], pool.at[3]
    early = jnp.where(lower, jnp.ones((1, LANES), f32), 0.0)
    carry = carry_part(
        head_width, 1, early, qkv, gmix, gq, gk, gv, pair_rows, pair_cols, taken_ref, given_ref, gate_ref, state_ref,
        leave, jnp.zeros((1, LANES), f32), vpad, gpad, taps_ref, gqkv, ggate_ref, conv_ref, bias_ref,
    )
    stores = []

    def begin():
        for copy in first:
            copy.wait()
        next(second)

    def states():
        again = fetch(9, qkv_in, qkv)
        stores.extend([fetch(10, pool.at[1], gmid_out), fetch(11, main.at[1], gout_out), fetch(12, xp_in, gb)])
        for ref in (gq, gk, gv, pair_rows, pair_cols):
            ref[...] = jnp.zeros_like(ref)
        again.wait()
        state_part(head_width, 1, lambda cols: qkv[0, :, cols], gmix, taken_ref, outbox)
        edge = pl.multiple_of((1 - here.x) * (length - GRID), GRID)

        def write_edge(t, value):
            outbox[0, width + t * GRID : width + (t + 1) * GRID, :] = value

        edge_part(gmixed[pl.ds(edge, GRID), :], write_edge)
        stores.append(push(outbox, inbox, swap_sem.at[0], swap_sem.at[1], here.over_x))

    def pairs(part):
        pairs_part(
            head_width, heads, part * heads // 4, (part + 1) * heads // 4, qkv, gmix, run_ref, runt_ref, gq, gk, gv,
            pair_rows, pair_cols, held,
        )

    def carry_first():
        swap = stores.pop()
        swap.wait_recv()
        leave[0] = inbox[0, :width, :]
        for t in range(width // LANES):
            cols = slice(t * LANES, (t + 1) * LANES)
            edge_rows = inbox[0, width + t * GRID : width + (t + 1) * GRID, :]
            rims[0, :, cols] = jnp.where(lower, 0, edge_rows).astype(bf16)
            rims[1, :, cols] = jnp.where(lower, edge_rows, 0).astype(bf16)
        fill_padded(vpad, vrims_ref, qkv[2])
        fill_padded(gpad, rims, gmixed[...])
        next(carry)
        swap.wait_send()

    def turn():
        stores.append(fetch(13, gqkv, gqkv_out))
        stores[2].wait()
        turned[...] = gb[...].T
        gforget_ref[...] = dot(turned[...], ggate_ref[...])
        fill_small(small, gforget_ref, conv_ref, bias_ref, flat, taps_share)
        fetch(17, small, small_out).wait()

    def weight(slot):
        buffer = main.at[slot % 2]
        if slot == 1:
            stores[1].wait()
        if slot == 2:
            stores[4].wait()
        projection_grads(slot, turned, gqkv.at[slot], buffer, gleft_ref)
        stores.append(fetch(14 + slot, buffer, gmain_out.at[:, pl.ds(32 * slot, 32)]))

    chain = [begin] + [functools.partial(next, second)] * 3 + [states]
    chain += [functools.partial(pairs, part) for part in range(4)] + [carry_first]
    chain += [functools.partial(next, carry)] * 3 + [turn] + [functools.partial(weight, slot) for slot in range(3)]
    here.greet()
    scatter.start()
    in_order(BACKWARD_PLAN, chain, {"u": scatter})
    scatter.finish()
    for number in (0, 3, 5, 6):
        stores[number].wait()


def backward_fused(heads, taps_share, small, arrays, grads):
    length, width = arrays[0].shape
    head_width = width // heads
    message = width + width // LANES * GRID
    anywhere, vm = pl.BlockSpec(memory_space=pl.ANY), pl.BlockSpec(memory_space=pltpu.VMEM)
    rows, wide = (length, width), (length, LANES)
    dma = pltpu.SemaphoreType.DMA
    return pl.pallas_call(
        functools.partial(backward_kernel, head_width, heads, taps_share),
        out_shape=(
            sds(rows), sds((3,) + rows, bf16), sds((GROUPS, 96, width), bf16), sds((GROUPS, 32, width), bf16),
            sds((GROUPS, 48, LANES)), sds((GROUPS, 16, width), bf16), sds(wide, bf16), sds((8, width)),
            sds((144 * width // LANES, LANES)),
        ),
        in_specs=[vm] * len(small) + [anywhere] * (len(arrays) + len(grads)),
        out_specs=(anywhere,) * 5 + (vm,) * 4,
        scratch_shapes=[
            pltpu.VMEM((4,) + rows, f32), pltpu.VMEM((width, width), bf16), pltpu.VMEM(rows, bf16), pltpu.VMEM(rows, bf16),
            pltpu.VMEM(rows, bf16), pltpu.VMEM((width, length), bf16),
            pltpu.VMEM((2, GROUPS, 32, width), bf16), pltpu.VMEM((GROUPS, 16, width), bf16), pltpu.VMEM((3,) + rows, bf16),
            pltpu.VMEM((3,) + rows, bf16), pltpu.VMEM((2, length, length), bf16),
            pltpu.VMEM((length + 2 * GRID, width), bf16), pltpu.VMEM((length + 2 * GRID, width), bf16),
            pltpu.VMEM((2,) + wide, f32), pltpu.VMEM((2, heads, length), f32),
            pltpu.VMEM((1, message, LANES), bf16), pltpu.VMEM((1, message, LANES), bf16),
            pltpu.VMEM((2, GRID, width), bf16), pltpu.VMEM((1, width, LANES), bf16), pltpu.VMEM((16, width), f32),
            pltpu.VMEM((1, LANES), f32), pltpu.VMEM((width, LANES), f32), pltpu.VMEM((96, LANES), f32),
            pltpu.VMEM((GROUPS, 48, LANES), f32), dma((18,)), dma((2,)),
        ] + scatter_scratch(grads),
        compiler_params=pltpu.CompilerParams(
            collective_id=3, has_side_effects=True, vmem_limit_bytes=62 * 1024 * 1024
        ),
        name="backward",
    )(*small, *arrays, *[six(g) for g in grads])


def finish_kernel(
    mod_ref, sums_two, gate_two, ggate_ref, wf_ref,
    weight_in, gqkv_in, perm_in, x_in, gmid_in, gmain_in, gout_in, gleft_in, small_in,
    gin_ref, all_mod, query_ref, key_ref, value_ref, out_ref, small_ref,
    main, left, gqkv, perm, x, gmid, ghp, gh, sums_one, own_mod, load_sem, *rest,
):
    width = perm.shape[0]
    here = Here()
    scatter = Scatter(
        "a", here, [gmain_in, gout_in, gleft_in], square_final((query_ref, key_ref, value_ref, out_ref)), rest[:12]
    )
    small = Scatter("s", here, [small_in], small_final(small_ref), rest[12:24])
    gather = Gather("g", here, (own_mod,), (all_mod,), rest[24:])
    scatter.prepare()
    small.prepare()

    def fetch(number, source, target):
        copy = pltpu.make_async_copy(source, target, load_sem.at[number])
        copy.start()
        return copy

    def load(slot):
        return fetch(slot, weight_in.at[:, pl.ds(32 * slot, 32)], main.at[slot % 2])

    grads = fetch(3, gqkv_in, gqkv)
    rest_rows = fetch(4, weight_in.at[:, pl.ds(128, 16)], left)
    loads = [load(0), load(1)]
    others = [fetch(5, perm_in, perm), fetch(6, x_in, x), fetch(7, gmid_in, gmid)]

    def back(slot):
        if slot == 0:
            ghp[...] = dot_bt(ggate_ref[...], wf_ref[...])
            grads.wait()
            rest_rows.wait()
        loads[slot].wait()
        projection_back(slot, gqkv.at[slot], main.at[slot % 2], left, ghp)
        if slot == 0:
            loads.append(load(2))

    def last():
        for copy in others:
            copy.wait()
        last_part(ghp, perm, x, mod_ref, gmid, gin_ref, sums_one, gh)
        lines = [sums_one[0:1, :], sums_one[1:2, :], sums_two[2:3, :], sums_two[0:1, :], sums_two[1:2, :], gate_two[...]]
        tiles = width // LANES
        for k, line in enumerate(lines):
            for t in range(tiles):
                own_mod[k * tiles + t : k * tiles + t + 1, :] = line[:, t * LANES : (t + 1) * LANES]
        own_mod[len(lines) * tiles :, :] = jnp.zeros_like(own_mod[len(lines) * tiles :, :])
        gather.start()

    here.greet()
    scatter.start()
    small.start()
    chain = [functools.partial(back, slot) for slot in range(3)] + [last]
    in_order(FINISH_PLAN, chain, {"a": scatter, "s": small, "g": gather})
    gather.arrived(0)
    for network in (scatter, small, gather):
        network.finish()


def finish_fused(small, arrays, grads, grad_small):
    length, width = arrays[3].shape
    anywhere, vm = pl.BlockSpec(memory_space=pl.ANY), pl.BlockSpec(memory_space=pltpu.VMEM)
    rows = (length, width)
    dma = pltpu.SemaphoreType.DMA
    own = sds((64, LANES))
    return pl.pallas_call(
        finish_kernel,
        out_shape=(sds(rows), gathered_shape(own)) + (sds((36 * width // LANES, LANES)),) * 4 + (sds(grad_small.shape[1:]),),
        in_specs=[vm] * len(small) + [anywhere] * (len(arrays) + len(grads) + 1),
        out_specs=(vm, anywhere) + (vm,) * 5,
        scratch_shapes=[
            pltpu.VMEM((2, GROUPS, 32, width), bf16), pltpu.VMEM((GROUPS, 16, width), bf16), pltpu.VMEM((3,) + rows, bf16),
            pltpu.VMEM((width, width), bf16), pltpu.VMEM(rows, bf16), pltpu.VMEM(rows, f32), pltpu.VMEM(rows, f32),
            pltpu.VMEM(rows, f32), pltpu.VMEM((8, width), f32), pltpu.VMEM(own.shape, f32), dma((8,)),
        ] + scatter_scratch(grads) + scatter_scratch([grad_small]) + gather_sems(1),
        compiler_params=pltpu.CompilerParams(
            collective_id=4, has_side_effects=True, vmem_limit_bytes=VMEM_LIMIT
        ),
        name="finish",
    )(*small, *arrays, *[six(g) for g in grads], six(grad_small))


def joined_states(messages, totals, width, head_width):
    count = lax.axis_size("seq")
    place = lax.axis_index("seq")

    def grid_rows(message):
        rows = message[width:].reshape(width // LANES, GRID, LANES)
        return rows.transpose(1, 0, 2).reshape(GRID, width)

    if count == 1:
        return jnp.zeros_like(messages[:, :width]), jnp.zeros((2, GRID, width), bf16)
    if count == 2:
        got = lax.ppermute(messages[0], "seq", [(0, 1), (1, 0)])
        rows = grid_rows(got)
        return got[None, :width], jnp.stack([jnp.where(place == 1, rows, 0), jnp.where(place == 0, rows, 0)])
    forward = [(i, i + 1) for i in range(count - 1)]
    backward = [(i + 1, i) for i in range(count - 1)]
    rims = jnp.stack([
        grid_rows(lax.ppermute(messages[0], "seq", forward)), grid_rows(lax.ppermute(messages[1], "seq", backward))
    ])
    states = lax.all_gather(messages[:, :width, :], "seq").astype(f32)
    passed = lax.all_gather(totals, "seq")
    heads_of_rows = np.arange(width) // head_width
    order = jnp.arange(count)
    ahead = jnp.zeros(states.shape[2:], f32)
    behind = jnp.zeros(states.shape[2:], f32)
    for source in range(count):
        between_up = jnp.where((order > source) & (order < place), 1.0, 0.0) @ passed
        between_down = jnp.where((order < source) & (order > place), 1.0, 0.0) @ passed
        ahead = ahead + jnp.where(source < place, jnp.exp(between_up), 0.0)[heads_of_rows, None] * states[source, 0]
        behind = behind + jnp.where(source > place, jnp.exp(between_down), 0.0)[heads_of_rows, None] * states[source, 1]
    return jnp.stack([ahead, behind]).astype(bf16), rims


def split_rows(matrix):
    grouped = matrix.reshape(GROUPS, -1, matrix.shape[1])
    return grouped[:, :32], grouped[:, 32:]


def pack_whole(parts, width):
    query, key, value, out, up, down = parts
    square = [piece.reshape(GROUPS, -1, width) for piece in (query, key, value, out)]
    up = up.reshape(GROUPS, square[0].shape[1], -1, width)
    columns = [up[:, :, j] for j in range(up.shape[2])]
    blocks = []
    for group in (square, columns):
        blocks.append(
            jnp.concatenate([piece[:, :32] for piece in group] + [piece[:, 32:] for piece in group], axis=1)
        )
    return blocks + [down.reshape(GROUPS, -1, width)]


def unpack_squares(block):
    return [
        jnp.concatenate([block[..., 32 * j : 32 * j + 32, :], block[..., 128 + 4 * j : 132 + 4 * j, :]], axis=-2)
        for j in range(4)
    ]


def unpack_blocks(blocks):
    squares = unpack_squares(blocks[0])
    columns = unpack_squares(blocks[1])
    lead = blocks[0].shape[:-2]
    up = jnp.stack(columns, axis=-2)
    return [piece.reshape(lead + (-1,)) for piece in squares] + [up.reshape(lead + (-1,)), blocks[2].reshape(lead + (-1,))]


def on_device(
    activations, conditioning, cotangent, w_ada, b_ada, w_query, w_key, w_value, w_forget, b_forget, conv_taps, w_out,
    w_up, w_down,
):
    _, length, width = activations.shape
    heads = b_forget.shape[0]
    head_width = width // heads
    data_count, seq_count = lax.axis_size("dp"), lax.axis_size("seq")
    devices = data_count * seq_count
    me = lax.axis_index("dp") * seq_count + lax.axis_index("seq")
    packed_here = (data_count, seq_count) == (16, 2)
    everywhere = ("dp", "seq")

    mod_width = 6 * width
    share = w_ada.shape[0]
    if share % mod_width == 0:
        ada_rows = share // mod_width
        first_row, inset = me * ada_rows, None
        ada_part = w_ada.reshape(ada_rows, mod_width)
    else:
        ada_rows = -(-share // mod_width) + 1
        first_row = (me * share) // mod_width
        inset = me * share - first_row * mod_width
        ada_part = lax.dynamic_update_slice(jnp.zeros((ada_rows * mod_width,), bf16), w_ada, (inset,))
        ada_part = ada_part.reshape(ada_rows, mod_width)

    def own_columns(cond_all):
        cond_act = jax.nn.silu(cond_all.astype(f32)).astype(bf16)
        cond_wide = jnp.pad(cond_act, ((0, 0), (0, ada_rows)))
        return lax.dynamic_slice_in_dim(cond_wide, first_row, ada_rows, axis=1)

    main_rows = 32 * GROUPS
    forget_b = jnp.pad(b_forget.astype(f32), (0, LANES - heads)).reshape(1, LANES)
    x = activations[0]
    cot = cotangent[0]
    rows = (length, width)

    def main_spec(block, columns=width):
        return pl.BlockSpec((GROUPS, 32, columns), block)

    def left_spec(block, columns=width):
        return pl.BlockSpec((GROUPS, 16, columns), block)

    def whole(shape):
        return pl.BlockSpec(shape, lambda *_: (0,) * len(shape))

    ways = 1 if seq_count == 2 else 2
    message_rows = width + width // LANES * GRID
    state_call = call(
        functools.partial(state_kernel, head_width, ways), sds((ways, message_rows, LANES), bf16), "states"
    )
    place = lax.axis_index("seq")

    def edges(values):
        low, high = values[:GRID], values[-GRID:]
        if ways == 1:
            return jnp.where(place == 0, high, low)[None]
        return jnp.stack([high, low])

    shards = (w_query, w_key, w_value, w_out, w_up, w_down)
    if packed_here:
        small = small_rows(conditioning[0], w_forget, conv_taps, me)
        bias_row = lax.dynamic_update_slice(jnp.zeros((1, mod_width), bf16), b_ada[None], (0, me * b_ada.shape[0]))
        ada = jnp.pad(jnp.concatenate([ada_part, bias_row]), ((0, LANES - 1 - ada_rows), (0, 0)))
        (small, attention_w, up_w), bulk, kept = forward_fused(
            x, ada, forget_b, small, [piece.reshape(-1, LANES) for piece in shards[:5]], heads, conv_taps.shape[0]
        )
        xp, qkv, mix, mixed_p, branch, middle, hidden_two_p, perm = bulk
        mod, forget_p, taps, gate_pre, run, runt, states, value_rims, given, taken = kept
        cond_part = own_columns(small[::seq_count, : width // LANES, :].reshape(data_count, width))
        output, ghp_two, gup_main, gup_left, ggate_two, g_down = feed_fused(
            hidden_two_p, cot, mod, w_down.reshape(-1, LANES), up_w, middle
        )
    else:
        lanes_at = np.arange(width)
        per_group = width // GROUPS
        order = np.where(
            lanes_at < main_rows,
            lanes_at // 32 * per_group + lanes_at % 32,
            (lanes_at - main_rows) // 4 * per_group + 32 + (lanes_at - main_rows) % 4,
        )
        perm = (jnp.arange(width, dtype=jnp.int32)[:, None] == jnp.asarray(order, jnp.int32)[None, :]).astype(bf16)
        small = [w_forget, conv_taps, b_ada]
        sizes = np.cumsum([0] + [piece.shape[0] for piece in small])
        small = lax.all_gather(jnp.concatenate(small), everywhere)
        forget_w = small[:, : sizes[1]].reshape(width, heads)
        taps = small[:, sizes[1] : sizes[2]].reshape(10, width).astype(f32)
        taps = jnp.pad(taps, ((0, 6), (0, 0)))
        ada_bias = small[:, sizes[2] :].reshape(6, width).astype(f32)
        forget_main, forget_left = split_rows(forget_w)
        forget_p = jnp.concatenate([forget_main.reshape(-1, heads), forget_left.reshape(-1, heads)])
        forget_p = jnp.pad(forget_p, ((0, 0), (0, LANES - heads)))
        cond_part = own_columns(lax.all_gather(conditioning, "dp", axis=0, tiled=True))
        partial_mod = jnp.dot(cond_part, ada_part, preferred_element_type=f32)
        mod = lax.psum(lax.psum_scatter(partial_mod, "dp", scatter_dimension=0, tiled=True), "seq")
        mod = jnp.pad(mod.reshape(6, width) + ada_bias, ((0, 2), (0, 0)))
        blocks = pack_whole([lax.all_gather(s, everywhere, axis=0, tiled=True) for s in shards], width)
        attention_w, up_w, down_w = blocks
        down_w = down_w.reshape(-1, width)
        xp, gate_pre, run, runt = call(
            first_part,
            (sds(rows, bf16), sds((length, LANES)), sds((2, length, LANES)), sds((2, LANES, length))),
            "first_norm",
        )(x, mod, perm, forget_p, forget_b)
        qkv = call(
            project_kernel,
            sds((3,) + rows, bf16),
            "project",
            grid=(3,),
            in_specs=[whole(rows), main_spec(lambda j: (0, j, 0)), left_spec(lambda j: (0, 8, 0))],
            out_specs=pl.BlockSpec((1,) + rows, lambda j: (j, 0, 0)),
        )(xp, attention_w, attention_w)
        total = run[0, -1]
        given = jnp.stack([jnp.exp(total - run[0]), jnp.exp(run[1])])
        taken = jnp.stack([jnp.exp(run[0]), jnp.exp(total - run[1])])
        if ways == 1:
            given = jnp.where(place == 0, given[0], given[1])[None]
            taken = jnp.where(place == 0, taken[1], taken[0])[None]
        messages = state_call(qkv[1], qkv[2], given, edges(qkv[2]))
        states, value_rims = joined_states(messages, total, width, head_width)
        mix_local = call(
            functools.partial(mix_kernel, head_width, heads), sds(rows), "mix"
        )(qkv, run, runt)
        mix, mixed_p, branch, middle, hidden_two_p = call(
            functools.partial(after_kernel, head_width, ways),
            (sds(rows), sds(rows, bf16), sds(rows, bf16), sds(rows), sds(rows, bf16)),
            "after",
            grid=(1,),
            in_specs=[
                whole(rows), whole((8, width)), whole((width, width)), whole((3,) + rows), whole(rows),
                whole((ways, length, LANES)), whole((ways, width, LANES)), whole((2, GRID, width)), whole((16, width)),
                main_spec(lambda i: (0, 3, 0)), left_spec(lambda i: (0, 8, 0)),
            ],
            out_specs=[whole(rows)] * 5,
            scratch_shapes=[pltpu.VMEM((length + 2 * GRID, width), bf16), pltpu.VMEM(rows, bf16)],
        )(x, mod, perm, qkv, mix_local, taken, states, value_rims, taps, attention_w, attention_w)
        output, ghp_two, gup_main, gup_left, gdown, ggate_two = call(
            feed_kernel,
            (
                sds(rows, bf16), sds(rows), sds((GROUPS, 128, width), bf16), sds((GROUPS, 16, width), bf16),
                sds(down_w.shape, bf16), sds((1, width)),
            ),
            "feed",
            grid=(4,),
            in_specs=[
                whole(rows), whole(rows), whole((8, width)), whole(rows), main_spec(lambda j: (0, j, 0)),
                left_spec(lambda j: (0, 8, 0)), pl.BlockSpec((width, width), lambda j: (j, 0)),
            ],
            out_specs=[
                whole(rows), whole(rows), main_spec(lambda j: (0, j, 0)), left_spec(lambda j: (0, 0, 0)),
                pl.BlockSpec((width, width), lambda j: (j, 0)), whole((1, width)),
            ],
            scratch_shapes=[
                pltpu.VMEM(rows, f32), pltpu.VMEM(rows, bf16), pltpu.VMEM((width, length), bf16), pltpu.VMEM(rows, bf16),
                pltpu.VMEM((width, length), bf16), pltpu.VMEM(rows, bf16), pltpu.VMEM((width - main_rows, width), bf16),
            ],
        )(hidden_two_p, cot, mod, middle, up_w, up_w, down_w)

    share_forget, share_taps, share_bias = w_forget.shape[0], conv_taps.shape[0], b_ada.shape[0]

    if packed_here:
        grad_middle, gqkv, gmain, gout_main, grad_small, gleft, grad_gate, sums_two, g_up = backward_fused(
            heads,
            share_taps,
            (mod, run, runt, taken, given, gate_pre, states, value_rims, taps),
            (ghp_two, perm, middle, cot, branch, mixed_p, mix, attention_w, qkv, xp),
            (gup_main, gup_left),
        )
        grad_input, mod_all, g_query, g_key, g_value, g_out, grad_small = finish_fused(
            (mod, sums_two, ggate_two, grad_gate, forget_p), (attention_w, gqkv, perm, x, grad_middle),
            (gmain, gout_main, gleft), grad_small,
        )
        g_forget = grad_small[:36, :heads].reshape(-1)
        g_taps = lax.dynamic_slice(grad_small[36:40].reshape(-1), (lax.rem(me * share_taps, LANES),), (share_taps,))
        grad_bias = grad_small[40, :heads]
        mod_all = mod_all.reshape(devices, -1)[:, :mod_width]
        shares = [piece.reshape(-1) for piece in (g_query, g_key, g_value, g_out, g_up, g_down)]
    else:
        grad_middle, grad_mixed, grad_mix, gout_main, gout_left, sums_two = call(
            functools.partial(second_kernel, head_width),
            (
                sds(rows), sds(rows, bf16), sds(rows, bf16), sds((GROUPS, 32, width), bf16),
                sds((GROUPS, 16, width), bf16), sds((8, width)),
            ),
            "second_norm",
            grid=(1,),
            in_specs=[
                whole(rows), whole((width, width)), whole(rows), whole((8, width)), whole(rows), whole(rows), whole(rows),
                whole(rows), main_spec(lambda i: (0, 3, 0)), left_spec(lambda i: (0, 8, 0)),
            ],
            out_specs=[
                whole(rows), whole(rows), whole(rows), whole((GROUPS, 32, width)), whole((GROUPS, 16, width)),
                whole((8, width)),
            ],
            scratch_shapes=[pltpu.VMEM(rows, f32), pltpu.VMEM(rows, bf16), pltpu.VMEM((width, length), bf16)],
        )(ghp_two, perm, middle, mod, cot, branch, mixed_p, mix, attention_w, attention_w)

        back = state_call(qkv[0], grad_mix, taken, edges(grad_mixed))
        if ways == 2:
            back = jnp.stack([
                jnp.concatenate([back[1, :width], back[0, width:]]), jnp.concatenate([back[0, :width], back[1, width:]])
            ])
        leaving, grad_rims = joined_states(back, total, width, head_width)
        if ways == 2:
            leaving = leaving[::-1]

        gq_local, gk_local, gv_local, pair_rows, pair_cols = call(
            functools.partial(pairs_kernel, head_width, heads),
            (sds(rows), sds(rows), sds(rows), sds((2, length, LANES)), sds((2, heads, length))),
            "pairs",
            scratch_shapes=[pltpu.VMEM((2, length, length), bf16)],
        )(qkv, grad_mix, run, runt)
        if seq_count > 2:
            rows_through = jnp.sum(states.astype(f32) * leaving.astype(f32), axis=(0, 2))
            through = jnp.exp(total[:heads]) * jnp.sum(rows_through.reshape(heads, head_width), axis=1)
            through = jnp.pad(through, (0, LANES - heads)).reshape(1, LANES)
        else:
            through = jnp.zeros((1, LANES), f32)
        early = jnp.where(place == 0, jnp.ones((1, LANES), f32), 0.0)

        pad_scratch = pltpu.VMEM((length + 2 * GRID, width), bf16)
        gqkv, grad_gate, grad_conv, grad_bias = call(
            functools.partial(carry_kernel, head_width, ways),
            (sds((3,) + rows, bf16), sds((length, LANES), bf16), sds((16, width)), sds((1, LANES))),
            "carry",
            scratch_shapes=[pad_scratch, pad_scratch],
        )(
            qkv, grad_mix, gq_local, gk_local, gv_local, pair_rows, pair_cols, taken, given, gate_pre, states, leaving,
            through, early, grad_mixed, grad_rims, value_rims, taps,
        )
        gmain, gleft, gforget, ghp_one = call(
            weights_kernel,
            (sds((GROUPS, 96, width), bf16), sds((GROUPS, 16, width), bf16), sds((width, LANES)), sds(rows)),
            "weights",
            grid=(3,),
            in_specs=[
                whole(rows), pl.BlockSpec((1,) + rows, lambda j: (j, 0, 0)), whole((length, LANES)),
                whole((width, LANES)), main_spec(lambda j: (0, j, 0)), left_spec(lambda j: (0, 8, 0)),
                left_spec(lambda j: (0, 0, 0)),
            ],
            out_specs=[
                main_spec(lambda j: (0, j, 0)), left_spec(lambda j: (0, 0, 0)), whole((width, LANES)), whole(rows),
            ],
            scratch_shapes=[pltpu.VMEM((width, length), bf16)],
        )(xp, gqkv, grad_gate, forget_p, attention_w, attention_w, gout_left)
        grad_input, sums_one = call(
            last_part, (sds(rows), sds((8, width))), "last_norm", scratch_shapes=[pltpu.VMEM(rows, f32)]
        )(ghp_one, perm, x, mod, grad_middle)

        gforget = gforget[:, :heads]
        gforget = jnp.concatenate(
            [gforget[:main_rows].reshape(GROUPS, 32, heads), gforget[main_rows:].reshape(GROUPS, 4, heads)], axis=1
        )
        grad_small = jnp.concatenate([gforget.reshape(devices, -1), grad_conv[:10].reshape(devices, -1)], axis=1)
        grad_small = lax.psum_scatter(grad_small, everywhere, scatter_dimension=0, tiled=True).reshape(-1)
        g_forget, g_taps = grad_small[:share_forget], grad_small[share_forget:]
        grad_bias = lax.psum(grad_bias[0, :heads], everywhere)
        grads = [
            jnp.concatenate([gmain, gout_main, gleft], axis=1), jnp.concatenate([gup_main, gup_left], axis=1),
            gdown.reshape(GROUPS, -1, width),
        ]
        shares = [
            lax.psum_scatter(g.reshape(-1), everywhere, scatter_dimension=0, tiled=True).astype(f32)
            for g in unpack_blocks(grads)
        ]
        grad_mod = jnp.concatenate([sums_one[:2], sums_two[2:3], sums_two[:2], ggate_two])
        mod_all = lax.all_gather(grad_mod.reshape(1, mod_width), everywhere, axis=0, tiled=True)

    mod_all = jnp.sum(mod_all.reshape(data_count, seq_count, mod_width), axis=1)
    grad_ada = jnp.dot(cond_part.astype(f32).T, mod_all, precision=lax.Precision.HIGHEST).reshape(-1)
    if inset is not None:
        grad_ada = lax.dynamic_slice(grad_ada, (inset,), (share,))
    grad_ada_bias = lax.dynamic_slice(jnp.sum(mod_all, axis=0), (me * share_bias,), (share_bias,))
    g_query, g_key, g_value, g_out, g_up, g_down = shares
    return (
        output[None], grad_input[None], grad_ada, grad_ada_bias, g_query, g_key, g_value, g_forget,
        grad_bias, g_taps, g_out, g_up, g_down,
    )


def solution(mesh):
    rows = P("dp", "seq", None)
    shard = P(("dp", "seq"))
    return jax.shard_map(
        on_device,
        mesh=mesh,
        in_specs=(
            rows, P("dp", None), rows, shard, shard, shard, shard, shard, shard, P(), shard, shard, shard, shard,
        ),
        out_specs=(
            rows, rows, shard, shard, shard, shard, shard, shard, P(), shard, shard, shard, shard,
        ),
        check_vma=False,
    )
```

```python
import functools

import jax
import jax.numpy as jnp
import numpy as np
from jax import lax
from jax.experimental import pallas as pl
from jax.experimental.pallas import tpu as pltpu
from jax.sharding import PartitionSpec as P

GRID = 32
LANES = 128
GROUPS = 32
epsilon = 1e-06
f32 = jnp.float32
bf16 = jnp.bfloat16
VMEM_LIMIT = 56 * 1024 * 1024
FORWARD_PLAN = (
    ("f", 0, 0, 0), ("g", 0, 0, 0), -1, ("g", 0, 1, 0), ("f", 1, 0, 0), ("g", 2, 0, 0), ("g", 1, 0, 0),
    ("g", 3, 0, 0), ("g", 0, 0, 1), ("f", 2, 0, 0), ("g", 1, 1, 0), ("g", 2, 1, 0), -1, ("g", 0, 0, 2),
    ("g", 4, 0, 0), ("g", 5, 0, 0), ("g", 2, 0, 1), ("g", 1, 0, 1), -1, ("s", 0, 0, 0), ("g", 2, 0, 2),
    ("g", 1, 0, 2), ("g", 0, 0, 3), ("g", 4, 0, 1), ("g", 5, 0, 1), ("g", 3, 1, 0), ("s", 1, 0, 0), ("g", 0, 1, 1),
    ("g", 1, 0, 3), ("g", 2, 0, 3), ("g", 4, 0, 2), ("g", 5, 0, 2), ("s", 2, 0, 0), -1, ("g", 2, 1, 1),
    ("g", 1, 1, 1), ("g", 4, 1, 0), ("g", 5, 1, 0), ("g", 4, 0, 3), ("g", 5, 0, 3), ("g", 0, 1, 2), ("g", 4, 1, 1),
    ("g", 5, 1, 1), ("g", 1, 1, 2), -1, ("g", 2, 1, 2), -1, ("g", 0, 1, 3), -1, -1, ("g", 4, 1, 2), ("g", 5, 1, 2),
    ("g", 2, 1, 3), -1, -1, ("g", 1, 1, 3), -1, ("g", 4, 1, 3), -1, -1, ("g", 5, 1, 3), -1, -1, -1,
)
FEED_PLAN = (
    ("g", 0, 0, 0), -1, -1, ("g", 2, 0, 0), ("g", 1, 0, 0), ("g", 3, 0, 0), ("g", 0, 0, 1), -1, -1, ("g", 0, 0, 2),
    ("g", 4, 0, 0), ("g", 5, 0, 0), ("d", 0, 0, 0), ("g", 2, 0, 1), ("d", 4, 0, 0), -1, ("g", 1, 0, 1),
    ("g", 2, 0, 2), -1, ("g", 0, 0, 3), ("g", 1, 0, 2), ("d", 1, 0, 0), ("d", 2, 0, 0), ("d", 0, 0, 1),
    ("g", 4, 0, 1), -1, -1, ("g", 5, 0, 1), ("g", 2, 0, 3), ("d", 4, 0, 1), ("d", 0, 0, 2), -1, ("g", 1, 0, 3),
    ("g", 4, 0, 2), ("g", 5, 0, 2), -1, ("d", 3, 0, 0), -1, ("d", 4, 0, 2), ("d", 0, 0, 3), ("d", 2, 0, 1),
    ("d", 1, 0, 1), -1, -1, ("g", 4, 0, 3), -1, ("d", 1, 0, 2), ("d", 2, 0, 2), -1, ("g", 5, 0, 3), ("d", 2, 0, 3),
    -1, -1, ("d", 4, 0, 3), ("d", 1, 0, 3), -1, ("d", 3, 0, 1), ("d", 5, 0, 0), -1, -1, -1, -1, ("d", 3, 0, 2), -1,
    -1, -1, -1, ("d", 3, 0, 3), ("d", 5, 0, 1),
)
BACKWARD_PLAN = (
    -1, -1, -1, -1, -1, ("u", 0, 0, 0), ("u", 4, 0, 0), -1, ("u", 0, 0, 1), -1, ("u", 0, 0, 2), ("u", 2, 0, 0),
    ("u", 4, 0, 1), ("u", 1, 0, 0), ("u", 2, 0, 1), -1, ("u", 1, 0, 1), -1, ("u", 0, 0, 3), ("u", 2, 0, 2),
    ("u", 4, 0, 2), ("u", 1, 0, 2), ("u", 3, 0, 0), -1, -1, ("u", 2, 0, 3), ("u", 4, 0, 3), ("u", 1, 0, 3), -1, -1,
    ("u", 3, 0, 1), ("u", 5, 0, 0), -1, -1, -1, ("u", 3, 0, 2), ("u", 3, 0, 3), ("u", 5, 0, 1),
)
FINISH_PLAN = (
    -1, ("a", 0, 0, 0), ("a", 4, 0, 0), -1, ("a", 0, 0, 1), -1, ("a", 2, 0, 0), ("a", 1, 0, 0), ("a", 0, 0, 2),
    ("a", 4, 0, 1), -1, ("g", 0, 0, 0), ("a", 2, 0, 1), ("s", 0, 0, 0), ("s", 0, 0, 1), ("s", 0, 0, 2),
    ("s", 0, 0, 3), ("a", 1, 0, 1), ("a", 3, 0, 0), ("a", 2, 0, 2), ("g", 1, 0, 0), ("s", 2, 0, 0), ("s", 2, 0, 1),
    ("s", 1, 0, 0), ("s", 2, 0, 2), ("s", 1, 0, 1), ("a", 4, 0, 2), ("s", 2, 0, 3), ("s", 1, 0, 2), ("s", 1, 0, 3),
    ("a", 0, 0, 3), ("a", 3, 0, 1), ("s", 3, 0, 0), ("g", 2, 0, 0), ("a", 1, 0, 2), ("a", 4, 0, 3), ("a", 2, 0, 3),
    ("a", 1, 0, 3), ("s", 3, 0, 1), ("a", 3, 0, 2), ("s", 3, 0, 2), ("a", 5, 0, 0), ("a", 3, 0, 3), ("a", 5, 0, 1),
    ("s", 3, 0, 3),
)


def dot(a, b):
    return jnp.dot(a, b, preferred_element_type=f32)


def dot_bt(a, b):
    return lax.dot_general(a, b, (((1,), (1,)), ((), ())), preferred_element_type=f32)


def dot_at(a, b):
    return lax.dot_general(a, b, (((0,), (0,)), ((), ())), preferred_element_type=f32)


def halves(a):
    high = a.astype(bf16)
    return high, (a - high.astype(f32)).astype(bf16)


def spans(width, size=512):
    return [slice(start, min(start + size, width)) for start in range(0, width, size)]


def head_lanes(rows, width, start, head_width):
    head = lax.broadcasted_iota(jnp.int32, (rows, width), 0)
    lane = lax.broadcasted_iota(jnp.int32, (rows, width), 1) + start
    return (lane >= head * head_width) & (lane < (head + 1) * head_width)


def pick_left(rows, slot):
    out = lax.broadcasted_iota(jnp.int32, (4 * GROUPS, 16 * GROUPS), 0)
    src = lax.broadcasted_iota(jnp.int32, (4 * GROUPS, 16 * GROUPS), 1)
    return (src == (out // 4) * 16 + slot * 4 + out % 4).astype(bf16)


def norm_parts(values):
    center = jnp.mean(values, axis=-1, keepdims=True)
    centered = values - center
    spread = jnp.mean(centered * centered, axis=-1, keepdims=True)
    rstd = lax.rsqrt(spread + epsilon)
    return centered * rstd, rstd


def row_loop(length, body):
    size = min(length, 64)

    @pl.loop(0, length // size)
    def _(r):
        body(pl.ds(pl.multiple_of(r * size, size), size))


def eight_rows(values):
    return jnp.sum(values.reshape(-1, 8, values.shape[1]), axis=0)


def call(kernel, out_shape, name, **kw):
    return pl.pallas_call(
        kernel,
        out_shape=out_shape,
        name=name,
        compiler_params=pltpu.CompilerParams(vmem_limit_bytes=VMEM_LIMIT),
        **kw,
    )


def sds(shape, dtype=f32):
    return jax.ShapeDtypeStruct(shape, dtype)


def first_part(x_ref, mod_ref, perm_ref, wf_ref, bf_ref, xp_ref, gate_ref, run_ref, runt_ref, hidden_ref):
    length = x_ref.shape[0]

    def norm(rows):
        normed, _ = norm_parts(x_ref[rows, :].astype(f32))
        hidden_ref[rows, :] = (normed * (1.0 + mod_ref[1:2, :]) + mod_ref[0:1, :]).astype(bf16)

    row_loop(length, norm)
    for cols in spans(x_ref.shape[1]):
        xp_ref[:, cols] = dot(hidden_ref[...], perm_ref[:, cols]).astype(bf16)

    gate = dot(xp_ref[...], wf_ref[...]) + bf_ref[...]
    gate_ref[...] = gate
    decay = -(jnp.maximum(gate, 0.0) + jnp.log1p(jnp.exp(-jnp.abs(gate))))
    row = lax.broadcasted_iota(jnp.int32, (length, length), 0)
    col = lax.broadcasted_iota(jnp.int32, (length, length), 1)
    tri = (row >= col).astype(bf16)
    high, rest = halves(decay)
    rest32 = decay - high.astype(f32)
    low = (rest32 - rest.astype(f32)).astype(bf16)
    inclusive = dot(tri, high) + dot(tri, rest) + dot(tri, low)
    exclusive = inclusive - decay
    run_ref[0] = inclusive
    run_ref[1] = exclusive
    runt_ref[0] = inclusive.T
    runt_ref[1] = exclusive.T


def project_part(slot, xp_ref, main_ref, left_ref, write):
    pick = pick_left(None, slot)
    main_rows = rows_in(main_ref)

    for cols in spans(xp_ref.shape[1]):
        main = main_ref[..., cols].reshape(main_rows, -1)
        left = dot(pick, left_ref[..., cols].reshape(16 * GROUPS, -1)).astype(bf16)
        write(cols, dot(xp_ref[:, :main_rows], main) + dot(xp_ref[:, main_rows:], left))


def two_terms(scale):
    return jnp.concatenate(halves(scale), axis=1)


def spread_heads(terms, cols, head_width):
    spread = head_lanes(LANES, cols.stop - cols.start, cols.start, head_width).astype(bf16)
    return dot(terms, jnp.concatenate([spread, spread], axis=0))


def head_sums(values, cols, head_width):
    return dot_bt(values, head_lanes(LANES, cols.stop - cols.start, cols.start, head_width).astype(bf16))


def own_block(shape, row_start, lane_start, head_width):
    row = lax.broadcasted_iota(jnp.int32, (shape[0], 1), 0) + row_start
    lane = lax.broadcasted_iota(jnp.int32, (1, shape[1]), 1) + lane_start
    same = None
    for head in range(
        max(row_start, lane_start) // head_width,
        min(row_start + shape[0] - 1, lane_start + shape[1] - 1) // head_width + 1,
    ):
        low, high = head * head_width, (head + 1) * head_width
        both = ((row >= low) & (row < high)) & ((lane >= low) & (lane < high))
        same = both if same is None else same | both
    if same is None:
        return jnp.broadcast_to(row < 0, shape)
    return same


def group_rows(ref, cols):
    per = rows_in(ref) // ref.shape[0]
    return ref[cols.start // per : cols.stop // per].reshape(-1, ref.shape[-1])


def rows_in(ref):
    return int(np.prod(ref.shape[:-1]))


def near_lanes(cols, width, head_width):
    low = cols.start // head_width * head_width // LANES * LANES
    last = (cols.stop - 1) // head_width
    return slice(low, min(width, -(-(last + 1) * head_width // LANES) * LANES))


def unfolded(ref, way, near, cols, head_width):
    folded = ref[way, near, :]
    return jnp.concatenate([
        jnp.where(own_block(folded.shape, near.start, at, head_width), folded, 0)
        for at in range(cols.start, cols.stop, LANES)
    ], axis=1)


def state_part(head_width, ways, left, right_ref, scale_ref, out_ref):
    width = right_ref.shape[1]
    terms = [two_terms(scale_ref[way]) for way in range(ways)]
    for cols in spans(width, 2 * LANES):
        near = near_lanes(cols, width, head_width)
        mask = own_block((cols.stop - cols.start, near.stop - near.start), cols.start, near.start, head_width)
        for way in range(ways):
            scaled = left(cols).astype(f32) * spread_heads(terms[way], cols, head_width)
            product = jnp.where(mask, dot_at(scaled.astype(bf16), right_ref[:, near]), 0.0)
            total = product[:, :LANES]
            for at in range(LANES, near.stop - near.start, LANES):
                total = total + product[:, at : at + LANES]
            out_ref[way, cols, :] = total.astype(bf16)


def edge_part(source, out):
    for t in range(source.shape[1] // LANES):
        out(t, source[:, t * LANES : (t + 1) * LANES])


def pair_weights(run_ref, runt_ref, head, rows, length):
    count = rows.size
    own = lax.broadcasted_iota(jnp.int32, (count, LANES), 1) == head
    inc_t = jnp.sum(jnp.where(own, run_ref[0, rows, :], 0.0), axis=1, keepdims=True)
    exc_t = jnp.sum(jnp.where(own, run_ref[1, rows, :], 0.0), axis=1, keepdims=True)
    inc_s = runt_ref[0, pl.ds(head, 1), :]
    exc_s = runt_ref[1, pl.ds(head, 1), :]
    weight = jnp.exp(jnp.minimum(inc_t - inc_s, exc_s - exc_t))
    row = lax.broadcasted_iota(jnp.int32, (count, length), 0) + rows.start
    col = lax.broadcasted_iota(jnp.int32, (count, length), 1)
    return jnp.where(row == col, 2.0, weight)


def window_of(head, heads, head_width):
    start = pl.multiple_of(((head * head_width) // LANES - head // (heads - 1)) * LANES, LANES)
    return pl.ds(start, 2 * LANES), start


def own_lanes(rows, start, head, head_width):
    lane = lax.broadcasted_iota(jnp.int32, (rows, 2 * LANES), 1) + start
    return (lane >= head * head_width) & (lane < (head + 1) * head_width)


def row_blocks(length, size):
    size = min(length, size)
    return [pl.ds(start, size) for start in range(0, length, size)]


def mix_part(head_width, heads, low, high, qkv_ref, run_ref, runt_ref, mix_ref):
    length, width = mix_ref.shape

    @pl.loop(low // 2, high // 2)
    def _(pair):
        for odd in range(2):
            head = pair * 2 + odd
            win, start = window_of(head, heads, head_width)
            mask = own_lanes(length, start, head, head_width)
            keys = jnp.where(mask, qkv_ref[1, :, win], 0)
            vals = jnp.where(mask, qkv_ref[2, :, win], 0)
            for rows in row_blocks(length, 2 * LANES):
                weight = pair_weights(run_ref, runt_ref, head, rows, length)
                score = dot_bt(qkv_ref[0, rows, win], keys)
                mix_ref[rows, win] += dot((score * weight).astype(bf16), vals)


def fill_padded(pad_ref, rims_ref, middle):
    length = pad_ref.shape[0] - 2 * GRID
    pad_ref[:GRID, :] = rims_ref[0]
    pad_ref[GRID : GRID + length, :] = middle
    pad_ref[GRID + length :, :] = rims_ref[1]


def mixed_part(head_width, ways, qkv_ref, taken_ref, state_ref, taps_ref, vpad, mix_ref, mixed):
    length, width = mix_ref.shape
    place = lax.broadcasted_iota(jnp.int32, (length, LANES), 0) % GRID
    sums = jnp.zeros((length, LANES), f32)
    terms = [two_terms(taken_ref[way]) for way in range(ways)]
    for cols in spans(width, 2 * LANES):
        gained = mix_ref[:, cols]
        near = near_lanes(cols, width, head_width)
        for way in range(ways):
            block = unfolded(state_ref, way, near, cols, head_width)
            gained = gained + spread_heads(terms[way], cols, head_width) * dot(qkv_ref[0, :, near], block)
        mix_ref[:, cols] = gained
        sums = sums + head_sums((gained * gained).astype(bf16), cols, head_width)
    inverse = two_terms(lax.rsqrt(sums * (1.0 / head_width) + epsilon))
    for span in spans(width, 2 * LANES):
        normed = mix_ref[:, span] * spread_heads(inverse, span, head_width)
        for start in range(span.start, span.stop, LANES):
            cols = slice(start, start + LANES)
            conv = jnp.zeros((length, LANES), f32)
            for lateral in range(3):
                column = jnp.zeros((length, LANES), f32)
                for vertical in range(3):
                    tap = taps_ref[3 * vertical + lateral : 3 * vertical + lateral + 1, cols]
                    column = column + tap * vpad[vertical * GRID : vertical * GRID + length, cols].astype(f32)
                if lateral == 0:
                    column = jnp.where(place > 0, pltpu.roll(column, 1, 0), 0.0)
                if lateral == 2:
                    column = jnp.where(place < GRID - 1, pltpu.roll(column, length - 1, 0), 0.0)
                conv = conv + column
            own = normed[:, start - span.start : start - span.start + LANES]
            mixed[:, cols] = (own + (conv + taps_ref[9:10, cols])).astype(bf16)


def permute_part(source, perm_ref, out_ref):
    for cols in spans(perm_ref.shape[1]):
        out_ref[:, cols] = dot(source[...], perm_ref[:, cols]).astype(bf16)


def branch_part(x_ref, mod_ref, mixedp_ref, main_ref, left_ref, branch_ref, middle_ref):
    def write(cols, branch):
        branch_ref[:, cols] = branch.astype(bf16)
        middle_ref[:, cols] = x_ref[:, cols].astype(f32) + mod_ref[2:3, cols] * branch

    project_part(3, mixedp_ref, main_ref, left_ref, write)


def second_hidden(mod_ref, middle_ref, mixed):
    def norm(rows):
        normed, _ = norm_parts(middle_ref[rows, :])
        mixed[rows, :] = (normed * (1.0 + mod_ref[4:5, :]) + mod_ref[3:4, :]).astype(bf16)

    row_loop(mixed.shape[0], norm)


def project_kernel(xp_ref, main_ref, left_ref, out_ref):
    def write(cols, value):
        out_ref[0, :, cols] = value.astype(bf16)

    project_part(pl.program_id(0), xp_ref, main_ref, left_ref, write)


def state_kernel(head_width, ways, left_ref, right_ref, scale_ref, edge_ref, out_ref):
    width = right_ref.shape[1]
    state_part(head_width, ways, lambda cols: left_ref[:, cols], right_ref, scale_ref, out_ref)
    for way in range(ways):

        def write(t, value, way=way):
            out_ref[way, width + t * GRID : width + (t + 1) * GRID, :] = value

        edge_part(edge_ref[way], write)


def mix_kernel(head_width, heads, qkv_ref, run_ref, runt_ref, mix_ref):
    mix_ref[...] = jnp.zeros_like(mix_ref)
    mix_part(head_width, heads, 0, heads, qkv_ref, run_ref, runt_ref, mix_ref)


def after_kernel(
    head_width, ways, x_ref, mod_ref, perm_ref, qkv_ref, mix_in_ref, taken_ref, state_ref, rims_ref, taps_ref,
    main_ref, left_ref, mix_ref, mixedp_ref, branch_ref, middle_ref, h2p_ref, vpad, mixed,
):
    mix_ref[...] = mix_in_ref[...]
    fill_padded(vpad, rims_ref, qkv_ref[2])
    mixed_part(head_width, ways, qkv_ref, taken_ref, state_ref, taps_ref, vpad, mix_ref, mixed)
    permute_part(mixed, perm_ref, mixedp_ref)
    branch_part(x_ref, mod_ref, mixedp_ref, main_ref, left_ref, branch_ref, middle_ref)
    second_hidden(mod_ref, middle_ref, mixed)
    permute_part(mixed, perm_ref, h2p_ref)


def gelu_both(v):
    c = np.float32(np.sqrt(2.0 / np.pi))
    square = v * v
    th = jnp.tanh(c * (v + np.float32(0.044715) * (square * v)))
    half = 0.5 * (1.0 + th)
    slope = half + 0.5 * v * (1.0 - th * th) * (c * (1.0 + np.float32(3 * 0.044715) * square))
    return v * half, slope


def feed_kernel(
    h2p_ref, cot_ref, mod_ref, middle_ref, main_ref, left_ref, down_ref,
    out_ref, gh_ref, gup_ref, gleft_ref, gdown_ref, ggate_ref, down_acc, gdi, h2pt, act, actt, gup, left,
):
    j = pl.program_id(0)
    main_rows = main_ref.shape[0] * main_ref.shape[1]
    length, width = h2p_ref.shape

    @pl.when(j == 0)
    def _():
        gdi[...] = (cot_ref[...].astype(f32) * mod_ref[5:6, :]).astype(bf16)
        h2pt[...] = h2p_ref[...].T
        down_acc[...] = jnp.zeros_like(down_acc)
        gh_ref[...] = jnp.zeros_like(gh_ref)
        gleft_ref[...] = jnp.zeros_like(gleft_ref)

    pick = pick_left(None, j)
    left[...] = dot(pick, left_ref[...].reshape(16 * GROUPS, width)).astype(bf16)
    for cols in spans(width):
        main = main_ref[:, :, cols].reshape(main_rows, -1)
        up = dot(h2p_ref[:, :main_rows], main) + dot(h2p_ref[:, main_rows:], left[:, cols])
        value, slope = gelu_both(up)
        value = value.astype(bf16)
        act[:, cols] = value
        actt[cols, :] = value.T
        gup[:, cols] = (dot_bt(gdi[...], down_ref[cols, :]) * slope).astype(bf16)
    for cols in spans(width):
        down_acc[:, cols] += dot(act[...], down_ref[:, cols])
        gdown_ref[:, cols] = dot(actt[...], gdi[:, cols]).astype(bf16)
        gup_ref[:, :, cols] = dot(h2pt[:main_rows, :], gup[:, cols]).astype(bf16).reshape(GROUPS, 32, -1)
        part = dot(h2pt[main_rows:, :], gup[:, cols]).astype(bf16)
        gleft_ref[:, :, cols] += dot_at(pick, part).astype(bf16).reshape(GROUPS, 16, -1)
    gh_ref[:, main_rows:] += dot_bt(gup[...], left[...])
    for cols in spans(main_rows):
        gh_ref[:, cols] += dot_bt(gup[...], group_rows(main_ref, cols))

    @pl.when(j == pl.num_programs(0) - 1)
    def _():
        out_ref[...] = (middle_ref[...] + mod_ref[5:6, :] * down_acc[...]).astype(bf16)
        ggate_ref[...] = jnp.sum(cot_ref[...].astype(f32) * down_acc[...], axis=0, keepdims=True)


def unpermute(perm_ref, source_ref, out_ref):
    source = source_ref[...].astype(bf16)
    for cols in spans(perm_ref.shape[0]):
        out_ref[:, cols] = dot_bt(source, perm_ref[cols, :])


def norm_back(normed, rstd, factor, grad):
    scaled = grad * (1.0 + factor)
    mean = jnp.mean(scaled, axis=-1, keepdims=True)
    along = jnp.mean(scaled * normed, axis=-1, keepdims=True)
    return (scaled - mean - normed * along) * rstd


def second_part(
    head_width, ghp_ref, perm_ref, middle_ref, mod_ref, cot_ref, branch_ref, mixedp_ref, mix_ref, main_ref, left_ref,
    gmid_ref, gmixed_ref, gmix_ref, gout_ref, gleft_ref, sums_ref, gh, gb, partial,
):
    length, width = middle_ref.shape
    main_rows = rows_in(main_ref)
    unpermute(perm_ref, ghp_ref, gh)
    yield
    partial[...] = jnp.zeros_like(partial)

    def norm(rows):
        normed, rstd = norm_parts(middle_ref[rows, :])
        grad = gh[rows, :]
        partial[0] += eight_rows(grad)
        partial[1] += eight_rows(grad * normed)
        grad_middle = cot_ref[rows, :].astype(f32) + norm_back(normed, rstd, mod_ref[4:5, :], grad)
        gmid_ref[rows, :] = grad_middle
        partial[2] += eight_rows(grad_middle * branch_ref[rows, :].astype(f32))
        gb[rows, :] = (grad_middle * mod_ref[2:3, :]).astype(bf16)

    row_loop(length, norm)
    for k in range(3):
        sums_ref[k : k + 1, :] = jnp.sum(partial[k], axis=0, keepdims=True)
    sums_ref[3:8, :] = jnp.zeros((5, width), f32)
    pick = pick_left(None, 3)
    yield
    left = dot(pick, left_ref[...].reshape(16 * GROUPS, width)).astype(bf16)
    for cols in spans(width):
        gout = dot_at(mixedp_ref[:, :main_rows], gb[:, cols]).astype(bf16)
        gout_ref[..., cols] = gout.reshape(gout_ref.shape[:-1] + (-1,))
        part = dot_at(mixedp_ref[:, main_rows:], gb[:, cols]).astype(bf16)
        gleft_ref[..., cols] = dot_at(pick, part).astype(bf16).reshape(gleft_ref.shape[:-1] + (-1,))
    gh[:, main_rows:] = dot_bt(gb[...], left)
    for cols in spans(main_rows):
        gh[:, cols] = dot_bt(gb[...], group_rows(main_ref, cols))
    gb[...] = gh[...].astype(bf16)
    yield
    for cols in spans(width):
        gmixed_ref[:, cols] = dot_bt(gb[...], perm_ref[cols, :]).astype(bf16)

    sums = jnp.zeros((length, LANES), f32)
    dots = jnp.zeros((length, LANES), f32)
    for cols in spans(width, 2 * LANES):
        mix = mix_ref[:, cols]
        sums = sums + head_sums((mix * mix).astype(bf16), cols, head_width)
        for term in halves(mix * gmixed_ref[:, cols].astype(f32)):
            dots = dots + head_sums(term, cols, head_width)
    inverse = lax.rsqrt(sums * (1.0 / head_width) + epsilon)
    along = two_terms(dots * (1.0 / head_width) * inverse * inverse * inverse)
    inverse = two_terms(inverse)
    for cols in spans(width, 2 * LANES):
        gmix_ref[:, cols] = (
            gmixed_ref[:, cols].astype(f32) * spread_heads(inverse, cols, head_width)
            - mix_ref[:, cols] * spread_heads(along, cols, head_width)
        ).astype(bf16)
    yield


def second_kernel(head_width, *refs):
    for _ in second_part(head_width, *refs):
        pass


def pairs_part(head_width, heads, low, high, qkv_ref, gmix_ref, run_ref, runt_ref, gq_ref, gk_ref, gv_ref, rows_ref, cols_ref, held):
    length, width = gmix_ref.shape

    @pl.loop(low, high)
    def _(head):
        win, start = window_of(head, heads, head_width)
        mask = own_lanes(length, start, head, head_width)
        queries = jnp.where(mask, qkv_ref[0, :, win], 0)
        keys = jnp.where(mask, qkv_ref[1, :, win], 0)
        vals = jnp.where(mask, qkv_ref[2, :, win], 0)
        grads = jnp.where(mask, gmix_ref[:, win], 0)
        own = lax.broadcasted_iota(jnp.int32, (LANES, LANES), 1) == head
        row = lax.broadcasted_iota(jnp.int32, (LANES, LANES), 0)
        col = lax.broadcasted_iota(jnp.int32, (LANES, LANES), 1)
        columns = [None, None]
        for rows in row_blocks(length, 2 * LANES):
            weight = pair_weights(run_ref, runt_ref, head, rows, length)
            at = slice(rows.start, rows.start + rows.size)
            score = dot_bt(queries[at], keys) * weight
            grad = dot_bt(grads[at], vals)
            both = score * grad
            held[0, rows, :] = score.astype(bf16)
            held[1, rows, :] = (grad * weight).astype(bf16)
            for step in range(rows.size // LANES):
                first = rows.start + step * LANES
                strip = both[step * LANES : (step + 1) * LANES]
                middle = strip[:, first : first + LANES]
                pieces = [
                    (0, strip[:, :first], jnp.where(row > col, middle, 0.0)),
                    (1, strip[:, first + LANES :], jnp.where(row < col, middle, 0.0)),
                ]
                for way, part, corner in pieces:
                    total = jnp.sum(corner, axis=1, keepdims=True)
                    lines = [jnp.sum(corner, axis=0, keepdims=True)]
                    if first if way == 0 else length - first - LANES:
                        total = total + jnp.sum(part, axis=1, keepdims=True)
                        lines.insert(0 if way == 0 else 1, jnp.sum(part, axis=0, keepdims=True))
                    blank = jnp.zeros((1, length - sum(line.shape[1] for line in lines)), f32)
                    if blank.shape[1]:
                        lines.insert(len(lines) if way == 0 else 0, blank)
                    line = jnp.concatenate(lines, axis=1)
                    columns[way] = line if columns[way] is None else columns[way] + line
                    rows_ref[way, first : first + LANES, :] += jnp.where(own, total, 0.0)
        for way in range(2):
            cols_ref[way, pl.ds(head, 1), :] = columns[way]
        gq_ref[:, win] += dot(held[1], keys)
        gk_ref[:, win] += dot_at(held[1], queries)
        gv_ref[:, win] += dot_at(held[0], grads)


def pairs_kernel(head_width, heads, qkv_ref, gmix_ref, run_ref, runt_ref, gq_ref, gk_ref, gv_ref, rows_ref, cols_ref, held):
    for ref in (gq_ref, gk_ref, gv_ref, rows_ref, cols_ref):
        ref[...] = jnp.zeros_like(ref)
    pairs_part(
        head_width, heads, 0, heads, qkv_ref, gmix_ref, run_ref, runt_ref, gq_ref, gk_ref, gv_ref, rows_ref, cols_ref, held
    )


def carry_part(
    head_width, ways, early, qkv_ref, gmix_ref, gq_in, gk_in, gv_in, rows_ref, cols_ref, taken_ref, given_ref, gate_ref,
    state_ref, leave_ref, through, vpad, gpad, taps_ref, gqkv_ref, ggate_ref, conv_ref, bias_ref,
):
    length, width = gmix_ref.shape
    place = lax.broadcasted_iota(jnp.int32, (length, LANES), 0) % GRID
    taken_sums = [jnp.zeros((length, LANES), f32) for _ in range(ways)]
    given_sums = [jnp.zeros((length, LANES), f32) for _ in range(ways)]
    take_terms = [two_terms(taken_ref[way]) for way in range(ways)]
    give_terms = [two_terms(given_ref[way]) for way in range(ways)]
    for span in spans(width, 2 * LANES):
        near = near_lanes(span, width, head_width)
        gq, gk, gv = gq_in[:, span], gk_in[:, span], gv_in[:, span]
        for way in range(ways):
            take = spread_heads(take_terms[way], span, head_width)
            give = spread_heads(give_terms[way], span, head_width)
            back_q = take * dot_bt(gmix_ref[:, near], unfolded(state_ref, way, span, near, head_width))
            gq = gq + back_q
            for term in halves(qkv_ref[0, :, span].astype(f32) * back_q):
                taken_sums[way] = taken_sums[way] + head_sums(term, span, head_width)
            back_k = give * dot_bt(qkv_ref[2, :, near], unfolded(leave_ref, way, span, near, head_width))
            gk = gk + back_k
            for term in halves(qkv_ref[1, :, span].astype(f32) * back_k):
                given_sums[way] = given_sums[way] + head_sums(term, span, head_width)
            gv = gv + give * dot(qkv_ref[1, :, near], unfolded(leave_ref, way, near, span, head_width))
        gqkv_ref[0, :, span] = gq.astype(bf16)
        gqkv_ref[1, :, span] = gk.astype(bf16)
        for first in range(span.start, span.stop, LANES):
            cols = slice(first, first + LANES)
            grad = gpad[GRID : GRID + length, cols].astype(f32)
            total = gv[:, first - span.start : first - span.start + LANES]
            for lateral in range(3):
                b = lateral - 1
                column = jnp.zeros((length, LANES), f32)
                for vertical in range(3):
                    tap = taps_ref[3 * vertical + lateral : 3 * vertical + lateral + 1, cols]
                    start = (2 - vertical) * GRID
                    column = column + tap * gpad[start : start + length, cols].astype(f32)
                shifted = grad
                if b == -1:
                    column = jnp.where(place < GRID - 1, pltpu.roll(column, length - 1, 0), 0.0)
                    shifted = jnp.where(place < GRID - 1, pltpu.roll(grad, length - 1, 0), 0.0)
                if b == 1:
                    column = jnp.where(place > 0, pltpu.roll(column, 1, 0), 0.0)
                    shifted = jnp.where(place > 0, pltpu.roll(grad, 1, 0), 0.0)
                total = total + column
                for vertical in range(3):
                    window = vpad[vertical * GRID : vertical * GRID + length, cols].astype(f32)
                    conv_ref[3 * vertical + lateral : 3 * vertical + lateral + 1, cols] = jnp.sum(
                        window * shifted, axis=0, keepdims=True
                    )
            conv_ref[9:10, cols] = jnp.sum(grad, axis=0, keepdims=True)
            gqkv_ref[2, :, cols] = total.astype(bf16)
        if span.start // (2 * LANES) in (1, 3) or span.stop == width:
            yield
    conv_ref[10:16, :] = jnp.zeros((6, width), f32)

    row = lax.broadcasted_iota(jnp.int32, (length, length), 0)
    col = lax.broadcasted_iota(jnp.int32, (length, length), 1)
    before = (col < row).astype(bf16)
    upto = (col <= row).astype(bf16)

    def summed(product, matrix, value):
        high, rest = halves(value)
        low = (value - high.astype(f32) - rest.astype(f32)).astype(bf16)
        return product(matrix, high) + product(matrix, rest) + product(matrix, low)

    def columns(way):
        lines = cols_ref[way]
        if lines.shape[0] < LANES:
            lines = jnp.concatenate([lines, jnp.zeros((LANES - lines.shape[0], length), f32)], axis=0)
        return lines.T

    ahead = rows_ref[0] - columns(0)
    behind = rows_ref[1] - columns(1)
    if ways == 2:
        ahead, behind = ahead + taken_sums[0], behind + taken_sums[1]
        given_ahead, given_behind = given_sums
    else:
        ahead = ahead + taken_sums[0] * (1.0 - early)
        behind = behind + taken_sums[0] * early
        given_ahead, given_behind = given_sums[0] * early, given_sums[0] * (1.0 - early)
    grad_decay = (
        summed(dot_at, upto, ahead)
        + summed(dot, before, given_ahead)
        + summed(dot, upto, behind)
        + summed(dot_at, before, given_behind)
        + through
    )
    gate = gate_ref[...]
    small = jnp.exp(-jnp.abs(gate))
    sigmoid = jnp.where(gate >= 0, 1.0, small) / (1.0 + small)
    grad_gate = (-grad_decay * sigmoid).astype(bf16)
    lane = lax.broadcasted_iota(jnp.int32, grad_gate.shape, 1)
    grad_gate = jnp.where(lane < width // head_width, grad_gate.astype(f32), 0.0)
    ggate_ref[...] = grad_gate.astype(bf16)
    bias_ref[...] = jnp.sum(grad_gate, axis=0, keepdims=True)
    yield


def carry_kernel(
    head_width, ways, qkv_ref, gmix_ref, gq_in, gk_in, gv_in, rows_ref, cols_ref, taken_ref, given_ref, gate_ref,
    state_ref, leave_ref, through_ref, early_ref, gmixed_ref, grims_ref, vrims_ref, taps_ref,
    gqkv_ref, ggate_ref, conv_ref, bias_ref, vpad, gpad,
):
    fill_padded(vpad, vrims_ref, qkv_ref[2])
    fill_padded(gpad, grims_ref, gmixed_ref[...])
    for _ in carry_part(
        head_width, ways, early_ref[...], qkv_ref, gmix_ref, gq_in, gk_in, gv_in, rows_ref, cols_ref, taken_ref,
        given_ref, gate_ref, state_ref, leave_ref, through_ref[...], vpad, gpad, taps_ref, gqkv_ref, ggate_ref, conv_ref,
        bias_ref,
    ):
        pass


def projection_grads(slot, turned, grad_ref, gmain_ref, gleft_ref):
    pick = pick_left(None, slot)
    main_rows = rows_in(gmain_ref)
    for cols in spans(grad_ref.shape[1]):
        grad = grad_ref[:, cols]
        gmain_ref[..., cols] = dot(turned[:main_rows, :], grad).astype(bf16).reshape(gmain_ref.shape[:-1] + (-1,))
        part = dot(turned[main_rows:, :], grad).astype(bf16)
        gleft_ref[..., cols] += dot_at(pick, part).astype(bf16).reshape(gleft_ref.shape[:-1] + (-1,))


def projection_back(slot, grad_ref, main_ref, left_ref, gh_ref):
    width = grad_ref.shape[1]
    main_rows = rows_in(main_ref)
    left = dot(pick_left(None, slot), left_ref[...].reshape(16 * GROUPS, width)).astype(bf16)
    gh_ref[:, main_rows:] += dot_bt(grad_ref[...], left)
    for cols in spans(main_rows):
        gh_ref[:, cols] += dot_bt(grad_ref[...], group_rows(main_ref, cols))


def weights_kernel(
    xp_ref, gqkv_ref, ggate_ref, wf_ref, main_ref, left_ref, gout_left_ref, gmain_ref, gleft_ref, gforget_ref, gh_ref, turned
):
    slot = pl.program_id(0)

    @pl.when(slot == 0)
    def _():
        turned[...] = xp_ref[...].T
        gleft_ref[...] = gout_left_ref[...]
        gh_ref[...] = dot_bt(ggate_ref[...], wf_ref[...])
        gforget_ref[...] = dot(turned[...], ggate_ref[...])

    projection_grads(slot, turned, gqkv_ref.at[0], gmain_ref, gleft_ref)
    projection_back(slot, gqkv_ref.at[0], main_ref, left_ref, gh_ref)


def last_part(ghp_ref, perm_ref, x_ref, mod_ref, gmid_ref, gin_ref, sums_ref, gh, partial):
    unpermute(perm_ref, ghp_ref, gh)
    partial[...] = jnp.zeros_like(partial)

    def norm(rows):
        normed, rstd = norm_parts(x_ref[rows, :].astype(f32))
        grad = gh[rows, :]
        partial[0] += eight_rows(grad)
        partial[1] += eight_rows(grad * normed)
        gin_ref[rows, :] = gmid_ref[rows, :] + norm_back(normed, rstd, mod_ref[1:2, :], grad)

    row_loop(x_ref.shape[0], norm)
    for k in range(2):
        sums_ref[k : k + 1, :] = jnp.sum(partial[k], axis=0, keepdims=True)


def ring_place(z):
    return z + (z // 2) * (5 - 2 * z)


class Here:
    def __init__(self):
        row, x = lax.axis_index("dp"), lax.axis_index("seq")
        z, y, core = row // 4, (row // 2) % 2, row % 2
        self.x, self.y, self.z, self.core = x, y, z, core
        self.p = ring_place(z)
        place = lambda z, y, core, x: ((z * 2 + y) * 2 + core, x)
        self.next = place(ring_place((self.p + 1) % 4), y, core, x)
        self.prev = place(ring_place((self.p + 3) % 4), y, core, x)
        self.over_y = place(z, 1 - y, core, x)
        self.over_x = place(z, y, core, 1 - x)
        self.sibling = place(z, y, 1 - core, x)
        self.along = [place(ring_place((self.p + o) % 4), y, core, x) for o in (1, 2, 3)]
        self.around = [self.over_y, self.over_x, place(z, 1 - y, core, 1 - x)]

    def ring_z(self, back):
        return ring_place((self.p + 8 - back) % 4)

    def greet(self, wide=False):
        barrier = pltpu.get_barrier_semaphore()
        devices = [self.next, self.prev, self.over_y, self.over_x, self.sibling]
        if wide:
            devices += [self.along[1], self.around[2]]
        for device in devices:
            pl.semaphore_signal(barrier, inc=1, device_id=device, device_id_type=pl.DeviceIdType.MESH)
        pl.semaphore_wait(barrier, len(devices))


def push(source, target, send, recv, device):
    copy = pltpu.make_async_remote_copy(
        src_ref=source, dst_ref=target, send_sem=send, recv_sem=recv, device_id=device,
        device_id_type=pl.DeviceIdType.MESH,
    )
    copy.start()
    return copy


def routes(rows):
    tiles = rows // 16
    third = 2 if tiles >= 7 else 0
    first = -(-(tiles - third) // 2)
    cuts = [0, 16 * first, 16 * (tiles - third), rows]
    return [pl.ds(low, high - low) for low, high in zip(cuts, cuts[1:])]


class Gather:
    def __init__(self, tag, here, ins, outs, sems):
        self.here, self.ins, self.outs, self.sems = here, ins, outs, sems
        self.flights, self.todo, self.own = {}, {}, {}
        for i in range(len(ins)):
            a, b, c = routes(ins[i].shape[0])
            self.todo[tag, 0, i, 0] = (), functools.partial(self.along_z, i, 0)
            for s in range(4):
                if s:
                    self.todo[tag, 0, i, s] = (("z", i, s - 1),), functools.partial(self.along_z, i, s)
                self.todo[tag, 1, i, s] = (("a1", i, s),), functools.partial(self.second, i, s, 0)
                waits = [("a2", i, s)]
                if b.size:
                    self.todo[tag, 2, i, s] = (("b1", i, s),), functools.partial(self.second, i, s, 1)
                    waits.append(("b2", i, s))
                if c.size:
                    waits.append(("cy", i, 0) if s == 0 else ("cz", i, s - 1))
                    self.todo[tag, 4, i, s] = (waits[-1],), functools.partial(self.third, i, s)
                    waits[-1] = ("c", i, s)
                self.todo[tag, 5, i, s] = tuple(waits), functools.partial(self.across, i, s)
            if c.size:
                self.todo[tag, 3, i, 0] = (("cx", i, 0),), functools.partial(self.third_over_y, i)

    def send(self, key, number, source, target, device):
        i, s = key[1:]
        self.flights[key] = push(source, target, self.sems[0].at[number, i, s], self.sems[1].at[number, i, s], device)

    def start(self):
        here = self.here
        for i, block in enumerate(self.ins):
            target = self.outs[i].at[here.z, here.y, here.core, here.x]
            self.own[i] = pltpu.make_async_copy(block, target, self.sems[2].at[i])
            self.own[i].start()

    def run(self, name):
        waits, action = self.todo.pop(name)
        for key in waits:
            if key[0] != "c":
                self.flights[key].wait_recv()
        action()

    def settle(self, i):
        if i in self.own:
            self.own.pop(i).wait()

    def along_z(self, i, s):
        here = self.here
        a, b, c = routes(self.ins[i].shape[0])
        slot = self.outs[i].at[here.ring_z(s), here.y, here.core, here.x]
        held = self.ins[i] if s == 0 else slot
        if s < 3:
            both = pl.ds(0, a.size + b.size)
            self.send(("z", i, s), 0, held.at[both], slot.at[both], here.next)
        self.send(("a1", i, s), 1, held.at[a], slot.at[a], here.over_y)
        if b.size:
            self.send(("b1", i, s), 2, held.at[b], slot.at[b], here.over_x)
        if s == 0 and c.size:
            self.send(("cx", i, 0), 5, held.at[c], slot.at[c], here.over_x)

    def second(self, i, s, half):
        here, out = self.here, self.outs[i]
        a, b, c = routes(self.ins[i].shape[0])
        z = here.ring_z(s)
        if s == 0:
            self.settle(i)
        if half:
            block = out.at[z, here.y, here.core, :, b]
            self.send(("b2", i, s), 4, block, block, here.over_y)
        else:
            block = out.at[z, :, here.core, here.x, a]
            self.send(("a2", i, s), 3, block, block, here.over_x)

    def third_over_y(self, i):
        here = self.here
        c = routes(self.ins[i].shape[0])[2]
        self.settle(i)
        block = self.outs[i].at[here.z, here.y, here.core, :, c]
        self.send(("cy", i, 0), 6, block, block, here.over_y)

    def third(self, i, s):
        here = self.here
        c = routes(self.ins[i].shape[0])[2]
        if s < 3:
            block = self.outs[i].at[here.ring_z(s), :, here.core, :, c]
            self.send(("cz", i, s), 7, block, block, here.next)

    def across(self, i, s):
        here = self.here
        block = self.outs[i].at[here.ring_z(s), :, here.core]
        self.send(("core", i, s), 8, block, block, here.sibling)

    def arrived(self, i, places=range(4)):
        for s in places:
            self.flights["core", i, s].wait_recv()

    def finish(self):
        for copy in self.flights.values():
            copy.wait_send()


def gather_sems(count):
    dma = pltpu.SemaphoreType.DMA
    return [dma((9, count, 4)), dma((9, count, 4)), dma((count,))]


class ShortGather:
    def __init__(self, tag, here, own, out, sems):
        self.here, self.own, self.out, self.sems = here, own, out, sems
        self.flights = {}
        self.todo = {
            (tag, 0, 0, 0): ((), self.along),
            (tag, 1, 0, 0): (tuple(("z", o) for o in range(3)), self.around),
            (tag, 2, 0, 0): (tuple(("xy", o) for o in range(3)), self.across),
        }

    def send(self, key, number, source, target, device):
        self.flights[key] = push(source, target, self.sems[0].at[number], self.sems[1].at[number], device)

    def start(self):
        here = self.here
        target = self.out.at[here.z, here.y, here.core, here.x]
        self.copy = pltpu.make_async_copy(self.own, target, self.sems[0].at[7])
        self.copy.start()

    def run(self, name):
        waits, action = self.todo.pop(name)
        for key in waits:
            self.flights[key].wait_recv()
        action()

    def along(self):
        here = self.here
        slot = self.out.at[here.z, here.y, here.core, here.x]
        for o, device in enumerate(here.along):
            self.send(("z", o), o, self.own, slot, device)

    def around(self):
        here = self.here
        self.copy.wait()
        block = self.out.at[:, here.y, here.core, here.x]
        for o, device in enumerate(here.around):
            self.send(("xy", o), 3 + o, block, block, device)

    def across(self):
        block = self.out.at[:, :, self.here.core]
        self.send(("core", 0), 6, block, block, self.here.sibling)

    def arrived(self):
        self.flights["core", 0].wait_recv()

    def finish(self):
        for copy in self.flights.values():
            copy.wait_send()


def short_gather_sems():
    return [pltpu.SemaphoreType.DMA((8,)), pltpu.SemaphoreType.DMA((8,))]


class ShortScatter:
    def __init__(self, tag, here, partial, final, scratch):
        self.acc, self.mate, self.xy_rows, self.z_rows, self.send_sem, self.recv_sem = scratch
        self.here, self.partial, self.final = here, partial, final
        self.flights = {}
        self.todo = {
            (tag, 0, 0, 0): (tuple(("core", n) for n in range(8)), self.from_sibling),
            (tag, 1, 0, 0): (tuple(("xy", o) for o in range(3)), self.around),
            (tag, 2, 0, 0): (tuple(("z", o) for o in range(3)), self.last),
        }

    def send(self, key, number, source, target, device):
        self.flights[key] = push(source, target, self.send_sem.at[number], self.recv_sem.at[number], device)

    def start(self):
        here = self.here
        for z in range(4):
            for y in range(2):
                rows = pl.ds(8 * z + 4 * y + 2 * (1 - here.core), 2)
                self.send(
                    ("core", 2 * z + y), 2 * z + y, self.partial.at[rows], self.mate.at[z, y], here.sibling
                )

    def run(self, name):
        waits, action = self.todo.pop(name)
        for key in waits:
            self.flights[key].wait_recv()
        action()

    def from_sibling(self):
        here = self.here
        for z in range(4):
            for y in range(2):
                rows = pl.ds(8 * z + 4 * y + 2 * here.core, 2)
                self.acc[z, y] = self.partial[rows] + self.mate[z, y]
        places = [(1 - here.y, here.x), (here.y, 1 - here.x), (1 - here.y, 1 - here.x)]
        for o, (y, x) in enumerate(places):
            self.send(("xy", o), 8 + o, self.acc.at[:, y, x], self.xy_rows.at[o], here.around[o])

    def around(self):
        here = self.here
        mine = self.acc.at[:, here.y, here.x]
        mine[...] = mine[...] + self.xy_rows[0] + self.xy_rows[1] + self.xy_rows[2]
        for o, device in enumerate(here.along):
            z = ring_place((here.p + o + 1) % 4)
            self.send(("z", o), 11 + o, mine.at[z], self.z_rows.at[o], device)

    def last(self):
        here = self.here
        self.final(self.acc[here.z, here.y, here.x] + self.z_rows[0] + self.z_rows[1] + self.z_rows[2])

    def finish(self):
        for copy in self.flights.values():
            copy.wait_send()


def short_scatter_scratch(block):
    rows, lanes = block.shape[-2:]
    dma = pltpu.SemaphoreType.DMA
    return [
        pltpu.VMEM((4, 2, 2, rows, lanes), f32), pltpu.VMEM((4, 2, 2, rows, lanes), f32),
        pltpu.VMEM((3, 4, rows, lanes), f32), pltpu.VMEM((3, rows, lanes), f32), dma((14,)), dma((14,)),
    ]


def gathered_shape(block):
    return sds((4, 2, 2, 2) + block.shape, block.dtype)


def add_rows(target, source, lead, low, size):
    chunk = 16

    @pl.loop(0, size // chunk)
    def _(r):
        start = pl.multiple_of(r * chunk, chunk)
        here, there = pl.ds(low + start, chunk), pl.ds(start, chunk)
        for at in lead:
            target[at + (here,)] = target[at + (here,)] + source[at + (there,)]


class Scatter:
    def __init__(self, tag, here, ins, final, scratch):
        (
            self.acc, self.mate, self.one_a, self.one_b, self.two_rows, self.ring_rows, self.ring_c, self.c_y, self.c_x,
            self.send_sem, self.recv_sem, self.load_sem,
        ) = scratch
        self.here, self.ins, self.final = here, ins, final
        self.rows = self.acc.shape[3]
        self.a, self.b, self.c = routes(self.rows)
        self.flights, self.loads, self.todo, self.released = {}, {}, {}, set()
        for k in range(4):
            self.todo[tag, 0, 0, k] = (("core", k),), functools.partial(self.from_sibling, k)
            self.todo[tag, 1, 0, k] = (("a1", k),), functools.partial(self.first_sum, k, 0)
            waits = [("a2", k)]
            if self.b.size:
                self.todo[tag, 2, 0, k] = (("b1", k),), functools.partial(self.first_sum, k, 1)
                waits.append(("b2", k))
            if k:
                waits.append(("z", k - 1))
            self.todo[tag, 3, 0, k] = tuple(waits), functools.partial(self.second_sum, k)
            if self.c.size:
                waits = (("c", k), ("cz", k - 1)) if k else (("c", k),)
                self.todo[tag, 4, 0, k] = waits, functools.partial(self.third_sum, k)
        if self.c.size:
            self.todo[tag, 5, 0, 0] = (("cy", 0),), self.third_over_y
            self.todo[tag, 5, 0, 1] = (("cx", 0), ("own", 0)), self.third_over_x

    def send(self, key, number, source, target, device, piece=0):
        at = (number + piece, key[1])
        self.flights[key] = push(source, target, self.send_sem.at[at], self.recv_sem.at[at], device)

    def pieces(self, k):
        z, low = self.here.ring_z(k + 1), 0
        for number, ref in enumerate(self.ins):
            if len(ref.shape) == 3:
                for y in range(2):
                    yield (
                        number + y, lambda core, y=y: ref.at[pl.ds(8 * z + 4 * y + 2 * core, 2)], lambda slot, y=y: slot.at[y]
                    )
            elif len(ref.shape) == 5:
                yield number, lambda core, ref=ref: ref.at[:, core], lambda slot: slot
            else:
                span = pl.ds(low, ref.shape[4])
                low += ref.shape[4]
                yield (
                    number, lambda core, ref=ref: ref.at[z, :, core], lambda slot, span=span: slot.at[:, :, span]
                )

    def load(self, k, numbers=None):
        for number, source, target in self.pieces(k):
            if numbers is not None and number not in numbers:
                continue
            self.loads[k, number] = pltpu.make_async_copy(
                source(self.here.core), target(self.acc.at[k]), self.load_sem.at[k, number]
            )
            self.loads[k, number].start()

    def to_sibling(self, k, numbers=None):
        for number, source, target in self.pieces(k):
            if numbers is not None and number not in numbers:
                continue
            self.send(
                ("core", k, number), 8, source(1 - self.here.core), target(self.mate.at[k]), self.here.sibling, number
            )

    def offer(self, k):
        self.load(k)
        self.to_sibling(k)

    def release(self, k):
        for number, _, _ in self.pieces(k):
            self.flights["core", k, number].wait_send()
        self.released.add(k)

    def prepare(self, numbers=None):
        for k in range(4):
            self.load(k, numbers)

    def start(self, numbers=None):
        for k in range(4):
            self.to_sibling(k, numbers)

    def run(self, name):
        waits, action = self.todo.pop(name)
        for key in waits:
            if key[0] == "core":
                for number, _, _ in self.pieces(key[1]):
                    self.loads[key[1], number].wait()
                    self.flights["core", key[1], number].wait_recv()
            elif key[0] not in ("c", "own"):
                self.flights[key].wait_recv()
        action()

    def from_sibling(self, k):
        here, acc = self.here, self.acc.at[k]
        add_rows(acc, self.mate.at[k], [(a, b) for a in range(2) for b in range(2)], 0, self.rows)
        self.send(("a1", k), 0, acc.at[:, 1 - here.x, self.a], self.one_a.at[k], here.over_x)
        if self.b.size:
            self.send(("b1", k), 1, acc.at[1 - here.y, :, self.b], self.one_b.at[k], here.over_y)

    def first_sum(self, k, half):
        here, acc = self.here, self.acc.at[k]
        if half:
            add_rows(acc.at[here.y], self.one_b.at[k], [(0,), (1,)], self.b.start, self.b.size)
            self.send(
                ("b2", k), 3, acc.at[here.y, 1 - here.x, self.b], self.two_rows.at[k, self.b], here.over_x
            )
        else:
            add_rows(acc.at[:, here.x], self.one_a.at[k], [(0,), (1,)], self.a.start, self.a.size)
            self.send(
                ("a2", k), 2, acc.at[1 - here.y, here.x, self.a], self.two_rows.at[k, self.a], here.over_y
            )

    def second_sum(self, k):
        here = self.here
        size = self.a.size + self.b.size
        mine = self.acc.at[k, here.y, here.x]
        add_rows(mine, self.two_rows.at[k], [()], 0, size)
        if k:
            add_rows(mine, self.ring_rows.at[k - 1], [()], 0, size)
        if k < 3:
            self.send(("z", k), 4, mine.at[pl.ds(0, size)], self.ring_rows.at[k], here.next)
        elif not self.c.size:
            self.final(mine)

    def third_sum(self, k):
        here, acc = self.here, self.acc.at[k]
        if k:
            add_rows(acc, self.ring_c.at[k - 1], [(a, b) for a in range(2) for b in range(2)], self.c.start, self.c.size)
        if k < 3:
            self.send(("cz", k), 5, acc.at[:, :, self.c], self.ring_c.at[k], here.next)
        else:
            self.send(("cy", 0), 6, acc.at[1 - here.y, :, self.c], self.c_y, here.over_y)

    def third_over_y(self):
        here, acc = self.here, self.acc.at[3]
        add_rows(acc.at[here.y], self.c_y, [(0,), (1,)], self.c.start, self.c.size)
        self.send(("cx", 0), 7, acc.at[here.y, 1 - here.x, self.c], self.c_x, here.over_x)

    def third_over_x(self):
        mine = self.acc.at[3, self.here.y, self.here.x]
        add_rows(mine, self.c_x, [()], self.c.start, self.c.size)
        self.final(mine)

    def finish(self):
        for key, copy in self.flights.items():
            if key[0] != "core" or key[1] not in self.released:
                copy.wait_send()


def scatter_scratch(block):
    dma = pltpu.SemaphoreType.DMA
    rows, lanes, kind = sum(b.shape[-2] for b in block), block[0].shape[-1], block[0].dtype
    a, b, c = (max(span.size, 16) for span in routes(rows))
    both = sum(span.size for span in routes(rows)[:2])
    return [
        pltpu.VMEM((4, 2, 2, rows, lanes), kind), pltpu.VMEM((4, 2, 2, rows, lanes), kind),
        pltpu.VMEM((4, 2, a, lanes), kind), pltpu.VMEM((4, 2, b, lanes), kind),
        pltpu.VMEM((4, both, lanes), kind), pltpu.VMEM((3, both, lanes), kind),
        pltpu.VMEM((3, 2, 2, c, lanes), kind), pltpu.VMEM((2, c, lanes), kind), pltpu.VMEM((c, lanes), kind),
        dma((11, 4)), dma((11, 4)), dma((4, 3)),
    ]


def in_order(plan, chain, networks):
    pieces = iter(chain)
    for item in plan:
        if item == -1:
            next(pieces)()
        else:
            networks[item[0]].run(item)
    assert next(pieces, None) is None and not any(net.todo for net in networks.values())


def small_rows(cond, forget, taps, place):
    at = lax.rem(place * taps.shape[0], LANES)
    taps = lax.dynamic_update_slice(jnp.zeros((4 * LANES,), bf16), taps, (at,)).reshape(4, LANES)
    cond = cond.reshape(-1, LANES)
    forget = forget.reshape(36, -1)
    return jnp.concatenate([
        jnp.pad(cond, ((0, 16 - cond.shape[0]), (0, 0))), jnp.pad(taps, ((0, 12), (0, 0))),
        jnp.pad(forget, ((0, 12), (0, LANES - forget.shape[1]))),
    ])


def unpack_small(small, taps_share, wf_ref, taps_ref, flat):
    wf_ref[: 32 * GROUPS, :] = small[:, 32:64, :].reshape(32 * GROUPS, LANES)
    wf_ref[32 * GROUPS :, :] = dot(pick_left(None, 0), small[:, 64:80, :].reshape(16 * GROUPS, LANES)).astype(bf16)
    flat[...] = jnp.zeros_like(flat)
    for d in range(GROUPS):
        row = d * taps_share // LANES
        flat[row : row + 4, :] += small[d, 16:32, :].astype(f32)[:4]
    tiles = taps_ref.shape[1] // LANES
    taps_ref[...] = jnp.zeros_like(taps_ref)
    for k in range(10):
        for t in range(tiles):
            taps_ref[k : k + 1, t * LANES : (t + 1) * LANES] = flat[k * tiles + t : k * tiles + t + 1, :]


def pack_rows(sources, wide, left, out, other=None):
    for j, (source, first, per_row) in enumerate(sources):
        target = other if other is not None and j == 3 else out.at[pl.ds(32 * j, 32)]
        if first == 0:
            wide[: source.shape[0], :] = source[...].astype(f32)
        for t in range(out.shape[1] // LANES):
            cols = slice(t * LANES, (t + 1) * LANES)
            rows = wide[pl.ds(first + t, 36, stride=per_row), :]
            target[:, cols] = rows[:32].astype(bf16)
            left[4 * j : 4 * j + 4, cols] = rows[32:]
    out[(128 if other is None else 96) : (144 if other is None else 112), :] = left[...].astype(bf16)


def fill_permutation(perm_ref):
    width = perm_ref.shape[0]
    at = lax.broadcasted_iota(jnp.int32, (1, width), 1)
    late = at - 32 * GROUPS
    order = jnp.where(late < 0, (at >> 5) * 36 + (at & 31), (late >> 2) * 36 + 32 + (late & 3))
    for rows in spans(width, 2 * LANES):
        row = lax.broadcasted_iota(jnp.int32, (rows.stop - rows.start, width), 0) + rows.start
        perm_ref[rows, :] = (row == order).astype(bf16)


def forward_kernel(
    head_width, heads, taps_share, x_ref, ada_ref, bias_ref, bf_ref, own_s, query_ref, key_ref, value_ref, out_ref, up_ref,
    all_s, all_a, all_u, xp_out, qkv_out, mix_out, mixedp_out, branch_out, middle_out, h2p_out, perm_out,
    mod_ref, wf_ref, taps_ref, gate_ref, run_ref, runt_ref, state_ref, rims_ref, given_ref, taken_ref,
    xp_ref, qkv_ref, mix_ref, mixedp_ref, branch_ref, middle_ref, h2p_ref, perm_ref,
    own_a, own_u, wide, ada_wide, rows_left, small, flat, partial, main, left, outbox, inbox, vpad, mixed, load_sem, swap_sem, *rest,
):
    length, width = x_ref.shape
    tiles = width // LANES
    here = Here()
    lower = here.x == 0
    squares = [(ref, 0, tiles) for ref in (query_ref, key_ref, value_ref, out_ref)]
    pack_rows(squares, wide, rows_left, own_a, own_u.at[pl.ds(144, 32)])
    pack_rows([(up_ref, j * tiles, 4 * tiles) for j in range(4)], wide, rows_left, own_u)
    first = ShortGather("f", here, own_s, all_s, rest[:2])
    gather = Gather("g", here, (own_a, own_u), (all_a, all_u), rest[2:5])

    def to_mod(total):
        for k in range(6):
            for t in range(tiles):
                mod_ref[k : k + 1, t * LANES : (t + 1) * LANES] = total[k * tiles + t : k * tiles + t + 1, :]
        mod_ref[6:8, :] = jnp.zeros((2, width), f32)

    scatter = ShortScatter("s", here, partial, to_mod, rest[5:])
    stores, loads = [], []

    def fetch(number, source, target):
        copy = pltpu.make_async_copy(source, target, load_sem.at[number])
        copy.start()
        return copy

    def modulation():
        first.arrived()
        fetch(5, all_s, small).wait()
        me = ((here.z * 2 + here.y) * 2 + here.core) * 2 + here.x
        row = lax.broadcasted_iota(jnp.int32, (width, LANES), 0)
        lane = lax.broadcasted_iota(jnp.int32, (width, LANES), 1)
        pick = ((row == lane + me * 36) & (lane < 36)).astype(bf16)
        lines = small[...].reshape(GROUPS, 80, LANES)[:, :16, :].astype(f32)
        mine = jnp.zeros((GROUPS, LANES), f32)
        for t in range(tiles):
            cond = lines[:, t, :]
            cond = (cond / (1.0 + jnp.exp(-cond))).astype(bf16)
            mine = mine + dot(cond, pick[t * LANES : (t + 1) * LANES])
        mine = mine[:, :36].astype(bf16)
        for t in range(6 * tiles):
            rows = ada_wide[pl.ds(t, 36, stride=6 * tiles), :].astype(bf16)
            partial[:, t, :] = dot(mine, rows) + bias_ref[t : t + 1, :].astype(f32)
        scatter.start()

    def small_arrays():
        unpack_small(small[...].reshape(GROUPS, 80, LANES), taps_share, wf_ref, taps_ref, flat)

    def norm_one():
        first_part(x_ref, mod_ref, perm_ref, wf_ref, bf_ref, xp_ref, gate_ref, run_ref, runt_ref, mixed)
        stores.extend([fetch(6, xp_ref, xp_out), fetch(13, perm_ref, perm_out)])
        total = run_ref[0, length - 1 : length, :]
        given_ref[0] = jnp.where(lower, jnp.exp(total - run_ref[0]), jnp.exp(run_ref[1]))
        taken_ref[0] = jnp.where(lower, jnp.exp(total - run_ref[1]), jnp.exp(run_ref[0]))
        mix_ref[...] = jnp.zeros_like(mix_ref)

    def load(slot):
        source = all_a.at[:, :, :, :, pl.ds(32 * slot, 32)] if slot < 3 else all_u.at[:, :, :, :, pl.ds(144, 32)]
        loads.append(fetch(slot, source, main.at[slot % 2]))

    def project(slot):
        if slot == 0:
            gather.arrived(0)
            others = fetch(4, all_a.at[:, :, :, :, pl.ds(96, 16)], left)
            load(0)
            load(1)
            others.wait()
        loads[slot].wait()

        def write(cols, value):
            qkv_ref[slot, :, cols] = value.astype(bf16)

        project_part(slot, xp_ref, main.at[slot % 2], left, write)
        if slot == 0:
            load(2)
        if slot == 2:
            stores.append(fetch(7, qkv_ref, qkv_out))

    def states():
        state_part(head_width, 1, lambda cols: qkv_ref[1, :, cols], qkv_ref.at[2], given_ref, outbox)
        edge = pl.multiple_of((1 - here.x) * (length - GRID), GRID)

        def write_edge(t, value):
            outbox[0, width + t * GRID : width + (t + 1) * GRID, :] = value

        edge_part(qkv_ref[2, pl.ds(edge, GRID), :], write_edge)
        stores.append(push(outbox, inbox, swap_sem.at[0], swap_sem.at[1], here.over_x))

    def mix(part):
        mix_part(head_width, heads, part * heads // 4, (part + 1) * heads // 4, qkv_ref, run_ref, runt_ref, mix_ref)

    def mixing():
        swap = stores.pop()
        swap.wait_recv()
        state_ref[0] = inbox[0, :width, :]
        for t in range(tiles):
            cols = slice(t * LANES, (t + 1) * LANES)
            rows = inbox[0, width + t * GRID : width + (t + 1) * GRID, :]
            rims_ref[0, :, cols] = jnp.where(lower, 0, rows).astype(bf16)
            rims_ref[1, :, cols] = jnp.where(lower, rows, 0).astype(bf16)
        fill_padded(vpad, rims_ref, qkv_ref[2])
        mixed_part(head_width, 1, qkv_ref, taken_ref, state_ref, taps_ref, vpad, mix_ref, mixed)
        stores.append(fetch(8, mix_ref, mix_out))
        swap.wait_send()

    def turn():
        gather.arrived(1)
        load(3)
        permute_part(mixed, perm_ref, mixedp_ref)
        stores.append(fetch(9, mixedp_ref, mixedp_out))

    def branch():
        loads[3].wait()
        branch_part(x_ref, mod_ref, mixedp_ref, main.at[1], left, branch_ref, middle_ref)
        stores.extend([fetch(10, branch_ref, branch_out), fetch(11, middle_ref, middle_out)])

    def norm_two():
        second_hidden(mod_ref, middle_ref, mixed)
        permute_part(mixed, perm_ref, h2p_ref)
        stores.append(fetch(12, h2p_ref, h2p_out))

    def prepare():
        fill_permutation(perm_ref)
        ada_wide[...] = ada_ref[...].astype(f32)
        partial[:, 6 * tiles :, :] = jnp.zeros((GROUPS, 64 - 6 * tiles, LANES), f32)

    chain = [prepare, modulation, small_arrays, norm_one]
    chain += [functools.partial(project, slot) for slot in range(3)] + [states]
    chain += [functools.partial(mix, part) for part in range(4)] + [mixing, turn, branch, norm_two]
    first.start()
    gather.start()
    here.greet(True)
    in_order(FORWARD_PLAN, chain, {"f": first, "g": gather, "s": scatter})
    for network in (first, gather, scatter):
        network.finish()
    for copy in stores:
        copy.wait()


def forward_fused(x, ada, bias, bf, small, shards, heads, taps_share):
    length, width = x.shape
    head_width = width // heads
    message = width + width // LANES * GRID
    anywhere, vm = pl.BlockSpec(memory_space=pl.ANY), pl.BlockSpec(memory_space=pltpu.VMEM)
    rows, wide = (length, width), (length, LANES)
    bulk = (
        sds(rows, bf16), sds((3,) + rows, bf16), sds(rows), sds(rows, bf16), sds(rows, bf16), sds(rows), sds(rows, bf16),
        sds((width, width), bf16),
    )
    kept = (
        sds((8, width)), sds((width, LANES), bf16), sds((16, width)), sds(wide), sds((2,) + wide), sds((2, LANES, length)),
        sds((1, width, LANES), bf16), sds((2, GRID, width), bf16), sds((1,) + wide), sds((1,) + wide),
    )
    partial = sds((GROUPS, 64, LANES))
    own, own_up = sds((112, width), bf16), sds((176, width), bf16)
    dma = pltpu.SemaphoreType.DMA
    out = pl.pallas_call(
        functools.partial(forward_kernel, head_width, heads, taps_share),
        out_shape=tuple(gathered_shape(b) for b in (small, own, own_up)) + bulk + kept,
        in_specs=[vm] * 10,
        out_specs=(anywhere,) * (3 + len(bulk)) + (vm,) * len(kept),
        scratch_shapes=[pltpu.VMEM(b.shape, b.dtype) for b in bulk] + [
            pltpu.VMEM(own.shape, bf16), pltpu.VMEM(own_up.shape, bf16), pltpu.VMEM(shards[4].shape, f32),
            pltpu.VMEM(ada.shape, f32), pltpu.VMEM((16, width), f32),
            pltpu.VMEM((4, 2, 2, 2) + small.shape, bf16), pltpu.VMEM((96, LANES), f32),
            pltpu.VMEM(partial.shape, f32), pltpu.VMEM((2, 4, 2, 2, 2, 32, width), bf16),
            pltpu.VMEM((4, 2, 2, 2, 16, width), bf16), pltpu.VMEM((1, message, LANES), bf16),
            pltpu.VMEM((1, message, LANES), bf16), pltpu.VMEM((length + 2 * GRID, width), bf16), pltpu.VMEM(rows, bf16),
            dma((14,)), dma((2,)),
        ] + short_gather_sems() + gather_sems(2) + short_scatter_scratch(partial),
        compiler_params=pltpu.CompilerParams(collective_id=0, has_side_effects=True, vmem_limit_bytes=VMEM_LIMIT),
        name="forward",
    )(x, ada, bias, bf, small, *shards)
    gathered = [g.reshape((GROUPS,) + g.shape[4:]) for g in out[:3]]
    return gathered, out[3 : 3 + len(bulk)], out[3 + len(bulk) :]


def feed_fused_kernel(
    h2p, cot, mod_ref, flat_d, up_in, middle_in,
    all_d, out_out, gh_out, gup_out, gleft_ref, ggate_ref, down_own,
    gdi, h2pt, act, slope, actt, gup, main, left, left_own, down, down_acc, gh, middle, stage_d, stage_u, own_d, wide, load_sem, *rest,
):
    length, width = h2p.shape
    main_rows = GROUPS * 32
    here = Here()
    gather = Gather("g", here, (own_d,), (all_d,), rest[:3])
    scatter = Scatter("d", here, [stage_d], plain_final(down_own), rest[3:])
    order = [here.ring_z(k + 1) for k in range(4)]

    def fetch(number, source, target):
        copy = pltpu.make_async_copy(source, target, load_sem.at[number])
        copy.start()
        return copy

    def load_up(k, number):
        rows = pl.ds(pl.multiple_of(32 * order[k], 32), 32)
        return fetch(number, up_in.at[:, rows], main.at[k % 2])

    def load_down(k):
        gather.arrived(0, [(k + 1) % 4])
        return fetch(8 + k, all_d.at[order[k]], down.at[k % 2])

    def left_rows(k):
        return dot(pick_left(None, order[k]), left[...].reshape(16 * GROUPS, width)).astype(bf16)

    def start():
        gdi[...] = (cot[...].astype(f32) * mod_ref[5:6, :]).astype(bf16)
        h2pt[...] = h2p[...].T
        gleft_ref[...] = jnp.zeros_like(gleft_ref)
        others.wait()

    def up_step(k):
        loads[k].wait()
        left_own[...] = left_rows(k)
        for cols in spans(width):
            up = dot(h2p[:, :main_rows], main[k % 2, :, :, cols].reshape(main_rows, -1))
            up = up + dot(h2p[:, main_rows:], left_own[:, cols])
            value, rate = gelu_both(up)
            value = value.astype(bf16)
            act[k, :, cols] = value
            actt[cols, :] = value.T
            slope[k, :, cols] = rate.astype(bf16)
        loads.append(load_up(k + 2, k + 2) if k < 2 else load_up(k - 2, k + 2))

    def down_grad(k):
        if k > 0:
            scatter.release(k - 1)
        for cols in spans(width):
            stage_d[:, :, :, :, cols] = dot(actt[...], gdi[:, cols]).astype(bf16).reshape(2, 2, 2, width // 8, -1)
        scatter.offer(k)

    def back_act(k):
        load_down(k).wait()
        rows_of = down[k % 2].reshape(width, width)
        for cols in spans(width):
            gup[:, cols] = (dot_bt(gdi[...], rows_of[cols]) * slope[k, :, cols].astype(f32)).astype(bf16)

    def down_step(k):
        rows_of = down[k % 2].reshape(width, width)
        for cols in spans(width):
            part = dot(act[k], rows_of[:, cols])
            if k == 0:
                down_acc[:, cols] = part
            else:
                down_acc[:, cols] += part
    def back_hidden(k):
        loads[4 + k].wait()
        for cols in spans(main_rows):
            part = dot_bt(gup[...], main[k % 2, cols.start // 32 : cols.stop // 32].reshape(-1, width))
            if k == 0:
                gh[:, cols] = part
            else:
                gh[:, cols] += part
        part = dot_bt(gup[...], left_rows(k))
        if k == 0:
            gh[:, main_rows:] = part
        else:
            gh[:, main_rows:] += part
        if k < 2:
            loads.append(load_up(k + 2, 6 + k))

    def up_grad(k):
        if k > 0:
            stores[k - 1].wait()
        projection_grads(order[k], h2pt, gup, stage_u, gleft_ref)
        rows = pl.ds(pl.multiple_of(32 * order[k], 32), 32)
        stores.append(fetch(13 + k, stage_u, gup_out.at[:, rows]))

    def end():
        keep = fetch(17, gh, gh_out)
        ggate_ref[...] = jnp.sum(cot[...].astype(f32) * down_acc[...], axis=0, keepdims=True)
        keep_middle.wait()
        for cols in spans(width):
            act[0, :, cols] = (middle[:, cols] + mod_ref[5:6, cols] * down_acc[:, cols]).astype(bf16)
        stores.extend([fetch(19, act.at[0], out_out), keep])

    chain = [start]
    for k in range(4):
        chain += [functools.partial(up_step, k), functools.partial(down_grad, k)]
    for k in range(4):
        chain += [functools.partial(step, k) for step in (back_act, down_step, back_hidden, up_grad)]
    others = fetch(12, up_in.at[:, pl.ds(128, 16)], left)
    loads = [load_up(0, 0), load_up(1, 1)]
    keep_middle = fetch(18, middle_in, middle)
    stores = []
    wide[...] = flat_d[...].astype(f32)
    for t in range(width // LANES):
        rows = wide[pl.ds(t, own_d.shape[0], stride=width // LANES), :]
        own_d[:, t * LANES : (t + 1) * LANES] = rows.astype(bf16)
    gather.start()
    here.greet()
    in_order(FEED_PLAN, chain + [end], {"d": scatter, "g": gather})
    scatter.finish()
    gather.finish()
    for copy in stores[3:]:
        copy.wait()


def feed_fused(h2p, cot, mod, flat_d, up_w, middle):
    length, width = h2p.shape
    anywhere, vm = pl.BlockSpec(memory_space=pl.ANY), pl.BlockSpec(memory_space=pltpu.VMEM)
    rows = (length, width)
    dma = pltpu.SemaphoreType.DMA
    stage = (2, 2, 2, width // 8, width)
    own = sds((width // 8, width), bf16)
    return pl.pallas_call(
        feed_fused_kernel,
        out_shape=(
            gathered_shape(own), sds(rows, bf16), sds(rows), sds((GROUPS, 128, width), bf16),
            sds((GROUPS, 16, width), bf16), sds((1, width)), sds(flat_d.shape),
        ),
        in_specs=[vm] * 4 + [anywhere] * 2,
        out_specs=(anywhere,) * 4 + (vm,) * 3,
        scratch_shapes=[
            pltpu.VMEM(rows, bf16), pltpu.VMEM((width, length), bf16), pltpu.VMEM((4,) + rows, bf16),
            pltpu.VMEM((4,) + rows, bf16), pltpu.VMEM((width, length), bf16), pltpu.VMEM(rows, bf16),
            pltpu.VMEM((2, GROUPS, 32, width), bf16), pltpu.VMEM((GROUPS, 16, width), bf16), pltpu.VMEM((128, width), bf16),
            pltpu.VMEM((2,) + stage, bf16), pltpu.VMEM(rows, f32), pltpu.VMEM(rows, f32), pltpu.VMEM(rows, f32),
            pltpu.VMEM(stage, bf16),
            pltpu.VMEM((GROUPS, 32, width), bf16), pltpu.VMEM(own.shape, bf16), pltpu.VMEM(flat_d.shape, f32), dma((20,)),
        ] + gather_sems(1) + scatter_scratch([sds(stage, bf16)]),
        compiler_params=pltpu.CompilerParams(
            collective_id=1, has_side_effects=True, vmem_limit_bytes=62 * 1024 * 1024
        ),
        name="feed",
    )(h2p, cot, mod, flat_d, up_w, middle)[1:]


def six(array):
    return array.reshape((4, 2, 2, 2) + array.shape[1:])


def flat_rows(out, first, value, per_row):
    for t in range(value.shape[1] // LANES):
        out[pl.ds(first + t, value.shape[0], stride=per_row), :] = value[:, t * LANES : (t + 1) * LANES]


def square_final(outs, out_left):
    def final(total):
        value = total[...].astype(f32)
        per_row = value.shape[1] // LANES
        for j, out in enumerate(outs):
            flat_rows(out, 0, value[32 * j : 32 * j + 32], per_row)
            flat_rows(out, 32 * per_row, value[96 + 4 * j : 100 + 4 * j], per_row)
        flat_rows(out_left, 0, value[108:112], per_row)

    return final


def columns_final(out, out_main):
    def final(total):
        value = total[...].astype(f32)
        tiles = value.shape[1] // LANES
        for j in range(4):
            flat_rows(out, j * tiles, value[32 * j : 32 * j + 32], 4 * tiles)
            flat_rows(out, 32 * 4 * tiles + j * tiles, value[128 + 4 * j : 132 + 4 * j], 4 * tiles)
        flat_rows(out_main, 0, value[144:176], tiles)

    return final


def plain_final(out):
    def final(total):
        value = total[...].astype(f32)
        flat_rows(out, 0, value, value.shape[1] // LANES)

    return final


def small_final(out):
    def final(total):
        out[...] = total[...]

    return final


def fill_small(block, gforget, conv, bias, flat, taps_share):
    tiles = conv.shape[1] // LANES
    for k in range(10):
        for t in range(tiles):
            flat[k * tiles + t : k * tiles + t + 1, :] = conv[k : k + 1, t * LANES : (t + 1) * LANES]
    flat[10 * tiles :, :] = jnp.zeros_like(flat[10 * tiles :, :])
    block[:, :32, :] = gforget[: 32 * GROUPS, :].reshape(GROUPS, 32, LANES)
    block[:, 40:, :] = jnp.broadcast_to(bias[...].reshape(1, 1, LANES), (GROUPS, 8, LANES))
    for d in range(GROUPS):
        at = 32 * GROUPS + 4 * d
        block[d, 32:36, :] = gforget[at : at + 4, :]
        row = d * taps_share // LANES
        block[d, 36:40, :] = flat[row : row + 4, :]


def backward_kernel(
    head_width, heads, taps_share,
    mod_ref, run_ref, runt_ref, taken_ref, given_ref, gate_ref, state_ref, vrims_ref, taps_ref,
    ghp_in, perm_in, middle_in, cot_in, branch_in, mixedp_in, mix_in, weight_in, up_in, qkv_in, xp_in, gup_in, gupl_in,
    gmid_out, gqkv_out, gmain_out, gout_out, small_out, gleft_ref, ggate_ref, sums_ref, up_ref, out_ref,
    pool, perm, gmix, gb, main, qkv, gqkv, held, vpad, gpad, pair_rows, pair_cols,
    outbox, inbox, rims, leave, conv_ref, bias_ref, gforget_ref, flat, small, partial, fetch_sem, swap_sem, *scratch,
):
    length, width = gmix.shape
    here = Here()
    lower = here.x == 0
    gmixed = gpad.at[pl.ds(GRID, length)]
    turned = perm.at[:, pl.ds(0, length)]
    scatter = Scatter("u", here, [gup_in, gupl_in, gout_out], columns_final(up_ref, out_ref), scratch)
    scatter.prepare((0, 1))

    def fetch(number, source, target):
        copy = pltpu.make_async_copy(source, target, fetch_sem.at[number])
        copy.start()
        return copy

    first = [
        fetch(0, ghp_in, pool.at[0]), fetch(1, perm_in, perm), fetch(2, middle_in, pool.at[1]), fetch(3, cot_in, qkv.at[0]),
        fetch(4, branch_in, qkv.at[1]), fetch(5, mixedp_in, qkv.at[2]),
        fetch(6, up_in.at[:, :, :, :, pl.ds(144, 32)], main.at[0]),
        fetch(7, weight_in.at[:, pl.ds(96, 16)], gleft_ref),
        fetch(8, mix_in, pool.at[2]),
    ]
    second = second_part(
        head_width, pool.at[0], perm, pool.at[1], mod_ref, qkv.at[0], qkv.at[1], qkv.at[2], pool.at[2], main.at[0], gleft_ref,
        pool.at[1], gmixed, gmix, main.at[1], gleft_ref, sums_ref, pool.at[3], gb, partial,
    )
    gq, gk, gv = pool.at[0], pool.at[2], pool.at[3]
    early = jnp.where(lower, jnp.ones((1, LANES), f32), 0.0)
    carry = carry_part(
        head_width, 1, early, qkv, gmix, gq, gk, gv, pair_rows, pair_cols, taken_ref, given_ref, gate_ref, state_ref,
        leave, jnp.zeros((1, LANES), f32), vpad, gpad, taps_ref, gqkv, ggate_ref, conv_ref, bias_ref,
    )
    stores = []

    def begin():
        first[0].wait()
        first[1].wait()
        next(second)
        for copy in first[2:]:
            copy.wait()

    def out_grad():
        next(second)
        stores.append(fetch(11, main.at[1], gout_out))
        next(second)
        stores.pop().wait()

    def states():
        again = fetch(9, qkv_in, qkv)
        scatter.prepare((2,))
        scatter.start((2,))
        stores.extend([fetch(10, pool.at[1], gmid_out), fetch(12, xp_in, gb)])
        for ref in (gq, gk, gv, pair_rows, pair_cols):
            ref[...] = jnp.zeros_like(ref)
        again.wait()
        state_part(head_width, 1, lambda cols: qkv[0, :, cols], gmix, taken_ref, outbox)
        edge = pl.multiple_of((1 - here.x) * (length - GRID), GRID)

        def write_edge(t, value):
            outbox[0, width + t * GRID : width + (t + 1) * GRID, :] = value

        edge_part(gmixed[pl.ds(edge, GRID), :], write_edge)
        stores.append(push(outbox, inbox, swap_sem.at[0], swap_sem.at[1], here.over_x))

    def pairs(part):
        pairs_part(
            head_width, heads, part * heads // 4, (part + 1) * heads // 4, qkv, gmix, run_ref, runt_ref, gq, gk, gv,
            pair_rows, pair_cols, held,
        )

    def carry_first():
        swap = stores.pop()
        swap.wait_recv()
        leave[0] = inbox[0, :width, :]
        for t in range(width // LANES):
            cols = slice(t * LANES, (t + 1) * LANES)
            edge_rows = inbox[0, width + t * GRID : width + (t + 1) * GRID, :]
            rims[0, :, cols] = jnp.where(lower, 0, edge_rows).astype(bf16)
            rims[1, :, cols] = jnp.where(lower, edge_rows, 0).astype(bf16)
        fill_padded(vpad, vrims_ref, qkv[2])
        gpad[:GRID, :] = rims[0]
        gpad[GRID + length :, :] = rims[1]
        next(carry)
        swap.wait_send()

    def turn():
        stores.append(fetch(13, gqkv, gqkv_out))
        stores[1].wait()
        turned[...] = gb[...].T
        gforget_ref[...] = dot(turned[...], ggate_ref[...])
        fill_small(small, gforget_ref, conv_ref, bias_ref, flat, taps_share)
        fetch(17, small, small_out).wait()

    def weight(slot):
        buffer = main.at[slot % 2]
        if slot == 2:
            stores[3].wait()
        projection_grads(slot, turned, gqkv.at[slot], buffer, gleft_ref)
        stores.append(fetch(14 + slot, buffer, gmain_out.at[:, :, :, :, pl.ds(32 * slot, 32)]))

    chain = [begin, functools.partial(next, second), out_grad, states]
    chain += [functools.partial(pairs, part) for part in range(4)] + [carry_first]
    chain += [functools.partial(next, carry)] * 3 + [turn] + [functools.partial(weight, slot) for slot in range(3)]
    here.greet()
    scatter.start((0, 1))
    in_order(BACKWARD_PLAN, chain, {"u": scatter})
    scatter.finish()
    for number in (0, 2, 4, 5):
        stores[number].wait()


def backward_fused(heads, taps_share, small, arrays, grads):
    length, width = arrays[0].shape
    head_width = width // heads
    message = width + width // LANES * GRID
    anywhere, vm = pl.BlockSpec(memory_space=pl.ANY), pl.BlockSpec(memory_space=pltpu.VMEM)
    rows, wide = (length, width), (length, LANES)
    dma = pltpu.SemaphoreType.DMA
    return pl.pallas_call(
        functools.partial(backward_kernel, head_width, heads, taps_share),
        out_shape=(
            sds(rows), sds((3,) + rows, bf16), sds((4, 2, 2, 2, 96, width), bf16), sds((4, 2, 2, 2, 32, width), bf16),
            sds((GROUPS, 48, LANES)), sds((GROUPS, 16, width), bf16), sds(wide, bf16), sds((8, width)),
            sds((144 * width // LANES, LANES)), sds((32 * width // LANES, LANES)),
        ),
        in_specs=[vm] * len(small) + [anywhere] * (len(arrays) + len(grads)),
        out_specs=(anywhere,) * 5 + (vm,) * 5,
        scratch_shapes=[
            pltpu.VMEM((4,) + rows, f32), pltpu.VMEM((width, width), bf16), pltpu.VMEM(rows, bf16), pltpu.VMEM(rows, bf16),
            pltpu.VMEM((2, 4, 2, 2, 2, 32, width), bf16), pltpu.VMEM((3,) + rows, bf16), pltpu.VMEM((3,) + rows, bf16), pltpu.VMEM((2, length, length), bf16),
            pltpu.VMEM((length + 2 * GRID, width), bf16), pltpu.VMEM((length + 2 * GRID, width), bf16),
            pltpu.VMEM((2,) + wide, f32), pltpu.VMEM((2, heads, length), f32),
            pltpu.VMEM((1, message, LANES), bf16), pltpu.VMEM((1, message, LANES), bf16),
            pltpu.VMEM((2, GRID, width), bf16), pltpu.VMEM((1, width, LANES), bf16), pltpu.VMEM((16, width), f32),
            pltpu.VMEM((1, LANES), f32), pltpu.VMEM((width, LANES), f32), pltpu.VMEM((96, LANES), f32),
            pltpu.VMEM((GROUPS, 48, LANES), f32), pltpu.VMEM((3, 8, width), f32), dma((18,)), dma((2,)),
        ] + scatter_scratch(list(grads) + [sds((4, 2, 2, 2, 32, width), bf16)]),
        compiler_params=pltpu.CompilerParams(
            collective_id=3, has_side_effects=True, vmem_limit_bytes=62 * 1024 * 1024
        ),
        name="backward",
    )(*small, *arrays, *[six(g) for g in grads])


def finish_kernel(
    mod_ref, sums_two, gate_two, ggate_ref, wf_ref,
    weight_in, gqkv_in, perm_in, x_in, gmid_in, gmain_in, gleft_in, small_in,
    gin_ref, all_mod, query_ref, key_ref, value_ref, out_ref, small_ref,
    main, left, gqkv, perm, x, gmid, ghp, gh, sums_one, own_mod, partial, load_sem, *rest,
):
    width = perm.shape[0]
    here = Here()
    scatter = Scatter(
        "a", here, [gmain_in, gleft_in], square_final((query_ref, key_ref, value_ref), out_ref), rest[:12]
    )
    small = Scatter("s", here, [small_in], small_final(small_ref), rest[12:24])
    gather = ShortGather("g", here, own_mod, all_mod, rest[24:])
    scatter.prepare()
    small.prepare()

    def fetch(number, source, target):
        copy = pltpu.make_async_copy(source, target, load_sem.at[number])
        copy.start()
        return copy

    def load(slot):
        return fetch(slot, weight_in.at[:, pl.ds(32 * slot, 32)], main.at[slot % 2])

    grads = fetch(3, gqkv_in, gqkv)
    rest_rows = fetch(4, weight_in.at[:, pl.ds(96, 16)], left)
    loads = [load(0), load(1)]
    others = [fetch(5, perm_in, perm), fetch(6, x_in, x), fetch(7, gmid_in, gmid)]

    def back(slot):
        if slot == 0:
            ghp[...] = dot_bt(ggate_ref[...], wf_ref[...])
            grads.wait()
            rest_rows.wait()
        loads[slot].wait()
        projection_back(slot, gqkv.at[slot], main.at[slot % 2], left, ghp)
        if slot == 0:
            loads.append(load(2))

    def last():
        for copy in others:
            copy.wait()
        last_part(ghp, perm, x, mod_ref, gmid, gin_ref, sums_one, gh, partial)
        lines = [sums_one[0:1, :], sums_one[1:2, :], sums_two[2:3, :], sums_two[0:1, :], sums_two[1:2, :], gate_two[...]]
        tiles = width // LANES
        for k, line in enumerate(lines):
            for t in range(tiles):
                own_mod[k * tiles + t : k * tiles + t + 1, :] = line[:, t * LANES : (t + 1) * LANES]
        own_mod[len(lines) * tiles :, :] = jnp.zeros_like(own_mod[len(lines) * tiles :, :])
        gather.start()

    here.greet(True)
    scatter.start()
    small.start()
    chain = [functools.partial(back, slot) for slot in range(3)] + [last]
    in_order(FINISH_PLAN, chain, {"a": scatter, "s": small, "g": gather})
    gather.arrived()
    for network in (scatter, small, gather):
        network.finish()


def finish_fused(small, arrays, grads, grad_small):
    length, width = arrays[3].shape
    anywhere, vm = pl.BlockSpec(memory_space=pl.ANY), pl.BlockSpec(memory_space=pltpu.VMEM)
    rows = (length, width)
    dma = pltpu.SemaphoreType.DMA
    own = sds((64, LANES))
    return pl.pallas_call(
        finish_kernel,
        out_shape=(sds(rows), gathered_shape(own)) + (sds((36 * width // LANES, LANES)),) * 3
        + (sds((4 * width // LANES, LANES)), sds(grad_small.shape[1:])),
        in_specs=[vm] * len(small) + [anywhere] * (len(arrays) + len(grads) + 1),
        out_specs=(vm, anywhere) + (vm,) * 5,
        scratch_shapes=[
            pltpu.VMEM((2, GROUPS, 32, width), bf16), pltpu.VMEM((GROUPS, 16, width), bf16), pltpu.VMEM((3,) + rows, bf16),
            pltpu.VMEM((width, width), bf16), pltpu.VMEM(rows, bf16), pltpu.VMEM(rows, f32), pltpu.VMEM(rows, f32),
            pltpu.VMEM(rows, f32), pltpu.VMEM((8, width), f32), pltpu.VMEM(own.shape, f32),
            pltpu.VMEM((2, 8, width), f32), dma((8,)),
        ] + scatter_scratch(grads) + scatter_scratch([grad_small]) + short_gather_sems(),
        compiler_params=pltpu.CompilerParams(
            collective_id=4, has_side_effects=True, vmem_limit_bytes=VMEM_LIMIT
        ),
        name="finish",
    )(*small, *arrays, *grads, six(grad_small))


def joined_states(messages, totals, width, head_width):
    count = lax.axis_size("seq")
    place = lax.axis_index("seq")

    def grid_rows(message):
        rows = message[width:].reshape(width // LANES, GRID, LANES)
        return rows.transpose(1, 0, 2).reshape(GRID, width)

    if count == 1:
        return jnp.zeros_like(messages[:, :width]), jnp.zeros((2, GRID, width), bf16)
    if count == 2:
        got = lax.ppermute(messages[0], "seq", [(0, 1), (1, 0)])
        rows = grid_rows(got)
        return got[None, :width], jnp.stack([jnp.where(place == 1, rows, 0), jnp.where(place == 0, rows, 0)])
    forward = [(i, i + 1) for i in range(count - 1)]
    backward = [(i + 1, i) for i in range(count - 1)]
    rims = jnp.stack([
        grid_rows(lax.ppermute(messages[0], "seq", forward)), grid_rows(lax.ppermute(messages[1], "seq", backward))
    ])
    states = lax.all_gather(messages[:, :width, :], "seq").astype(f32)
    passed = lax.all_gather(totals, "seq")
    heads_of_rows = np.arange(width) // head_width
    order = jnp.arange(count)
    ahead = jnp.zeros(states.shape[2:], f32)
    behind = jnp.zeros(states.shape[2:], f32)
    for source in range(count):
        between_up = jnp.where((order > source) & (order < place), 1.0, 0.0) @ passed
        between_down = jnp.where((order < source) & (order > place), 1.0, 0.0) @ passed
        ahead = ahead + jnp.where(source < place, jnp.exp(between_up), 0.0)[heads_of_rows, None] * states[source, 0]
        behind = behind + jnp.where(source > place, jnp.exp(between_down), 0.0)[heads_of_rows, None] * states[source, 1]
    return jnp.stack([ahead, behind]).astype(bf16), rims


def split_rows(matrix):
    grouped = matrix.reshape(GROUPS, -1, matrix.shape[1])
    return grouped[:, :32], grouped[:, 32:]


def pack_whole(parts, width):
    query, key, value, out, up, down = parts
    square = [piece.reshape(GROUPS, -1, width) for piece in (query, key, value, out)]
    up = up.reshape(GROUPS, square[0].shape[1], -1, width)
    columns = [up[:, :, j] for j in range(up.shape[2])]
    blocks = []
    for group in (square, columns):
        blocks.append(
            jnp.concatenate([piece[:, :32] for piece in group] + [piece[:, 32:] for piece in group], axis=1)
        )
    return blocks + [down.reshape(GROUPS, -1, width)]


def unpack_squares(block):
    return [
        jnp.concatenate([block[..., 32 * j : 32 * j + 32, :], block[..., 128 + 4 * j : 132 + 4 * j, :]], axis=-2)
        for j in range(4)
    ]


def unpack_blocks(blocks):
    squares = unpack_squares(blocks[0])
    columns = unpack_squares(blocks[1])
    lead = blocks[0].shape[:-2]
    up = jnp.stack(columns, axis=-2)
    return [piece.reshape(lead + (-1,)) for piece in squares] + [up.reshape(lead + (-1,)), blocks[2].reshape(lead + (-1,))]


def on_device(
    activations, conditioning, cotangent, w_ada, b_ada, w_query, w_key, w_value, w_forget, b_forget, conv_taps, w_out,
    w_up, w_down,
):
    _, length, width = activations.shape
    heads = b_forget.shape[0]
    head_width = width // heads
    data_count, seq_count = lax.axis_size("dp"), lax.axis_size("seq")
    devices = data_count * seq_count
    me = lax.axis_index("dp") * seq_count + lax.axis_index("seq")
    packed_here = (data_count, seq_count) == (16, 2)
    everywhere = ("dp", "seq")

    mod_width = 6 * width
    share = w_ada.shape[0]
    if share % mod_width == 0:
        ada_rows = share // mod_width
        first_row, inset = me * ada_rows, None
        ada_part = w_ada.reshape(ada_rows, mod_width)
    else:
        ada_rows = -(-share // mod_width) + 1
        first_row = (me * share) // mod_width
        inset = me * share - first_row * mod_width
        ada_part = lax.dynamic_update_slice(jnp.zeros((ada_rows * mod_width,), bf16), w_ada, (inset,))
        ada_part = ada_part.reshape(ada_rows, mod_width)

    def own_columns(cond_all):
        cond_act = jax.nn.silu(cond_all.astype(f32)).astype(bf16)
        cond_wide = jnp.pad(cond_act, ((0, 0), (0, ada_rows)))
        return lax.dynamic_slice_in_dim(cond_wide, first_row, ada_rows, axis=1)

    main_rows = 32 * GROUPS
    forget_b = jnp.pad(b_forget.astype(f32), (0, LANES - heads)).reshape(1, LANES)
    x = activations[0]
    cot = cotangent[0]
    rows = (length, width)

    def main_spec(block, columns=width):
        return pl.BlockSpec((GROUPS, 32, columns), block)

    def left_spec(block, columns=width):
        return pl.BlockSpec((GROUPS, 16, columns), block)

    def whole(shape):
        return pl.BlockSpec(shape, lambda *_: (0,) * len(shape))

    ways = 1 if seq_count == 2 else 2
    message_rows = width + width // LANES * GRID
    state_call = call(
        functools.partial(state_kernel, head_width, ways), sds((ways, message_rows, LANES), bf16), "states"
    )
    place = lax.axis_index("seq")

    def edges(values):
        low, high = values[:GRID], values[-GRID:]
        if ways == 1:
            return jnp.where(place == 0, high, low)[None]
        return jnp.stack([high, low])

    shards = (w_query, w_key, w_value, w_out, w_up, w_down)
    if packed_here:
        small = small_rows(conditioning[0], w_forget, conv_taps, me)
        bias = lax.dynamic_update_slice(jnp.zeros((mod_width,), bf16), b_ada, (me * b_ada.shape[0],)).reshape(-1, LANES)
        (small, attention_w, up_w), bulk, kept = forward_fused(
            x, w_ada.reshape(-1, LANES), bias, forget_b, small, [piece.reshape(-1, LANES) for piece in shards[:5]], heads, conv_taps.shape[0]
        )
        xp, qkv, mix, mixed_p, branch, middle, hidden_two_p, perm = bulk
        mod, forget_p, taps, gate_pre, run, runt, states, value_rims, given, taken = kept
        cond_part = own_columns(small[::seq_count, : width // LANES, :].reshape(data_count, width))
        output, ghp_two, gup_main, gup_left, ggate_two, g_down = feed_fused(
            hidden_two_p, cot, mod, w_down.reshape(-1, LANES), up_w, middle
        )
    else:
        lanes_at = np.arange(width)
        per_group = width // GROUPS
        order = np.where(
            lanes_at < main_rows,
            lanes_at // 32 * per_group + lanes_at % 32,
            (lanes_at - main_rows) // 4 * per_group + 32 + (lanes_at - main_rows) % 4,
        )
        perm = (jnp.arange(width, dtype=jnp.int32)[:, None] == jnp.asarray(order, jnp.int32)[None, :]).astype(bf16)
        small = [w_forget, conv_taps, b_ada]
        sizes = np.cumsum([0] + [piece.shape[0] for piece in small])
        small = lax.all_gather(jnp.concatenate(small), everywhere)
        forget_w = small[:, : sizes[1]].reshape(width, heads)
        taps = small[:, sizes[1] : sizes[2]].reshape(10, width).astype(f32)
        taps = jnp.pad(taps, ((0, 6), (0, 0)))
        ada_bias = small[:, sizes[2] :].reshape(6, width).astype(f32)
        forget_main, forget_left = split_rows(forget_w)
        forget_p = jnp.concatenate([forget_main.reshape(-1, heads), forget_left.reshape(-1, heads)])
        forget_p = jnp.pad(forget_p, ((0, 0), (0, LANES - heads)))
        cond_part = own_columns(lax.all_gather(conditioning, "dp", axis=0, tiled=True))
        partial_mod = jnp.dot(cond_part, ada_part, preferred_element_type=f32)
        mod = lax.psum(lax.psum_scatter(partial_mod, "dp", scatter_dimension=0, tiled=True), "seq")
        mod = jnp.pad(mod.reshape(6, width) + ada_bias, ((0, 2), (0, 0)))
        blocks = pack_whole([lax.all_gather(s, everywhere, axis=0, tiled=True) for s in shards], width)
        attention_w, up_w, down_w = blocks
        down_w = down_w.reshape(-1, width)
        xp, gate_pre, run, runt = call(
            first_part,
            (sds(rows, bf16), sds((length, LANES)), sds((2, length, LANES)), sds((2, LANES, length))),
            "first_norm",
            scratch_shapes=[pltpu.VMEM(rows, bf16)],
        )(x, mod, perm, forget_p, forget_b)
        qkv = call(
            project_kernel,
            sds((3,) + rows, bf16),
            "project",
            grid=(3,),
            in_specs=[whole(rows), main_spec(lambda j: (0, j, 0)), left_spec(lambda j: (0, 8, 0))],
            out_specs=pl.BlockSpec((1,) + rows, lambda j: (j, 0, 0)),
        )(xp, attention_w, attention_w)
        total = run[0, -1]
        given = jnp.stack([jnp.exp(total - run[0]), jnp.exp(run[1])])
        taken = jnp.stack([jnp.exp(run[0]), jnp.exp(total - run[1])])
        if ways == 1:
            given = jnp.where(place == 0, given[0], given[1])[None]
            taken = jnp.where(place == 0, taken[1], taken[0])[None]
        messages = state_call(qkv[1], qkv[2], given, edges(qkv[2]))
        states, value_rims = joined_states(messages, total, width, head_width)
        mix_local = call(
            functools.partial(mix_kernel, head_width, heads), sds(rows), "mix"
        )(qkv, run, runt)
        mix, mixed_p, branch, middle, hidden_two_p = call(
            functools.partial(after_kernel, head_width, ways),
            (sds(rows), sds(rows, bf16), sds(rows, bf16), sds(rows), sds(rows, bf16)),
            "after",
            grid=(1,),
            in_specs=[
                whole(rows), whole((8, width)), whole((width, width)), whole((3,) + rows), whole(rows),
                whole((ways, length, LANES)), whole((ways, width, LANES)), whole((2, GRID, width)), whole((16, width)),
                main_spec(lambda i: (0, 3, 0)), left_spec(lambda i: (0, 8, 0)),
            ],
            out_specs=[whole(rows)] * 5,
            scratch_shapes=[pltpu.VMEM((length + 2 * GRID, width), bf16), pltpu.VMEM(rows, bf16)],
        )(x, mod, perm, qkv, mix_local, taken, states, value_rims, taps, attention_w, attention_w)
        output, ghp_two, gup_main, gup_left, gdown, ggate_two = call(
            feed_kernel,
            (
                sds(rows, bf16), sds(rows), sds((GROUPS, 128, width), bf16), sds((GROUPS, 16, width), bf16),
                sds(down_w.shape, bf16), sds((1, width)),
            ),
            "feed",
            grid=(4,),
            in_specs=[
                whole(rows), whole(rows), whole((8, width)), whole(rows), main_spec(lambda j: (0, j, 0)),
                left_spec(lambda j: (0, 8, 0)), pl.BlockSpec((width, width), lambda j: (j, 0)),
            ],
            out_specs=[
                whole(rows), whole(rows), main_spec(lambda j: (0, j, 0)), left_spec(lambda j: (0, 0, 0)),
                pl.BlockSpec((width, width), lambda j: (j, 0)), whole((1, width)),
            ],
            scratch_shapes=[
                pltpu.VMEM(rows, f32), pltpu.VMEM(rows, bf16), pltpu.VMEM((width, length), bf16), pltpu.VMEM(rows, bf16),
                pltpu.VMEM((width, length), bf16), pltpu.VMEM(rows, bf16), pltpu.VMEM((width - main_rows, width), bf16),
            ],
        )(hidden_two_p, cot, mod, middle, up_w, up_w, down_w)

    share_forget, share_taps, share_bias = w_forget.shape[0], conv_taps.shape[0], b_ada.shape[0]

    if packed_here:
        grad_middle, gqkv, gmain, _, grad_small, gleft, grad_gate, sums_two, g_up, g_out = backward_fused(
            heads,
            share_taps,
            (mod, run, runt, taken, given, gate_pre, states, value_rims, taps),
            (ghp_two, perm, middle, cot, branch, mixed_p, mix, attention_w, six(up_w), qkv, xp),
            (gup_main, gup_left),
        )
        grad_input, mod_all, g_query, g_key, g_value, out_left, grad_small = finish_fused(
            (mod, sums_two, ggate_two, grad_gate, forget_p), (attention_w, gqkv, perm, x, grad_middle),
            (gmain, six(gleft)), grad_small,
        )
        g_forget = grad_small[:36, :heads].reshape(-1)
        g_taps = lax.dynamic_slice(grad_small[36:40].reshape(-1), (lax.rem(me * share_taps, LANES),), (share_taps,))
        grad_bias = grad_small[40, :heads]
        mod_all = mod_all.reshape(devices, -1)[:, :mod_width]
        g_out = jnp.concatenate([g_out.reshape(-1), out_left.reshape(-1)])
        shares = [piece.reshape(-1) for piece in (g_query, g_key, g_value, g_out, g_up, g_down)]
    else:
        grad_middle, grad_mixed, grad_mix, gout_main, gout_left, sums_two = call(
            functools.partial(second_kernel, head_width),
            (
                sds(rows), sds(rows, bf16), sds(rows, bf16), sds((GROUPS, 32, width), bf16),
                sds((GROUPS, 16, width), bf16), sds((8, width)),
            ),
            "second_norm",
            grid=(1,),
            in_specs=[
                whole(rows), whole((width, width)), whole(rows), whole((8, width)), whole(rows), whole(rows), whole(rows),
                whole(rows), main_spec(lambda i: (0, 3, 0)), left_spec(lambda i: (0, 8, 0)),
            ],
            out_specs=[
                whole(rows), whole(rows), whole(rows), whole((GROUPS, 32, width)), whole((GROUPS, 16, width)),
                whole((8, width)),
            ],
            scratch_shapes=[
                pltpu.VMEM(rows, f32), pltpu.VMEM(rows, bf16), pltpu.VMEM((3, 8, width), f32),
            ],
        )(ghp_two, perm, middle, mod, cot, branch, mixed_p, mix, attention_w, attention_w)

        back = state_call(qkv[0], grad_mix, taken, edges(grad_mixed))
        if ways == 2:
            back = jnp.stack([
                jnp.concatenate([back[1, :width], back[0, width:]]), jnp.concatenate([back[0, :width], back[1, width:]])
            ])
        leaving, grad_rims = joined_states(back, total, width, head_width)
        if ways == 2:
            leaving = leaving[::-1]

        gq_local, gk_local, gv_local, pair_rows, pair_cols = call(
            functools.partial(pairs_kernel, head_width, heads),
            (sds(rows), sds(rows), sds(rows), sds((2, length, LANES)), sds((2, heads, length))),
            "pairs",
            scratch_shapes=[pltpu.VMEM((2, length, length), bf16)],
        )(qkv, grad_mix, run, runt)
        if seq_count > 2:
            rows_through = jnp.sum(states.astype(f32) * leaving.astype(f32), axis=(0, 2))
            through = jnp.exp(total[:heads]) * jnp.sum(rows_through.reshape(heads, head_width), axis=1)
            through = jnp.pad(through, (0, LANES - heads)).reshape(1, LANES)
        else:
            through = jnp.zeros((1, LANES), f32)
        early = jnp.where(place == 0, jnp.ones((1, LANES), f32), 0.0)

        pad_scratch = pltpu.VMEM((length + 2 * GRID, width), bf16)
        gqkv, grad_gate, grad_conv, grad_bias = call(
            functools.partial(carry_kernel, head_width, ways),
            (sds((3,) + rows, bf16), sds((length, LANES), bf16), sds((16, width)), sds((1, LANES))),
            "carry",
            scratch_shapes=[pad_scratch, pad_scratch],
        )(
            qkv, grad_mix, gq_local, gk_local, gv_local, pair_rows, pair_cols, taken, given, gate_pre, states, leaving,
            through, early, grad_mixed, grad_rims, value_rims, taps,
        )
        gmain, gleft, gforget, ghp_one = call(
            weights_kernel,
            (sds((GROUPS, 96, width), bf16), sds((GROUPS, 16, width), bf16), sds((width, LANES)), sds(rows)),
            "weights",
            grid=(3,),
            in_specs=[
                whole(rows), pl.BlockSpec((1,) + rows, lambda j: (j, 0, 0)), whole((length, LANES)),
                whole((width, LANES)), main_spec(lambda j: (0, j, 0)), left_spec(lambda j: (0, 8, 0)),
                left_spec(lambda j: (0, 0, 0)),
            ],
            out_specs=[
                main_spec(lambda j: (0, j, 0)), left_spec(lambda j: (0, 0, 0)), whole((width, LANES)), whole(rows),
            ],
            scratch_shapes=[pltpu.VMEM((width, length), bf16)],
        )(xp, gqkv, grad_gate, forget_p, attention_w, attention_w, gout_left)
        grad_input, sums_one = call(
            last_part, (sds(rows), sds((8, width))), "last_norm",
            scratch_shapes=[pltpu.VMEM(rows, f32), pltpu.VMEM((2, 8, width), f32)],
        )(ghp_one, perm, x, mod, grad_middle)

        gforget = gforget[:, :heads]
        gforget = jnp.concatenate(
            [gforget[:main_rows].reshape(GROUPS, 32, heads), gforget[main_rows:].reshape(GROUPS, 4, heads)], axis=1
        )
        grad_small = jnp.concatenate([gforget.reshape(devices, -1), grad_conv[:10].reshape(devices, -1)], axis=1)
        grad_small = lax.psum_scatter(grad_small, everywhere, scatter_dimension=0, tiled=True).reshape(-1)
        g_forget, g_taps = grad_small[:share_forget], grad_small[share_forget:]
        grad_bias = lax.psum(grad_bias[0, :heads], everywhere)
        grads = [
            jnp.concatenate([gmain, gout_main, gleft], axis=1), jnp.concatenate([gup_main, gup_left], axis=1),
            gdown.reshape(GROUPS, -1, width),
        ]
        shares = [
            lax.psum_scatter(g.reshape(-1), everywhere, scatter_dimension=0, tiled=True).astype(f32)
            for g in unpack_blocks(grads)
        ]
        grad_mod = jnp.concatenate([sums_one[:2], sums_two[2:3], sums_two[:2], ggate_two])
        mod_all = lax.all_gather(grad_mod.reshape(1, mod_width), everywhere, axis=0, tiled=True)

    mod_all = jnp.sum(mod_all.reshape(data_count, seq_count, mod_width), axis=1)
    grad_ada = jnp.dot(cond_part.astype(f32).T, mod_all, precision=lax.Precision.HIGHEST).reshape(-1)
    if inset is not None:
        grad_ada = lax.dynamic_slice(grad_ada, (inset,), (share,))
    grad_ada_bias = lax.dynamic_slice(jnp.sum(mod_all, axis=0), (me * share_bias,), (share_bias,))
    g_query, g_key, g_value, g_out, g_up, g_down = shares
    return (
        output[None], grad_input[None], grad_ada, grad_ada_bias, g_query, g_key, g_value, g_forget,
        grad_bias, g_taps, g_out, g_up, g_down,
    )


def solution(mesh):
    rows = P("dp", "seq", None)
    shard = P(("dp", "seq"))
    return jax.shard_map(
        on_device,
        mesh=mesh,
        in_specs=(
            rows, P("dp", None), rows, shard, shard, shard, shard, shard, shard, P(), shard, shard, shard, shard,
        ),
        out_specs=(
            rows, rows, shard, shard, shard, shard, shard, shard, P(), shard, shard, shard, shard,
        ),
        check_vma=False,
    )
```

```python
import functools

import jax
import jax.numpy as jnp
import numpy as np
from jax import lax
from jax.experimental import pallas as pl
from jax.experimental.pallas import tpu as pltpu
from jax.sharding import PartitionSpec as P

GRID = 32
LANES = 128
GROUPS = 32
epsilon = 1e-06
f32 = jnp.float32
bf16 = jnp.bfloat16
VMEM_LIMIT = 56 * 1024 * 1024
FORWARD_PLAN = (
    ("f", 0, 0, 0), ("g", 0, 0, 0), -1, ("g", 0, 1, 0), ("f", 1, 0, 0), ("g", 2, 0, 0), ("g", 1, 0, 0),
    ("g", 3, 0, 0), ("g", 0, 0, 1), ("f", 2, 0, 0), ("g", 1, 1, 0), ("g", 2, 1, 0), -1, ("g", 0, 0, 2),
    ("g", 4, 0, 0), ("g", 5, 0, 0), ("g", 2, 0, 1), ("g", 1, 0, 1), -1, ("s", 0, 0, 0), ("g", 2, 0, 2),
    ("g", 1, 0, 2), ("g", 0, 0, 3), ("g", 4, 0, 1), ("g", 5, 0, 1), ("g", 3, 1, 0), ("s", 1, 0, 0), ("g", 0, 1, 1),
    ("g", 1, 0, 3), ("g", 2, 0, 3), ("g", 4, 0, 2), ("g", 5, 0, 2), ("s", 2, 0, 0), -1, ("g", 2, 1, 1),
    ("g", 1, 1, 1), ("g", 4, 1, 0), ("g", 5, 1, 0), ("g", 4, 0, 3), ("g", 5, 0, 3), ("g", 0, 1, 2), ("g", 4, 1, 1),
    ("g", 5, 1, 1), ("g", 1, 1, 2), -1, ("g", 2, 1, 2), -1, ("g", 0, 1, 3), -1, -1, ("g", 4, 1, 2), ("g", 5, 1, 2),
    ("g", 2, 1, 3), -1, -1, ("g", 1, 1, 3), -1, ("g", 4, 1, 3), -1, -1, ("g", 5, 1, 3), -1, -1, -1,
)
FEED_PLAN = (
    ("g", 0, 0, 0), -1, -1, ("g", 2, 0, 0), ("g", 1, 0, 0), ("g", 3, 0, 0), ("g", 0, 0, 1), -1, -1, ("g", 0, 0, 2),
    ("g", 4, 0, 0), ("g", 5, 0, 0), ("d", 0, 0, 0), ("g", 2, 0, 1), ("d", 4, 0, 0), -1, ("g", 1, 0, 1),
    ("g", 2, 0, 2), -1, ("g", 0, 0, 3), ("g", 1, 0, 2), ("d", 1, 0, 0), ("d", 2, 0, 0), ("d", 0, 0, 1),
    ("g", 4, 0, 1), -1, -1, ("g", 5, 0, 1), ("g", 2, 0, 3), ("d", 4, 0, 1), ("d", 0, 0, 2), -1, ("g", 1, 0, 3),
    ("g", 4, 0, 2), ("g", 5, 0, 2), -1, ("d", 3, 0, 0), -1, ("d", 4, 0, 2), ("d", 0, 0, 3), ("d", 2, 0, 1),
    ("d", 1, 0, 1), -1, -1, ("g", 4, 0, 3), -1, ("d", 1, 0, 2), ("d", 2, 0, 2), -1, ("g", 5, 0, 3), ("d", 2, 0, 3),
    -1, -1, ("d", 4, 0, 3), ("d", 1, 0, 3), -1, ("d", 3, 0, 1), ("d", 5, 0, 0), -1, -1, -1, -1, ("d", 3, 0, 2), -1,
    -1, -1, -1, ("d", 3, 0, 3), ("d", 5, 0, 1),
)
BACKWARD_PLAN = (
    -1, -1, -1, -1, -1, ("u", 0, 0, 0), ("u", 4, 0, 0), -1, ("u", 0, 0, 1), -1, ("u", 0, 0, 2), ("u", 2, 0, 0),
    ("u", 4, 0, 1), ("u", 1, 0, 0), ("u", 2, 0, 1), -1, ("u", 1, 0, 1), -1, ("u", 0, 0, 3), ("u", 2, 0, 2),
    ("u", 4, 0, 2), ("u", 1, 0, 2), ("u", 3, 0, 0), -1, -1, ("u", 2, 0, 3), ("u", 4, 0, 3), ("u", 1, 0, 3), -1, -1,
    ("u", 3, 0, 1), ("u", 5, 0, 0), -1, -1, -1, ("u", 3, 0, 2), ("u", 3, 0, 3), ("u", 5, 0, 1),
)
FINISH_PLAN = (
    -1, ("a", 0, 0, 0), ("a", 4, 0, 0), -1, ("a", 0, 0, 1), -1, ("a", 2, 0, 0), ("a", 1, 0, 0), ("a", 0, 0, 2),
    ("a", 4, 0, 1), -1, ("g", 0, 0, 0), ("a", 2, 0, 1), ("s", 0, 0, 0), ("s", 0, 0, 1), ("s", 0, 0, 2),
    ("s", 0, 0, 3), ("a", 1, 0, 1), ("a", 3, 0, 0), ("a", 2, 0, 2), ("g", 1, 0, 0), ("s", 2, 0, 0), ("s", 2, 0, 1),
    ("s", 1, 0, 0), ("s", 2, 0, 2), ("s", 1, 0, 1), ("a", 4, 0, 2), ("s", 2, 0, 3), ("s", 1, 0, 2), ("s", 1, 0, 3),
    ("a", 0, 0, 3), ("a", 3, 0, 1), ("s", 3, 0, 0), ("g", 2, 0, 0), ("a", 1, 0, 2), ("a", 4, 0, 3), ("a", 2, 0, 3),
    ("a", 1, 0, 3), ("s", 3, 0, 1), ("a", 3, 0, 2), ("s", 3, 0, 2), ("a", 5, 0, 0), ("a", 3, 0, 3), ("a", 5, 0, 1),
    ("s", 3, 0, 3),
)


def dot(a, b):
    return jnp.dot(a, b, preferred_element_type=f32)


def dot_bt(a, b):
    return lax.dot_general(a, b, (((1,), (1,)), ((), ())), preferred_element_type=f32)


def dot_at(a, b):
    return lax.dot_general(a, b, (((0,), (0,)), ((), ())), preferred_element_type=f32)


def halves(a):
    high = a.astype(bf16)
    return high, (a - high.astype(f32)).astype(bf16)


def spans(width, size=512):
    return [slice(start, min(start + size, width)) for start in range(0, width, size)]


def head_lanes(rows, width, start, head_width):
    head = lax.broadcasted_iota(jnp.int32, (rows, width), 0)
    lane = lax.broadcasted_iota(jnp.int32, (rows, width), 1) + start
    return (lane >= head * head_width) & (lane < (head + 1) * head_width)


def pick_left(rows, slot):
    out = lax.broadcasted_iota(jnp.int32, (4 * GROUPS, 16 * GROUPS), 0)
    src = lax.broadcasted_iota(jnp.int32, (4 * GROUPS, 16 * GROUPS), 1)
    return (src == (out // 4) * 16 + slot * 4 + out % 4).astype(bf16)


def norm_parts(values):
    center = jnp.mean(values, axis=-1, keepdims=True)
    centered = values - center
    spread = jnp.mean(centered * centered, axis=-1, keepdims=True)
    rstd = lax.rsqrt(spread + epsilon)
    return centered * rstd, rstd


def row_loop(length, body):
    size = min(length, 64)

    @pl.loop(0, length // size)
    def _(r):
        body(pl.ds(pl.multiple_of(r * size, size), size))


def eight_rows(values):
    return jnp.sum(values.reshape(-1, 8, values.shape[1]), axis=0)


def call(kernel, out_shape, name, **kw):
    return pl.pallas_call(
        kernel,
        out_shape=out_shape,
        name=name,
        compiler_params=pltpu.CompilerParams(vmem_limit_bytes=VMEM_LIMIT),
        **kw,
    )


def sds(shape, dtype=f32):
    return jax.ShapeDtypeStruct(shape, dtype)


def first_part(x_ref, mod_ref, perm_ref, wf_ref, bf_ref, xp_ref, gate_ref, run_ref, runt_ref, hidden_ref):
    length = x_ref.shape[0]

    def norm(rows):
        normed, _ = norm_parts(x_ref[rows, :].astype(f32))
        hidden_ref[rows, :] = (normed * (1.0 + mod_ref[1:2, :]) + mod_ref[0:1, :]).astype(bf16)

    row_loop(length, norm)
    for cols in spans(x_ref.shape[1]):
        xp_ref[:, cols] = dot(hidden_ref[...], perm_ref[:, cols]).astype(bf16)

    gate = dot(xp_ref[...], wf_ref[...]) + bf_ref[...]
    gate_ref[...] = gate
    decay = -(jnp.maximum(gate, 0.0) + jnp.log1p(jnp.exp(-jnp.abs(gate))))
    row = lax.broadcasted_iota(jnp.int32, (length, length), 0)
    col = lax.broadcasted_iota(jnp.int32, (length, length), 1)
    tri = (row >= col).astype(bf16)
    high, rest = halves(decay)
    rest32 = decay - high.astype(f32)
    low = (rest32 - rest.astype(f32)).astype(bf16)
    inclusive = dot(tri, high) + dot(tri, rest) + dot(tri, low)
    exclusive = inclusive - decay
    run_ref[0] = inclusive
    run_ref[1] = exclusive
    runt_ref[0] = inclusive.T
    runt_ref[1] = exclusive.T


def project_part(slot, xp_ref, main_ref, left_ref, write):
    pick = pick_left(None, slot)
    main_rows = rows_in(main_ref)

    for cols in spans(xp_ref.shape[1]):
        main = main_ref[..., cols].reshape(main_rows, -1)
        left = dot(pick, left_ref[..., cols].reshape(16 * GROUPS, -1)).astype(bf16)
        write(cols, dot(xp_ref[:, :main_rows], main) + dot(xp_ref[:, main_rows:], left))


def two_terms(scale):
    return jnp.concatenate(halves(scale), axis=1)


def spread_heads(terms, cols, head_width):
    spread = head_lanes(LANES, cols.stop - cols.start, cols.start, head_width).astype(bf16)
    return dot(terms, jnp.concatenate([spread, spread], axis=0))


def head_sums(values, cols, head_width):
    return dot_bt(values, head_lanes(LANES, cols.stop - cols.start, cols.start, head_width).astype(bf16))


def own_block(shape, row_start, lane_start, head_width):
    row = lax.broadcasted_iota(jnp.int32, (shape[0], 1), 0) + row_start
    lane = lax.broadcasted_iota(jnp.int32, (1, shape[1]), 1) + lane_start
    same = None
    for head in range(
        max(row_start, lane_start) // head_width,
        min(row_start + shape[0] - 1, lane_start + shape[1] - 1) // head_width + 1,
    ):
        low, high = head * head_width, (head + 1) * head_width
        both = ((row >= low) & (row < high)) & ((lane >= low) & (lane < high))
        same = both if same is None else same | both
    if same is None:
        return jnp.broadcast_to(row < 0, shape)
    return same


def group_rows(ref, cols):
    per = rows_in(ref) // ref.shape[0]
    return ref[cols.start // per : cols.stop // per].reshape(-1, ref.shape[-1])


def rows_in(ref):
    return int(np.prod(ref.shape[:-1]))


def near_lanes(cols, width, head_width):
    low = cols.start // head_width * head_width // LANES * LANES
    last = (cols.stop - 1) // head_width
    return slice(low, min(width, -(-(last + 1) * head_width // LANES) * LANES))


def unfolded(ref, way, near, cols, head_width):
    folded = ref[way, near, :]
    return jnp.concatenate([
        jnp.where(own_block(folded.shape, near.start, at, head_width), folded, 0)
        for at in range(cols.start, cols.stop, LANES)
    ], axis=1)


def state_part(head_width, ways, left, right_ref, scale_ref, out_ref):
    width = right_ref.shape[1]
    terms = [two_terms(scale_ref[way]) for way in range(ways)]
    for cols in spans(width, 2 * LANES):
        near = near_lanes(cols, width, head_width)
        mask = own_block((cols.stop - cols.start, near.stop - near.start), cols.start, near.start, head_width)
        for way in range(ways):
            scaled = left(cols).astype(f32) * spread_heads(terms[way], cols, head_width)
            product = jnp.where(mask, dot_at(scaled.astype(bf16), right_ref[:, near]), 0.0)
            total = product[:, :LANES]
            for at in range(LANES, near.stop - near.start, LANES):
                total = total + product[:, at : at + LANES]
            out_ref[way, cols, :] = total.astype(bf16)


def edge_part(source, out):
    for t in range(source.shape[1] // LANES):
        out(t, source[:, t * LANES : (t + 1) * LANES])


def pair_weights(run_ref, runt_ref, head, rows, length):
    count = rows.size
    own = lax.broadcasted_iota(jnp.int32, (count, LANES), 1) == head
    inc_t = jnp.sum(jnp.where(own, run_ref[0, rows, :], 0.0), axis=1, keepdims=True)
    exc_t = jnp.sum(jnp.where(own, run_ref[1, rows, :], 0.0), axis=1, keepdims=True)
    inc_s = runt_ref[0, pl.ds(head, 1), :]
    exc_s = runt_ref[1, pl.ds(head, 1), :]
    weight = jnp.exp(jnp.minimum(inc_t - inc_s, exc_s - exc_t))
    row = lax.broadcasted_iota(jnp.int32, (count, length), 0) + rows.start
    col = lax.broadcasted_iota(jnp.int32, (count, length), 1)
    return jnp.where(row == col, 2.0, weight)


def window_of(head, heads, head_width):
    start = pl.multiple_of(((head * head_width) // LANES - head // (heads - 1)) * LANES, LANES)
    return pl.ds(start, 2 * LANES), start


def own_lanes(rows, start, head, head_width):
    lane = lax.broadcasted_iota(jnp.int32, (rows, 2 * LANES), 1) + start
    return (lane >= head * head_width) & (lane < (head + 1) * head_width)


def row_blocks(length, size):
    size = min(length, size)
    return [pl.ds(start, size) for start in range(0, length, size)]


def mix_part(head_width, heads, low, high, qkv_ref, run_ref, runt_ref, mix_ref):
    length, width = mix_ref.shape

    @pl.loop(low // 2, high // 2)
    def _(pair):
        for odd in range(2):
            head = pair * 2 + odd
            win, start = window_of(head, heads, head_width)
            mask = own_lanes(length, start, head, head_width)
            keys = jnp.where(mask, qkv_ref[1, :, win], 0)
            vals = jnp.where(mask, qkv_ref[2, :, win], 0)
            for rows in row_blocks(length, 2 * LANES):
                weight = pair_weights(run_ref, runt_ref, head, rows, length)
                score = dot_bt(qkv_ref[0, rows, win], keys)
                mix_ref[rows, win] += dot((score * weight).astype(bf16), vals)


def fill_padded(pad_ref, rims_ref, middle):
    length = pad_ref.shape[0] - 2 * GRID
    pad_ref[:GRID, :] = rims_ref[0]
    pad_ref[GRID : GRID + length, :] = middle
    pad_ref[GRID + length :, :] = rims_ref[1]


def mixed_part(head_width, ways, qkv_ref, taken_ref, state_ref, taps_ref, vpad, mix_ref, mixed):
    length, width = mix_ref.shape
    place = lax.broadcasted_iota(jnp.int32, (length, LANES), 0) % GRID
    sums = jnp.zeros((length, LANES), f32)
    terms = [two_terms(taken_ref[way]) for way in range(ways)]
    for cols in spans(width, 2 * LANES):
        gained = mix_ref[:, cols]
        near = near_lanes(cols, width, head_width)
        for way in range(ways):
            block = unfolded(state_ref, way, near, cols, head_width)
            gained = gained + spread_heads(terms[way], cols, head_width) * dot(qkv_ref[0, :, near], block)
        mix_ref[:, cols] = gained
        sums = sums + head_sums((gained * gained).astype(bf16), cols, head_width)
    inverse = two_terms(lax.rsqrt(sums * (1.0 / head_width) + epsilon))
    for span in spans(width, 2 * LANES):
        normed = mix_ref[:, span] * spread_heads(inverse, span, head_width)
        for start in range(span.start, span.stop, LANES):
            cols = slice(start, start + LANES)
            conv = jnp.zeros((length, LANES), f32)
            for lateral in range(3):
                column = jnp.zeros((length, LANES), f32)
                for vertical in range(3):
                    tap = taps_ref[3 * vertical + lateral : 3 * vertical + lateral + 1, cols]
                    column = column + tap * vpad[vertical * GRID : vertical * GRID + length, cols].astype(f32)
                if lateral == 0:
                    column = jnp.where(place > 0, pltpu.roll(column, 1, 0), 0.0)
                if lateral == 2:
                    column = jnp.where(place < GRID - 1, pltpu.roll(column, length - 1, 0), 0.0)
                conv = conv + column
            own = normed[:, start - span.start : start - span.start + LANES]
            mixed[:, cols] = (own + (conv + taps_ref[9:10, cols])).astype(bf16)


def permute_part(source, perm_ref, out_ref):
    for cols in spans(perm_ref.shape[1]):
        out_ref[:, cols] = dot(source[...], perm_ref[:, cols]).astype(bf16)


def branch_part(x_ref, mod_ref, mixedp_ref, main_ref, left_ref, branch_ref, middle_ref):
    def write(cols, branch):
        branch_ref[:, cols] = branch.astype(bf16)
        middle_ref[:, cols] = x_ref[:, cols].astype(f32) + mod_ref[2:3, cols] * branch

    project_part(3, mixedp_ref, main_ref, left_ref, write)


def second_hidden(mod_ref, middle_ref, mixed):
    def norm(rows):
        normed, _ = norm_parts(middle_ref[rows, :])
        mixed[rows, :] = (normed * (1.0 + mod_ref[4:5, :]) + mod_ref[3:4, :]).astype(bf16)

    row_loop(mixed.shape[0], norm)


def project_kernel(xp_ref, main_ref, left_ref, out_ref):
    def write(cols, value):
        out_ref[0, :, cols] = value.astype(bf16)

    project_part(pl.program_id(0), xp_ref, main_ref, left_ref, write)


def state_kernel(head_width, ways, left_ref, right_ref, scale_ref, edge_ref, out_ref):
    width = right_ref.shape[1]
    state_part(head_width, ways, lambda cols: left_ref[:, cols], right_ref, scale_ref, out_ref)
    for way in range(ways):

        def write(t, value, way=way):
            out_ref[way, width + t * GRID : width + (t + 1) * GRID, :] = value

        edge_part(edge_ref[way], write)


def mix_kernel(head_width, heads, qkv_ref, run_ref, runt_ref, mix_ref):
    mix_ref[...] = jnp.zeros_like(mix_ref)
    mix_part(head_width, heads, 0, heads, qkv_ref, run_ref, runt_ref, mix_ref)


def after_kernel(
    head_width, ways, x_ref, mod_ref, perm_ref, qkv_ref, mix_in_ref, taken_ref, state_ref, rims_ref, taps_ref,
    main_ref, left_ref, mix_ref, mixedp_ref, branch_ref, middle_ref, h2p_ref, vpad, mixed,
):
    mix_ref[...] = mix_in_ref[...]
    fill_padded(vpad, rims_ref, qkv_ref[2])
    mixed_part(head_width, ways, qkv_ref, taken_ref, state_ref, taps_ref, vpad, mix_ref, mixed)
    permute_part(mixed, perm_ref, mixedp_ref)
    branch_part(x_ref, mod_ref, mixedp_ref, main_ref, left_ref, branch_ref, middle_ref)
    second_hidden(mod_ref, middle_ref, mixed)
    permute_part(mixed, perm_ref, h2p_ref)


def gelu_both(v):
    c = np.float32(np.sqrt(2.0 / np.pi))
    square = v * v
    th = jnp.tanh(c * (v + np.float32(0.044715) * (square * v)))
    half = 0.5 * (1.0 + th)
    slope = half + 0.5 * v * (1.0 - th * th) * (c * (1.0 + np.float32(3 * 0.044715) * square))
    return v * half, slope


def feed_kernel(
    h2p_ref, cot_ref, mod_ref, middle_ref, main_ref, left_ref, down_ref,
    out_ref, gh_ref, gup_ref, gleft_ref, gdown_ref, ggate_ref, down_acc, gdi, h2pt, act, actt, gup, left,
):
    j = pl.program_id(0)
    main_rows = main_ref.shape[0] * main_ref.shape[1]
    length, width = h2p_ref.shape

    @pl.when(j == 0)
    def _():
        gdi[...] = (cot_ref[...].astype(f32) * mod_ref[5:6, :]).astype(bf16)
        h2pt[...] = h2p_ref[...].T
        down_acc[...] = jnp.zeros_like(down_acc)
        gh_ref[...] = jnp.zeros_like(gh_ref)
        gleft_ref[...] = jnp.zeros_like(gleft_ref)

    pick = pick_left(None, j)
    left[...] = dot(pick, left_ref[...].reshape(16 * GROUPS, width)).astype(bf16)
    for cols in spans(width):
        main = main_ref[:, :, cols].reshape(main_rows, -1)
        up = dot(h2p_ref[:, :main_rows], main) + dot(h2p_ref[:, main_rows:], left[:, cols])
        value, slope = gelu_both(up)
        value = value.astype(bf16)
        act[:, cols] = value
        actt[cols, :] = value.T
        gup[:, cols] = (dot_bt(gdi[...], down_ref[cols, :]) * slope).astype(bf16)
    for cols in spans(width):
        down_acc[:, cols] += dot(act[...], down_ref[:, cols])
        gdown_ref[:, cols] = dot(actt[...], gdi[:, cols]).astype(bf16)
        gup_ref[:, :, cols] = dot(h2pt[:main_rows, :], gup[:, cols]).astype(bf16).reshape(GROUPS, 32, -1)
        part = dot(h2pt[main_rows:, :], gup[:, cols]).astype(bf16)
        gleft_ref[:, :, cols] += dot_at(pick, part).astype(bf16).reshape(GROUPS, 16, -1)
    gh_ref[:, main_rows:] += dot_bt(gup[...], left[...])
    for cols in spans(main_rows):
        gh_ref[:, cols] += dot_bt(gup[...], group_rows(main_ref, cols))

    @pl.when(j == pl.num_programs(0) - 1)
    def _():
        out_ref[...] = (middle_ref[...] + mod_ref[5:6, :] * down_acc[...]).astype(bf16)
        ggate_ref[...] = jnp.sum(cot_ref[...].astype(f32) * down_acc[...], axis=0, keepdims=True)


def unpermute(perm_ref, source_ref, out_ref):
    source = source_ref[...].astype(bf16)
    for cols in spans(perm_ref.shape[0]):
        out_ref[:, cols] = dot_bt(source, perm_ref[cols, :])


def norm_back(normed, rstd, factor, grad):
    scaled = grad * (1.0 + factor)
    mean = jnp.mean(scaled, axis=-1, keepdims=True)
    along = jnp.mean(scaled * normed, axis=-1, keepdims=True)
    return (scaled - mean - normed * along) * rstd


def second_part(
    head_width, ghp_ref, perm_ref, middle_ref, mod_ref, cot_ref, branch_ref, mixedp_ref, mix_ref, main_ref, left_ref,
    gmid_ref, gmixed_ref, gmix_ref, gout_ref, gleft_ref, sums_ref, gh, gb, partial,
):
    length, width = middle_ref.shape
    main_rows = rows_in(main_ref)
    unpermute(perm_ref, ghp_ref, gh)
    yield
    partial[...] = jnp.zeros_like(partial)

    def norm(rows):
        normed, rstd = norm_parts(middle_ref[rows, :])
        grad = gh[rows, :]
        partial[0] += eight_rows(grad)
        partial[1] += eight_rows(grad * normed)
        grad_middle = cot_ref[rows, :].astype(f32) + norm_back(normed, rstd, mod_ref[4:5, :], grad)
        gmid_ref[rows, :] = grad_middle
        partial[2] += eight_rows(grad_middle * branch_ref[rows, :].astype(f32))
        gb[rows, :] = (grad_middle * mod_ref[2:3, :]).astype(bf16)

    row_loop(length, norm)
    for k in range(3):
        sums_ref[k : k + 1, :] = jnp.sum(partial[k], axis=0, keepdims=True)
    sums_ref[3:8, :] = jnp.zeros((5, width), f32)
    pick = pick_left(None, 3)
    yield
    left = dot(pick, left_ref[...].reshape(16 * GROUPS, width)).astype(bf16)
    for cols in spans(width):
        gout = dot_at(mixedp_ref[:, :main_rows], gb[:, cols]).astype(bf16)
        gout_ref[..., cols] = gout.reshape(gout_ref.shape[:-1] + (-1,))
        part = dot_at(mixedp_ref[:, main_rows:], gb[:, cols]).astype(bf16)
        gleft_ref[..., cols] = dot_at(pick, part).astype(bf16).reshape(gleft_ref.shape[:-1] + (-1,))
    gh[:, main_rows:] = dot_bt(gb[...], left)
    for cols in spans(main_rows):
        gh[:, cols] = dot_bt(gb[...], group_rows(main_ref, cols))
    gb[...] = gh[...].astype(bf16)
    yield
    for cols in spans(width):
        gmixed_ref[:, cols] = dot_bt(gb[...], perm_ref[cols, :]).astype(bf16)

    sums = jnp.zeros((length, LANES), f32)
    dots = jnp.zeros((length, LANES), f32)
    for cols in spans(width, 2 * LANES):
        mix = mix_ref[:, cols]
        sums = sums + head_sums((mix * mix).astype(bf16), cols, head_width)
        for term in halves(mix * gmixed_ref[:, cols].astype(f32)):
            dots = dots + head_sums(term, cols, head_width)
    inverse = lax.rsqrt(sums * (1.0 / head_width) + epsilon)
    along = two_terms(dots * (1.0 / head_width) * inverse * inverse * inverse)
    inverse = two_terms(inverse)
    for cols in spans(width, 2 * LANES):
        gmix_ref[:, cols] = (
            gmixed_ref[:, cols].astype(f32) * spread_heads(inverse, cols, head_width)
            - mix_ref[:, cols] * spread_heads(along, cols, head_width)
        ).astype(bf16)
    yield


def second_kernel(head_width, *refs):
    for _ in second_part(head_width, *refs):
        pass


def pairs_part(head_width, heads, low, high, qkv_ref, gmix_ref, run_ref, runt_ref, gq_ref, gk_ref, gv_ref, rows_ref, cols_ref, held):
    length, width = gmix_ref.shape

    @pl.loop(low, high)
    def _(head):
        win, start = window_of(head, heads, head_width)
        mask = own_lanes(length, start, head, head_width)
        queries = jnp.where(mask, qkv_ref[0, :, win], 0)
        keys = jnp.where(mask, qkv_ref[1, :, win], 0)
        vals = jnp.where(mask, qkv_ref[2, :, win], 0)
        grads = jnp.where(mask, gmix_ref[:, win], 0)
        own = lax.broadcasted_iota(jnp.int32, (LANES, LANES), 1) == head
        row = lax.broadcasted_iota(jnp.int32, (LANES, LANES), 0)
        col = lax.broadcasted_iota(jnp.int32, (LANES, LANES), 1)
        columns = [None, None]
        for rows in row_blocks(length, 2 * LANES):
            weight = pair_weights(run_ref, runt_ref, head, rows, length)
            at = slice(rows.start, rows.start + rows.size)
            score = dot_bt(queries[at], keys) * weight
            grad = dot_bt(grads[at], vals)
            both = score * grad
            held[0, rows, :] = score.astype(bf16)
            held[1, rows, :] = (grad * weight).astype(bf16)
            for step in range(rows.size // LANES):
                first = rows.start + step * LANES
                strip = both[step * LANES : (step + 1) * LANES]
                middle = strip[:, first : first + LANES]
                pieces = [
                    (0, strip[:, :first], jnp.where(row > col, middle, 0.0)),
                    (1, strip[:, first + LANES :], jnp.where(row < col, middle, 0.0)),
                ]
                for way, part, corner in pieces:
                    total = jnp.sum(corner, axis=1, keepdims=True)
                    lines = [jnp.sum(corner, axis=0, keepdims=True)]
                    if first if way == 0 else length - first - LANES:
                        total = total + jnp.sum(part, axis=1, keepdims=True)
                        lines.insert(0 if way == 0 else 1, jnp.sum(part, axis=0, keepdims=True))
                    blank = jnp.zeros((1, length - sum(line.shape[1] for line in lines)), f32)
                    if blank.shape[1]:
                        lines.insert(len(lines) if way == 0 else 0, blank)
                    line = jnp.concatenate(lines, axis=1)
                    columns[way] = line if columns[way] is None else columns[way] + line
                    rows_ref[way, first : first + LANES, :] += jnp.where(own, total, 0.0)
        for way in range(2):
            cols_ref[way, pl.ds(head, 1), :] = columns[way]
        gq_ref[:, win] += dot(held[1], keys)
        gk_ref[:, win] += dot_at(held[1], queries)
        gv_ref[:, win] += dot_at(held[0], grads)


def pairs_kernel(head_width, heads, qkv_ref, gmix_ref, run_ref, runt_ref, gq_ref, gk_ref, gv_ref, rows_ref, cols_ref, held):
    for ref in (gq_ref, gk_ref, gv_ref, rows_ref, cols_ref):
        ref[...] = jnp.zeros_like(ref)
    pairs_part(
        head_width, heads, 0, heads, qkv_ref, gmix_ref, run_ref, runt_ref, gq_ref, gk_ref, gv_ref, rows_ref, cols_ref, held
    )


def carry_part(
    head_width, ways, early, qkv_ref, gmix_ref, gq_in, gk_in, gv_in, rows_ref, cols_ref, taken_ref, given_ref, gate_ref,
    state_ref, leave_ref, through, vpad, gpad, taps_ref, gqkv_ref, ggate_ref, conv_ref, bias_ref,
):
    length, width = gmix_ref.shape
    place = lax.broadcasted_iota(jnp.int32, (length, LANES), 0) % GRID
    taken_sums = [jnp.zeros((length, LANES), f32) for _ in range(ways)]
    given_sums = [jnp.zeros((length, LANES), f32) for _ in range(ways)]
    take_terms = [two_terms(taken_ref[way]) for way in range(ways)]
    give_terms = [two_terms(given_ref[way]) for way in range(ways)]
    for span in spans(width, 2 * LANES):
        near = near_lanes(span, width, head_width)
        gq, gk, gv = gq_in[:, span], gk_in[:, span], gv_in[:, span]
        for way in range(ways):
            take = spread_heads(take_terms[way], span, head_width)
            give = spread_heads(give_terms[way], span, head_width)
            back_q = take * dot_bt(gmix_ref[:, near], unfolded(state_ref, way, span, near, head_width))
            gq = gq + back_q
            for term in halves(qkv_ref[0, :, span].astype(f32) * back_q):
                taken_sums[way] = taken_sums[way] + head_sums(term, span, head_width)
            back_k = give * dot_bt(qkv_ref[2, :, near], unfolded(leave_ref, way, span, near, head_width))
            gk = gk + back_k
            for term in halves(qkv_ref[1, :, span].astype(f32) * back_k):
                given_sums[way] = given_sums[way] + head_sums(term, span, head_width)
            gv = gv + give * dot(qkv_ref[1, :, near], unfolded(leave_ref, way, near, span, head_width))
        gqkv_ref[0, :, span] = gq.astype(bf16)
        gqkv_ref[1, :, span] = gk.astype(bf16)
        for first in range(span.start, span.stop, LANES):
            cols = slice(first, first + LANES)
            grad = gpad[GRID : GRID + length, cols].astype(f32)
            total = gv[:, first - span.start : first - span.start + LANES]
            for lateral in range(3):
                b = lateral - 1
                column = jnp.zeros((length, LANES), f32)
                for vertical in range(3):
                    tap = taps_ref[3 * vertical + lateral : 3 * vertical + lateral + 1, cols]
                    start = (2 - vertical) * GRID
                    column = column + tap * gpad[start : start + length, cols].astype(f32)
                shifted = grad
                if b == -1:
                    column = jnp.where(place < GRID - 1, pltpu.roll(column, length - 1, 0), 0.0)
                    shifted = jnp.where(place < GRID - 1, pltpu.roll(grad, length - 1, 0), 0.0)
                if b == 1:
                    column = jnp.where(place > 0, pltpu.roll(column, 1, 0), 0.0)
                    shifted = jnp.where(place > 0, pltpu.roll(grad, 1, 0), 0.0)
                total = total + column
                for vertical in range(3):
                    window = vpad[vertical * GRID : vertical * GRID + length, cols].astype(f32)
                    conv_ref[3 * vertical + lateral : 3 * vertical + lateral + 1, cols] = jnp.sum(
                        window * shifted, axis=0, keepdims=True
                    )
            conv_ref[9:10, cols] = jnp.sum(grad, axis=0, keepdims=True)
            gqkv_ref[2, :, cols] = total.astype(bf16)
        if span.start // (2 * LANES) in (1, 3) or span.stop == width:
            yield
    conv_ref[10:16, :] = jnp.zeros((6, width), f32)

    row = lax.broadcasted_iota(jnp.int32, (length, length), 0)
    col = lax.broadcasted_iota(jnp.int32, (length, length), 1)
    before = (col < row).astype(bf16)
    upto = (col <= row).astype(bf16)

    def summed(product, matrix, value):
        high, rest = halves(value)
        low = (value - high.astype(f32) - rest.astype(f32)).astype(bf16)
        return product(matrix, high) + product(matrix, rest) + product(matrix, low)

    def columns(way):
        lines = cols_ref[way]
        if lines.shape[0] < LANES:
            lines = jnp.concatenate([lines, jnp.zeros((LANES - lines.shape[0], length), f32)], axis=0)
        return lines.T

    ahead = rows_ref[0] - columns(0)
    behind = rows_ref[1] - columns(1)
    if ways == 2:
        ahead, behind = ahead + taken_sums[0], behind + taken_sums[1]
        given_ahead, given_behind = given_sums
    else:
        ahead = ahead + taken_sums[0] * (1.0 - early)
        behind = behind + taken_sums[0] * early
        given_ahead, given_behind = given_sums[0] * early, given_sums[0] * (1.0 - early)
    grad_decay = (
        summed(dot_at, upto, ahead)
        + summed(dot, before, given_ahead)
        + summed(dot, upto, behind)
        + summed(dot_at, before, given_behind)
        + through
    )
    gate = gate_ref[...]
    small = jnp.exp(-jnp.abs(gate))
    sigmoid = jnp.where(gate >= 0, 1.0, small) / (1.0 + small)
    grad_gate = (-grad_decay * sigmoid).astype(bf16)
    lane = lax.broadcasted_iota(jnp.int32, grad_gate.shape, 1)
    grad_gate = jnp.where(lane < width // head_width, grad_gate.astype(f32), 0.0)
    ggate_ref[...] = grad_gate.astype(bf16)
    bias_ref[...] = jnp.sum(grad_gate, axis=0, keepdims=True)
    yield


def carry_kernel(
    head_width, ways, qkv_ref, gmix_ref, gq_in, gk_in, gv_in, rows_ref, cols_ref, taken_ref, given_ref, gate_ref,
    state_ref, leave_ref, through_ref, early_ref, gmixed_ref, grims_ref, vrims_ref, taps_ref,
    gqkv_ref, ggate_ref, conv_ref, bias_ref, vpad, gpad,
):
    fill_padded(vpad, vrims_ref, qkv_ref[2])
    fill_padded(gpad, grims_ref, gmixed_ref[...])
    for _ in carry_part(
        head_width, ways, early_ref[...], qkv_ref, gmix_ref, gq_in, gk_in, gv_in, rows_ref, cols_ref, taken_ref,
        given_ref, gate_ref, state_ref, leave_ref, through_ref[...], vpad, gpad, taps_ref, gqkv_ref, ggate_ref, conv_ref,
        bias_ref,
    ):
        pass


def projection_grads(slot, turned, grad_ref, gmain_ref, gleft_ref):
    pick = pick_left(None, slot)
    main_rows = rows_in(gmain_ref)
    for cols in spans(grad_ref.shape[1]):
        grad = grad_ref[:, cols]
        gmain_ref[..., cols] = dot(turned[:main_rows, :], grad).astype(bf16).reshape(gmain_ref.shape[:-1] + (-1,))
        part = dot(turned[main_rows:, :], grad).astype(bf16)
        gleft_ref[..., cols] += dot_at(pick, part).astype(bf16).reshape(gleft_ref.shape[:-1] + (-1,))


def projection_back(slot, grad_ref, main_ref, left_ref, gh_ref):
    width = grad_ref.shape[1]
    main_rows = rows_in(main_ref)
    left = dot(pick_left(None, slot), left_ref[...].reshape(16 * GROUPS, width)).astype(bf16)
    gh_ref[:, main_rows:] += dot_bt(grad_ref[...], left)
    for cols in spans(main_rows):
        gh_ref[:, cols] += dot_bt(grad_ref[...], group_rows(main_ref, cols))


def weights_kernel(
    xp_ref, gqkv_ref, ggate_ref, wf_ref, main_ref, left_ref, gout_left_ref, gmain_ref, gleft_ref, gforget_ref, gh_ref, turned
):
    slot = pl.program_id(0)

    @pl.when(slot == 0)
    def _():
        turned[...] = xp_ref[...].T
        gleft_ref[...] = gout_left_ref[...]
        gh_ref[...] = dot_bt(ggate_ref[...], wf_ref[...])
        gforget_ref[...] = dot(turned[...], ggate_ref[...])

    projection_grads(slot, turned, gqkv_ref.at[0], gmain_ref, gleft_ref)
    projection_back(slot, gqkv_ref.at[0], main_ref, left_ref, gh_ref)


def last_part(ghp_ref, perm_ref, x_ref, mod_ref, gmid_ref, gin_ref, sums_ref, gh, partial):
    unpermute(perm_ref, ghp_ref, gh)
    partial[...] = jnp.zeros_like(partial)

    def norm(rows):
        normed, rstd = norm_parts(x_ref[rows, :].astype(f32))
        grad = gh[rows, :]
        partial[0] += eight_rows(grad)
        partial[1] += eight_rows(grad * normed)
        gin_ref[rows, :] = gmid_ref[rows, :] + norm_back(normed, rstd, mod_ref[1:2, :], grad)

    row_loop(x_ref.shape[0], norm)
    for k in range(2):
        sums_ref[k : k + 1, :] = jnp.sum(partial[k], axis=0, keepdims=True)


def ring_place(z):
    return z + lax.div(z, 2) * (5 - 2 * z)


class Here:
    def __init__(self):
        row, x = lax.axis_index("dp"), lax.axis_index("seq")
        z, y, core = lax.div(row, 4), lax.rem(lax.div(row, 2), 2), lax.rem(row, 2)
        self.x, self.y, self.z, self.core = x, y, z, core
        self.p = ring_place(z)
        place = lambda z, y, core, x: ((z * 2 + y) * 2 + core, x)
        self.back = [ring_place(lax.rem(self.p + 4 - back, 4)) for back in range(4)]
        self.along = [place(self.back[4 - o], y, core, x) for o in (1, 2, 3)]
        self.next, self.prev = self.along[0], self.along[2]
        self.over_y = place(z, 1 - y, core, x)
        self.over_x = place(z, y, core, 1 - x)
        self.sibling = place(z, y, 1 - core, x)
        self.around = [self.over_y, self.over_x, place(z, 1 - y, core, 1 - x)]

    def ring_z(self, back):
        return self.back[back % 4]

    def partners(self, wide):
        devices = [self.next, self.prev, self.over_y, self.over_x, self.sibling]
        return devices + [self.along[1], self.around[2]] if wide else devices

    def greet(self, wide=False):
        barrier = pltpu.get_barrier_semaphore()
        for device in self.partners(wide):
            pl.semaphore_signal(barrier, inc=1, device_id=device, device_id_type=pl.DeviceIdType.MESH)

    def meet(self, wide=False):
        pl.semaphore_wait(pltpu.get_barrier_semaphore(), len(self.partners(wide)))


def push(source, target, send, recv, device):
    copy = pltpu.make_async_remote_copy(
        src_ref=source, dst_ref=target, send_sem=send, recv_sem=recv, device_id=device,
        device_id_type=pl.DeviceIdType.MESH,
    )
    copy.start()
    return copy


def routes(rows):
    tiles = rows // 16
    third = 2 if tiles >= 7 else 0
    first = -(-(tiles - third) // 2)
    cuts = [0, 16 * first, 16 * (tiles - third), rows]
    return [pl.ds(low, high - low) for low, high in zip(cuts, cuts[1:])]


class Gather:
    def __init__(self, tag, here, ins, outs, sems):
        self.here, self.ins, self.outs, self.sems = here, ins, outs, sems
        self.flights, self.todo, self.own = {}, {}, {}
        for i in range(len(ins)):
            a, b, c = routes(ins[i].shape[0])
            self.todo[tag, 0, i, 0] = (), functools.partial(self.along_z, i, 0)
            for s in range(4):
                if s:
                    self.todo[tag, 0, i, s] = (("z", i, s - 1),), functools.partial(self.along_z, i, s)
                self.todo[tag, 1, i, s] = (("a1", i, s),), functools.partial(self.second, i, s, 0)
                waits = [("a2", i, s)]
                if b.size:
                    self.todo[tag, 2, i, s] = (("b1", i, s),), functools.partial(self.second, i, s, 1)
                    waits.append(("b2", i, s))
                if c.size:
                    waits.append(("cy", i, 0) if s == 0 else ("cz", i, s - 1))
                    self.todo[tag, 4, i, s] = (waits[-1],), functools.partial(self.third, i, s)
                    waits[-1] = ("c", i, s)
                self.todo[tag, 5, i, s] = tuple(waits), functools.partial(self.across, i, s)
            if c.size:
                self.todo[tag, 3, i, 0] = (("cx", i, 0),), functools.partial(self.third_over_y, i)

    def send(self, key, number, source, target, device):
        i, s = key[1:]
        self.flights[key] = push(source, target, self.sems[0].at[number, i, s], self.sems[1].at[number, i, s], device)

    def start(self):
        here = self.here
        for i, block in enumerate(self.ins):
            target = self.outs[i].at[here.z, here.y, here.core, here.x]
            self.own[i] = pltpu.make_async_copy(block, target, self.sems[2].at[i])
            self.own[i].start()

    def run(self, name):
        waits, action = self.todo.pop(name)
        for key in waits:
            if key[0] != "c":
                self.flights[key].wait_recv()
        action()

    def settle(self, i):
        if i in self.own:
            self.own.pop(i).wait()

    def along_z(self, i, s):
        here = self.here
        a, b, c = routes(self.ins[i].shape[0])
        slot = self.outs[i].at[here.ring_z(s), here.y, here.core, here.x]
        held = self.ins[i] if s == 0 else slot
        if s < 3:
            both = pl.ds(0, a.size + b.size)
            self.send(("z", i, s), 0, held.at[both], slot.at[both], here.next)
        self.send(("a1", i, s), 1, held.at[a], slot.at[a], here.over_y)
        if b.size:
            self.send(("b1", i, s), 2, held.at[b], slot.at[b], here.over_x)
        if s == 0 and c.size:
            self.send(("cx", i, 0), 5, held.at[c], slot.at[c], here.over_x)

    def second(self, i, s, half):
        here, out = self.here, self.outs[i]
        a, b, c = routes(self.ins[i].shape[0])
        z = here.ring_z(s)
        if s == 0:
            self.settle(i)
        if half:
            block = out.at[z, here.y, here.core, :, b]
            self.send(("b2", i, s), 4, block, block, here.over_y)
        else:
            block = out.at[z, :, here.core, here.x, a]
            self.send(("a2", i, s), 3, block, block, here.over_x)

    def third_over_y(self, i):
        here = self.here
        c = routes(self.ins[i].shape[0])[2]
        self.settle(i)
        block = self.outs[i].at[here.z, here.y, here.core, :, c]
        self.send(("cy", i, 0), 6, block, block, here.over_y)

    def third(self, i, s):
        here = self.here
        c = routes(self.ins[i].shape[0])[2]
        if s < 3:
            block = self.outs[i].at[here.ring_z(s), :, here.core, :, c]
            self.send(("cz", i, s), 7, block, block, here.next)

    def across(self, i, s):
        here = self.here
        block = self.outs[i].at[here.ring_z(s), :, here.core]
        self.send(("core", i, s), 8, block, block, here.sibling)

    def arrived(self, i, places=range(4)):
        for s in places:
            self.flights["core", i, s].wait_recv()

    def finish(self):
        for copy in self.flights.values():
            copy.wait_send()


def gather_sems(count):
    dma = pltpu.SemaphoreType.DMA
    return [dma((9, count, 4)), dma((9, count, 4)), dma((count,))]


class ShortGather:
    def __init__(self, tag, here, own, out, sems):
        self.here, self.own, self.out, self.sems = here, own, out, sems
        self.flights = {}
        self.todo = {
            (tag, 0, 0, 0): ((), self.along),
            (tag, 1, 0, 0): (tuple(("z", o) for o in range(3)), self.around),
            (tag, 2, 0, 0): (tuple(("xy", o) for o in range(3)), self.across),
        }

    def send(self, key, number, source, target, device):
        self.flights[key] = push(source, target, self.sems[0].at[number], self.sems[1].at[number], device)

    def start(self):
        here = self.here
        target = self.out.at[here.z, here.y, here.core, here.x]
        self.copy = pltpu.make_async_copy(self.own, target, self.sems[0].at[7])
        self.copy.start()

    def run(self, name):
        waits, action = self.todo.pop(name)
        for key in waits:
            self.flights[key].wait_recv()
        action()

    def along(self):
        here = self.here
        slot = self.out.at[here.z, here.y, here.core, here.x]
        for o, device in enumerate(here.along):
            self.send(("z", o), o, self.own, slot, device)

    def around(self):
        here = self.here
        self.copy.wait()
        block = self.out.at[:, here.y, here.core, here.x]
        for o, device in enumerate(here.around):
            self.send(("xy", o), 3 + o, block, block, device)

    def across(self):
        block = self.out.at[:, :, self.here.core]
        self.send(("core", 0), 6, block, block, self.here.sibling)

    def arrived(self):
        self.flights["core", 0].wait_recv()

    def finish(self):
        for copy in self.flights.values():
            copy.wait_send()


def short_gather_sems():
    return [pltpu.SemaphoreType.DMA((8,)), pltpu.SemaphoreType.DMA((8,))]


class ShortScatter:
    def __init__(self, tag, here, partial, final, scratch):
        self.acc, self.mate, self.xy_rows, self.z_rows, self.send_sem, self.recv_sem = scratch
        self.here, self.partial, self.final = here, partial, final
        self.flights = {}
        self.todo = {
            (tag, 0, 0, 0): (tuple(("core", n) for n in range(8)), self.from_sibling),
            (tag, 1, 0, 0): (tuple(("xy", o) for o in range(3)), self.around),
            (tag, 2, 0, 0): (tuple(("z", o) for o in range(3)), self.last),
        }

    def send(self, key, number, source, target, device):
        self.flights[key] = push(source, target, self.send_sem.at[number], self.recv_sem.at[number], device)

    def start(self):
        here = self.here
        for z in range(4):
            for y in range(2):
                rows = pl.ds(8 * z + 4 * y + 2 * (1 - here.core), 2)
                self.send(
                    ("core", 2 * z + y), 2 * z + y, self.partial.at[rows], self.mate.at[z, y], here.sibling
                )

    def run(self, name):
        waits, action = self.todo.pop(name)
        for key in waits:
            self.flights[key].wait_recv()
        action()

    def from_sibling(self):
        here = self.here
        for z in range(4):
            for y in range(2):
                rows = pl.ds(8 * z + 4 * y + 2 * here.core, 2)
                self.acc[z, y] = self.partial[rows] + self.mate[z, y]
        places = [(1 - here.y, here.x), (here.y, 1 - here.x), (1 - here.y, 1 - here.x)]
        for o, (y, x) in enumerate(places):
            self.send(("xy", o), 8 + o, self.acc.at[:, y, x], self.xy_rows.at[o], here.around[o])

    def around(self):
        here = self.here
        mine = self.acc.at[:, here.y, here.x]
        mine[...] = mine[...] + self.xy_rows[0] + self.xy_rows[1] + self.xy_rows[2]
        for o, device in enumerate(here.along):
            z = here.ring_z(3 - o)
            self.send(("z", o), 11 + o, mine.at[z], self.z_rows.at[o], device)

    def last(self):
        here = self.here
        self.final(self.acc[here.z, here.y, here.x] + self.z_rows[0] + self.z_rows[1] + self.z_rows[2])

    def finish(self):
        for copy in self.flights.values():
            copy.wait_send()


def short_scatter_scratch(block):
    rows, lanes = block.shape[-2:]
    dma = pltpu.SemaphoreType.DMA
    return [
        pltpu.VMEM((4, 2, 2, rows, lanes), f32), pltpu.VMEM((4, 2, 2, rows, lanes), f32),
        pltpu.VMEM((3, 4, rows, lanes), f32), pltpu.VMEM((3, rows, lanes), f32), dma((14,)), dma((14,)),
    ]


def gathered_shape(block):
    return sds((4, 2, 2, 2) + block.shape, block.dtype)


def add_rows(target, source, lead, low, size):
    chunk = 16

    @pl.loop(0, size // chunk)
    def _(r):
        start = pl.multiple_of(r * chunk, chunk)
        here, there = pl.ds(low + start, chunk), pl.ds(start, chunk)
        for at in lead:
            target[at + (here,)] = target[at + (here,)] + source[at + (there,)]


class Scatter:
    def __init__(self, tag, here, ins, final, scratch):
        (
            self.acc, self.mate, self.one_a, self.one_b, self.two_rows, self.ring_rows, self.ring_c, self.c_y, self.c_x,
            self.send_sem, self.recv_sem, self.load_sem,
        ) = scratch
        self.here, self.ins, self.final = here, ins, final
        self.rows = self.acc.shape[3]
        self.a, self.b, self.c = routes(self.rows)
        self.flights, self.loads, self.todo, self.released = {}, {}, {}, set()
        for k in range(4):
            self.todo[tag, 0, 0, k] = (("core", k),), functools.partial(self.from_sibling, k)
            self.todo[tag, 1, 0, k] = (("a1", k),), functools.partial(self.first_sum, k, 0)
            waits = [("a2", k)]
            if self.b.size:
                self.todo[tag, 2, 0, k] = (("b1", k),), functools.partial(self.first_sum, k, 1)
                waits.append(("b2", k))
            if k:
                waits.append(("z", k - 1))
            self.todo[tag, 3, 0, k] = tuple(waits), functools.partial(self.second_sum, k)
            if self.c.size:
                waits = (("c", k), ("cz", k - 1)) if k else (("c", k),)
                self.todo[tag, 4, 0, k] = waits, functools.partial(self.third_sum, k)
        if self.c.size:
            self.todo[tag, 5, 0, 0] = (("cy", 0),), self.third_over_y
            self.todo[tag, 5, 0, 1] = (("cx", 0), ("own", 0)), self.third_over_x

    def send(self, key, number, source, target, device, piece=0):
        at = (number + piece, key[1])
        self.flights[key] = push(source, target, self.send_sem.at[at], self.recv_sem.at[at], device)

    def pieces(self, k):
        z, low = self.here.ring_z(k + 1), 0
        for number, ref in enumerate(self.ins):
            if len(ref.shape) == 3:
                for y in range(2):
                    yield (
                        number + y, lambda core, y=y: ref.at[pl.ds(8 * z + 4 * y + 2 * core, 2)], lambda slot, y=y: slot.at[y]
                    )
            elif len(ref.shape) == 5:
                yield number, lambda core, ref=ref: ref.at[:, core], lambda slot: slot
            else:
                span = pl.ds(low, ref.shape[4])
                low += ref.shape[4]
                yield (
                    number, lambda core, ref=ref: ref.at[z, :, core], lambda slot, span=span: slot.at[:, :, span]
                )

    def load(self, k, numbers=None):
        for number, source, target in self.pieces(k):
            if numbers is not None and number not in numbers:
                continue
            self.loads[k, number] = pltpu.make_async_copy(
                source(self.here.core), target(self.acc.at[k]), self.load_sem.at[k, number]
            )
            self.loads[k, number].start()

    def to_sibling(self, k, numbers=None):
        for number, source, target in self.pieces(k):
            if numbers is not None and number not in numbers:
                continue
            self.send(
                ("core", k, number), 8, source(1 - self.here.core), target(self.mate.at[k]), self.here.sibling, number
            )

    def offer(self, k):
        self.load(k)
        self.to_sibling(k)

    def release(self, k):
        for number, _, _ in self.pieces(k):
            self.flights["core", k, number].wait_send()
        self.released.add(k)

    def prepare(self, numbers=None):
        for k in range(4):
            self.load(k, numbers)

    def start(self, numbers=None):
        for k in range(4):
            self.to_sibling(k, numbers)

    def run(self, name):
        waits, action = self.todo.pop(name)
        for key in waits:
            if key[0] == "core":
                for number, _, _ in self.pieces(key[1]):
                    self.loads[key[1], number].wait()
                    self.flights["core", key[1], number].wait_recv()
            elif key[0] not in ("c", "own"):
                self.flights[key].wait_recv()
        action()

    def from_sibling(self, k):
        here, acc = self.here, self.acc.at[k]
        add_rows(acc, self.mate.at[k], [(a, b) for a in range(2) for b in range(2)], 0, self.rows)
        self.send(("a1", k), 0, acc.at[:, 1 - here.x, self.a], self.one_a.at[k], here.over_x)
        if self.b.size:
            self.send(("b1", k), 1, acc.at[1 - here.y, :, self.b], self.one_b.at[k], here.over_y)

    def first_sum(self, k, half):
        here, acc = self.here, self.acc.at[k]
        if half:
            add_rows(acc.at[here.y], self.one_b.at[k], [(0,), (1,)], self.b.start, self.b.size)
            self.send(
                ("b2", k), 3, acc.at[here.y, 1 - here.x, self.b], self.two_rows.at[k, self.b], here.over_x
            )
        else:
            add_rows(acc.at[:, here.x], self.one_a.at[k], [(0,), (1,)], self.a.start, self.a.size)
            self.send(
                ("a2", k), 2, acc.at[1 - here.y, here.x, self.a], self.two_rows.at[k, self.a], here.over_y
            )

    def second_sum(self, k):
        here = self.here
        size = self.a.size + self.b.size
        mine = self.acc.at[k, here.y, here.x]
        add_rows(mine, self.two_rows.at[k], [()], 0, size)
        if k:
            add_rows(mine, self.ring_rows.at[k - 1], [()], 0, size)
        if k < 3:
            self.send(("z", k), 4, mine.at[pl.ds(0, size)], self.ring_rows.at[k], here.next)
        elif not self.c.size:
            self.final(mine)

    def third_sum(self, k):
        here, acc = self.here, self.acc.at[k]
        if k:
            add_rows(acc, self.ring_c.at[k - 1], [(a, b) for a in range(2) for b in range(2)], self.c.start, self.c.size)
        if k < 3:
            self.send(("cz", k), 5, acc.at[:, :, self.c], self.ring_c.at[k], here.next)
        else:
            self.send(("cy", 0), 6, acc.at[1 - here.y, :, self.c], self.c_y, here.over_y)

    def third_over_y(self):
        here, acc = self.here, self.acc.at[3]
        add_rows(acc.at[here.y], self.c_y, [(0,), (1,)], self.c.start, self.c.size)
        self.send(("cx", 0), 7, acc.at[here.y, 1 - here.x, self.c], self.c_x, here.over_x)

    def third_over_x(self):
        mine = self.acc.at[3, self.here.y, self.here.x]
        add_rows(mine, self.c_x, [()], self.c.start, self.c.size)
        self.final(mine)

    def finish(self):
        for key, copy in self.flights.items():
            if key[0] != "core" or key[1] not in self.released:
                copy.wait_send()


def scatter_scratch(block):
    dma = pltpu.SemaphoreType.DMA
    rows, lanes, kind = sum(b.shape[-2] for b in block), block[0].shape[-1], block[0].dtype
    a, b, c = (max(span.size, 16) for span in routes(rows))
    both = sum(span.size for span in routes(rows)[:2])
    return [
        pltpu.VMEM((4, 2, 2, rows, lanes), kind), pltpu.VMEM((4, 2, 2, rows, lanes), kind),
        pltpu.VMEM((4, 2, a, lanes), kind), pltpu.VMEM((4, 2, b, lanes), kind),
        pltpu.VMEM((4, both, lanes), kind), pltpu.VMEM((3, both, lanes), kind),
        pltpu.VMEM((3, 2, 2, c, lanes), kind), pltpu.VMEM((2, c, lanes), kind), pltpu.VMEM((c, lanes), kind),
        dma((11, 4)), dma((11, 4)), dma((4, 3)),
    ]


def in_order(plan, chain, networks):
    pieces = iter(chain)
    for item in plan:
        if item == -1:
            next(pieces)()
        else:
            networks[item[0]].run(item)
    assert next(pieces, None) is None and not any(net.todo for net in networks.values())


def small_rows(cond, forget, taps, place):
    at = lax.rem(place * taps.shape[0], LANES)
    taps = lax.dynamic_update_slice(jnp.zeros((4 * LANES,), bf16), taps, (at,)).reshape(4, LANES)
    cond = cond.reshape(-1, LANES)
    forget = forget.reshape(36, -1)
    return jnp.concatenate([
        jnp.pad(cond, ((0, 16 - cond.shape[0]), (0, 0))), jnp.pad(taps, ((0, 12), (0, 0))),
        jnp.pad(forget, ((0, 12), (0, LANES - forget.shape[1]))),
    ])


def unpack_small(small, taps_share, wf_ref, taps_ref, flat):
    wf_ref[: 32 * GROUPS, :] = small[:, 32:64, :].reshape(32 * GROUPS, LANES)
    wf_ref[32 * GROUPS :, :] = dot(pick_left(None, 0), small[:, 64:80, :].reshape(16 * GROUPS, LANES)).astype(bf16)
    flat[...] = jnp.zeros_like(flat)
    for d in range(GROUPS):
        row = d * taps_share // LANES
        flat[row : row + 4, :] += small[d, 16:32, :].astype(f32)[:4]
    tiles = taps_ref.shape[1] // LANES
    taps_ref[...] = jnp.zeros_like(taps_ref)
    for k in range(10):
        for t in range(tiles):
            taps_ref[k : k + 1, t * LANES : (t + 1) * LANES] = flat[k * tiles + t : k * tiles + t + 1, :]


def pack_rows(sources, wide, left, out, other=None):
    for j, (source, first, per_row) in enumerate(sources):
        target = other if other is not None and j == 3 else out.at[pl.ds(32 * j, 32)]
        if first == 0:
            wide[: source.shape[0], :] = source[...].astype(f32)
        for t in range(out.shape[1] // LANES):
            cols = slice(t * LANES, (t + 1) * LANES)
            rows = wide[pl.ds(first + t, 36, stride=per_row), :]
            target[:, cols] = rows[:32].astype(bf16)
            left[4 * j : 4 * j + 4, cols] = rows[32:]
    out[(128 if other is None else 96) : (144 if other is None else 112), :] = left[...].astype(bf16)


def fill_permutation(perm_ref):
    width = perm_ref.shape[0]
    at = lax.broadcasted_iota(jnp.int32, (1, width), 1)
    late = at - 32 * GROUPS
    order = jnp.where(late < 0, (at >> 5) * 36 + (at & 31), (late >> 2) * 36 + 32 + (late & 3))
    for rows in spans(width, 2 * LANES):
        row = lax.broadcasted_iota(jnp.int32, (rows.stop - rows.start, width), 0) + rows.start
        perm_ref[rows, :] = (row == order).astype(bf16)


def forward_kernel(
    head_width, heads, taps_share, x_ref, ada_ref, bias_ref, bf_ref, own_s, query_ref, key_ref, value_ref, out_ref, up_ref,
    all_s, all_a, all_u, xp_out, qkv_out, mix_out, mixedp_out, branch_out, middle_out, h2p_out, perm_out,
    mod_ref, wf_ref, taps_ref, gate_ref, run_ref, runt_ref, state_ref, rims_ref, given_ref, taken_ref, cond_ref,
    xp_ref, qkv_ref, mix_ref, mixedp_ref, branch_ref, middle_ref, h2p_ref, perm_ref,
    own_a, own_u, wide, ada_wide, rows_left, small, flat, partial, main, left, outbox, inbox, vpad, mixed, load_sem, swap_sem, *rest,
):
    length, width = x_ref.shape
    tiles = width // LANES
    here = Here()
    here.greet(True)
    lower = here.x == 0
    squares = [(ref, 0, tiles) for ref in (query_ref, key_ref, value_ref, out_ref)]
    pack_rows(squares, wide, rows_left, own_a, own_u.at[pl.ds(144, 32)])
    pack_rows([(up_ref, j * tiles, 4 * tiles) for j in range(4)], wide, rows_left, own_u)
    first = ShortGather("f", here, own_s, all_s, rest[:2])
    gather = Gather("g", here, (own_a, own_u), (all_a, all_u), rest[2:5])

    def to_mod(total):
        for k in range(6):
            for t in range(tiles):
                mod_ref[k : k + 1, t * LANES : (t + 1) * LANES] = total[k * tiles + t : k * tiles + t + 1, :]
        mod_ref[6:8, :] = jnp.zeros((2, width), f32)

    scatter = ShortScatter("s", here, partial, to_mod, rest[5:])
    stores, loads = [], []

    def fetch(number, source, target):
        copy = pltpu.make_async_copy(source, target, load_sem.at[number])
        copy.start()
        return copy

    def modulation():
        first.arrived()
        fetch(5, all_s, small).wait()
        me = ((here.z * 2 + here.y) * 2 + here.core) * 2 + here.x
        row = lax.broadcasted_iota(jnp.int32, (width, LANES), 0)
        lane = lax.broadcasted_iota(jnp.int32, (width, LANES), 1)
        pick = ((row == lane + me * 36) & (lane < 36)).astype(bf16)
        lines = small[...].reshape(GROUPS, 80, LANES)[:, :16, :].astype(f32)
        mine = jnp.zeros((GROUPS, LANES), f32)
        for t in range(tiles):
            cond = lines[:, t, :]
            cond = (cond / (1.0 + jnp.exp(-cond))).astype(bf16)
            mine = mine + dot(cond, pick[t * LANES : (t + 1) * LANES])
        cond_ref[...] = mine.astype(bf16)
        mine = mine[:, :36].astype(bf16)
        for t in range(6 * tiles):
            rows = ada_wide[pl.ds(t, 36, stride=6 * tiles), :].astype(bf16)
            partial[:, t, :] = dot(mine, rows) + bias_ref[t : t + 1, :].astype(f32)
        scatter.start()

    def small_arrays():
        unpack_small(small[...].reshape(GROUPS, 80, LANES), taps_share, wf_ref, taps_ref, flat)

    def norm_one():
        first_part(x_ref, mod_ref, perm_ref, wf_ref, bf_ref, xp_ref, gate_ref, run_ref, runt_ref, mixed)
        stores.extend([fetch(6, xp_ref, xp_out), fetch(13, perm_ref, perm_out)])
        total = run_ref[0, length - 1 : length, :]
        given_ref[0] = jnp.where(lower, jnp.exp(total - run_ref[0]), jnp.exp(run_ref[1]))
        taken_ref[0] = jnp.where(lower, jnp.exp(total - run_ref[1]), jnp.exp(run_ref[0]))
        mix_ref[...] = jnp.zeros_like(mix_ref)

    def load(slot):
        source = all_a.at[:, :, :, :, pl.ds(32 * slot, 32)] if slot < 3 else all_u.at[:, :, :, :, pl.ds(144, 32)]
        loads.append(fetch(slot, source, main.at[slot % 2]))

    def project(slot):
        if slot == 0:
            gather.arrived(0)
            others = fetch(4, all_a.at[:, :, :, :, pl.ds(96, 16)], left)
            load(0)
            load(1)
            others.wait()
        loads[slot].wait()

        def write(cols, value):
            qkv_ref[slot, :, cols] = value.astype(bf16)

        project_part(slot, xp_ref, main.at[slot % 2], left, write)
        if slot == 0:
            load(2)
        if slot == 2:
            stores.append(fetch(7, qkv_ref, qkv_out))

    def states():
        state_part(head_width, 1, lambda cols: qkv_ref[1, :, cols], qkv_ref.at[2], given_ref, outbox)
        edge = pl.multiple_of((1 - here.x) * (length - GRID), GRID)

        def write_edge(t, value):
            outbox[0, width + t * GRID : width + (t + 1) * GRID, :] = value

        edge_part(qkv_ref[2, pl.ds(edge, GRID), :], write_edge)
        stores.append(push(outbox, inbox, swap_sem.at[0], swap_sem.at[1], here.over_x))

    def mix(part):
        mix_part(head_width, heads, part * heads // 4, (part + 1) * heads // 4, qkv_ref, run_ref, runt_ref, mix_ref)

    def mixing():
        swap = stores.pop()
        swap.wait_recv()
        state_ref[0] = inbox[0, :width, :]
        for t in range(tiles):
            cols = slice(t * LANES, (t + 1) * LANES)
            rows = inbox[0, width + t * GRID : width + (t + 1) * GRID, :]
            rims_ref[0, :, cols] = jnp.where(lower, 0, rows).astype(bf16)
            rims_ref[1, :, cols] = jnp.where(lower, rows, 0).astype(bf16)
        fill_padded(vpad, rims_ref, qkv_ref[2])
        mixed_part(head_width, 1, qkv_ref, taken_ref, state_ref, taps_ref, vpad, mix_ref, mixed)
        stores.append(fetch(8, mix_ref, mix_out))
        swap.wait_send()

    def turn():
        gather.arrived(1)
        load(3)
        permute_part(mixed, perm_ref, mixedp_ref)
        stores.append(fetch(9, mixedp_ref, mixedp_out))

    def branch():
        loads[3].wait()
        branch_part(x_ref, mod_ref, mixedp_ref, main.at[1], left, branch_ref, middle_ref)
        stores.extend([fetch(10, branch_ref, branch_out), fetch(11, middle_ref, middle_out)])

    def norm_two():
        second_hidden(mod_ref, middle_ref, mixed)
        permute_part(mixed, perm_ref, h2p_ref)
        stores.append(fetch(12, h2p_ref, h2p_out))

    def prepare():
        fill_permutation(perm_ref)
        ada_wide[...] = ada_ref[...].astype(f32)
        partial[:, 6 * tiles :, :] = jnp.zeros((GROUPS, 64 - 6 * tiles, LANES), f32)

    chain = [prepare, modulation, small_arrays, norm_one]
    chain += [functools.partial(project, slot) for slot in range(3)] + [states]
    chain += [functools.partial(mix, part) for part in range(4)] + [mixing, turn, branch, norm_two]
    first.start()
    gather.start()
    here.meet(True)
    in_order(FORWARD_PLAN, chain, {"f": first, "g": gather, "s": scatter})
    for network in (first, gather, scatter):
        network.finish()
    for copy in stores:
        copy.wait()


def forward_fused(x, ada, bias, bf, small, shards, heads, taps_share):
    length, width = x.shape
    head_width = width // heads
    message = width + width // LANES * GRID
    anywhere, vm = pl.BlockSpec(memory_space=pl.ANY), pl.BlockSpec(memory_space=pltpu.VMEM)
    rows, wide = (length, width), (length, LANES)
    bulk = (
        sds(rows, bf16), sds((3,) + rows, bf16), sds(rows), sds(rows, bf16), sds(rows, bf16), sds(rows), sds(rows, bf16),
        sds((width, width), bf16),
    )
    kept = (
        sds((8, width)), sds((width, LANES), bf16), sds((16, width)), sds(wide), sds((2,) + wide), sds((2, LANES, length)),
        sds((1, width, LANES), bf16), sds((2, GRID, width), bf16), sds((1,) + wide), sds((1,) + wide),
        sds((GROUPS, LANES), bf16),
    )
    partial = sds((GROUPS, 64, LANES))
    own, own_up = sds((112, width), bf16), sds((176, width), bf16)
    dma = pltpu.SemaphoreType.DMA
    out = pl.pallas_call(
        functools.partial(forward_kernel, head_width, heads, taps_share),
        out_shape=tuple(gathered_shape(b) for b in (small, own, own_up)) + bulk + kept,
        in_specs=[vm] * 10,
        out_specs=(anywhere,) * (3 + len(bulk)) + (vm,) * len(kept),
        scratch_shapes=[pltpu.VMEM(b.shape, b.dtype) for b in bulk] + [
            pltpu.VMEM(own.shape, bf16), pltpu.VMEM(own_up.shape, bf16), pltpu.VMEM(shards[4].shape, f32),
            pltpu.VMEM(ada.shape, f32), pltpu.VMEM((16, width), f32),
            pltpu.VMEM((4, 2, 2, 2) + small.shape, bf16), pltpu.VMEM((96, LANES), f32),
            pltpu.VMEM(partial.shape, f32), pltpu.VMEM((2, 4, 2, 2, 2, 32, width), bf16),
            pltpu.VMEM((4, 2, 2, 2, 16, width), bf16), pltpu.VMEM((1, message, LANES), bf16),
            pltpu.VMEM((1, message, LANES), bf16), pltpu.VMEM((length + 2 * GRID, width), bf16), pltpu.VMEM(rows, bf16),
            dma((14,)), dma((2,)),
        ] + short_gather_sems() + gather_sems(2) + short_scatter_scratch(partial),
        compiler_params=pltpu.CompilerParams(collective_id=0, has_side_effects=True, vmem_limit_bytes=VMEM_LIMIT),
        name="forward",
    )(x, ada, bias, bf, small, *shards)
    gathered = [g.reshape((GROUPS,) + g.shape[4:]) for g in out[:3]]
    return gathered, out[3 : 3 + len(bulk)], out[3 + len(bulk) :]


def feed_fused_kernel(
    h2p, cot, mod_ref, flat_d, up_in, middle_in,
    all_d, out_out, gh_out, gup_out, gleft_ref, ggate_ref, down_own,
    gdi, h2pt, act, slope, actt, gup, main, left, left_own, down, down_acc, gh, middle, stage_d, stage_u, own_d, wide, load_sem, *rest,
):
    length, width = h2p.shape
    main_rows = GROUPS * 32
    here = Here()
    here.greet()
    gather = Gather("g", here, (own_d,), (all_d,), rest[:3])
    scatter = Scatter("d", here, [stage_d], plain_final(down_own), rest[3:])
    order = [here.ring_z(k + 1) for k in range(4)]

    def fetch(number, source, target):
        copy = pltpu.make_async_copy(source, target, load_sem.at[number])
        copy.start()
        return copy

    def load_up(k, number):
        rows = pl.ds(pl.multiple_of(32 * order[k], 32), 32)
        return fetch(number, up_in.at[:, rows], main.at[k % 2])

    def load_down(k):
        gather.arrived(0, [(k + 1) % 4])
        return fetch(8 + k, all_d.at[order[k]], down.at[k % 2])

    def left_rows(k):
        return dot(pick_left(None, order[k]), left[...].reshape(16 * GROUPS, width)).astype(bf16)

    def start():
        gdi[...] = (cot[...].astype(f32) * mod_ref[5:6, :]).astype(bf16)
        h2pt[...] = h2p[...].T
        gleft_ref[...] = jnp.zeros_like(gleft_ref)
        others.wait()

    def up_step(k):
        loads[k].wait()
        left_own[...] = left_rows(k)
        for cols in spans(width):
            up = dot(h2p[:, :main_rows], main[k % 2, :, :, cols].reshape(main_rows, -1))
            up = up + dot(h2p[:, main_rows:], left_own[:, cols])
            value, rate = gelu_both(up)
            value = value.astype(bf16)
            act[k, :, cols] = value
            actt[cols, :] = value.T
            slope[k, :, cols] = rate.astype(bf16)
        loads.append(load_up(k + 2, k + 2) if k < 2 else load_up(k - 2, k + 2))

    def down_grad(k):
        if k > 0:
            scatter.release(k - 1)
        for cols in spans(width):
            stage_d[:, :, :, :, cols] = dot(actt[...], gdi[:, cols]).astype(bf16).reshape(2, 2, 2, width // 8, -1)
        scatter.offer(k)

    def back_act(k):
        load_down(k).wait()
        rows_of = down[k % 2].reshape(width, width)
        for cols in spans(width):
            gup[:, cols] = (dot_bt(gdi[...], rows_of[cols]) * slope[k, :, cols].astype(f32)).astype(bf16)

    def down_step(k):
        rows_of = down[k % 2].reshape(width, width)
        for cols in spans(width):
            part = dot(act[k], rows_of[:, cols])
            if k == 0:
                down_acc[:, cols] = part
            else:
                down_acc[:, cols] += part
    def back_hidden(k):
        loads[4 + k].wait()
        for cols in spans(main_rows):
            part = dot_bt(gup[...], main[k % 2, cols.start // 32 : cols.stop // 32].reshape(-1, width))
            if k == 0:
                gh[:, cols] = part
            else:
                gh[:, cols] += part
        part = dot_bt(gup[...], left_rows(k))
        if k == 0:
            gh[:, main_rows:] = part
        else:
            gh[:, main_rows:] += part
        if k < 2:
            loads.append(load_up(k + 2, 6 + k))

    def up_grad(k):
        if k > 0:
            stores[k - 1].wait()
        projection_grads(order[k], h2pt, gup, stage_u, gleft_ref)
        rows = pl.ds(pl.multiple_of(32 * order[k], 32), 32)
        stores.append(fetch(13 + k, stage_u, gup_out.at[:, rows]))

    def end():
        keep = fetch(17, gh, gh_out)
        ggate_ref[...] = jnp.sum(cot[...].astype(f32) * down_acc[...], axis=0, keepdims=True)
        keep_middle.wait()
        for cols in spans(width):
            act[0, :, cols] = (middle[:, cols] + mod_ref[5:6, cols] * down_acc[:, cols]).astype(bf16)
        stores.extend([fetch(19, act.at[0], out_out), keep])

    chain = [start]
    for k in range(4):
        chain += [functools.partial(up_step, k), functools.partial(down_grad, k)]
    for k in range(4):
        chain += [functools.partial(step, k) for step in (back_act, down_step, back_hidden, up_grad)]
    others = fetch(12, up_in.at[:, pl.ds(128, 16)], left)
    loads = [load_up(0, 0), load_up(1, 1)]
    keep_middle = fetch(18, middle_in, middle)
    stores = []
    wide[...] = flat_d[...].astype(f32)
    for t in range(width // LANES):
        rows = wide[pl.ds(t, own_d.shape[0], stride=width // LANES), :]
        own_d[:, t * LANES : (t + 1) * LANES] = rows.astype(bf16)
    gather.start()
    here.meet()
    in_order(FEED_PLAN, chain + [end], {"d": scatter, "g": gather})
    scatter.finish()
    gather.finish()
    for copy in stores[3:]:
        copy.wait()


def feed_fused(h2p, cot, mod, flat_d, up_w, middle):
    length, width = h2p.shape
    anywhere, vm = pl.BlockSpec(memory_space=pl.ANY), pl.BlockSpec(memory_space=pltpu.VMEM)
    rows = (length, width)
    dma = pltpu.SemaphoreType.DMA
    stage = (2, 2, 2, width // 8, width)
    own = sds((width // 8, width), bf16)
    return pl.pallas_call(
        feed_fused_kernel,
        out_shape=(
            gathered_shape(own), sds(rows, bf16), sds(rows), sds((GROUPS, 128, width), bf16),
            sds((GROUPS, 16, width), bf16), sds((1, width)), sds(flat_d.shape),
        ),
        in_specs=[vm] * 4 + [anywhere] * 2,
        out_specs=(anywhere,) * 4 + (vm,) * 3,
        scratch_shapes=[
            pltpu.VMEM(rows, bf16), pltpu.VMEM((width, length), bf16), pltpu.VMEM((4,) + rows, bf16),
            pltpu.VMEM((4,) + rows, bf16), pltpu.VMEM((width, length), bf16), pltpu.VMEM(rows, bf16),
            pltpu.VMEM((2, GROUPS, 32, width), bf16), pltpu.VMEM((GROUPS, 16, width), bf16), pltpu.VMEM((128, width), bf16),
            pltpu.VMEM((2,) + stage, bf16), pltpu.VMEM(rows, f32), pltpu.VMEM(rows, f32), pltpu.VMEM(rows, f32),
            pltpu.VMEM(stage, bf16),
            pltpu.VMEM((GROUPS, 32, width), bf16), pltpu.VMEM(own.shape, bf16), pltpu.VMEM(flat_d.shape, f32), dma((20,)),
        ] + gather_sems(1) + scatter_scratch([sds(stage, bf16)]),
        compiler_params=pltpu.CompilerParams(
            collective_id=1, has_side_effects=True, vmem_limit_bytes=62 * 1024 * 1024
        ),
        name="feed",
    )(h2p, cot, mod, flat_d, up_w, middle)[1:]


def six(array):
    return array.reshape((4, 2, 2, 2) + array.shape[1:])


def flat_rows(out, first, value, per_row):
    for t in range(value.shape[1] // LANES):
        out[pl.ds(first + t, value.shape[0], stride=per_row), :] = value[:, t * LANES : (t + 1) * LANES]


def square_final(outs, out_left):
    def final(total):
        value = total[...].astype(f32)
        per_row = value.shape[1] // LANES
        for j, out in enumerate(outs):
            flat_rows(out, 0, value[32 * j : 32 * j + 32], per_row)
            flat_rows(out, 32 * per_row, value[96 + 4 * j : 100 + 4 * j], per_row)
        flat_rows(out_left, 0, value[108:112], per_row)

    return final


def columns_final(out, out_main):
    def final(total):
        value = total[...].astype(f32)
        tiles = value.shape[1] // LANES
        for j in range(4):
            flat_rows(out, j * tiles, value[32 * j : 32 * j + 32], 4 * tiles)
            flat_rows(out, 32 * 4 * tiles + j * tiles, value[128 + 4 * j : 132 + 4 * j], 4 * tiles)
        flat_rows(out_main, 0, value[144:176], tiles)

    return final


def plain_final(out):
    def final(total):
        value = total[...].astype(f32)
        flat_rows(out, 0, value, value.shape[1] // LANES)

    return final


def small_final(out):
    def final(total):
        out[...] = total[...]

    return final


def fill_small(block, gforget, conv, bias, flat, taps_share):
    tiles = conv.shape[1] // LANES
    for k in range(10):
        for t in range(tiles):
            flat[k * tiles + t : k * tiles + t + 1, :] = conv[k : k + 1, t * LANES : (t + 1) * LANES]
    flat[10 * tiles :, :] = jnp.zeros_like(flat[10 * tiles :, :])
    block[:, :32, :] = gforget[: 32 * GROUPS, :].reshape(GROUPS, 32, LANES)
    block[:, 40:, :] = jnp.broadcast_to(bias[...].reshape(1, 1, LANES), (GROUPS, 8, LANES))
    for d in range(GROUPS):
        at = 32 * GROUPS + 4 * d
        block[d, 32:36, :] = gforget[at : at + 4, :]
        row = d * taps_share // LANES
        block[d, 36:40, :] = flat[row : row + 4, :]


def backward_kernel(
    head_width, heads, taps_share,
    mod_ref, run_ref, runt_ref, taken_ref, given_ref, gate_ref, state_ref, vrims_ref, taps_ref,
    ghp_in, perm_in, middle_in, cot_in, branch_in, mixedp_in, mix_in, weight_in, up_in, qkv_in, xp_in, gup_in, gupl_in,
    gmid_out, gqkv_out, gmain_out, gout_out, small_out, gleft_ref, ggate_ref, sums_ref, up_ref, out_ref,
    pool, perm, gmix, gb, main, qkv, gqkv, held, vpad, gpad, pair_rows, pair_cols,
    outbox, inbox, rims, leave, conv_ref, bias_ref, gforget_ref, flat, small, partial, fetch_sem, swap_sem, *scratch,
):
    length, width = gmix.shape
    here = Here()
    here.greet()
    lower = here.x == 0
    gmixed = gpad.at[pl.ds(GRID, length)]
    turned = perm.at[:, pl.ds(0, length)]
    scatter = Scatter("u", here, [gup_in, gupl_in, gout_out], columns_final(up_ref, out_ref), scratch)
    scatter.prepare((0, 1))

    def fetch(number, source, target):
        copy = pltpu.make_async_copy(source, target, fetch_sem.at[number])
        copy.start()
        return copy

    first = [
        fetch(0, ghp_in, pool.at[0]), fetch(1, perm_in, perm), fetch(2, middle_in, pool.at[1]), fetch(3, cot_in, qkv.at[0]),
        fetch(4, branch_in, qkv.at[1]), fetch(5, mixedp_in, qkv.at[2]),
        fetch(6, up_in.at[:, :, :, :, pl.ds(144, 32)], main.at[0]),
        fetch(7, weight_in.at[:, pl.ds(96, 16)], gleft_ref),
        fetch(8, mix_in, pool.at[2]),
    ]
    second = second_part(
        head_width, pool.at[0], perm, pool.at[1], mod_ref, qkv.at[0], qkv.at[1], qkv.at[2], pool.at[2], main.at[0], gleft_ref,
        pool.at[1], gmixed, gmix, main.at[1], gleft_ref, sums_ref, pool.at[3], gb, partial,
    )
    gq, gk, gv = pool.at[0], pool.at[2], pool.at[3]
    early = jnp.where(lower, jnp.ones((1, LANES), f32), 0.0)
    carry = carry_part(
        head_width, 1, early, qkv, gmix, gq, gk, gv, pair_rows, pair_cols, taken_ref, given_ref, gate_ref, state_ref,
        leave, jnp.zeros((1, LANES), f32), vpad, gpad, taps_ref, gqkv, ggate_ref, conv_ref, bias_ref,
    )
    stores = []

    def begin():
        first[0].wait()
        first[1].wait()
        next(second)
        for copy in first[2:]:
            copy.wait()

    def out_grad():
        next(second)
        stores.append(fetch(11, main.at[1], gout_out))
        next(second)
        stores.pop().wait()

    def states():
        again = fetch(9, qkv_in, qkv)
        scatter.prepare((2,))
        scatter.start((2,))
        stores.extend([fetch(10, pool.at[1], gmid_out), fetch(12, xp_in, gb)])
        for ref in (gq, gk, gv, pair_rows, pair_cols):
            ref[...] = jnp.zeros_like(ref)
        again.wait()
        state_part(head_width, 1, lambda cols: qkv[0, :, cols], gmix, taken_ref, outbox)
        edge = pl.multiple_of((1 - here.x) * (length - GRID), GRID)

        def write_edge(t, value):
            outbox[0, width + t * GRID : width + (t + 1) * GRID, :] = value

        edge_part(gmixed[pl.ds(edge, GRID), :], write_edge)
        stores.append(push(outbox, inbox, swap_sem.at[0], swap_sem.at[1], here.over_x))

    def pairs(part):
        pairs_part(
            head_width, heads, part * heads // 4, (part + 1) * heads // 4, qkv, gmix, run_ref, runt_ref, gq, gk, gv,
            pair_rows, pair_cols, held,
        )

    def carry_first():
        swap = stores.pop()
        swap.wait_recv()
        leave[0] = inbox[0, :width, :]
        for t in range(width // LANES):
            cols = slice(t * LANES, (t + 1) * LANES)
            edge_rows = inbox[0, width + t * GRID : width + (t + 1) * GRID, :]
            rims[0, :, cols] = jnp.where(lower, 0, edge_rows).astype(bf16)
            rims[1, :, cols] = jnp.where(lower, edge_rows, 0).astype(bf16)
        fill_padded(vpad, vrims_ref, qkv[2])
        gpad[:GRID, :] = rims[0]
        gpad[GRID + length :, :] = rims[1]
        next(carry)
        swap.wait_send()

    def turn():
        stores.append(fetch(13, gqkv, gqkv_out))
        stores[1].wait()
        turned[...] = gb[...].T
        gforget_ref[...] = dot(turned[...], ggate_ref[...])
        fill_small(small, gforget_ref, conv_ref, bias_ref, flat, taps_share)
        fetch(17, small, small_out).wait()

    def weight(slot):
        buffer = main.at[slot % 2]
        if slot == 2:
            stores[3].wait()
        projection_grads(slot, turned, gqkv.at[slot], buffer, gleft_ref)
        stores.append(fetch(14 + slot, buffer, gmain_out.at[:, :, :, :, pl.ds(32 * slot, 32)]))

    chain = [begin, functools.partial(next, second), out_grad, states]
    chain += [functools.partial(pairs, part) for part in range(4)] + [carry_first]
    chain += [functools.partial(next, carry)] * 3 + [turn] + [functools.partial(weight, slot) for slot in range(3)]
    here.meet()
    scatter.start((0, 1))
    in_order(BACKWARD_PLAN, chain, {"u": scatter})
    scatter.finish()
    for number in (0, 2, 4, 5):
        stores[number].wait()


def backward_fused(heads, taps_share, small, arrays, grads):
    length, width = arrays[0].shape
    head_width = width // heads
    message = width + width // LANES * GRID
    anywhere, vm = pl.BlockSpec(memory_space=pl.ANY), pl.BlockSpec(memory_space=pltpu.VMEM)
    rows, wide = (length, width), (length, LANES)
    dma = pltpu.SemaphoreType.DMA
    return pl.pallas_call(
        functools.partial(backward_kernel, head_width, heads, taps_share),
        out_shape=(
            sds(rows), sds((3,) + rows, bf16), sds((4, 2, 2, 2, 96, width), bf16), sds((4, 2, 2, 2, 32, width), bf16),
            sds((GROUPS, 48, LANES)), sds((GROUPS, 16, width), bf16), sds(wide, bf16), sds((8, width)),
            sds((144 * width // LANES, LANES)), sds((32 * width // LANES, LANES)),
        ),
        in_specs=[vm] * len(small) + [anywhere] * (len(arrays) + len(grads)),
        out_specs=(anywhere,) * 5 + (vm,) * 5,
        scratch_shapes=[
            pltpu.VMEM((4,) + rows, f32), pltpu.VMEM((width, width), bf16), pltpu.VMEM(rows, bf16), pltpu.VMEM(rows, bf16),
            pltpu.VMEM((2, 4, 2, 2, 2, 32, width), bf16), pltpu.VMEM((3,) + rows, bf16), pltpu.VMEM((3,) + rows, bf16), pltpu.VMEM((2, length, length), bf16),
            pltpu.VMEM((length + 2 * GRID, width), bf16), pltpu.VMEM((length + 2 * GRID, width), bf16),
            pltpu.VMEM((2,) + wide, f32), pltpu.VMEM((2, heads, length), f32),
            pltpu.VMEM((1, message, LANES), bf16), pltpu.VMEM((1, message, LANES), bf16),
            pltpu.VMEM((2, GRID, width), bf16), pltpu.VMEM((1, width, LANES), bf16), pltpu.VMEM((16, width), f32),
            pltpu.VMEM((1, LANES), f32), pltpu.VMEM((width, LANES), f32), pltpu.VMEM((96, LANES), f32),
            pltpu.VMEM((GROUPS, 48, LANES), f32), pltpu.VMEM((3, 8, width), f32), dma((18,)), dma((2,)),
        ] + scatter_scratch(list(grads) + [sds((4, 2, 2, 2, 32, width), bf16)]),
        compiler_params=pltpu.CompilerParams(
            collective_id=3, has_side_effects=True, vmem_limit_bytes=62 * 1024 * 1024
        ),
        name="backward",
    )(*small, *arrays, *[six(g) for g in grads])


def finish_kernel(
    mod_ref, sums_two, gate_two, ggate_ref, wf_ref,
    weight_in, gqkv_in, perm_in, x_in, gmid_in, gmain_in, gleft_in, small_in,
    gin_ref, all_mod, query_ref, key_ref, value_ref, out_ref, small_ref,
    main, left, gqkv, perm, x, gmid, ghp, gh, sums_one, own_mod, partial, load_sem, *rest,
):
    width = perm.shape[0]
    here = Here()
    here.greet(True)
    scatter = Scatter(
        "a", here, [gmain_in, gleft_in], square_final((query_ref, key_ref, value_ref), out_ref), rest[:12]
    )
    small = Scatter("s", here, [small_in], small_final(small_ref), rest[12:24])
    gather = ShortGather("g", here, own_mod, all_mod, rest[24:])
    scatter.prepare()
    small.prepare()

    def fetch(number, source, target):
        copy = pltpu.make_async_copy(source, target, load_sem.at[number])
        copy.start()
        return copy

    def load(slot):
        return fetch(slot, weight_in.at[:, pl.ds(32 * slot, 32)], main.at[slot % 2])

    grads = fetch(3, gqkv_in, gqkv)
    rest_rows = fetch(4, weight_in.at[:, pl.ds(96, 16)], left)
    loads = [load(0), load(1)]
    others = [fetch(5, perm_in, perm), fetch(6, x_in, x), fetch(7, gmid_in, gmid)]

    def back(slot):
        if slot == 0:
            ghp[...] = dot_bt(ggate_ref[...], wf_ref[...])
            grads.wait()
            rest_rows.wait()
        loads[slot].wait()
        projection_back(slot, gqkv.at[slot], main.at[slot % 2], left, ghp)
        if slot == 0:
            loads.append(load(2))

    def last():
        for copy in others:
            copy.wait()
        last_part(ghp, perm, x, mod_ref, gmid, gin_ref, sums_one, gh, partial)
        lines = [sums_one[0:1, :], sums_one[1:2, :], sums_two[2:3, :], sums_two[0:1, :], sums_two[1:2, :], gate_two[...]]
        tiles = width // LANES
        for k, line in enumerate(lines):
            for t in range(tiles):
                own_mod[k * tiles + t : k * tiles + t + 1, :] = line[:, t * LANES : (t + 1) * LANES]
        own_mod[len(lines) * tiles :, :] = jnp.zeros_like(own_mod[len(lines) * tiles :, :])
        gather.start()

    here.meet(True)
    scatter.start()
    small.start()
    chain = [functools.partial(back, slot) for slot in range(3)] + [last]
    in_order(FINISH_PLAN, chain, {"a": scatter, "s": small, "g": gather})
    gather.arrived()
    for network in (scatter, small, gather):
        network.finish()


def results_kernel(sources, cond_ref, mod_in, *refs):
    ins, outs = refs[: len(sources)], refs[len(sources) : -4]
    all_mod, ada, sems, own_sem = refs[-4:]
    ada_out, total_ref = outs[-2:]
    copies = []
    for number, (ref, (target, low)) in enumerate(zip(ins, sources)):
        place = outs[target] if low is None else outs[target].at[pl.ds(low, ref.shape[0])]
        copies.append(pltpu.make_async_copy(ref, place, sems.at[number]))
    fetch = pltpu.make_async_copy(mod_in, all_mod, own_sem.at[0])
    for copy in [fetch] + copies:
        copy.start()
    cond = cond_ref[...]
    cond = jnp.concatenate([cond, cond, cond], axis=0)
    fetch.wait()
    tiles = ada.shape[0] // 36
    for t in range(tiles):
        rows = all_mod[:, t, :]
        high, middle = halves(rows)
        low = (rows - high.astype(f32) - middle.astype(f32)).astype(bf16)
        product = dot_at(cond, jnp.concatenate([high, middle, low], axis=0))
        ada[pl.ds(t, 36, stride=tiles), :] = product[:36]
        total_ref[t : t + 1, :] = jnp.sum(rows, axis=0, keepdims=True)
    last = pltpu.make_async_copy(ada, ada_out, own_sem.at[1])
    last.start()
    for copy in copies + [last]:
        copy.wait()


def results(pieces, cond, all_mod, ada_rows):
    flat, sources, shapes = [], [], []
    for target, arrays in enumerate(pieces):
        rows = 0
        for array in arrays:
            sources.append((target, None if len(arrays) == 1 else rows))
            flat.append(array)
            rows += array.shape[0]
        shapes.append(sds((rows,) + arrays[0].shape[1:], arrays[0].dtype))
    anywhere, vm = pl.BlockSpec(memory_space=pl.ANY), pl.BlockSpec(memory_space=pltpu.VMEM)
    dma = pltpu.SemaphoreType.DMA
    return pl.pallas_call(
        functools.partial(results_kernel, tuple(sources)),
        out_shape=tuple(shapes) + (sds((ada_rows, LANES)), sds((ada_rows // 36, LANES))),
        in_specs=[vm, anywhere] + [anywhere] * len(flat),
        out_specs=(anywhere,) * (len(shapes) + 1) + (vm,),
        scratch_shapes=[
            pltpu.VMEM(all_mod.shape, f32), pltpu.VMEM((ada_rows, LANES), f32), dma((len(flat),)), dma((2,)),
        ],
        compiler_params=pltpu.CompilerParams(vmem_limit_bytes=16 * 1024 * 1024),
        name="results",
    )(cond, all_mod, *flat)


def finish_fused(small, arrays, grads, grad_small):
    length, width = arrays[3].shape
    anywhere, vm = pl.BlockSpec(memory_space=pl.ANY), pl.BlockSpec(memory_space=pltpu.VMEM)
    rows = (length, width)
    dma = pltpu.SemaphoreType.DMA
    own = sds((64, LANES))
    return pl.pallas_call(
        finish_kernel,
        out_shape=(sds(rows), gathered_shape(own)) + (sds((36 * width // LANES, LANES)),) * 3
        + (sds((4 * width // LANES, LANES)), sds(grad_small.shape[1:])),
        in_specs=[vm] * len(small) + [anywhere] * (len(arrays) + len(grads) + 1),
        out_specs=(vm, anywhere) + (vm,) * 5,
        scratch_shapes=[
            pltpu.VMEM((2, GROUPS, 32, width), bf16), pltpu.VMEM((GROUPS, 16, width), bf16), pltpu.VMEM((3,) + rows, bf16),
            pltpu.VMEM((width, width), bf16), pltpu.VMEM(rows, bf16), pltpu.VMEM(rows, f32), pltpu.VMEM(rows, f32),
            pltpu.VMEM(rows, f32), pltpu.VMEM((8, width), f32), pltpu.VMEM(own.shape, f32),
            pltpu.VMEM((2, 8, width), f32), dma((8,)),
        ] + scatter_scratch(grads) + scatter_scratch([grad_small]) + short_gather_sems(),
        compiler_params=pltpu.CompilerParams(
            collective_id=4, has_side_effects=True, vmem_limit_bytes=VMEM_LIMIT
        ),
        name="finish",
    )(*small, *arrays, *grads, six(grad_small))


def joined_states(messages, totals, width, head_width):
    count = lax.axis_size("seq")
    place = lax.axis_index("seq")

    def grid_rows(message):
        rows = message[width:].reshape(width // LANES, GRID, LANES)
        return rows.transpose(1, 0, 2).reshape(GRID, width)

    if count == 1:
        return jnp.zeros_like(messages[:, :width]), jnp.zeros((2, GRID, width), bf16)
    if count == 2:
        got = lax.ppermute(messages[0], "seq", [(0, 1), (1, 0)])
        rows = grid_rows(got)
        return got[None, :width], jnp.stack([jnp.where(place == 1, rows, 0), jnp.where(place == 0, rows, 0)])
    forward = [(i, i + 1) for i in range(count - 1)]
    backward = [(i + 1, i) for i in range(count - 1)]
    rims = jnp.stack([
        grid_rows(lax.ppermute(messages[0], "seq", forward)), grid_rows(lax.ppermute(messages[1], "seq", backward))
    ])
    states = lax.all_gather(messages[:, :width, :], "seq").astype(f32)
    passed = lax.all_gather(totals, "seq")
    heads_of_rows = np.arange(width) // head_width
    order = jnp.arange(count)
    ahead = jnp.zeros(states.shape[2:], f32)
    behind = jnp.zeros(states.shape[2:], f32)
    for source in range(count):
        between_up = jnp.where((order > source) & (order < place), 1.0, 0.0) @ passed
        between_down = jnp.where((order < source) & (order > place), 1.0, 0.0) @ passed
        ahead = ahead + jnp.where(source < place, jnp.exp(between_up), 0.0)[heads_of_rows, None] * states[source, 0]
        behind = behind + jnp.where(source > place, jnp.exp(between_down), 0.0)[heads_of_rows, None] * states[source, 1]
    return jnp.stack([ahead, behind]).astype(bf16), rims


def split_rows(matrix):
    grouped = matrix.reshape(GROUPS, -1, matrix.shape[1])
    return grouped[:, :32], grouped[:, 32:]


def pack_whole(parts, width):
    query, key, value, out, up, down = parts
    square = [piece.reshape(GROUPS, -1, width) for piece in (query, key, value, out)]
    up = up.reshape(GROUPS, square[0].shape[1], -1, width)
    columns = [up[:, :, j] for j in range(up.shape[2])]
    blocks = []
    for group in (square, columns):
        blocks.append(
            jnp.concatenate([piece[:, :32] for piece in group] + [piece[:, 32:] for piece in group], axis=1)
        )
    return blocks + [down.reshape(GROUPS, -1, width)]


def unpack_squares(block):
    return [
        jnp.concatenate([block[..., 32 * j : 32 * j + 32, :], block[..., 128 + 4 * j : 132 + 4 * j, :]], axis=-2)
        for j in range(4)
    ]


def unpack_blocks(blocks):
    squares = unpack_squares(blocks[0])
    columns = unpack_squares(blocks[1])
    lead = blocks[0].shape[:-2]
    up = jnp.stack(columns, axis=-2)
    return [piece.reshape(lead + (-1,)) for piece in squares] + [up.reshape(lead + (-1,)), blocks[2].reshape(lead + (-1,))]


def on_device(
    activations, conditioning, cotangent, w_ada, b_ada, w_query, w_key, w_value, w_forget, b_forget, conv_taps, w_out,
    w_up, w_down,
):
    _, length, width = activations.shape
    heads = b_forget.shape[0]
    head_width = width // heads
    data_count, seq_count = lax.axis_size("dp"), lax.axis_size("seq")
    devices = data_count * seq_count
    me = lax.axis_index("dp") * seq_count + lax.axis_index("seq")
    packed_here = (data_count, seq_count) == (16, 2)
    everywhere = ("dp", "seq")

    mod_width = 6 * width
    share = w_ada.shape[0]
    if share % mod_width == 0:
        ada_rows = share // mod_width
        first_row, inset = me * ada_rows, None
        ada_part = w_ada.reshape(ada_rows, mod_width)
    else:
        ada_rows = -(-share // mod_width) + 1
        first_row = (me * share) // mod_width
        inset = me * share - first_row * mod_width
        ada_part = lax.dynamic_update_slice(jnp.zeros((ada_rows * mod_width,), bf16), w_ada, (inset,))
        ada_part = ada_part.reshape(ada_rows, mod_width)

    def own_columns(cond_all):
        cond_act = jax.nn.silu(cond_all.astype(f32)).astype(bf16)
        cond_wide = jnp.pad(cond_act, ((0, 0), (0, ada_rows)))
        return lax.dynamic_slice_in_dim(cond_wide, first_row, ada_rows, axis=1)

    main_rows = 32 * GROUPS
    forget_b = jnp.pad(b_forget.astype(f32), (0, LANES - heads)).reshape(1, LANES)
    x = activations[0]
    cot = cotangent[0]
    rows = (length, width)

    def main_spec(block, columns=width):
        return pl.BlockSpec((GROUPS, 32, columns), block)

    def left_spec(block, columns=width):
        return pl.BlockSpec((GROUPS, 16, columns), block)

    def whole(shape):
        return pl.BlockSpec(shape, lambda *_: (0,) * len(shape))

    ways = 1 if seq_count == 2 else 2
    message_rows = width + width // LANES * GRID
    state_call = call(
        functools.partial(state_kernel, head_width, ways), sds((ways, message_rows, LANES), bf16), "states"
    )
    place = lax.axis_index("seq")

    def edges(values):
        low, high = values[:GRID], values[-GRID:]
        if ways == 1:
            return jnp.where(place == 0, high, low)[None]
        return jnp.stack([high, low])

    shards = (w_query, w_key, w_value, w_out, w_up, w_down)
    if packed_here:
        small = small_rows(conditioning[0], w_forget, conv_taps, me)
        bias = lax.dynamic_update_slice(jnp.zeros((mod_width,), bf16), b_ada, (me * b_ada.shape[0],)).reshape(-1, LANES)
        (small, attention_w, up_w), bulk, kept = forward_fused(
            x, w_ada.reshape(-1, LANES), bias, forget_b, small, [piece.reshape(-1, LANES) for piece in shards[:5]], heads, conv_taps.shape[0]
        )
        xp, qkv, mix, mixed_p, branch, middle, hidden_two_p, perm = bulk
        mod, forget_p, taps, gate_pre, run, runt, states, value_rims, given, taken, cond_mine = kept
        output, ghp_two, gup_main, gup_left, ggate_two, g_down = feed_fused(
            hidden_two_p, cot, mod, w_down.reshape(-1, LANES), up_w, middle
        )
    else:
        lanes_at = np.arange(width)
        per_group = width // GROUPS
        order = np.where(
            lanes_at < main_rows,
            lanes_at // 32 * per_group + lanes_at % 32,
            (lanes_at - main_rows) // 4 * per_group + 32 + (lanes_at - main_rows) % 4,
        )
        perm = (jnp.arange(width, dtype=jnp.int32)[:, None] == jnp.asarray(order, jnp.int32)[None, :]).astype(bf16)
        small = [w_forget, conv_taps, b_ada]
        sizes = np.cumsum([0] + [piece.shape[0] for piece in small])
        small = lax.all_gather(jnp.concatenate(small), everywhere)
        forget_w = small[:, : sizes[1]].reshape(width, heads)
        taps = small[:, sizes[1] : sizes[2]].reshape(10, width).astype(f32)
        taps = jnp.pad(taps, ((0, 6), (0, 0)))
        ada_bias = small[:, sizes[2] :].reshape(6, width).astype(f32)
        forget_main, forget_left = split_rows(forget_w)
        forget_p = jnp.concatenate([forget_main.reshape(-1, heads), forget_left.reshape(-1, heads)])
        forget_p = jnp.pad(forget_p, ((0, 0), (0, LANES - heads)))
        cond_part = own_columns(lax.all_gather(conditioning, "dp", axis=0, tiled=True))
        partial_mod = jnp.dot(cond_part, ada_part, preferred_element_type=f32)
        mod = lax.psum(lax.psum_scatter(partial_mod, "dp", scatter_dimension=0, tiled=True), "seq")
        mod = jnp.pad(mod.reshape(6, width) + ada_bias, ((0, 2), (0, 0)))
        blocks = pack_whole([lax.all_gather(s, everywhere, axis=0, tiled=True) for s in shards], width)
        attention_w, up_w, down_w = blocks
        down_w = down_w.reshape(-1, width)
        xp, gate_pre, run, runt = call(
            first_part,
            (sds(rows, bf16), sds((length, LANES)), sds((2, length, LANES)), sds((2, LANES, length))),
            "first_norm",
            scratch_shapes=[pltpu.VMEM(rows, bf16)],
        )(x, mod, perm, forget_p, forget_b)
        qkv = call(
            project_kernel,
            sds((3,) + rows, bf16),
            "project",
            grid=(3,),
            in_specs=[whole(rows), main_spec(lambda j: (0, j, 0)), left_spec(lambda j: (0, 8, 0))],
            out_specs=pl.BlockSpec((1,) + rows, lambda j: (j, 0, 0)),
        )(xp, attention_w, attention_w)
        total = run[0, -1]
        given = jnp.stack([jnp.exp(total - run[0]), jnp.exp(run[1])])
        taken = jnp.stack([jnp.exp(run[0]), jnp.exp(total - run[1])])
        if ways == 1:
            given = jnp.where(place == 0, given[0], given[1])[None]
            taken = jnp.where(place == 0, taken[1], taken[0])[None]
        messages = state_call(qkv[1], qkv[2], given, edges(qkv[2]))
        states, value_rims = joined_states(messages, total, width, head_width)
        mix_local = call(
            functools.partial(mix_kernel, head_width, heads), sds(rows), "mix"
        )(qkv, run, runt)
        mix, mixed_p, branch, middle, hidden_two_p = call(
            functools.partial(after_kernel, head_width, ways),
            (sds(rows), sds(rows, bf16), sds(rows, bf16), sds(rows), sds(rows, bf16)),
            "after",
            grid=(1,),
            in_specs=[
                whole(rows), whole((8, width)), whole((width, width)), whole((3,) + rows), whole(rows),
                whole((ways, length, LANES)), whole((ways, width, LANES)), whole((2, GRID, width)), whole((16, width)),
                main_spec(lambda i: (0, 3, 0)), left_spec(lambda i: (0, 8, 0)),
            ],
            out_specs=[whole(rows)] * 5,
            scratch_shapes=[pltpu.VMEM((length + 2 * GRID, width), bf16), pltpu.VMEM(rows, bf16)],
        )(x, mod, perm, qkv, mix_local, taken, states, value_rims, taps, attention_w, attention_w)
        output, ghp_two, gup_main, gup_left, gdown, ggate_two = call(
            feed_kernel,
            (
                sds(rows, bf16), sds(rows), sds((GROUPS, 128, width), bf16), sds((GROUPS, 16, width), bf16),
                sds(down_w.shape, bf16), sds((1, width)),
            ),
            "feed",
            grid=(4,),
            in_specs=[
                whole(rows), whole(rows), whole((8, width)), whole(rows), main_spec(lambda j: (0, j, 0)),
                left_spec(lambda j: (0, 8, 0)), pl.BlockSpec((width, width), lambda j: (j, 0)),
            ],
            out_specs=[
                whole(rows), whole(rows), main_spec(lambda j: (0, j, 0)), left_spec(lambda j: (0, 0, 0)),
                pl.BlockSpec((width, width), lambda j: (j, 0)), whole((1, width)),
            ],
            scratch_shapes=[
                pltpu.VMEM(rows, f32), pltpu.VMEM(rows, bf16), pltpu.VMEM((width, length), bf16), pltpu.VMEM(rows, bf16),
                pltpu.VMEM((width, length), bf16), pltpu.VMEM(rows, bf16), pltpu.VMEM((width - main_rows, width), bf16),
            ],
        )(hidden_two_p, cot, mod, middle, up_w, up_w, down_w)

    share_forget, share_taps, share_bias = w_forget.shape[0], conv_taps.shape[0], b_ada.shape[0]

    if packed_here:
        grad_middle, gqkv, gmain, _, grad_small, gleft, grad_gate, sums_two, g_up, g_out = backward_fused(
            heads,
            share_taps,
            (mod, run, runt, taken, given, gate_pre, states, value_rims, taps),
            (ghp_two, perm, middle, cot, branch, mixed_p, mix, attention_w, six(up_w), qkv, xp),
            (gup_main, gup_left),
        )
        grad_input, mod_all, g_query, g_key, g_value, out_left, grad_small = finish_fused(
            (mod, sums_two, ggate_two, grad_gate, forget_p), (attention_w, gqkv, perm, x, grad_middle),
            (gmain, six(gleft)), grad_small,
        )
        g_forget = grad_small[:36, :heads].reshape(-1)
        g_taps = lax.dynamic_slice(grad_small[36:40].reshape(-1), (lax.rem(me * share_taps, LANES),), (share_taps,))
        grad_bias = grad_small[40, :heads]
        *shares, grad_ada, mod_sum = results(
            [[output], [grad_input], [g_query], [g_key], [g_value], [g_out, out_left], [g_up], [g_down]], cond_mine,
            mod_all.reshape(devices, 64, LANES), share // LANES,
        )
        output, grad_input, *shares = shares
        shares = [piece.reshape(-1) for piece in shares]
        grad_ada, mod_sum = grad_ada.reshape(-1), mod_sum.reshape(-1)
    else:
        grad_middle, grad_mixed, grad_mix, gout_main, gout_left, sums_two = call(
            functools.partial(second_kernel, head_width),
            (
                sds(rows), sds(rows, bf16), sds(rows, bf16), sds((GROUPS, 32, width), bf16),
                sds((GROUPS, 16, width), bf16), sds((8, width)),
            ),
            "second_norm",
            grid=(1,),
            in_specs=[
                whole(rows), whole((width, width)), whole(rows), whole((8, width)), whole(rows), whole(rows), whole(rows),
                whole(rows), main_spec(lambda i: (0, 3, 0)), left_spec(lambda i: (0, 8, 0)),
            ],
            out_specs=[
                whole(rows), whole(rows), whole(rows), whole((GROUPS, 32, width)), whole((GROUPS, 16, width)),
                whole((8, width)),
            ],
            scratch_shapes=[
                pltpu.VMEM(rows, f32), pltpu.VMEM(rows, bf16), pltpu.VMEM((3, 8, width), f32),
            ],
        )(ghp_two, perm, middle, mod, cot, branch, mixed_p, mix, attention_w, attention_w)

        back = state_call(qkv[0], grad_mix, taken, edges(grad_mixed))
        if ways == 2:
            back = jnp.stack([
                jnp.concatenate([back[1, :width], back[0, width:]]), jnp.concatenate([back[0, :width], back[1, width:]])
            ])
        leaving, grad_rims = joined_states(back, total, width, head_width)
        if ways == 2:
            leaving = leaving[::-1]

        gq_local, gk_local, gv_local, pair_rows, pair_cols = call(
            functools.partial(pairs_kernel, head_width, heads),
            (sds(rows), sds(rows), sds(rows), sds((2, length, LANES)), sds((2, heads, length))),
            "pairs",
            scratch_shapes=[pltpu.VMEM((2, length, length), bf16)],
        )(qkv, grad_mix, run, runt)
        if seq_count > 2:
            rows_through = jnp.sum(states.astype(f32) * leaving.astype(f32), axis=(0, 2))
            through = jnp.exp(total[:heads]) * jnp.sum(rows_through.reshape(heads, head_width), axis=1)
            through = jnp.pad(through, (0, LANES - heads)).reshape(1, LANES)
        else:
            through = jnp.zeros((1, LANES), f32)
        early = jnp.where(place == 0, jnp.ones((1, LANES), f32), 0.0)

        pad_scratch = pltpu.VMEM((length + 2 * GRID, width), bf16)
        gqkv, grad_gate, grad_conv, grad_bias = call(
            functools.partial(carry_kernel, head_width, ways),
            (sds((3,) + rows, bf16), sds((length, LANES), bf16), sds((16, width)), sds((1, LANES))),
            "carry",
            scratch_shapes=[pad_scratch, pad_scratch],
        )(
            qkv, grad_mix, gq_local, gk_local, gv_local, pair_rows, pair_cols, taken, given, gate_pre, states, leaving,
            through, early, grad_mixed, grad_rims, value_rims, taps,
        )
        gmain, gleft, gforget, ghp_one = call(
            weights_kernel,
            (sds((GROUPS, 96, width), bf16), sds((GROUPS, 16, width), bf16), sds((width, LANES)), sds(rows)),
            "weights",
            grid=(3,),
            in_specs=[
                whole(rows), pl.BlockSpec((1,) + rows, lambda j: (j, 0, 0)), whole((length, LANES)),
                whole((width, LANES)), main_spec(lambda j: (0, j, 0)), left_spec(lambda j: (0, 8, 0)),
                left_spec(lambda j: (0, 0, 0)),
            ],
            out_specs=[
                main_spec(lambda j: (0, j, 0)), left_spec(lambda j: (0, 0, 0)), whole((width, LANES)), whole(rows),
            ],
            scratch_shapes=[pltpu.VMEM((width, length), bf16)],
        )(xp, gqkv, grad_gate, forget_p, attention_w, attention_w, gout_left)
        grad_input, sums_one = call(
            last_part, (sds(rows), sds((8, width))), "last_norm",
            scratch_shapes=[pltpu.VMEM(rows, f32), pltpu.VMEM((2, 8, width), f32)],
        )(ghp_one, perm, x, mod, grad_middle)

        gforget = gforget[:, :heads]
        gforget = jnp.concatenate(
            [gforget[:main_rows].reshape(GROUPS, 32, heads), gforget[main_rows:].reshape(GROUPS, 4, heads)], axis=1
        )
        grad_small = jnp.concatenate([gforget.reshape(devices, -1), grad_conv[:10].reshape(devices, -1)], axis=1)
        grad_small = lax.psum_scatter(grad_small, everywhere, scatter_dimension=0, tiled=True).reshape(-1)
        g_forget, g_taps = grad_small[:share_forget], grad_small[share_forget:]
        grad_bias = lax.psum(grad_bias[0, :heads], everywhere)
        grads = [
            jnp.concatenate([gmain, gout_main, gleft], axis=1), jnp.concatenate([gup_main, gup_left], axis=1),
            gdown.reshape(GROUPS, -1, width),
        ]
        shares = [
            lax.psum_scatter(g.reshape(-1), everywhere, scatter_dimension=0, tiled=True).astype(f32)
            for g in unpack_blocks(grads)
        ]
        grad_mod = jnp.concatenate([sums_one[:2], sums_two[2:3], sums_two[:2], ggate_two])
        mod_all = lax.all_gather(grad_mod.reshape(1, mod_width), everywhere, axis=0, tiled=True)

        mod_all = jnp.sum(mod_all.reshape(data_count, seq_count, mod_width), axis=1)
        mod_sum = jnp.sum(mod_all, axis=0)
        grad_ada = jnp.dot(cond_part.astype(f32).T, mod_all, precision=lax.Precision.HIGHEST).reshape(-1)
        if inset is not None:
            grad_ada = lax.dynamic_slice(grad_ada, (inset,), (share,))
    grad_ada_bias = lax.dynamic_slice(mod_sum, (me * share_bias,), (share_bias,))
    g_query, g_key, g_value, g_out, g_up, g_down = shares
    return (
        output[None], grad_input[None], grad_ada, grad_ada_bias, g_query, g_key, g_value, g_forget,
        grad_bias, g_taps, g_out, g_up, g_down,
    )


def solution(mesh):
    rows = P("dp", "seq", None)
    shard = P(("dp", "seq"))
    return jax.shard_map(
        on_device,
        mesh=mesh,
        in_specs=(
            rows, P("dp", None), rows, shard, shard, shard, shard, shard, shard, P(), shard, shard, shard, shard,
        ),
        out_specs=(
            rows, rows, shard, shard, shard, shard, shard, shard, P(), shard, shard, shard, shard,
        ),
        check_vma=False,
    )
```

```python
import functools

import jax
import jax.numpy as jnp
import numpy as np
from jax import lax
from jax.experimental import pallas as pl
from jax.experimental.pallas import tpu as pltpu
from jax.sharding import PartitionSpec as P

GRID = 32
LANES = 128
GROUPS = 32
epsilon = 1e-06
f32 = jnp.float32
bf16 = jnp.bfloat16
VMEM_LIMIT = 56 * 1024 * 1024
FORWARD_PLAN = (
    ("f", 0, 0, 0), ("g", 0, 0, 0), -1, ("g", 0, 1, 0), ("f", 1, 0, 0), ("g", 2, 0, 0), ("g", 1, 0, 0),
    ("g", 3, 0, 0), ("g", 0, 0, 1), ("f", 2, 0, 0), ("g", 1, 1, 0), ("g", 2, 1, 0), -1, ("g", 0, 0, 2),
    ("g", 4, 0, 0), ("g", 5, 0, 0), ("g", 2, 0, 1), ("g", 1, 0, 1), -1, ("s", 0, 0, 0), ("g", 2, 0, 2),
    ("g", 1, 0, 2), ("g", 0, 0, 3), ("g", 4, 0, 1), ("g", 5, 0, 1), ("g", 3, 1, 0), ("s", 1, 0, 0), ("g", 0, 1, 1),
    ("g", 1, 0, 3), ("g", 2, 0, 3), ("g", 4, 0, 2), ("g", 5, 0, 2), ("s", 2, 0, 0), -1, ("g", 2, 1, 1),
    ("g", 1, 1, 1), ("g", 4, 1, 0), ("g", 5, 1, 0), ("g", 4, 0, 3), ("g", 5, 0, 3), ("g", 0, 1, 2), ("g", 4, 1, 1),
    ("g", 5, 1, 1), ("g", 1, 1, 2), -1, ("g", 2, 1, 2), -1, ("g", 0, 1, 3), -1, -1, ("g", 4, 1, 2), ("g", 5, 1, 2),
    ("g", 2, 1, 3), -1, -1, ("g", 1, 1, 3), -1, ("g", 4, 1, 3), -1, -1, ("g", 5, 1, 3), -1, -1, -1,
)
FEED_PLAN = (
    ("g", 0, 0, 0), -1, -1, ("g", 2, 0, 0), ("g", 1, 0, 0), ("g", 3, 0, 0), ("g", 0, 0, 1), -1, -1, ("g", 0, 0, 2),
    ("g", 4, 0, 0), ("g", 5, 0, 0), ("d", 0, 0, 0), ("g", 2, 0, 1), ("d", 4, 0, 0), -1, ("g", 1, 0, 1),
    ("g", 2, 0, 2), -1, ("g", 0, 0, 3), ("g", 1, 0, 2), ("d", 1, 0, 0), ("d", 2, 0, 0), ("d", 0, 0, 1),
    ("g", 4, 0, 1), -1, -1, ("g", 5, 0, 1), ("g", 2, 0, 3), ("d", 4, 0, 1), ("d", 0, 0, 2), -1, ("g", 1, 0, 3),
    ("g", 4, 0, 2), ("g", 5, 0, 2), -1, ("d", 3, 0, 0), -1, ("d", 4, 0, 2), ("d", 0, 0, 3), ("d", 2, 0, 1),
    ("d", 1, 0, 1), -1, -1, ("g", 4, 0, 3), -1, ("d", 1, 0, 2), ("d", 2, 0, 2), -1, ("g", 5, 0, 3), ("d", 2, 0, 3),
    -1, -1, ("d", 4, 0, 3), ("d", 1, 0, 3), -1, ("d", 3, 0, 1), ("d", 5, 0, 0), -1, -1, -1, -1, ("d", 3, 0, 2), -1,
    -1, -1, -1, ("d", 3, 0, 3), ("d", 5, 0, 1),
)
BACKWARD_PLAN = (
    -1, ("u", 0, 0, 0), -1, -1, ("u", 0, 0, 1), -1, ("u", 1, 0, 0), -1, -1, ("u", 0, 0, 2), ("u", 3, 0, 0),
    ("u", 1, 0, 1), -1, -1, ("u", 3, 0, 1), -1, ("u", 0, 0, 3), -1, ("u", 1, 0, 2), -1, -1, -1, ("u", 3, 0, 2), -1,
    ("u", 1, 0, 3), -1, -1, ("u", 3, 0, 3),
)
FINISH_PLAN = (
    -1, ("a", 0, 0, 0), ("a", 4, 0, 0), -1, -1, ("a", 0, 0, 1), -1, ("g", 0, 0, 0), ("a", 2, 0, 0), ("a", 1, 0, 0),
    ("s", 0, 0, 0), ("s", 0, 0, 1), ("s", 0, 0, 2), ("a", 4, 0, 1), ("s", 0, 0, 3), ("g", 1, 0, 0), ("s", 1, 0, 0),
    ("s", 1, 0, 1), ("s", 2, 0, 0), ("s", 2, 0, 1), ("s", 1, 0, 2), ("s", 2, 0, 2), ("s", 2, 0, 3), ("s", 1, 0, 3),
    ("a", 3, 0, 0), ("a", 2, 0, 1), ("a", 1, 0, 1), ("s", 3, 0, 0), ("g", 2, 0, 0), ("a", 0, 0, 2), ("a", 4, 0, 2),
    ("s", 3, 0, 1), ("a", 0, 0, 3), ("a", 3, 0, 1), ("a", 1, 0, 2), ("s", 3, 0, 2), ("a", 2, 0, 2), ("a", 4, 0, 3),
    ("a", 2, 0, 3), ("a", 1, 0, 3), ("s", 3, 0, 3), ("a", 3, 0, 2), ("a", 5, 0, 0), ("a", 3, 0, 3), ("a", 5, 0, 1),
)
FEED_WAYS, BACKWARD_WAYS = (3, 3), 1


def dot(a, b):
    return jnp.dot(a, b, preferred_element_type=f32)


def dot_bt(a, b):
    return lax.dot_general(a, b, (((1,), (1,)), ((), ())), preferred_element_type=f32)


def dot_at(a, b):
    return lax.dot_general(a, b, (((0,), (0,)), ((), ())), preferred_element_type=f32)


def halves(a):
    high = a.astype(bf16)
    return high, (a - high.astype(f32)).astype(bf16)


def spans(width, size=512):
    return [slice(start, min(start + size, width)) for start in range(0, width, size)]


def head_lanes(rows, width, start, head_width):
    head = lax.broadcasted_iota(jnp.int32, (rows, width), 0)
    lane = lax.broadcasted_iota(jnp.int32, (rows, width), 1) + start
    return (lane >= head * head_width) & (lane < (head + 1) * head_width)


def pick_left(rows, slot):
    out = lax.broadcasted_iota(jnp.int32, (4 * GROUPS, 16 * GROUPS), 0)
    src = lax.broadcasted_iota(jnp.int32, (4 * GROUPS, 16 * GROUPS), 1)
    return (src == (out // 4) * 16 + slot * 4 + out % 4).astype(bf16)


def norm_parts(values):
    center = jnp.mean(values, axis=-1, keepdims=True)
    centered = values - center
    spread = jnp.mean(centered * centered, axis=-1, keepdims=True)
    rstd = lax.rsqrt(spread + epsilon)
    return centered * rstd, rstd


def row_loop(length, body):
    size = min(length, 64)

    @pl.loop(0, length // size)
    def _(r):
        body(pl.ds(pl.multiple_of(r * size, size), size))


def eight_rows(values):
    return jnp.sum(values.reshape(-1, 8, values.shape[1]), axis=0)


def call(kernel, out_shape, name, **kw):
    return pl.pallas_call(
        kernel,
        out_shape=out_shape,
        name=name,
        compiler_params=pltpu.CompilerParams(vmem_limit_bytes=VMEM_LIMIT),
        **kw,
    )


def sds(shape, dtype=f32):
    return jax.ShapeDtypeStruct(shape, dtype)


def first_part(x_ref, mod_ref, perm_ref, wf_ref, bf_ref, xp_ref, gate_ref, run_ref, runt_ref, hidden_ref):
    length = x_ref.shape[0]

    def norm(rows):
        normed, _ = norm_parts(x_ref[rows, :].astype(f32))
        hidden_ref[rows, :] = (normed * (1.0 + mod_ref[1:2, :]) + mod_ref[0:1, :]).astype(bf16)

    row_loop(length, norm)
    for cols in spans(x_ref.shape[1]):
        xp_ref[:, cols] = dot(hidden_ref[...], perm_ref[:, cols]).astype(bf16)

    gate = dot(xp_ref[...], wf_ref[...]) + bf_ref[...]
    gate_ref[...] = gate
    decay = -(jnp.maximum(gate, 0.0) + jnp.log1p(jnp.exp(-jnp.abs(gate))))
    row = lax.broadcasted_iota(jnp.int32, (length, length), 0)
    col = lax.broadcasted_iota(jnp.int32, (length, length), 1)
    tri = (row >= col).astype(bf16)
    high, rest = halves(decay)
    rest32 = decay - high.astype(f32)
    low = (rest32 - rest.astype(f32)).astype(bf16)
    inclusive = dot(tri, high) + dot(tri, rest) + dot(tri, low)
    exclusive = inclusive - decay
    run_ref[0] = inclusive
    run_ref[1] = exclusive
    runt_ref[0] = inclusive.T
    runt_ref[1] = exclusive.T


def project_part(slot, xp_ref, main_ref, left_ref, write):
    pick = pick_left(None, slot)
    main_rows = rows_in(main_ref)

    for cols in spans(xp_ref.shape[1]):
        main = main_ref[..., cols].reshape(main_rows, -1)
        left = dot(pick, left_ref[..., cols].reshape(16 * GROUPS, -1)).astype(bf16)
        write(cols, dot(xp_ref[:, :main_rows], main) + dot(xp_ref[:, main_rows:], left))


def two_terms(scale):
    return jnp.concatenate(halves(scale), axis=1)


def spread_heads(terms, cols, head_width):
    spread = head_lanes(LANES, cols.stop - cols.start, cols.start, head_width).astype(bf16)
    return dot(terms, jnp.concatenate([spread, spread], axis=0))


def head_sums(values, cols, head_width):
    return dot_bt(values, head_lanes(LANES, cols.stop - cols.start, cols.start, head_width).astype(bf16))


def own_block(shape, row_start, lane_start, head_width):
    row = lax.broadcasted_iota(jnp.int32, (shape[0], 1), 0) + row_start
    lane = lax.broadcasted_iota(jnp.int32, (1, shape[1]), 1) + lane_start
    same = None
    for head in range(
        max(row_start, lane_start) // head_width,
        min(row_start + shape[0] - 1, lane_start + shape[1] - 1) // head_width + 1,
    ):
        low, high = head * head_width, (head + 1) * head_width
        both = ((row >= low) & (row < high)) & ((lane >= low) & (lane < high))
        same = both if same is None else same | both
    if same is None:
        return jnp.broadcast_to(row < 0, shape)
    return same


def group_rows(ref, cols):
    per = rows_in(ref) // ref.shape[0]
    return ref[cols.start // per : cols.stop // per].reshape(-1, ref.shape[-1])


def rows_in(ref):
    return int(np.prod(ref.shape[:-1]))


def near_lanes(cols, width, head_width):
    low = cols.start // head_width * head_width // LANES * LANES
    last = (cols.stop - 1) // head_width
    return slice(low, min(width, -(-(last + 1) * head_width // LANES) * LANES))


def unfolded(ref, way, near, cols, head_width):
    folded = ref[way, near, :]
    return jnp.concatenate([
        jnp.where(own_block(folded.shape, near.start, at, head_width), folded, 0)
        for at in range(cols.start, cols.stop, LANES)
    ], axis=1)


def state_part(head_width, ways, left, right_ref, scale_ref, out_ref):
    width = right_ref.shape[1]
    terms = [two_terms(scale_ref[way]) for way in range(ways)]
    for cols in spans(width, 2 * LANES):
        near = near_lanes(cols, width, head_width)
        mask = own_block((cols.stop - cols.start, near.stop - near.start), cols.start, near.start, head_width)
        for way in range(ways):
            scaled = left(cols).astype(f32) * spread_heads(terms[way], cols, head_width)
            product = jnp.where(mask, dot_at(scaled.astype(bf16), right_ref[:, near]), 0.0)
            total = product[:, :LANES]
            for at in range(LANES, near.stop - near.start, LANES):
                total = total + product[:, at : at + LANES]
            out_ref[way, cols, :] = total.astype(bf16)


def edge_part(source, out):
    for t in range(source.shape[1] // LANES):
        out(t, source[:, t * LANES : (t + 1) * LANES])


def pair_weights(run_ref, runt_ref, head, rows, length):
    count = rows.size
    own = lax.broadcasted_iota(jnp.int32, (count, LANES), 1) == head
    inc_t = jnp.sum(jnp.where(own, run_ref[0, rows, :], 0.0), axis=1, keepdims=True)
    exc_t = jnp.sum(jnp.where(own, run_ref[1, rows, :], 0.0), axis=1, keepdims=True)
    inc_s = runt_ref[0, pl.ds(head, 1), :]
    exc_s = runt_ref[1, pl.ds(head, 1), :]
    weight = jnp.exp(jnp.minimum(inc_t - inc_s, exc_s - exc_t))
    row = lax.broadcasted_iota(jnp.int32, (count, length), 0) + rows.start
    col = lax.broadcasted_iota(jnp.int32, (count, length), 1)
    return jnp.where(row == col, 2.0, weight)


def window_of(head, heads, head_width):
    start = pl.multiple_of(((head * head_width) // LANES - head // (heads - 1)) * LANES, LANES)
    return pl.ds(start, 2 * LANES), start


def own_lanes(rows, start, head, head_width):
    lane = lax.broadcasted_iota(jnp.int32, (rows, 2 * LANES), 1) + start
    return (lane >= head * head_width) & (lane < (head + 1) * head_width)


def row_blocks(length, size):
    size = min(length, size)
    return [pl.ds(start, size) for start in range(0, length, size)]


def mix_part(head_width, heads, low, high, qkv_ref, run_ref, runt_ref, mix_ref):
    length, width = mix_ref.shape

    @pl.loop(low // 2, high // 2)
    def _(pair):
        for odd in range(2):
            head = pair * 2 + odd
            win, start = window_of(head, heads, head_width)
            mask = own_lanes(length, start, head, head_width)
            keys = jnp.where(mask, qkv_ref[1, :, win], 0)
            vals = jnp.where(mask, qkv_ref[2, :, win], 0)
            for rows in row_blocks(length, 2 * LANES):
                weight = pair_weights(run_ref, runt_ref, head, rows, length)
                score = dot_bt(qkv_ref[0, rows, win], keys)
                mix_ref[rows, win] += dot((score * weight).astype(bf16), vals)


def fill_padded(pad_ref, rims_ref, middle):
    length = pad_ref.shape[0] - 2 * GRID
    pad_ref[:GRID, :] = rims_ref[0]
    pad_ref[GRID : GRID + length, :] = middle
    pad_ref[GRID + length :, :] = rims_ref[1]


def mixed_part(head_width, ways, qkv_ref, taken_ref, state_ref, taps_ref, vpad, mix_ref, mixed):
    length, width = mix_ref.shape
    place = lax.broadcasted_iota(jnp.int32, (length, LANES), 0) % GRID
    sums = jnp.zeros((length, LANES), f32)
    terms = [two_terms(taken_ref[way]) for way in range(ways)]
    for cols in spans(width, 2 * LANES):
        gained = mix_ref[:, cols]
        near = near_lanes(cols, width, head_width)
        for way in range(ways):
            block = unfolded(state_ref, way, near, cols, head_width)
            gained = gained + spread_heads(terms[way], cols, head_width) * dot(qkv_ref[0, :, near], block)
        mix_ref[:, cols] = gained
        sums = sums + head_sums((gained * gained).astype(bf16), cols, head_width)
    inverse = two_terms(lax.rsqrt(sums * (1.0 / head_width) + epsilon))
    for span in spans(width, 2 * LANES):
        normed = mix_ref[:, span] * spread_heads(inverse, span, head_width)
        for start in range(span.start, span.stop, LANES):
            cols = slice(start, start + LANES)
            conv = jnp.zeros((length, LANES), f32)
            for lateral in range(3):
                column = jnp.zeros((length, LANES), f32)
                for vertical in range(3):
                    tap = taps_ref[3 * vertical + lateral : 3 * vertical + lateral + 1, cols]
                    column = column + tap * vpad[vertical * GRID : vertical * GRID + length, cols].astype(f32)
                if lateral == 0:
                    column = jnp.where(place > 0, pltpu.roll(column, 1, 0), 0.0)
                if lateral == 2:
                    column = jnp.where(place < GRID - 1, pltpu.roll(column, length - 1, 0), 0.0)
                conv = conv + column
            own = normed[:, start - span.start : start - span.start + LANES]
            mixed[:, cols] = (own + (conv + taps_ref[9:10, cols])).astype(bf16)


def permute_part(source, perm_ref, out_ref):
    for cols in spans(perm_ref.shape[1]):
        out_ref[:, cols] = dot(source[...], perm_ref[:, cols]).astype(bf16)


def branch_part(x_ref, mod_ref, mixedp_ref, main_ref, left_ref, branch_ref, middle_ref):
    def write(cols, branch):
        branch_ref[:, cols] = branch.astype(bf16)
        middle_ref[:, cols] = x_ref[:, cols].astype(f32) + mod_ref[2:3, cols] * branch

    project_part(3, mixedp_ref, main_ref, left_ref, write)


def second_hidden(mod_ref, middle_ref, mixed):
    def norm(rows):
        normed, _ = norm_parts(middle_ref[rows, :])
        mixed[rows, :] = (normed * (1.0 + mod_ref[4:5, :]) + mod_ref[3:4, :]).astype(bf16)

    row_loop(mixed.shape[0], norm)


def project_kernel(xp_ref, main_ref, left_ref, out_ref):
    def write(cols, value):
        out_ref[0, :, cols] = value.astype(bf16)

    project_part(pl.program_id(0), xp_ref, main_ref, left_ref, write)


def state_kernel(head_width, ways, left_ref, right_ref, scale_ref, edge_ref, out_ref):
    width = right_ref.shape[1]
    state_part(head_width, ways, lambda cols: left_ref[:, cols], right_ref, scale_ref, out_ref)
    for way in range(ways):

        def write(t, value, way=way):
            out_ref[way, width + t * GRID : width + (t + 1) * GRID, :] = value

        edge_part(edge_ref[way], write)


def mix_kernel(head_width, heads, qkv_ref, run_ref, runt_ref, mix_ref):
    mix_ref[...] = jnp.zeros_like(mix_ref)
    mix_part(head_width, heads, 0, heads, qkv_ref, run_ref, runt_ref, mix_ref)


def after_kernel(
    head_width, ways, x_ref, mod_ref, perm_ref, qkv_ref, mix_in_ref, taken_ref, state_ref, rims_ref, taps_ref,
    main_ref, left_ref, mix_ref, mixedp_ref, branch_ref, middle_ref, h2p_ref, vpad, mixed,
):
    mix_ref[...] = mix_in_ref[...]
    fill_padded(vpad, rims_ref, qkv_ref[2])
    mixed_part(head_width, ways, qkv_ref, taken_ref, state_ref, taps_ref, vpad, mix_ref, mixed)
    permute_part(mixed, perm_ref, mixedp_ref)
    branch_part(x_ref, mod_ref, mixedp_ref, main_ref, left_ref, branch_ref, middle_ref)
    second_hidden(mod_ref, middle_ref, mixed)
    permute_part(mixed, perm_ref, h2p_ref)


def gelu_both(v):
    c = np.float32(np.sqrt(2.0 / np.pi))
    square = v * v
    th = jnp.tanh(c * (v + np.float32(0.044715) * (square * v)))
    half = 0.5 * (1.0 + th)
    slope = half + 0.5 * v * (1.0 - th * th) * (c * (1.0 + np.float32(3 * 0.044715) * square))
    return v * half, slope


def feed_kernel(
    h2p_ref, cot_ref, mod_ref, middle_ref, main_ref, left_ref, down_ref,
    out_ref, gh_ref, gup_ref, gleft_ref, gdown_ref, ggate_ref, down_acc, gdi, h2pt, act, actt, gup, left,
):
    j = pl.program_id(0)
    main_rows = main_ref.shape[0] * main_ref.shape[1]
    length, width = h2p_ref.shape

    @pl.when(j == 0)
    def _():
        gdi[...] = (cot_ref[...].astype(f32) * mod_ref[5:6, :]).astype(bf16)
        h2pt[...] = h2p_ref[...].T
        down_acc[...] = jnp.zeros_like(down_acc)
        gh_ref[...] = jnp.zeros_like(gh_ref)
        gleft_ref[...] = jnp.zeros_like(gleft_ref)

    pick = pick_left(None, j)
    left[...] = dot(pick, left_ref[...].reshape(16 * GROUPS, width)).astype(bf16)
    for cols in spans(width):
        main = main_ref[:, :, cols].reshape(main_rows, -1)
        up = dot(h2p_ref[:, :main_rows], main) + dot(h2p_ref[:, main_rows:], left[:, cols])
        value, slope = gelu_both(up)
        value = value.astype(bf16)
        act[:, cols] = value
        actt[cols, :] = value.T
        gup[:, cols] = (dot_bt(gdi[...], down_ref[cols, :]) * slope).astype(bf16)
    for cols in spans(width):
        down_acc[:, cols] += dot(act[...], down_ref[:, cols])
        gdown_ref[:, cols] = dot(actt[...], gdi[:, cols]).astype(bf16)
        gup_ref[:, :, cols] = dot(h2pt[:main_rows, :], gup[:, cols]).astype(bf16).reshape(GROUPS, 32, -1)
        part = dot(h2pt[main_rows:, :], gup[:, cols]).astype(bf16)
        gleft_ref[:, :, cols] += dot_at(pick, part).astype(bf16).reshape(GROUPS, 16, -1)
    gh_ref[:, main_rows:] += dot_bt(gup[...], left[...])
    for cols in spans(main_rows):
        gh_ref[:, cols] += dot_bt(gup[...], group_rows(main_ref, cols))

    @pl.when(j == pl.num_programs(0) - 1)
    def _():
        out_ref[...] = (middle_ref[...] + mod_ref[5:6, :] * down_acc[...]).astype(bf16)
        ggate_ref[...] = jnp.sum(cot_ref[...].astype(f32) * down_acc[...], axis=0, keepdims=True)


def unpermute(perm_ref, source_ref, out_ref):
    source = source_ref[...].astype(bf16)
    for cols in spans(perm_ref.shape[0]):
        out_ref[:, cols] = dot_bt(source, perm_ref[cols, :])


def norm_back(normed, rstd, factor, grad):
    scaled = grad * (1.0 + factor)
    mean = jnp.mean(scaled, axis=-1, keepdims=True)
    along = jnp.mean(scaled * normed, axis=-1, keepdims=True)
    return (scaled - mean - normed * along) * rstd


def second_part(
    head_width, ghp_ref, perm_ref, middle_ref, mod_ref, cot_ref, branch_ref, mixedp_ref, mix_ref, main_ref, left_ref,
    gmid_ref, gmixed_ref, gmix_ref, gout_ref, gleft_ref, sums_ref, gh, gb, partial,
):
    length, width = middle_ref.shape
    main_rows = rows_in(main_ref)
    unpermute(perm_ref, ghp_ref, gh)
    yield
    partial[...] = jnp.zeros_like(partial)

    def norm(rows):
        normed, rstd = norm_parts(middle_ref[rows, :])
        grad = gh[rows, :]
        partial[0] += eight_rows(grad)
        partial[1] += eight_rows(grad * normed)
        grad_middle = cot_ref[rows, :].astype(f32) + norm_back(normed, rstd, mod_ref[4:5, :], grad)
        gmid_ref[rows, :] = grad_middle
        partial[2] += eight_rows(grad_middle * branch_ref[rows, :].astype(f32))
        gb[rows, :] = (grad_middle * mod_ref[2:3, :]).astype(bf16)

    row_loop(length, norm)
    for k in range(3):
        sums_ref[k : k + 1, :] = jnp.sum(partial[k], axis=0, keepdims=True)
    sums_ref[3:8, :] = jnp.zeros((5, width), f32)
    pick = pick_left(None, 3)
    yield
    left = dot(pick, left_ref[...].reshape(16 * GROUPS, width)).astype(bf16)
    for cols in spans(width):
        gout = dot_at(mixedp_ref[:, :main_rows], gb[:, cols]).astype(bf16)
        gout_ref[..., cols] = gout.reshape(gout_ref.shape[:-1] + (-1,))
        part = dot_at(mixedp_ref[:, main_rows:], gb[:, cols]).astype(bf16)
        gleft_ref[..., cols] = dot_at(pick, part).astype(bf16).reshape(gleft_ref.shape[:-1] + (-1,))
    gh[:, main_rows:] = dot_bt(gb[...], left)
    for cols in spans(main_rows):
        gh[:, cols] = dot_bt(gb[...], group_rows(main_ref, cols))
    gb[...] = gh[...].astype(bf16)
    yield
    for cols in spans(width):
        gmixed_ref[:, cols] = dot_bt(gb[...], perm_ref[cols, :]).astype(bf16)

    sums = jnp.zeros((length, LANES), f32)
    dots = jnp.zeros((length, LANES), f32)
    for cols in spans(width, 2 * LANES):
        mix = mix_ref[:, cols]
        sums = sums + head_sums((mix * mix).astype(bf16), cols, head_width)
        for term in halves(mix * gmixed_ref[:, cols].astype(f32)):
            dots = dots + head_sums(term, cols, head_width)
    inverse = lax.rsqrt(sums * (1.0 / head_width) + epsilon)
    along = two_terms(dots * (1.0 / head_width) * inverse * inverse * inverse)
    inverse = two_terms(inverse)
    for cols in spans(width, 2 * LANES):
        gmix_ref[:, cols] = (
            gmixed_ref[:, cols].astype(f32) * spread_heads(inverse, cols, head_width)
            - mix_ref[:, cols] * spread_heads(along, cols, head_width)
        ).astype(bf16)
    yield


def second_kernel(head_width, *refs):
    for _ in second_part(head_width, *refs):
        pass


def pairs_part(head_width, heads, low, high, qkv_ref, gmix_ref, run_ref, runt_ref, gq_ref, gk_ref, gv_ref, rows_ref, cols_ref, held):
    length, width = gmix_ref.shape

    @pl.loop(low, high)
    def _(head):
        win, start = window_of(head, heads, head_width)
        mask = own_lanes(length, start, head, head_width)
        queries = jnp.where(mask, qkv_ref[0, :, win], 0)
        keys = jnp.where(mask, qkv_ref[1, :, win], 0)
        vals = jnp.where(mask, qkv_ref[2, :, win], 0)
        grads = jnp.where(mask, gmix_ref[:, win], 0)
        own = lax.broadcasted_iota(jnp.int32, (LANES, LANES), 1) == head
        row = lax.broadcasted_iota(jnp.int32, (LANES, LANES), 0)
        col = lax.broadcasted_iota(jnp.int32, (LANES, LANES), 1)
        columns = [None, None]
        for rows in row_blocks(length, 2 * LANES):
            weight = pair_weights(run_ref, runt_ref, head, rows, length)
            at = slice(rows.start, rows.start + rows.size)
            score = dot_bt(queries[at], keys) * weight
            grad = dot_bt(grads[at], vals)
            both = score * grad
            held[0, rows, :] = score.astype(bf16)
            held[1, rows, :] = (grad * weight).astype(bf16)
            for step in range(rows.size // LANES):
                first = rows.start + step * LANES
                strip = both[step * LANES : (step + 1) * LANES]
                middle = strip[:, first : first + LANES]
                pieces = [
                    (0, strip[:, :first], jnp.where(row > col, middle, 0.0)),
                    (1, strip[:, first + LANES :], jnp.where(row < col, middle, 0.0)),
                ]
                for way, part, corner in pieces:
                    total = jnp.sum(corner, axis=1, keepdims=True)
                    lines = [jnp.sum(corner, axis=0, keepdims=True)]
                    if first if way == 0 else length - first - LANES:
                        total = total + jnp.sum(part, axis=1, keepdims=True)
                        lines.insert(0 if way == 0 else 1, jnp.sum(part, axis=0, keepdims=True))
                    blank = jnp.zeros((1, length - sum(line.shape[1] for line in lines)), f32)
                    if blank.shape[1]:
                        lines.insert(len(lines) if way == 0 else 0, blank)
                    line = jnp.concatenate(lines, axis=1)
                    columns[way] = line if columns[way] is None else columns[way] + line
                    rows_ref[way, first : first + LANES, :] += jnp.where(own, total, 0.0)
        for way in range(2):
            cols_ref[way, pl.ds(head, 1), :] = columns[way]
        gq_ref[:, win] += dot(held[1], keys)
        gk_ref[:, win] += dot_at(held[1], queries)
        gv_ref[:, win] += dot_at(held[0], grads)


def pairs_kernel(head_width, heads, qkv_ref, gmix_ref, run_ref, runt_ref, gq_ref, gk_ref, gv_ref, rows_ref, cols_ref, held):
    for ref in (gq_ref, gk_ref, gv_ref, rows_ref, cols_ref):
        ref[...] = jnp.zeros_like(ref)
    pairs_part(
        head_width, heads, 0, heads, qkv_ref, gmix_ref, run_ref, runt_ref, gq_ref, gk_ref, gv_ref, rows_ref, cols_ref, held
    )


def carry_part(
    head_width, ways, early, qkv_ref, gmix_ref, gq_in, gk_in, gv_in, rows_ref, cols_ref, taken_ref, given_ref, gate_ref,
    state_ref, leave_ref, through, vpad, gpad, taps_ref, gqkv_ref, ggate_ref, conv_ref, bias_ref,
):
    length, width = gmix_ref.shape
    place = lax.broadcasted_iota(jnp.int32, (length, LANES), 0) % GRID
    taken_sums = [jnp.zeros((length, LANES), f32) for _ in range(ways)]
    given_sums = [jnp.zeros((length, LANES), f32) for _ in range(ways)]
    take_terms = [two_terms(taken_ref[way]) for way in range(ways)]
    give_terms = [two_terms(given_ref[way]) for way in range(ways)]
    for span in spans(width, 2 * LANES):
        near = near_lanes(span, width, head_width)
        gq, gk, gv = gq_in[:, span], gk_in[:, span], gv_in[:, span]
        for way in range(ways):
            take = spread_heads(take_terms[way], span, head_width)
            give = spread_heads(give_terms[way], span, head_width)
            back_q = take * dot_bt(gmix_ref[:, near], unfolded(state_ref, way, span, near, head_width))
            gq = gq + back_q
            for term in halves(qkv_ref[0, :, span].astype(f32) * back_q):
                taken_sums[way] = taken_sums[way] + head_sums(term, span, head_width)
            back_k = give * dot_bt(qkv_ref[2, :, near], unfolded(leave_ref, way, span, near, head_width))
            gk = gk + back_k
            for term in halves(qkv_ref[1, :, span].astype(f32) * back_k):
                given_sums[way] = given_sums[way] + head_sums(term, span, head_width)
            gv = gv + give * dot(qkv_ref[1, :, near], unfolded(leave_ref, way, near, span, head_width))
        gqkv_ref[0, :, span] = gq.astype(bf16)
        gqkv_ref[1, :, span] = gk.astype(bf16)
        for first in range(span.start, span.stop, LANES):
            cols = slice(first, first + LANES)
            grad = gpad[GRID : GRID + length, cols].astype(f32)
            total = gv[:, first - span.start : first - span.start + LANES]
            for lateral in range(3):
                b = lateral - 1
                column = jnp.zeros((length, LANES), f32)
                for vertical in range(3):
                    tap = taps_ref[3 * vertical + lateral : 3 * vertical + lateral + 1, cols]
                    start = (2 - vertical) * GRID
                    column = column + tap * gpad[start : start + length, cols].astype(f32)
                shifted = grad
                if b == -1:
                    column = jnp.where(place < GRID - 1, pltpu.roll(column, length - 1, 0), 0.0)
                    shifted = jnp.where(place < GRID - 1, pltpu.roll(grad, length - 1, 0), 0.0)
                if b == 1:
                    column = jnp.where(place > 0, pltpu.roll(column, 1, 0), 0.0)
                    shifted = jnp.where(place > 0, pltpu.roll(grad, 1, 0), 0.0)
                total = total + column
                for vertical in range(3):
                    window = vpad[vertical * GRID : vertical * GRID + length, cols].astype(f32)
                    conv_ref[3 * vertical + lateral : 3 * vertical + lateral + 1, cols] = jnp.sum(
                        window * shifted, axis=0, keepdims=True
                    )
            conv_ref[9:10, cols] = jnp.sum(grad, axis=0, keepdims=True)
            gqkv_ref[2, :, cols] = total.astype(bf16)
        if span.start // (2 * LANES) in (1, 3) or span.stop == width:
            yield
    conv_ref[10:16, :] = jnp.zeros((6, width), f32)

    row = lax.broadcasted_iota(jnp.int32, (length, length), 0)
    col = lax.broadcasted_iota(jnp.int32, (length, length), 1)
    before = (col < row).astype(bf16)
    upto = (col <= row).astype(bf16)

    def summed(product, matrix, value):
        high, rest = halves(value)
        low = (value - high.astype(f32) - rest.astype(f32)).astype(bf16)
        return product(matrix, high) + product(matrix, rest) + product(matrix, low)

    def columns(way):
        lines = cols_ref[way]
        if lines.shape[0] < LANES:
            lines = jnp.concatenate([lines, jnp.zeros((LANES - lines.shape[0], length), f32)], axis=0)
        return lines.T

    ahead = rows_ref[0] - columns(0)
    behind = rows_ref[1] - columns(1)
    if ways == 2:
        ahead, behind = ahead + taken_sums[0], behind + taken_sums[1]
        given_ahead, given_behind = given_sums
    else:
        ahead = ahead + taken_sums[0] * (1.0 - early)
        behind = behind + taken_sums[0] * early
        given_ahead, given_behind = given_sums[0] * early, given_sums[0] * (1.0 - early)
    grad_decay = (
        summed(dot_at, upto, ahead)
        + summed(dot, before, given_ahead)
        + summed(dot, upto, behind)
        + summed(dot_at, before, given_behind)
        + through
    )
    gate = gate_ref[...]
    small = jnp.exp(-jnp.abs(gate))
    sigmoid = jnp.where(gate >= 0, 1.0, small) / (1.0 + small)
    grad_gate = (-grad_decay * sigmoid).astype(bf16)
    lane = lax.broadcasted_iota(jnp.int32, grad_gate.shape, 1)
    grad_gate = jnp.where(lane < width // head_width, grad_gate.astype(f32), 0.0)
    ggate_ref[...] = grad_gate.astype(bf16)
    bias_ref[...] = jnp.sum(grad_gate, axis=0, keepdims=True)
    yield


def carry_kernel(
    head_width, ways, qkv_ref, gmix_ref, gq_in, gk_in, gv_in, rows_ref, cols_ref, taken_ref, given_ref, gate_ref,
    state_ref, leave_ref, through_ref, early_ref, gmixed_ref, grims_ref, vrims_ref, taps_ref,
    gqkv_ref, ggate_ref, conv_ref, bias_ref, vpad, gpad,
):
    fill_padded(vpad, vrims_ref, qkv_ref[2])
    fill_padded(gpad, grims_ref, gmixed_ref[...])
    for _ in carry_part(
        head_width, ways, early_ref[...], qkv_ref, gmix_ref, gq_in, gk_in, gv_in, rows_ref, cols_ref, taken_ref,
        given_ref, gate_ref, state_ref, leave_ref, through_ref[...], vpad, gpad, taps_ref, gqkv_ref, ggate_ref, conv_ref,
        bias_ref,
    ):
        pass


def projection_grads(slot, turned, grad_ref, gmain_ref, gleft_ref):
    pick = pick_left(None, slot)
    main_rows = rows_in(gmain_ref)
    for cols in spans(grad_ref.shape[1]):
        grad = grad_ref[:, cols]
        gmain_ref[..., cols] = dot(turned[:main_rows, :], grad).astype(bf16).reshape(gmain_ref.shape[:-1] + (-1,))
        part = dot(turned[main_rows:, :], grad).astype(bf16)
        gleft_ref[..., cols] += dot_at(pick, part).astype(bf16).reshape(gleft_ref.shape[:-1] + (-1,))


def projection_back(slot, grad_ref, main_ref, left_ref, gh_ref):
    width = grad_ref.shape[1]
    main_rows = rows_in(main_ref)
    left = dot(pick_left(None, slot), left_ref[...].reshape(16 * GROUPS, width)).astype(bf16)
    gh_ref[:, main_rows:] += dot_bt(grad_ref[...], left)
    for cols in spans(main_rows):
        gh_ref[:, cols] += dot_bt(grad_ref[...], group_rows(main_ref, cols))


def weights_kernel(
    xp_ref, gqkv_ref, ggate_ref, wf_ref, main_ref, left_ref, gout_left_ref, gmain_ref, gleft_ref, gforget_ref, gh_ref, turned
):
    slot = pl.program_id(0)

    @pl.when(slot == 0)
    def _():
        turned[...] = xp_ref[...].T
        gleft_ref[...] = gout_left_ref[...]
        gh_ref[...] = dot_bt(ggate_ref[...], wf_ref[...])
        gforget_ref[...] = dot(turned[...], ggate_ref[...])

    projection_grads(slot, turned, gqkv_ref.at[0], gmain_ref, gleft_ref)
    projection_back(slot, gqkv_ref.at[0], main_ref, left_ref, gh_ref)


def last_part(ghp_ref, perm_ref, x_ref, mod_ref, gmid_ref, gin_ref, sums_ref, gh, partial):
    unpermute(perm_ref, ghp_ref, gh)
    partial[...] = jnp.zeros_like(partial)

    def norm(rows):
        normed, rstd = norm_parts(x_ref[rows, :].astype(f32))
        grad = gh[rows, :]
        partial[0] += eight_rows(grad)
        partial[1] += eight_rows(grad * normed)
        gin_ref[rows, :] = gmid_ref[rows, :] + norm_back(normed, rstd, mod_ref[1:2, :], grad)

    row_loop(x_ref.shape[0], norm)
    for k in range(2):
        sums_ref[k : k + 1, :] = jnp.sum(partial[k], axis=0, keepdims=True)


def ring_place(z):
    return z + lax.div(z, 2) * (5 - 2 * z)


class Here:
    def __init__(self):
        row, x = lax.axis_index("dp"), lax.axis_index("seq")
        z, y, core = lax.div(row, 4), lax.rem(lax.div(row, 2), 2), lax.rem(row, 2)
        self.x, self.y, self.z, self.core = x, y, z, core
        self.p = ring_place(z)
        place = lambda z, y, core, x: ((z * 2 + y) * 2 + core, x)
        self.back = [ring_place(lax.rem(self.p + 4 - back, 4)) for back in range(4)]
        self.along = [place(self.back[4 - o], y, core, x) for o in (1, 2, 3)]
        self.next, self.prev = self.along[0], self.along[2]
        self.over_y = place(z, 1 - y, core, x)
        self.over_x = place(z, y, core, 1 - x)
        self.sibling = place(z, y, 1 - core, x)
        self.around = [self.over_y, self.over_x, place(z, 1 - y, core, 1 - x)]

    def ring_z(self, back):
        return self.back[back % 4]

    def partners(self, wide):
        devices = [self.next, self.prev, self.over_y, self.over_x, self.sibling]
        return devices + [self.along[1], self.around[2]] if wide else devices

    def greet(self, wide=False):
        barrier = pltpu.get_barrier_semaphore()
        for device in self.partners(wide):
            pl.semaphore_signal(barrier, inc=1, device_id=device, device_id_type=pl.DeviceIdType.MESH)

    def meet(self, wide=False):
        pl.semaphore_wait(pltpu.get_barrier_semaphore(), len(self.partners(wide)))


def push(source, target, send, recv, device):
    copy = pltpu.make_async_remote_copy(
        src_ref=source, dst_ref=target, send_sem=send, recv_sem=recv, device_id=device,
        device_id_type=pl.DeviceIdType.MESH,
    )
    copy.start()
    return copy


def routes(rows, ways=3):
    tiles = rows // 16
    third = 2 if tiles >= 7 and ways == 3 else 0
    first = tiles if ways == 1 else -(-(tiles - third) // 2)
    cuts = [0, 16 * first, 16 * (tiles - third), rows]
    return [pl.ds(low, high - low) for low, high in zip(cuts, cuts[1:])]


class Gather:
    def __init__(self, tag, here, ins, outs, sems, ways=3):
        self.here, self.ins, self.outs, self.sems, self.ways = here, ins, outs, sems, ways
        self.flights, self.todo, self.own = {}, {}, {}
        for i in range(len(ins)):
            a, b, c = routes(ins[i].shape[0], ways)
            self.todo[tag, 0, i, 0] = (), functools.partial(self.along_z, i, 0)
            for s in range(4):
                if s:
                    self.todo[tag, 0, i, s] = (("z", i, s - 1),), functools.partial(self.along_z, i, s)
                self.todo[tag, 1, i, s] = (("a1", i, s),), functools.partial(self.second, i, s, 0)
                waits = [("a2", i, s)]
                if b.size:
                    self.todo[tag, 2, i, s] = (("b1", i, s),), functools.partial(self.second, i, s, 1)
                    waits.append(("b2", i, s))
                if c.size:
                    waits.append(("cy", i, 0) if s == 0 else ("cz", i, s - 1))
                    self.todo[tag, 4, i, s] = (waits[-1],), functools.partial(self.third, i, s)
                    waits[-1] = ("c", i, s)
                self.todo[tag, 5, i, s] = tuple(waits), functools.partial(self.across, i, s)
            if c.size:
                self.todo[tag, 3, i, 0] = (("cx", i, 0),), functools.partial(self.third_over_y, i)

    def send(self, key, number, source, target, device):
        i, s = key[1:]
        self.flights[key] = push(source, target, self.sems[0].at[number, i, s], self.sems[1].at[number, i, s], device)

    def start(self):
        here = self.here
        for i, block in enumerate(self.ins):
            target = self.outs[i].at[here.z, here.y, here.core, here.x]
            self.own[i] = pltpu.make_async_copy(block, target, self.sems[2].at[i])
            self.own[i].start()

    def run(self, name):
        waits, action = self.todo.pop(name)
        for key in waits:
            if key[0] != "c":
                self.flights[key].wait_recv()
        action()

    def settle(self, i):
        if i in self.own:
            self.own.pop(i).wait()

    def along_z(self, i, s):
        here = self.here
        a, b, c = routes(self.ins[i].shape[0], self.ways)
        slot = self.outs[i].at[here.ring_z(s), here.y, here.core, here.x]
        held = self.ins[i] if s == 0 else slot
        if s < 3:
            both = pl.ds(0, a.size + b.size)
            self.send(("z", i, s), 0, held.at[both], slot.at[both], here.next)
        self.send(("a1", i, s), 1, held.at[a], slot.at[a], here.over_y)
        if b.size:
            self.send(("b1", i, s), 2, held.at[b], slot.at[b], here.over_x)
        if s == 0 and c.size:
            self.send(("cx", i, 0), 5, held.at[c], slot.at[c], here.over_x)

    def second(self, i, s, half):
        here, out = self.here, self.outs[i]
        a, b, c = routes(self.ins[i].shape[0], self.ways)
        z = here.ring_z(s)
        if s == 0:
            self.settle(i)
        if half:
            block = out.at[z, here.y, here.core, :, b]
            self.send(("b2", i, s), 4, block, block, here.over_y)
        else:
            block = out.at[z, :, here.core, here.x, a]
            self.send(("a2", i, s), 3, block, block, here.over_x)

    def third_over_y(self, i):
        here = self.here
        c = routes(self.ins[i].shape[0], self.ways)[2]
        self.settle(i)
        block = self.outs[i].at[here.z, here.y, here.core, :, c]
        self.send(("cy", i, 0), 6, block, block, here.over_y)

    def third(self, i, s):
        here = self.here
        c = routes(self.ins[i].shape[0], self.ways)[2]
        if s < 3:
            block = self.outs[i].at[here.ring_z(s), :, here.core, :, c]
            self.send(("cz", i, s), 7, block, block, here.next)

    def across(self, i, s):
        here = self.here
        block = self.outs[i].at[here.ring_z(s), :, here.core]
        self.send(("core", i, s), 8, block, block, here.sibling)

    def arrived(self, i, places=range(4)):
        for s in places:
            self.flights["core", i, s].wait_recv()

    def finish(self):
        for copy in self.flights.values():
            copy.wait_send()


def gather_sems(count):
    dma = pltpu.SemaphoreType.DMA
    return [dma((9, count, 4)), dma((9, count, 4)), dma((count,))]


class ShortGather:
    def __init__(self, tag, here, own, out, sems):
        self.here, self.own, self.out, self.sems = here, own, out, sems
        self.flights = {}
        self.todo = {
            (tag, 0, 0, 0): ((), self.along),
            (tag, 1, 0, 0): (tuple(("z", o) for o in range(3)), self.around),
            (tag, 2, 0, 0): (tuple(("xy", o) for o in range(3)), self.across),
        }

    def send(self, key, number, source, target, device):
        self.flights[key] = push(source, target, self.sems[0].at[number], self.sems[1].at[number], device)

    def start(self):
        here = self.here
        target = self.out.at[here.z, here.y, here.core, here.x]
        self.copy = pltpu.make_async_copy(self.own, target, self.sems[0].at[7])
        self.copy.start()

    def run(self, name):
        waits, action = self.todo.pop(name)
        for key in waits:
            self.flights[key].wait_recv()
        action()

    def along(self):
        here = self.here
        slot = self.out.at[here.z, here.y, here.core, here.x]
        for o, device in enumerate(here.along):
            self.send(("z", o), o, self.own, slot, device)

    def around(self):
        here = self.here
        self.copy.wait()
        block = self.out.at[:, here.y, here.core, here.x]
        for o, device in enumerate(here.around):
            self.send(("xy", o), 3 + o, block, block, device)

    def across(self):
        block = self.out.at[:, :, self.here.core]
        self.send(("core", 0), 6, block, block, self.here.sibling)

    def arrived(self):
        self.flights["core", 0].wait_recv()

    def finish(self):
        for copy in self.flights.values():
            copy.wait_send()


def short_gather_sems():
    return [pltpu.SemaphoreType.DMA((8,)), pltpu.SemaphoreType.DMA((8,))]


class ShortScatter:
    def __init__(self, tag, here, partial, final, scratch):
        self.acc, self.mate, self.xy_rows, self.z_rows, self.send_sem, self.recv_sem = scratch
        self.here, self.partial, self.final = here, partial, final
        self.flights = {}
        self.todo = {
            (tag, 0, 0, 0): (tuple(("core", n) for n in range(8)), self.from_sibling),
            (tag, 1, 0, 0): (tuple(("xy", o) for o in range(3)), self.around),
            (tag, 2, 0, 0): (tuple(("z", o) for o in range(3)), self.last),
        }

    def send(self, key, number, source, target, device):
        self.flights[key] = push(source, target, self.send_sem.at[number], self.recv_sem.at[number], device)

    def start(self):
        here = self.here
        for z in range(4):
            for y in range(2):
                rows = pl.ds(8 * z + 4 * y + 2 * (1 - here.core), 2)
                self.send(
                    ("core", 2 * z + y), 2 * z + y, self.partial.at[rows], self.mate.at[z, y], here.sibling
                )

    def run(self, name):
        waits, action = self.todo.pop(name)
        for key in waits:
            self.flights[key].wait_recv()
        action()

    def from_sibling(self):
        here = self.here
        for z in range(4):
            for y in range(2):
                rows = pl.ds(8 * z + 4 * y + 2 * here.core, 2)
                self.acc[z, y] = self.partial[rows] + self.mate[z, y]
        places = [(1 - here.y, here.x), (here.y, 1 - here.x), (1 - here.y, 1 - here.x)]
        for o, (y, x) in enumerate(places):
            self.send(("xy", o), 8 + o, self.acc.at[:, y, x], self.xy_rows.at[o], here.around[o])

    def around(self):
        here = self.here
        mine = self.acc.at[:, here.y, here.x]
        mine[...] = mine[...] + self.xy_rows[0] + self.xy_rows[1] + self.xy_rows[2]
        for o, device in enumerate(here.along):
            z = here.ring_z(3 - o)
            self.send(("z", o), 11 + o, mine.at[z], self.z_rows.at[o], device)

    def last(self):
        here = self.here
        self.final(self.acc[here.z, here.y, here.x] + self.z_rows[0] + self.z_rows[1] + self.z_rows[2])

    def finish(self):
        for copy in self.flights.values():
            copy.wait_send()


def short_scatter_scratch(block):
    rows, lanes = block.shape[-2:]
    dma = pltpu.SemaphoreType.DMA
    return [
        pltpu.VMEM((4, 2, 2, rows, lanes), f32), pltpu.VMEM((4, 2, 2, rows, lanes), f32),
        pltpu.VMEM((3, 4, rows, lanes), f32), pltpu.VMEM((3, rows, lanes), f32), dma((14,)), dma((14,)),
    ]


def gathered_shape(block):
    return sds((4, 2, 2, 2) + block.shape, block.dtype)


def add_rows(target, source, lead, low, size):
    chunk = 16

    @pl.loop(0, size // chunk)
    def _(r):
        start = pl.multiple_of(r * chunk, chunk)
        here, there = pl.ds(low + start, chunk), pl.ds(start, chunk)
        for at in lead:
            target[at + (here,)] = target[at + (here,)] + source[at + (there,)]


class Scatter:
    def __init__(self, tag, here, ins, final, scratch, ways=3):
        (
            self.acc, self.mate, self.one_a, self.one_b, self.two_rows, self.ring_rows, self.ring_c, self.c_y, self.c_x,
            self.send_sem, self.recv_sem, self.load_sem,
        ) = scratch
        self.here, self.ins, self.final = here, ins, final
        self.rows = self.acc.shape[3]
        self.a, self.b, self.c = routes(self.rows, ways)
        self.flights, self.loads, self.todo, self.released = {}, {}, {}, set()
        for k in range(4):
            self.todo[tag, 0, 0, k] = (("core", k),), functools.partial(self.from_sibling, k)
            self.todo[tag, 1, 0, k] = (("a1", k),), functools.partial(self.first_sum, k, 0)
            waits = [("a2", k)]
            if self.b.size:
                self.todo[tag, 2, 0, k] = (("b1", k),), functools.partial(self.first_sum, k, 1)
                waits.append(("b2", k))
            if k:
                waits.append(("z", k - 1))
            self.todo[tag, 3, 0, k] = tuple(waits), functools.partial(self.second_sum, k)
            if self.c.size:
                waits = (("c", k), ("cz", k - 1)) if k else (("c", k),)
                self.todo[tag, 4, 0, k] = waits, functools.partial(self.third_sum, k)
        if self.c.size:
            self.todo[tag, 5, 0, 0] = (("cy", 0),), self.third_over_y
            self.todo[tag, 5, 0, 1] = (("cx", 0), ("own", 0)), self.third_over_x

    def send(self, key, number, source, target, device, piece=0):
        at = (number + piece, key[1])
        self.flights[key] = push(source, target, self.send_sem.at[at], self.recv_sem.at[at], device)

    def pieces(self, k):
        z, low = self.here.ring_z(k + 1), 0
        for number, ref in enumerate(self.ins):
            if len(ref.shape) == 3:
                for y in range(2):
                    yield (
                        number + y, lambda core, y=y: ref.at[pl.ds(8 * z + 4 * y + 2 * core, 2)], lambda slot, y=y: slot.at[y]
                    )
            elif len(ref.shape) == 5:
                yield number, lambda core, ref=ref: ref.at[:, core], lambda slot: slot
            else:
                span = pl.ds(low, ref.shape[4])
                low += ref.shape[4]
                yield (
                    number, lambda core, ref=ref: ref.at[z, :, core], lambda slot, span=span: slot.at[:, :, span]
                )

    def load(self, k, numbers=None):
        for number, source, target in self.pieces(k):
            if numbers is not None and number not in numbers:
                continue
            self.loads[k, number] = pltpu.make_async_copy(
                source(self.here.core), target(self.acc.at[k]), self.load_sem.at[k, number]
            )
            self.loads[k, number].start()

    def to_sibling(self, k, numbers=None):
        for number, source, target in self.pieces(k):
            if numbers is not None and number not in numbers:
                continue
            self.send(
                ("core", k, number), 8, source(1 - self.here.core), target(self.mate.at[k]), self.here.sibling, number
            )

    def offer(self, k):
        self.load(k)
        self.to_sibling(k)

    def release(self, k):
        for number, _, _ in self.pieces(k):
            self.flights["core", k, number].wait_send()
        self.released.add(k)

    def prepare(self, numbers=None):
        for k in range(4):
            self.load(k, numbers)

    def start(self, numbers=None):
        for k in range(4):
            self.to_sibling(k, numbers)

    def run(self, name):
        waits, action = self.todo.pop(name)
        for key in waits:
            if key[0] == "core":
                for number, _, _ in self.pieces(key[1]):
                    self.loads[key[1], number].wait()
                    self.flights["core", key[1], number].wait_recv()
            elif key[0] not in ("c", "own"):
                self.flights[key].wait_recv()
        action()

    def from_sibling(self, k):
        here, acc = self.here, self.acc.at[k]
        add_rows(acc, self.mate.at[k], [(a, b) for a in range(2) for b in range(2)], 0, self.rows)
        self.send(("a1", k), 0, acc.at[:, 1 - here.x, self.a], self.one_a.at[k], here.over_x)
        if self.b.size:
            self.send(("b1", k), 1, acc.at[1 - here.y, :, self.b], self.one_b.at[k], here.over_y)

    def first_sum(self, k, half):
        here, acc = self.here, self.acc.at[k]
        if half:
            add_rows(acc.at[here.y], self.one_b.at[k], [(0,), (1,)], self.b.start, self.b.size)
            self.send(
                ("b2", k), 3, acc.at[here.y, 1 - here.x, self.b], self.two_rows.at[k, self.b], here.over_x
            )
        else:
            add_rows(acc.at[:, here.x], self.one_a.at[k], [(0,), (1,)], self.a.start, self.a.size)
            self.send(
                ("a2", k), 2, acc.at[1 - here.y, here.x, self.a], self.two_rows.at[k, self.a], here.over_y
            )

    def second_sum(self, k):
        here = self.here
        size = self.a.size + self.b.size
        mine = self.acc.at[k, here.y, here.x]
        add_rows(mine, self.two_rows.at[k], [()], 0, size)
        if k:
            add_rows(mine, self.ring_rows.at[k - 1], [()], 0, size)
        if k < 3:
            self.send(("z", k), 4, mine.at[pl.ds(0, size)], self.ring_rows.at[k], here.next)
        elif not self.c.size:
            self.final(mine)

    def third_sum(self, k):
        here, acc = self.here, self.acc.at[k]
        if k:
            add_rows(acc, self.ring_c.at[k - 1], [(a, b) for a in range(2) for b in range(2)], self.c.start, self.c.size)
        if k < 3:
            self.send(("cz", k), 5, acc.at[:, :, self.c], self.ring_c.at[k], here.next)
        else:
            self.send(("cy", 0), 6, acc.at[1 - here.y, :, self.c], self.c_y, here.over_y)

    def third_over_y(self):
        here, acc = self.here, self.acc.at[3]
        add_rows(acc.at[here.y], self.c_y, [(0,), (1,)], self.c.start, self.c.size)
        self.send(("cx", 0), 7, acc.at[here.y, 1 - here.x, self.c], self.c_x, here.over_x)

    def third_over_x(self):
        mine = self.acc.at[3, self.here.y, self.here.x]
        add_rows(mine, self.c_x, [()], self.c.start, self.c.size)
        self.final(mine)

    def finish(self):
        for key, copy in self.flights.items():
            if key[0] != "core" or key[1] not in self.released:
                copy.wait_send()


def scatter_scratch(block, ways=3):
    dma = pltpu.SemaphoreType.DMA
    rows, lanes, kind = sum(b.shape[-2] for b in block), block[0].shape[-1], block[0].dtype
    a, b, c = (max(span.size, 16) for span in routes(rows, ways))
    both = sum(span.size for span in routes(rows, ways)[:2])
    return [
        pltpu.VMEM((4, 2, 2, rows, lanes), kind), pltpu.VMEM((4, 2, 2, rows, lanes), kind),
        pltpu.VMEM((4, 2, a, lanes), kind), pltpu.VMEM((4, 2, b, lanes), kind),
        pltpu.VMEM((4, both, lanes), kind), pltpu.VMEM((3, both, lanes), kind),
        pltpu.VMEM((3, 2, 2, c, lanes), kind), pltpu.VMEM((2, c, lanes), kind), pltpu.VMEM((c, lanes), kind),
        dma((11, 4)), dma((11, 4)), dma((4, 3)),
    ]


def in_order(plan, chain, networks):
    pieces = iter(chain)
    for item in plan:
        if item == -1:
            next(pieces)()
        else:
            networks[item[0]].run(item)
    assert next(pieces, None) is None and not any(net.todo for net in networks.values())


def small_rows(cond, forget, taps, place):
    at = lax.rem(place * taps.shape[0], LANES)
    taps = lax.dynamic_update_slice(jnp.zeros((4 * LANES,), bf16), taps, (at,)).reshape(4, LANES)
    cond = cond.reshape(-1, LANES)
    forget = forget.reshape(36, -1)
    return jnp.concatenate([
        jnp.pad(cond, ((0, 16 - cond.shape[0]), (0, 0))), jnp.pad(taps, ((0, 12), (0, 0))),
        jnp.pad(forget, ((0, 12), (0, LANES - forget.shape[1]))),
    ])


def unpack_small(small, taps_share, wf_ref, taps_ref, flat):
    wf_ref[: 32 * GROUPS, :] = small[:, 32:64, :].reshape(32 * GROUPS, LANES)
    wf_ref[32 * GROUPS :, :] = dot(pick_left(None, 0), small[:, 64:80, :].reshape(16 * GROUPS, LANES)).astype(bf16)
    flat[...] = jnp.zeros_like(flat)
    for d in range(GROUPS):
        row = d * taps_share // LANES
        flat[row : row + 4, :] += small[d, 16:32, :].astype(f32)[:4]
    tiles = taps_ref.shape[1] // LANES
    taps_ref[...] = jnp.zeros_like(taps_ref)
    for k in range(10):
        for t in range(tiles):
            taps_ref[k : k + 1, t * LANES : (t + 1) * LANES] = flat[k * tiles + t : k * tiles + t + 1, :]


def pack_rows(sources, wide, left, out, other=None):
    for j, (source, first, per_row) in enumerate(sources):
        target = other if other is not None and j == 3 else out.at[pl.ds(32 * j, 32)]
        if first == 0:
            wide[: source.shape[0], :] = source[...].astype(f32)
        for t in range(out.shape[1] // LANES):
            cols = slice(t * LANES, (t + 1) * LANES)
            rows = wide[pl.ds(first + t, 36, stride=per_row), :]
            target[:, cols] = rows[:32].astype(bf16)
            left[4 * j : 4 * j + 4, cols] = rows[32:]
    out[(128 if other is None else 96) : (144 if other is None else 112), :] = left[...].astype(bf16)


def fill_permutation(perm_ref):
    width = perm_ref.shape[0]
    at = lax.broadcasted_iota(jnp.int32, (1, width), 1)
    late = at - 32 * GROUPS
    order = jnp.where(late < 0, (at >> 5) * 36 + (at & 31), (late >> 2) * 36 + 32 + (late & 3))
    for rows in spans(width, 2 * LANES):
        row = lax.broadcasted_iota(jnp.int32, (rows.stop - rows.start, width), 0) + rows.start
        perm_ref[rows, :] = (row == order).astype(bf16)


def forward_kernel(
    head_width, heads, taps_share, x_ref, ada_ref, bias_ref, bf_ref, own_s, query_ref, key_ref, value_ref, out_ref, up_ref,
    all_s, all_a, all_u, xp_out, qkv_out, mix_out, mixedp_out, branch_out, middle_out, h2p_out, perm_out,
    mod_ref, wf_ref, taps_ref, gate_ref, run_ref, runt_ref, state_ref, rims_ref, given_ref, taken_ref, cond_ref,
    xp_ref, qkv_ref, mix_ref, mixedp_ref, branch_ref, middle_ref, h2p_ref, perm_ref,
    own_a, own_u, wide, ada_wide, rows_left, small, flat, partial, main, left, outbox, inbox, vpad, mixed, load_sem, swap_sem, *rest,
):
    length, width = x_ref.shape
    tiles = width // LANES
    here = Here()
    here.greet(True)
    lower = here.x == 0
    squares = [(ref, 0, tiles) for ref in (query_ref, key_ref, value_ref, out_ref)]
    pack_rows(squares, wide, rows_left, own_a, own_u.at[pl.ds(144, 32)])
    pack_rows([(up_ref, j * tiles, 4 * tiles) for j in range(4)], wide, rows_left, own_u)
    first = ShortGather("f", here, own_s, all_s, rest[:2])
    gather = Gather("g", here, (own_a, own_u), (all_a, all_u), rest[2:5])

    def to_mod(total):
        for k in range(6):
            for t in range(tiles):
                mod_ref[k : k + 1, t * LANES : (t + 1) * LANES] = total[k * tiles + t : k * tiles + t + 1, :]
        mod_ref[6:8, :] = jnp.zeros((2, width), f32)

    scatter = ShortScatter("s", here, partial, to_mod, rest[5:])
    stores, loads = [], []

    def fetch(number, source, target):
        copy = pltpu.make_async_copy(source, target, load_sem.at[number])
        copy.start()
        return copy

    def modulation():
        first.arrived()
        fetch(5, all_s, small).wait()
        me = ((here.z * 2 + here.y) * 2 + here.core) * 2 + here.x
        row = lax.broadcasted_iota(jnp.int32, (width, LANES), 0)
        lane = lax.broadcasted_iota(jnp.int32, (width, LANES), 1)
        pick = ((row == lane + me * 36) & (lane < 36)).astype(bf16)
        lines = small[...].reshape(GROUPS, 80, LANES)[:, :16, :].astype(f32)
        mine = jnp.zeros((GROUPS, LANES), f32)
        for t in range(tiles):
            cond = lines[:, t, :]
            cond = (cond / (1.0 + jnp.exp(-cond))).astype(bf16)
            mine = mine + dot(cond, pick[t * LANES : (t + 1) * LANES])
        cond_ref[...] = mine.astype(bf16)
        mine = mine[:, :36].astype(bf16)
        for t in range(6 * tiles):
            rows = ada_wide[pl.ds(t, 36, stride=6 * tiles), :].astype(bf16)
            partial[:, t, :] = dot(mine, rows) + bias_ref[t : t + 1, :].astype(f32)
        scatter.start()

    def small_arrays():
        unpack_small(small[...].reshape(GROUPS, 80, LANES), taps_share, wf_ref, taps_ref, flat)

    def norm_one():
        first_part(x_ref, mod_ref, perm_ref, wf_ref, bf_ref, xp_ref, gate_ref, run_ref, runt_ref, mixed)
        stores.extend([fetch(6, xp_ref, xp_out), fetch(13, perm_ref, perm_out)])
        total = run_ref[0, length - 1 : length, :]
        given_ref[0] = jnp.where(lower, jnp.exp(total - run_ref[0]), jnp.exp(run_ref[1]))
        taken_ref[0] = jnp.where(lower, jnp.exp(total - run_ref[1]), jnp.exp(run_ref[0]))
        mix_ref[...] = jnp.zeros_like(mix_ref)

    def load(slot):
        source = all_a.at[:, :, :, :, pl.ds(32 * slot, 32)] if slot < 3 else all_u.at[:, :, :, :, pl.ds(144, 32)]
        loads.append(fetch(slot, source, main.at[slot % 2]))

    def project(slot):
        if slot == 0:
            gather.arrived(0)
            others = fetch(4, all_a.at[:, :, :, :, pl.ds(96, 16)], left)
            load(0)
            load(1)
            others.wait()
        loads[slot].wait()

        def write(cols, value):
            qkv_ref[slot, :, cols] = value.astype(bf16)

        project_part(slot, xp_ref, main.at[slot % 2], left, write)
        if slot == 0:
            load(2)
        if slot == 2:
            stores.append(fetch(7, qkv_ref, qkv_out))

    def states():
        state_part(head_width, 1, lambda cols: qkv_ref[1, :, cols], qkv_ref.at[2], given_ref, outbox)
        edge = pl.multiple_of((1 - here.x) * (length - GRID), GRID)

        def write_edge(t, value):
            outbox[0, width + t * GRID : width + (t + 1) * GRID, :] = value

        edge_part(qkv_ref[2, pl.ds(edge, GRID), :], write_edge)
        stores.append(push(outbox, inbox, swap_sem.at[0], swap_sem.at[1], here.over_x))

    def mix(part):
        mix_part(head_width, heads, part * heads // 4, (part + 1) * heads // 4, qkv_ref, run_ref, runt_ref, mix_ref)

    def mixing():
        swap = stores.pop()
        swap.wait_recv()
        state_ref[0] = inbox[0, :width, :]
        for t in range(tiles):
            cols = slice(t * LANES, (t + 1) * LANES)
            rows = inbox[0, width + t * GRID : width + (t + 1) * GRID, :]
            rims_ref[0, :, cols] = jnp.where(lower, 0, rows).astype(bf16)
            rims_ref[1, :, cols] = jnp.where(lower, rows, 0).astype(bf16)
        fill_padded(vpad, rims_ref, qkv_ref[2])
        mixed_part(head_width, 1, qkv_ref, taken_ref, state_ref, taps_ref, vpad, mix_ref, mixed)
        stores.append(fetch(8, mix_ref, mix_out))
        swap.wait_send()

    def turn():
        gather.arrived(1)
        load(3)
        permute_part(mixed, perm_ref, mixedp_ref)
        stores.append(fetch(9, mixedp_ref, mixedp_out))

    def branch():
        loads[3].wait()
        branch_part(x_ref, mod_ref, mixedp_ref, main.at[1], left, branch_ref, middle_ref)
        stores.extend([fetch(10, branch_ref, branch_out), fetch(11, middle_ref, middle_out)])

    def norm_two():
        second_hidden(mod_ref, middle_ref, mixed)
        permute_part(mixed, perm_ref, h2p_ref)
        stores.append(fetch(12, h2p_ref, h2p_out))

    def prepare():
        fill_permutation(perm_ref)
        ada_wide[...] = ada_ref[...].astype(f32)
        partial[:, 6 * tiles :, :] = jnp.zeros((GROUPS, 64 - 6 * tiles, LANES), f32)

    chain = [prepare, modulation, small_arrays, norm_one]
    chain += [functools.partial(project, slot) for slot in range(3)] + [states]
    chain += [functools.partial(mix, part) for part in range(4)] + [mixing, turn, branch, norm_two]
    first.start()
    gather.start()
    here.meet(True)
    in_order(FORWARD_PLAN, chain, {"f": first, "g": gather, "s": scatter})
    for network in (first, gather, scatter):
        network.finish()
    for copy in stores:
        copy.wait()


def forward_fused(x, ada, bias, bf, small, shards, heads, taps_share):
    length, width = x.shape
    head_width = width // heads
    message = width + width // LANES * GRID
    anywhere, vm = pl.BlockSpec(memory_space=pl.ANY), pl.BlockSpec(memory_space=pltpu.VMEM)
    rows, wide = (length, width), (length, LANES)
    bulk = (
        sds(rows, bf16), sds((3,) + rows, bf16), sds(rows), sds(rows, bf16), sds(rows, bf16), sds(rows), sds(rows, bf16),
        sds((width, width), bf16),
    )
    kept = (
        sds((8, width)), sds((width, LANES), bf16), sds((16, width)), sds(wide), sds((2,) + wide), sds((2, LANES, length)),
        sds((1, width, LANES), bf16), sds((2, GRID, width), bf16), sds((1,) + wide), sds((1,) + wide),
        sds((GROUPS, LANES), bf16),
    )
    partial = sds((GROUPS, 64, LANES))
    own, own_up = sds((112, width), bf16), sds((176, width), bf16)
    dma = pltpu.SemaphoreType.DMA
    out = pl.pallas_call(
        functools.partial(forward_kernel, head_width, heads, taps_share),
        out_shape=tuple(gathered_shape(b) for b in (small, own, own_up)) + bulk + kept,
        in_specs=[vm] * 10,
        out_specs=(anywhere,) * (3 + len(bulk)) + (vm,) * len(kept),
        scratch_shapes=[pltpu.VMEM(b.shape, b.dtype) for b in bulk] + [
            pltpu.VMEM(own.shape, bf16), pltpu.VMEM(own_up.shape, bf16), pltpu.VMEM(shards[4].shape, f32),
            pltpu.VMEM(ada.shape, f32), pltpu.VMEM((16, width), f32),
            pltpu.VMEM((4, 2, 2, 2) + small.shape, bf16), pltpu.VMEM((96, LANES), f32),
            pltpu.VMEM(partial.shape, f32), pltpu.VMEM((2, 4, 2, 2, 2, 32, width), bf16),
            pltpu.VMEM((4, 2, 2, 2, 16, width), bf16), pltpu.VMEM((1, message, LANES), bf16),
            pltpu.VMEM((1, message, LANES), bf16), pltpu.VMEM((length + 2 * GRID, width), bf16), pltpu.VMEM(rows, bf16),
            dma((14,)), dma((2,)),
        ] + short_gather_sems() + gather_sems(2) + short_scatter_scratch(partial),
        compiler_params=pltpu.CompilerParams(collective_id=0, has_side_effects=True, vmem_limit_bytes=VMEM_LIMIT),
        name="forward",
    )(x, ada, bias, bf, small, *shards)
    gathered = [g.reshape((GROUPS,) + g.shape[4:]) for g in out[:3]]
    return gathered, out[3 : 3 + len(bulk)], out[3 + len(bulk) :]


def feed_fused_kernel(
    h2p, cot, mod_ref, flat_d, up_in, middle_in,
    all_d, out_out, gh_out, gup_out, gleft_ref, ggate_ref, down_own,
    gdi, h2pt, act, slope, actt, gup, main, left, left_own, down, down_acc, gh, middle, stage_d, stage_u, own_d, wide, load_sem, *rest,
):
    length, width = h2p.shape
    main_rows = GROUPS * 32
    here = Here()
    here.greet()
    gather = Gather("g", here, (own_d,), (all_d,), rest[:3], FEED_WAYS[0])
    scatter = Scatter("d", here, [stage_d], plain_final(down_own), rest[3:], FEED_WAYS[1])
    order = [here.ring_z(k + 1) for k in range(4)]

    def fetch(number, source, target):
        copy = pltpu.make_async_copy(source, target, load_sem.at[number])
        copy.start()
        return copy

    def load_up(k, number):
        rows = pl.ds(pl.multiple_of(32 * order[k], 32), 32)
        return fetch(number, up_in.at[:, rows], main.at[k % 2])

    def load_down(k):
        gather.arrived(0, [(k + 1) % 4])
        return fetch(8 + k, all_d.at[order[k]], down.at[k % 2])

    def left_rows(k):
        return dot(pick_left(None, order[k]), left[...].reshape(16 * GROUPS, width)).astype(bf16)

    def start():
        gdi[...] = (cot[...].astype(f32) * mod_ref[5:6, :]).astype(bf16)
        h2pt[...] = h2p[...].T
        gleft_ref[...] = jnp.zeros_like(gleft_ref)
        others.wait()

    def up_step(k):
        loads[k].wait()
        left_own[...] = left_rows(k)
        for cols in spans(width):
            up = dot(h2p[:, :main_rows], main[k % 2, :, :, cols].reshape(main_rows, -1))
            up = up + dot(h2p[:, main_rows:], left_own[:, cols])
            value, rate = gelu_both(up)
            value = value.astype(bf16)
            act[k, :, cols] = value
            actt[cols, :] = value.T
            slope[k, :, cols] = rate.astype(bf16)
        loads.append(load_up(k + 2, k + 2) if k < 2 else load_up(k - 2, k + 2))

    def down_grad(k):
        if k > 0:
            scatter.release(k - 1)
        for cols in spans(width):
            stage_d[:, :, :, :, cols] = dot(actt[...], gdi[:, cols]).astype(bf16).reshape(2, 2, 2, width // 8, -1)
        scatter.offer(k)

    def back_act(k):
        load_down(k).wait()
        rows_of = down[k % 2].reshape(width, width)
        for cols in spans(width):
            gup[:, cols] = (dot_bt(gdi[...], rows_of[cols]) * slope[k, :, cols].astype(f32)).astype(bf16)

    def down_step(k):
        rows_of = down[k % 2].reshape(width, width)
        for cols in spans(width):
            part = dot(act[k], rows_of[:, cols])
            if k == 0:
                down_acc[:, cols] = part
            else:
                down_acc[:, cols] += part
    def back_hidden(k):
        loads[4 + k].wait()
        for cols in spans(main_rows):
            part = dot_bt(gup[...], main[k % 2, cols.start // 32 : cols.stop // 32].reshape(-1, width))
            if k == 0:
                gh[:, cols] = part
            else:
                gh[:, cols] += part
        part = dot_bt(gup[...], left_rows(k))
        if k == 0:
            gh[:, main_rows:] = part
        else:
            gh[:, main_rows:] += part
        if k < 2:
            loads.append(load_up(k + 2, 6 + k))

    def up_grad(k):
        if k > 0:
            stores[k - 1].wait()
        projection_grads(order[k], h2pt, gup, stage_u, gleft_ref)
        rows = pl.ds(pl.multiple_of(32 * order[k], 32), 32)
        stores.append(fetch(13 + k, stage_u, gup_out.at[:, rows]))

    def end():
        keep = fetch(17, gh, gh_out)
        ggate_ref[...] = jnp.sum(cot[...].astype(f32) * down_acc[...], axis=0, keepdims=True)
        keep_middle.wait()
        for cols in spans(width):
            act[0, :, cols] = (middle[:, cols] + mod_ref[5:6, cols] * down_acc[:, cols]).astype(bf16)
        stores.extend([fetch(19, act.at[0], out_out), keep])

    chain = [start]
    for k in range(4):
        chain += [functools.partial(up_step, k), functools.partial(down_grad, k)]
    for k in range(4):
        chain += [functools.partial(step, k) for step in (back_act, down_step, back_hidden, up_grad)]
    others = fetch(12, up_in.at[:, pl.ds(128, 16)], left)
    loads = [load_up(0, 0), load_up(1, 1)]
    keep_middle = fetch(18, middle_in, middle)
    stores = []
    wide[...] = flat_d[...].astype(f32)
    for t in range(width // LANES):
        rows = wide[pl.ds(t, own_d.shape[0], stride=width // LANES), :]
        own_d[:, t * LANES : (t + 1) * LANES] = rows.astype(bf16)
    gather.start()
    here.meet()
    in_order(FEED_PLAN, chain + [end], {"d": scatter, "g": gather})
    scatter.finish()
    gather.finish()
    for copy in stores[3:]:
        copy.wait()


def feed_fused(h2p, cot, mod, flat_d, up_w, middle):
    length, width = h2p.shape
    anywhere, vm = pl.BlockSpec(memory_space=pl.ANY), pl.BlockSpec(memory_space=pltpu.VMEM)
    rows = (length, width)
    dma = pltpu.SemaphoreType.DMA
    stage = (2, 2, 2, width // 8, width)
    own = sds((width // 8, width), bf16)
    return pl.pallas_call(
        feed_fused_kernel,
        out_shape=(
            gathered_shape(own), sds(rows, bf16), sds(rows), sds((GROUPS, 128, width), bf16),
            sds((GROUPS, 16, width), bf16), sds((1, width)), sds(flat_d.shape),
        ),
        in_specs=[vm] * 4 + [anywhere] * 2,
        out_specs=(anywhere,) * 4 + (vm,) * 3,
        scratch_shapes=[
            pltpu.VMEM(rows, bf16), pltpu.VMEM((width, length), bf16), pltpu.VMEM((4,) + rows, bf16),
            pltpu.VMEM((4,) + rows, bf16), pltpu.VMEM((width, length), bf16), pltpu.VMEM(rows, bf16),
            pltpu.VMEM((2, GROUPS, 32, width), bf16), pltpu.VMEM((GROUPS, 16, width), bf16), pltpu.VMEM((128, width), bf16),
            pltpu.VMEM((2,) + stage, bf16), pltpu.VMEM(rows, f32), pltpu.VMEM(rows, f32), pltpu.VMEM(rows, f32),
            pltpu.VMEM(stage, bf16),
            pltpu.VMEM((GROUPS, 32, width), bf16), pltpu.VMEM(own.shape, bf16), pltpu.VMEM(flat_d.shape, f32), dma((20,)),
        ] + gather_sems(1) + scatter_scratch([sds(stage, bf16)], FEED_WAYS[1]),
        compiler_params=pltpu.CompilerParams(
            collective_id=1, has_side_effects=True, vmem_limit_bytes=62 * 1024 * 1024
        ),
        name="feed",
    )(h2p, cot, mod, flat_d, up_w, middle)[1:]


def six(array):
    return array.reshape((4, 2, 2, 2) + array.shape[1:])


def flat_rows(out, first, value, per_row):
    for t in range(value.shape[1] // LANES):
        out[pl.ds(first + t, value.shape[0], stride=per_row), :] = value[:, t * LANES : (t + 1) * LANES]


def square_final(outs):
    def final(total):
        value = total[...].astype(f32)
        per_row = value.shape[1] // LANES
        for j, out in enumerate(outs):
            flat_rows(out, 0, value[32 * j : 32 * j + 32], per_row)
            flat_rows(out, 32 * per_row, value[128 + 4 * j : 132 + 4 * j], per_row)

    return final


def columns_final(out):
    def final(total):
        value = total[...].astype(f32)
        tiles = value.shape[1] // LANES
        for j in range(4):
            flat_rows(out, j * tiles, value[32 * j : 32 * j + 32], 4 * tiles)
            flat_rows(out, 32 * 4 * tiles + j * tiles, value[128 + 4 * j : 132 + 4 * j], 4 * tiles)

    return final


def plain_final(out):
    def final(total):
        value = total[...].astype(f32)
        flat_rows(out, 0, value, value.shape[1] // LANES)

    return final


def small_final(out):
    def final(total):
        out[...] = total[...]

    return final


def fill_small(block, gforget, conv, bias, flat, taps_share):
    tiles = conv.shape[1] // LANES
    for k in range(10):
        for t in range(tiles):
            flat[k * tiles + t : k * tiles + t + 1, :] = conv[k : k + 1, t * LANES : (t + 1) * LANES]
    flat[10 * tiles :, :] = jnp.zeros_like(flat[10 * tiles :, :])
    block[:, :32, :] = gforget[: 32 * GROUPS, :].reshape(GROUPS, 32, LANES)
    block[:, 40:, :] = jnp.broadcast_to(bias[...].reshape(1, 1, LANES), (GROUPS, 8, LANES))
    for d in range(GROUPS):
        at = 32 * GROUPS + 4 * d
        block[d, 32:36, :] = gforget[at : at + 4, :]
        row = d * taps_share // LANES
        block[d, 36:40, :] = flat[row : row + 4, :]


def backward_kernel(
    head_width, heads, taps_share,
    mod_ref, run_ref, runt_ref, taken_ref, given_ref, gate_ref, state_ref, vrims_ref, taps_ref,
    ghp_in, perm_in, middle_in, cot_in, branch_in, mixedp_in, mix_in, weight_in, up_in, qkv_in, xp_in, gup_in, gupl_in,
    gmid_out, gqkv_out, gmain_out, gout_out, small_out, gleft_ref, ggate_ref, sums_ref, up_ref,
    pool, perm, gmix, gb, main, qkv, gqkv, held, vpad, gpad, pair_rows, pair_cols,
    outbox, inbox, rims, leave, conv_ref, bias_ref, gforget_ref, flat, small, partial, fetch_sem, swap_sem, *scratch,
):
    length, width = gmix.shape
    here = Here()
    here.greet()
    lower = here.x == 0
    gmixed = gpad.at[pl.ds(GRID, length)]
    turned = perm.at[:, pl.ds(0, length)]
    scatter = Scatter("u", here, [gup_in, gupl_in], columns_final(up_ref), scratch, BACKWARD_WAYS)
    scatter.prepare()

    def fetch(number, source, target):
        copy = pltpu.make_async_copy(source, target, fetch_sem.at[number])
        copy.start()
        return copy

    first = [
        fetch(0, ghp_in, pool.at[0]), fetch(1, perm_in, perm), fetch(2, middle_in, pool.at[1]), fetch(3, cot_in, qkv.at[0]),
        fetch(4, branch_in, qkv.at[1]), fetch(5, mixedp_in, qkv.at[2]),
        fetch(6, up_in.at[:, :, :, :, pl.ds(144, 32)], main.at[0]),
        fetch(7, weight_in.at[:, pl.ds(96, 16)], gleft_ref),
        fetch(8, mix_in, pool.at[2]),
    ]
    second = second_part(
        head_width, pool.at[0], perm, pool.at[1], mod_ref, qkv.at[0], qkv.at[1], qkv.at[2], pool.at[2], main.at[0], gleft_ref,
        pool.at[1], gmixed, gmix, main.at[1], gleft_ref, sums_ref, pool.at[3], gb, partial,
    )
    gq, gk, gv = pool.at[0], pool.at[2], pool.at[3]
    early = jnp.where(lower, jnp.ones((1, LANES), f32), 0.0)
    carry = carry_part(
        head_width, 1, early, qkv, gmix, gq, gk, gv, pair_rows, pair_cols, taken_ref, given_ref, gate_ref, state_ref,
        leave, jnp.zeros((1, LANES), f32), vpad, gpad, taps_ref, gqkv, ggate_ref, conv_ref, bias_ref,
    )
    stores = []

    def begin():
        first[0].wait()
        first[1].wait()
        next(second)
        for copy in first[2:]:
            copy.wait()

    def out_grad():
        next(second)
        stores.append(fetch(11, main.at[1], gout_out))
        next(second)
        stores.pop().wait()

    def states():
        again = fetch(9, qkv_in, qkv)
        stores.extend([fetch(10, pool.at[1], gmid_out), fetch(12, xp_in, gb)])
        for ref in (gq, gk, gv, pair_rows, pair_cols):
            ref[...] = jnp.zeros_like(ref)
        again.wait()
        state_part(head_width, 1, lambda cols: qkv[0, :, cols], gmix, taken_ref, outbox)
        edge = pl.multiple_of((1 - here.x) * (length - GRID), GRID)

        def write_edge(t, value):
            outbox[0, width + t * GRID : width + (t + 1) * GRID, :] = value

        edge_part(gmixed[pl.ds(edge, GRID), :], write_edge)
        stores.append(push(outbox, inbox, swap_sem.at[0], swap_sem.at[1], here.over_x))

    def pairs(part):
        pairs_part(
            head_width, heads, part * heads // 4, (part + 1) * heads // 4, qkv, gmix, run_ref, runt_ref, gq, gk, gv,
            pair_rows, pair_cols, held,
        )

    def carry_first():
        swap = stores.pop()
        swap.wait_recv()
        leave[0] = inbox[0, :width, :]
        for t in range(width // LANES):
            cols = slice(t * LANES, (t + 1) * LANES)
            edge_rows = inbox[0, width + t * GRID : width + (t + 1) * GRID, :]
            rims[0, :, cols] = jnp.where(lower, 0, edge_rows).astype(bf16)
            rims[1, :, cols] = jnp.where(lower, edge_rows, 0).astype(bf16)
        fill_padded(vpad, vrims_ref, qkv[2])
        gpad[:GRID, :] = rims[0]
        gpad[GRID + length :, :] = rims[1]
        next(carry)
        swap.wait_send()

    def turn():
        stores.append(fetch(13, gqkv, gqkv_out))
        stores[1].wait()
        turned[...] = gb[...].T
        gforget_ref[...] = dot(turned[...], ggate_ref[...])
        fill_small(small, gforget_ref, conv_ref, bias_ref, flat, taps_share)
        fetch(17, small, small_out).wait()

    def weight(slot):
        buffer = main.at[slot % 2]
        if slot == 2:
            stores[3].wait()
        projection_grads(slot, turned, gqkv.at[slot], buffer, gleft_ref)
        stores.append(fetch(14 + slot, buffer, gmain_out.at[:, :, :, :, pl.ds(32 * slot, 32)]))

    chain = [begin, functools.partial(next, second), out_grad, states]
    chain += [functools.partial(pairs, part) for part in range(4)] + [carry_first]
    chain += [functools.partial(next, carry)] * 3 + [turn] + [functools.partial(weight, slot) for slot in range(3)]
    here.meet()
    scatter.start()
    in_order(BACKWARD_PLAN, chain, {"u": scatter})
    scatter.finish()
    for number in (0, 2, 4, 5):
        stores[number].wait()


def backward_fused(heads, taps_share, small, arrays, grads):
    length, width = arrays[0].shape
    head_width = width // heads
    message = width + width // LANES * GRID
    anywhere, vm = pl.BlockSpec(memory_space=pl.ANY), pl.BlockSpec(memory_space=pltpu.VMEM)
    rows, wide = (length, width), (length, LANES)
    dma = pltpu.SemaphoreType.DMA
    return pl.pallas_call(
        functools.partial(backward_kernel, head_width, heads, taps_share),
        out_shape=(
            sds(rows), sds((3,) + rows, bf16), sds((4, 2, 2, 2, 96, width), bf16), sds((4, 2, 2, 2, 32, width), bf16),
            sds((GROUPS, 48, LANES)), sds((GROUPS, 16, width), bf16), sds(wide, bf16), sds((8, width)),
            sds((144 * width // LANES, LANES)),
        ),
        in_specs=[vm] * len(small) + [anywhere] * (len(arrays) + len(grads)),
        out_specs=(anywhere,) * 5 + (vm,) * 4,
        scratch_shapes=[
            pltpu.VMEM((4,) + rows, f32), pltpu.VMEM((width, width), bf16), pltpu.VMEM(rows, bf16), pltpu.VMEM(rows, bf16),
            pltpu.VMEM((2, 4, 2, 2, 2, 32, width), bf16), pltpu.VMEM((3,) + rows, bf16), pltpu.VMEM((3,) + rows, bf16), pltpu.VMEM((2, length, length), bf16),
            pltpu.VMEM((length + 2 * GRID, width), bf16), pltpu.VMEM((length + 2 * GRID, width), bf16),
            pltpu.VMEM((2,) + wide, f32), pltpu.VMEM((2, heads, length), f32),
            pltpu.VMEM((1, message, LANES), bf16), pltpu.VMEM((1, message, LANES), bf16),
            pltpu.VMEM((2, GRID, width), bf16), pltpu.VMEM((1, width, LANES), bf16), pltpu.VMEM((16, width), f32),
            pltpu.VMEM((1, LANES), f32), pltpu.VMEM((width, LANES), f32), pltpu.VMEM((96, LANES), f32),
            pltpu.VMEM((GROUPS, 48, LANES), f32), pltpu.VMEM((3, 8, width), f32), dma((18,)), dma((2,)),
        ] + scatter_scratch(grads, BACKWARD_WAYS),
        compiler_params=pltpu.CompilerParams(
            collective_id=3, has_side_effects=True, vmem_limit_bytes=62 * 1024 * 1024
        ),
        name="backward",
    )(*small, *arrays, *[six(g) for g in grads])


def finish_kernel(
    mod_ref, sums_two, gate_two, ggate_ref, wf_ref,
    weight_in, gqkv_in, perm_in, x_in, gmid_in, gmain_in, gout_in, gleft_in, small_in,
    gin_ref, all_mod, query_ref, key_ref, value_ref, out_ref, small_ref,
    main, left, gqkv, perm, x, gmid, ghp, gh, sums_one, own_mod, partial, load_sem, *rest,
):
    width = perm.shape[0]
    here = Here()
    here.greet(True)
    scatter = Scatter(
        "a", here, [gmain_in, gout_in, gleft_in], square_final((query_ref, key_ref, value_ref, out_ref)), rest[:12]
    )
    small = Scatter("s", here, [small_in], small_final(small_ref), rest[12:24])
    gather = ShortGather("g", here, own_mod, all_mod, rest[24:])
    scatter.prepare()
    small.prepare()

    def fetch(number, source, target):
        copy = pltpu.make_async_copy(source, target, load_sem.at[number])
        copy.start()
        return copy

    def load(slot):
        return fetch(slot, weight_in.at[:, pl.ds(32 * slot, 32)], main.at[slot % 2])

    grads = fetch(3, gqkv_in, gqkv)
    rest_rows = fetch(4, weight_in.at[:, pl.ds(96, 16)], left)
    loads = [load(0), load(1)]
    others = [fetch(5, perm_in, perm), fetch(6, x_in, x), fetch(7, gmid_in, gmid)]

    def back(slot):
        if slot == 0:
            ghp[...] = dot_bt(ggate_ref[...], wf_ref[...])
            grads.wait()
            rest_rows.wait()
        loads[slot].wait()
        projection_back(slot, gqkv.at[slot], main.at[slot % 2], left, ghp)
        if slot == 0:
            loads.append(load(2))

    def last():
        for copy in others:
            copy.wait()
        last_part(ghp, perm, x, mod_ref, gmid, gin_ref, sums_one, gh, partial)
        lines = [sums_one[0:1, :], sums_one[1:2, :], sums_two[2:3, :], sums_two[0:1, :], sums_two[1:2, :], gate_two[...]]
        tiles = width // LANES
        for k, line in enumerate(lines):
            for t in range(tiles):
                own_mod[k * tiles + t : k * tiles + t + 1, :] = line[:, t * LANES : (t + 1) * LANES]
        own_mod[len(lines) * tiles :, :] = jnp.zeros_like(own_mod[len(lines) * tiles :, :])
        gather.start()

    here.meet(True)
    scatter.start()
    small.start()
    chain = [functools.partial(back, slot) for slot in range(3)] + [last]
    in_order(FINISH_PLAN, chain, {"a": scatter, "s": small, "g": gather})
    gather.arrived()
    for network in (scatter, small, gather):
        network.finish()


def results_kernel(sources, cond_ref, mod_in, *refs):
    ins, outs = refs[: len(sources)], refs[len(sources) : -4]
    all_mod, ada, sems, own_sem = refs[-4:]
    ada_out, total_ref = outs[-2:]
    copies = []
    for number, (ref, (target, low)) in enumerate(zip(ins, sources)):
        place = outs[target] if low is None else outs[target].at[pl.ds(low, ref.shape[0])]
        copies.append(pltpu.make_async_copy(ref, place, sems.at[number]))
    fetch = pltpu.make_async_copy(mod_in, all_mod, own_sem.at[0])
    for copy in [fetch] + copies:
        copy.start()
    cond = cond_ref[...]
    cond = jnp.concatenate([cond, cond, cond], axis=0)
    fetch.wait()
    tiles = ada.shape[0] // 36
    for t in range(tiles):
        rows = all_mod[:, t, :]
        high, middle = halves(rows)
        low = (rows - high.astype(f32) - middle.astype(f32)).astype(bf16)
        product = dot_at(cond, jnp.concatenate([high, middle, low], axis=0))
        ada[pl.ds(t, 36, stride=tiles), :] = product[:36]
        total_ref[t : t + 1, :] = jnp.sum(rows, axis=0, keepdims=True)
    last = pltpu.make_async_copy(ada, ada_out, own_sem.at[1])
    last.start()
    for copy in copies + [last]:
        copy.wait()


def results(pieces, cond, all_mod, ada_rows):
    flat, sources, shapes = [], [], []
    for target, arrays in enumerate(pieces):
        rows = 0
        for array in arrays:
            sources.append((target, None if len(arrays) == 1 else rows))
            flat.append(array)
            rows += array.shape[0]
        shapes.append(sds((rows,) + arrays[0].shape[1:], arrays[0].dtype))
    anywhere, vm = pl.BlockSpec(memory_space=pl.ANY), pl.BlockSpec(memory_space=pltpu.VMEM)
    dma = pltpu.SemaphoreType.DMA
    return pl.pallas_call(
        functools.partial(results_kernel, tuple(sources)),
        out_shape=tuple(shapes) + (sds((ada_rows, LANES)), sds((ada_rows // 36, LANES))),
        in_specs=[vm, anywhere, anywhere] + [vm] * (len(flat) - 1),
        out_specs=(anywhere,) * (len(shapes) + 1) + (vm,),
        scratch_shapes=[
            pltpu.VMEM(all_mod.shape, f32), pltpu.VMEM((ada_rows, LANES), f32), dma((len(flat),)), dma((2,)),
        ],
        compiler_params=pltpu.CompilerParams(vmem_limit_bytes=20 * 1024 * 1024),
        name="results",
    )(cond, all_mod, *flat)


def finish_fused(small, arrays, grads, grad_small):
    length, width = arrays[3].shape
    anywhere, vm = pl.BlockSpec(memory_space=pl.ANY), pl.BlockSpec(memory_space=pltpu.VMEM)
    rows = (length, width)
    dma = pltpu.SemaphoreType.DMA
    own = sds((64, LANES))
    return pl.pallas_call(
        finish_kernel,
        out_shape=(sds(rows), gathered_shape(own)) + (sds((36 * width // LANES, LANES)),) * 4
        + (sds(grad_small.shape[1:]),),
        in_specs=[vm] * len(small) + [anywhere] * (len(arrays) + len(grads) + 1),
        out_specs=(vm, anywhere) + (vm,) * 5,
        scratch_shapes=[
            pltpu.VMEM((2, GROUPS, 32, width), bf16), pltpu.VMEM((GROUPS, 16, width), bf16), pltpu.VMEM((3,) + rows, bf16),
            pltpu.VMEM((width, width), bf16), pltpu.VMEM(rows, bf16), pltpu.VMEM(rows, f32), pltpu.VMEM(rows, f32),
            pltpu.VMEM(rows, f32), pltpu.VMEM((8, width), f32), pltpu.VMEM(own.shape, f32),
            pltpu.VMEM((2, 8, width), f32), dma((8,)),
        ] + scatter_scratch(grads) + scatter_scratch([grad_small]) + short_gather_sems(),
        compiler_params=pltpu.CompilerParams(
            collective_id=4, has_side_effects=True, vmem_limit_bytes=VMEM_LIMIT
        ),
        name="finish",
    )(*small, *arrays, *grads, six(grad_small))


def joined_states(messages, totals, width, head_width):
    count = lax.axis_size("seq")
    place = lax.axis_index("seq")

    def grid_rows(message):
        rows = message[width:].reshape(width // LANES, GRID, LANES)
        return rows.transpose(1, 0, 2).reshape(GRID, width)

    if count == 1:
        return jnp.zeros_like(messages[:, :width]), jnp.zeros((2, GRID, width), bf16)
    if count == 2:
        got = lax.ppermute(messages[0], "seq", [(0, 1), (1, 0)])
        rows = grid_rows(got)
        return got[None, :width], jnp.stack([jnp.where(place == 1, rows, 0), jnp.where(place == 0, rows, 0)])
    forward = [(i, i + 1) for i in range(count - 1)]
    backward = [(i + 1, i) for i in range(count - 1)]
    rims = jnp.stack([
        grid_rows(lax.ppermute(messages[0], "seq", forward)), grid_rows(lax.ppermute(messages[1], "seq", backward))
    ])
    states = lax.all_gather(messages[:, :width, :], "seq").astype(f32)
    passed = lax.all_gather(totals, "seq")
    heads_of_rows = np.arange(width) // head_width
    order = jnp.arange(count)
    ahead = jnp.zeros(states.shape[2:], f32)
    behind = jnp.zeros(states.shape[2:], f32)
    for source in range(count):
        between_up = jnp.where((order > source) & (order < place), 1.0, 0.0) @ passed
        between_down = jnp.where((order < source) & (order > place), 1.0, 0.0) @ passed
        ahead = ahead + jnp.where(source < place, jnp.exp(between_up), 0.0)[heads_of_rows, None] * states[source, 0]
        behind = behind + jnp.where(source > place, jnp.exp(between_down), 0.0)[heads_of_rows, None] * states[source, 1]
    return jnp.stack([ahead, behind]).astype(bf16), rims


def split_rows(matrix):
    grouped = matrix.reshape(GROUPS, -1, matrix.shape[1])
    return grouped[:, :32], grouped[:, 32:]


def pack_whole(parts, width):
    query, key, value, out, up, down = parts
    square = [piece.reshape(GROUPS, -1, width) for piece in (query, key, value, out)]
    up = up.reshape(GROUPS, square[0].shape[1], -1, width)
    columns = [up[:, :, j] for j in range(up.shape[2])]
    blocks = []
    for group in (square, columns):
        blocks.append(
            jnp.concatenate([piece[:, :32] for piece in group] + [piece[:, 32:] for piece in group], axis=1)
        )
    return blocks + [down.reshape(GROUPS, -1, width)]


def unpack_squares(block):
    return [
        jnp.concatenate([block[..., 32 * j : 32 * j + 32, :], block[..., 128 + 4 * j : 132 + 4 * j, :]], axis=-2)
        for j in range(4)
    ]


def unpack_blocks(blocks):
    squares = unpack_squares(blocks[0])
    columns = unpack_squares(blocks[1])
    lead = blocks[0].shape[:-2]
    up = jnp.stack(columns, axis=-2)
    return [piece.reshape(lead + (-1,)) for piece in squares] + [up.reshape(lead + (-1,)), blocks[2].reshape(lead + (-1,))]


def on_device(
    activations, conditioning, cotangent, w_ada, b_ada, w_query, w_key, w_value, w_forget, b_forget, conv_taps, w_out,
    w_up, w_down,
):
    _, length, width = activations.shape
    heads = b_forget.shape[0]
    head_width = width // heads
    data_count, seq_count = lax.axis_size("dp"), lax.axis_size("seq")
    devices = data_count * seq_count
    me = lax.axis_index("dp") * seq_count + lax.axis_index("seq")
    packed_here = (data_count, seq_count) == (16, 2)
    everywhere = ("dp", "seq")

    mod_width = 6 * width
    share = w_ada.shape[0]
    if share % mod_width == 0:
        ada_rows = share // mod_width
        first_row, inset = me * ada_rows, None
        ada_part = w_ada.reshape(ada_rows, mod_width)
    else:
        ada_rows = -(-share // mod_width) + 1
        first_row = (me * share) // mod_width
        inset = me * share - first_row * mod_width
        ada_part = lax.dynamic_update_slice(jnp.zeros((ada_rows * mod_width,), bf16), w_ada, (inset,))
        ada_part = ada_part.reshape(ada_rows, mod_width)

    def own_columns(cond_all):
        cond_act = jax.nn.silu(cond_all.astype(f32)).astype(bf16)
        cond_wide = jnp.pad(cond_act, ((0, 0), (0, ada_rows)))
        return lax.dynamic_slice_in_dim(cond_wide, first_row, ada_rows, axis=1)

    main_rows = 32 * GROUPS
    forget_b = jnp.pad(b_forget.astype(f32), (0, LANES - heads)).reshape(1, LANES)
    x = activations[0]
    cot = cotangent[0]
    rows = (length, width)

    def main_spec(block, columns=width):
        return pl.BlockSpec((GROUPS, 32, columns), block)

    def left_spec(block, columns=width):
        return pl.BlockSpec((GROUPS, 16, columns), block)

    def whole(shape):
        return pl.BlockSpec(shape, lambda *_: (0,) * len(shape))

    ways = 1 if seq_count == 2 else 2
    message_rows = width + width // LANES * GRID
    state_call = call(
        functools.partial(state_kernel, head_width, ways), sds((ways, message_rows, LANES), bf16), "states"
    )
    place = lax.axis_index("seq")

    def edges(values):
        low, high = values[:GRID], values[-GRID:]
        if ways == 1:
            return jnp.where(place == 0, high, low)[None]
        return jnp.stack([high, low])

    shards = (w_query, w_key, w_value, w_out, w_up, w_down)
    if packed_here:
        small = small_rows(conditioning[0], w_forget, conv_taps, me)
        bias = lax.dynamic_update_slice(jnp.zeros((mod_width,), bf16), b_ada, (me * b_ada.shape[0],)).reshape(-1, LANES)
        (small, attention_w, up_w), bulk, kept = forward_fused(
            x, w_ada.reshape(-1, LANES), bias, forget_b, small, [piece.reshape(-1, LANES) for piece in shards[:5]], heads, conv_taps.shape[0]
        )
        xp, qkv, mix, mixed_p, branch, middle, hidden_two_p, perm = bulk
        mod, forget_p, taps, gate_pre, run, runt, states, value_rims, given, taken, cond_mine = kept
        output, ghp_two, gup_main, gup_left, ggate_two, g_down = feed_fused(
            hidden_two_p, cot, mod, w_down.reshape(-1, LANES), up_w, middle
        )
    else:
        lanes_at = np.arange(width)
        per_group = width // GROUPS
        order = np.where(
            lanes_at < main_rows,
            lanes_at // 32 * per_group + lanes_at % 32,
            (lanes_at - main_rows) // 4 * per_group + 32 + (lanes_at - main_rows) % 4,
        )
        perm = (jnp.arange(width, dtype=jnp.int32)[:, None] == jnp.asarray(order, jnp.int32)[None, :]).astype(bf16)
        small = [w_forget, conv_taps, b_ada]
        sizes = np.cumsum([0] + [piece.shape[0] for piece in small])
        small = lax.all_gather(jnp.concatenate(small), everywhere)
        forget_w = small[:, : sizes[1]].reshape(width, heads)
        taps = small[:, sizes[1] : sizes[2]].reshape(10, width).astype(f32)
        taps = jnp.pad(taps, ((0, 6), (0, 0)))
        ada_bias = small[:, sizes[2] :].reshape(6, width).astype(f32)
        forget_main, forget_left = split_rows(forget_w)
        forget_p = jnp.concatenate([forget_main.reshape(-1, heads), forget_left.reshape(-1, heads)])
        forget_p = jnp.pad(forget_p, ((0, 0), (0, LANES - heads)))
        cond_part = own_columns(lax.all_gather(conditioning, "dp", axis=0, tiled=True))
        partial_mod = jnp.dot(cond_part, ada_part, preferred_element_type=f32)
        mod = lax.psum(lax.psum_scatter(partial_mod, "dp", scatter_dimension=0, tiled=True), "seq")
        mod = jnp.pad(mod.reshape(6, width) + ada_bias, ((0, 2), (0, 0)))
        blocks = pack_whole([lax.all_gather(s, everywhere, axis=0, tiled=True) for s in shards], width)
        attention_w, up_w, down_w = blocks
        down_w = down_w.reshape(-1, width)
        xp, gate_pre, run, runt = call(
            first_part,
            (sds(rows, bf16), sds((length, LANES)), sds((2, length, LANES)), sds((2, LANES, length))),
            "first_norm",
            scratch_shapes=[pltpu.VMEM(rows, bf16)],
        )(x, mod, perm, forget_p, forget_b)
        qkv = call(
            project_kernel,
            sds((3,) + rows, bf16),
            "project",
            grid=(3,),
            in_specs=[whole(rows), main_spec(lambda j: (0, j, 0)), left_spec(lambda j: (0, 8, 0))],
            out_specs=pl.BlockSpec((1,) + rows, lambda j: (j, 0, 0)),
        )(xp, attention_w, attention_w)
        total = run[0, -1]
        given = jnp.stack([jnp.exp(total - run[0]), jnp.exp(run[1])])
        taken = jnp.stack([jnp.exp(run[0]), jnp.exp(total - run[1])])
        if ways == 1:
            given = jnp.where(place == 0, given[0], given[1])[None]
            taken = jnp.where(place == 0, taken[1], taken[0])[None]
        messages = state_call(qkv[1], qkv[2], given, edges(qkv[2]))
        states, value_rims = joined_states(messages, total, width, head_width)
        mix_local = call(
            functools.partial(mix_kernel, head_width, heads), sds(rows), "mix"
        )(qkv, run, runt)
        mix, mixed_p, branch, middle, hidden_two_p = call(
            functools.partial(after_kernel, head_width, ways),
            (sds(rows), sds(rows, bf16), sds(rows, bf16), sds(rows), sds(rows, bf16)),
            "after",
            grid=(1,),
            in_specs=[
                whole(rows), whole((8, width)), whole((width, width)), whole((3,) + rows), whole(rows),
                whole((ways, length, LANES)), whole((ways, width, LANES)), whole((2, GRID, width)), whole((16, width)),
                main_spec(lambda i: (0, 3, 0)), left_spec(lambda i: (0, 8, 0)),
            ],
            out_specs=[whole(rows)] * 5,
            scratch_shapes=[pltpu.VMEM((length + 2 * GRID, width), bf16), pltpu.VMEM(rows, bf16)],
        )(x, mod, perm, qkv, mix_local, taken, states, value_rims, taps, attention_w, attention_w)
        output, ghp_two, gup_main, gup_left, gdown, ggate_two = call(
            feed_kernel,
            (
                sds(rows, bf16), sds(rows), sds((GROUPS, 128, width), bf16), sds((GROUPS, 16, width), bf16),
                sds(down_w.shape, bf16), sds((1, width)),
            ),
            "feed",
            grid=(4,),
            in_specs=[
                whole(rows), whole(rows), whole((8, width)), whole(rows), main_spec(lambda j: (0, j, 0)),
                left_spec(lambda j: (0, 8, 0)), pl.BlockSpec((width, width), lambda j: (j, 0)),
            ],
            out_specs=[
                whole(rows), whole(rows), main_spec(lambda j: (0, j, 0)), left_spec(lambda j: (0, 0, 0)),
                pl.BlockSpec((width, width), lambda j: (j, 0)), whole((1, width)),
            ],
            scratch_shapes=[
                pltpu.VMEM(rows, f32), pltpu.VMEM(rows, bf16), pltpu.VMEM((width, length), bf16), pltpu.VMEM(rows, bf16),
                pltpu.VMEM((width, length), bf16), pltpu.VMEM(rows, bf16), pltpu.VMEM((width - main_rows, width), bf16),
            ],
        )(hidden_two_p, cot, mod, middle, up_w, up_w, down_w)

    share_forget, share_taps, share_bias = w_forget.shape[0], conv_taps.shape[0], b_ada.shape[0]

    if packed_here:
        grad_middle, gqkv, gmain, gout_main, grad_small, gleft, grad_gate, sums_two, g_up = backward_fused(
            heads,
            share_taps,
            (mod, run, runt, taken, given, gate_pre, states, value_rims, taps),
            (ghp_two, perm, middle, cot, branch, mixed_p, mix, attention_w, six(up_w), qkv, xp),
            (gup_main, gup_left),
        )
        grad_input, mod_all, g_query, g_key, g_value, g_out, grad_small = finish_fused(
            (mod, sums_two, ggate_two, grad_gate, forget_p), (attention_w, gqkv, perm, x, grad_middle),
            (gmain, gout_main, six(gleft)), grad_small,
        )
        g_forget = grad_small[:36, :heads].reshape(-1)
        g_taps = lax.dynamic_slice(grad_small[36:40].reshape(-1), (lax.rem(me * share_taps, LANES),), (share_taps,))
        grad_bias = grad_small[40, :heads]
        *shares, grad_ada, mod_sum = results(
            [[output], [grad_input], [g_query], [g_key], [g_value], [g_out], [g_up], [g_down]], cond_mine,
            mod_all.reshape(devices, 64, LANES), share // LANES,
        )
        output, grad_input, *shares = shares
        shares = [piece.reshape(-1) for piece in shares]
        grad_ada, mod_sum = grad_ada.reshape(-1), mod_sum.reshape(-1)
    else:
        grad_middle, grad_mixed, grad_mix, gout_main, gout_left, sums_two = call(
            functools.partial(second_kernel, head_width),
            (
                sds(rows), sds(rows, bf16), sds(rows, bf16), sds((GROUPS, 32, width), bf16),
                sds((GROUPS, 16, width), bf16), sds((8, width)),
            ),
            "second_norm",
            grid=(1,),
            in_specs=[
                whole(rows), whole((width, width)), whole(rows), whole((8, width)), whole(rows), whole(rows), whole(rows),
                whole(rows), main_spec(lambda i: (0, 3, 0)), left_spec(lambda i: (0, 8, 0)),
            ],
            out_specs=[
                whole(rows), whole(rows), whole(rows), whole((GROUPS, 32, width)), whole((GROUPS, 16, width)),
                whole((8, width)),
            ],
            scratch_shapes=[
                pltpu.VMEM(rows, f32), pltpu.VMEM(rows, bf16), pltpu.VMEM((3, 8, width), f32),
            ],
        )(ghp_two, perm, middle, mod, cot, branch, mixed_p, mix, attention_w, attention_w)

        back = state_call(qkv[0], grad_mix, taken, edges(grad_mixed))
        if ways == 2:
            back = jnp.stack([
                jnp.concatenate([back[1, :width], back[0, width:]]), jnp.concatenate([back[0, :width], back[1, width:]])
            ])
        leaving, grad_rims = joined_states(back, total, width, head_width)
        if ways == 2:
            leaving = leaving[::-1]

        gq_local, gk_local, gv_local, pair_rows, pair_cols = call(
            functools.partial(pairs_kernel, head_width, heads),
            (sds(rows), sds(rows), sds(rows), sds((2, length, LANES)), sds((2, heads, length))),
            "pairs",
            scratch_shapes=[pltpu.VMEM((2, length, length), bf16)],
        )(qkv, grad_mix, run, runt)
        if seq_count > 2:
            rows_through = jnp.sum(states.astype(f32) * leaving.astype(f32), axis=(0, 2))
            through = jnp.exp(total[:heads]) * jnp.sum(rows_through.reshape(heads, head_width), axis=1)
            through = jnp.pad(through, (0, LANES - heads)).reshape(1, LANES)
        else:
            through = jnp.zeros((1, LANES), f32)
        early = jnp.where(place == 0, jnp.ones((1, LANES), f32), 0.0)

        pad_scratch = pltpu.VMEM((length + 2 * GRID, width), bf16)
        gqkv, grad_gate, grad_conv, grad_bias = call(
            functools.partial(carry_kernel, head_width, ways),
            (sds((3,) + rows, bf16), sds((length, LANES), bf16), sds((16, width)), sds((1, LANES))),
            "carry",
            scratch_shapes=[pad_scratch, pad_scratch],
        )(
            qkv, grad_mix, gq_local, gk_local, gv_local, pair_rows, pair_cols, taken, given, gate_pre, states, leaving,
            through, early, grad_mixed, grad_rims, value_rims, taps,
        )
        gmain, gleft, gforget, ghp_one = call(
            weights_kernel,
            (sds((GROUPS, 96, width), bf16), sds((GROUPS, 16, width), bf16), sds((width, LANES)), sds(rows)),
            "weights",
            grid=(3,),
            in_specs=[
                whole(rows), pl.BlockSpec((1,) + rows, lambda j: (j, 0, 0)), whole((length, LANES)),
                whole((width, LANES)), main_spec(lambda j: (0, j, 0)), left_spec(lambda j: (0, 8, 0)),
                left_spec(lambda j: (0, 0, 0)),
            ],
            out_specs=[
                main_spec(lambda j: (0, j, 0)), left_spec(lambda j: (0, 0, 0)), whole((width, LANES)), whole(rows),
            ],
            scratch_shapes=[pltpu.VMEM((width, length), bf16)],
        )(xp, gqkv, grad_gate, forget_p, attention_w, attention_w, gout_left)
        grad_input, sums_one = call(
            last_part, (sds(rows), sds((8, width))), "last_norm",
            scratch_shapes=[pltpu.VMEM(rows, f32), pltpu.VMEM((2, 8, width), f32)],
        )(ghp_one, perm, x, mod, grad_middle)

        gforget = gforget[:, :heads]
        gforget = jnp.concatenate(
            [gforget[:main_rows].reshape(GROUPS, 32, heads), gforget[main_rows:].reshape(GROUPS, 4, heads)], axis=1
        )
        grad_small = jnp.concatenate([gforget.reshape(devices, -1), grad_conv[:10].reshape(devices, -1)], axis=1)
        grad_small = lax.psum_scatter(grad_small, everywhere, scatter_dimension=0, tiled=True).reshape(-1)
        g_forget, g_taps = grad_small[:share_forget], grad_small[share_forget:]
        grad_bias = lax.psum(grad_bias[0, :heads], everywhere)
        grads = [
            jnp.concatenate([gmain, gout_main, gleft], axis=1), jnp.concatenate([gup_main, gup_left], axis=1),
            gdown.reshape(GROUPS, -1, width),
        ]
        shares = [
            lax.psum_scatter(g.reshape(-1), everywhere, scatter_dimension=0, tiled=True).astype(f32)
            for g in unpack_blocks(grads)
        ]
        grad_mod = jnp.concatenate([sums_one[:2], sums_two[2:3], sums_two[:2], ggate_two])
        mod_all = lax.all_gather(grad_mod.reshape(1, mod_width), everywhere, axis=0, tiled=True)

        mod_all = jnp.sum(mod_all.reshape(data_count, seq_count, mod_width), axis=1)
        mod_sum = jnp.sum(mod_all, axis=0)
        grad_ada = jnp.dot(cond_part.astype(f32).T, mod_all, precision=lax.Precision.HIGHEST).reshape(-1)
        if inset is not None:
            grad_ada = lax.dynamic_slice(grad_ada, (inset,), (share,))
    grad_ada_bias = lax.dynamic_slice(mod_sum, (me * share_bias,), (share_bias,))
    g_query, g_key, g_value, g_out, g_up, g_down = shares
    return (
        output[None], grad_input[None], grad_ada, grad_ada_bias, g_query, g_key, g_value, g_forget,
        grad_bias, g_taps, g_out, g_up, g_down,
    )


def solution(mesh):
    rows = P("dp", "seq", None)
    shard = P(("dp", "seq"))
    return jax.shard_map(
        on_device,
        mesh=mesh,
        in_specs=(
            rows, P("dp", None), rows, shard, shard, shard, shard, shard, shard, P(), shard, shard, shard, shard,
        ),
        out_specs=(
            rows, rows, shard, shard, shard, shard, shard, shard, P(), shard, shard, shard, shard,
        ),
        check_vma=False,
    )
```

```python
import functools

import jax
import jax.numpy as jnp
import numpy as np
from jax import lax
from jax.experimental import pallas as pl
from jax.experimental.pallas import tpu as pltpu
from jax.sharding import PartitionSpec as P

GRID = 32
LANES = 128
GROUPS = 32
epsilon = 1e-06
f32 = jnp.float32
bf16 = jnp.bfloat16
VMEM_LIMIT = 56 * 1024 * 1024
FORWARD_PLAN = (
    ("f", 0, 0, 0), ("g", 0, 0, 0), -1, ("g", 0, 1, 0), ("f", 1, 0, 0), ("g", 2, 0, 0), ("g", 1, 0, 0),
    ("g", 3, 0, 0), ("g", 0, 0, 1), ("f", 2, 0, 0), ("g", 1, 1, 0), ("g", 2, 1, 0), -1, ("g", 0, 0, 2),
    ("g", 4, 0, 0), ("g", 5, 0, 0), ("g", 2, 0, 1), ("g", 1, 0, 1), -1, ("s", 0, 0, 0), ("g", 2, 0, 2),
    ("g", 1, 0, 2), ("g", 0, 0, 3), ("g", 4, 0, 1), ("g", 5, 0, 1), ("g", 3, 1, 0), ("s", 1, 0, 0), ("g", 0, 1, 1),
    ("g", 1, 0, 3), ("g", 2, 0, 3), ("g", 4, 0, 2), ("g", 5, 0, 2), ("s", 2, 0, 0), -1, ("g", 2, 1, 1),
    ("g", 1, 1, 1), ("g", 4, 1, 0), ("g", 5, 1, 0), ("g", 4, 0, 3), ("g", 5, 0, 3), ("g", 0, 1, 2), ("g", 4, 1, 1),
    ("g", 5, 1, 1), ("g", 1, 1, 2), -1, ("g", 2, 1, 2), -1, ("g", 0, 1, 3), -1, -1, ("g", 4, 1, 2), ("g", 5, 1, 2),
    ("g", 2, 1, 3), -1, -1, ("g", 1, 1, 3), -1, ("g", 4, 1, 3), -1, -1, ("g", 5, 1, 3), -1, -1, -1,
)
FEED_PLAN = (
    ("g", 0, 0, 0), -1, -1, ("g", 2, 0, 0), ("g", 1, 0, 0), ("g", 3, 0, 0), ("g", 0, 0, 1), -1, -1, ("g", 0, 0, 2),
    ("g", 4, 0, 0), ("g", 5, 0, 0), ("d", 0, 0, 0), ("g", 2, 0, 1), ("d", 4, 0, 0), -1, ("g", 1, 0, 1),
    ("g", 2, 0, 2), -1, ("g", 0, 0, 3), ("g", 1, 0, 2), ("d", 1, 0, 0), ("d", 2, 0, 0), ("d", 0, 0, 1),
    ("g", 4, 0, 1), -1, -1, ("g", 5, 0, 1), ("g", 2, 0, 3), ("d", 4, 0, 1), ("d", 0, 0, 2), -1, ("g", 1, 0, 3),
    ("g", 4, 0, 2), ("g", 5, 0, 2), -1, ("d", 3, 0, 0), -1, ("d", 4, 0, 2), ("d", 0, 0, 3), ("d", 2, 0, 1),
    ("d", 1, 0, 1), -1, -1, ("g", 4, 0, 3), -1, ("d", 1, 0, 2), ("d", 2, 0, 2), -1, ("g", 5, 0, 3), ("d", 2, 0, 3),
    -1, -1, ("d", 4, 0, 3), ("d", 1, 0, 3), -1, ("d", 3, 0, 1), ("d", 5, 0, 0), -1, -1, -1, -1, ("d", 3, 0, 2), -1,
    -1, -1, -1, ("d", 3, 0, 3), ("d", 5, 0, 1),
)
BACKWARD_PLAN = (
    -1, ("u", 0, 0, 0), -1, -1, ("u", 0, 0, 1), -1, ("u", 1, 0, 0), -1, -1, ("u", 0, 0, 2), ("u", 3, 0, 0),
    ("u", 1, 0, 1), -1, -1, ("u", 3, 0, 1), -1, ("u", 0, 0, 3), -1, ("u", 1, 0, 2), -1, -1, -1, ("u", 3, 0, 2), -1,
    ("u", 1, 0, 3), -1, -1, ("u", 3, 0, 3),
)
FINISH_PLAN = (
    -1, ("a", 0, 0, 0), ("a", 4, 0, 0), -1, -1, ("a", 0, 0, 1), -1, ("g", 0, 0, 0), ("a", 2, 0, 0), ("a", 1, 0, 0),
    ("s", 0, 0, 0), ("s", 0, 0, 1), ("s", 0, 0, 2), ("a", 4, 0, 1), ("s", 0, 0, 3), ("g", 1, 0, 0), ("s", 1, 0, 0),
    ("s", 1, 0, 1), ("s", 2, 0, 0), ("s", 2, 0, 1), ("s", 1, 0, 2), ("s", 2, 0, 2), ("s", 2, 0, 3), ("s", 1, 0, 3),
    ("a", 3, 0, 0), ("a", 2, 0, 1), ("a", 1, 0, 1), ("s", 3, 0, 0), ("g", 2, 0, 0), ("a", 0, 0, 2), ("a", 4, 0, 2),
    ("s", 3, 0, 1), ("a", 0, 0, 3), ("a", 3, 0, 1), ("a", 1, 0, 2), ("s", 3, 0, 2), ("a", 2, 0, 2), ("a", 4, 0, 3),
    ("a", 2, 0, 3), ("a", 1, 0, 3), ("s", 3, 0, 3), ("a", 3, 0, 2), ("a", 5, 0, 0), ("a", 3, 0, 3), ("a", 5, 0, 1),
)
FEED_WAYS, BACKWARD_WAYS = (3, 3), 1


def dot(a, b):
    return jnp.dot(a, b, preferred_element_type=f32)


def dot_bt(a, b):
    return lax.dot_general(a, b, (((1,), (1,)), ((), ())), preferred_element_type=f32)


def dot_at(a, b):
    return lax.dot_general(a, b, (((0,), (0,)), ((), ())), preferred_element_type=f32)


def halves(a):
    high = a.astype(bf16)
    return high, (a - high.astype(f32)).astype(bf16)


def spans(width, size=512):
    return [slice(start, min(start + size, width)) for start in range(0, width, size)]


def head_lanes(rows, width, start, head_width):
    head = lax.broadcasted_iota(jnp.int32, (rows, width), 0)
    lane = lax.broadcasted_iota(jnp.int32, (rows, width), 1) + start
    return (lane >= head * head_width) & (lane < (head + 1) * head_width)


def pick_left(rows, slot):
    out = lax.broadcasted_iota(jnp.int32, (4 * GROUPS, 16 * GROUPS), 0)
    src = lax.broadcasted_iota(jnp.int32, (4 * GROUPS, 16 * GROUPS), 1)
    return (src == (out // 4) * 16 + slot * 4 + out % 4).astype(bf16)


def norm_parts(values):
    center = jnp.mean(values, axis=-1, keepdims=True)
    centered = values - center
    spread = jnp.mean(centered * centered, axis=-1, keepdims=True)
    rstd = lax.rsqrt(spread + epsilon)
    return centered * rstd, rstd


def row_loop(length, body):
    size = min(length, 64)

    @pl.loop(0, length // size)
    def _(r):
        body(pl.ds(pl.multiple_of(r * size, size), size))


def eight_rows(values):
    return jnp.sum(values.reshape(-1, 8, values.shape[1]), axis=0)


def call(kernel, out_shape, name, **kw):
    return pl.pallas_call(
        kernel,
        out_shape=out_shape,
        name=name,
        compiler_params=pltpu.CompilerParams(vmem_limit_bytes=VMEM_LIMIT),
        **kw,
    )


def sds(shape, dtype=f32):
    return jax.ShapeDtypeStruct(shape, dtype)


def first_part(x_ref, mod_ref, perm_ref, wf_ref, bf_ref, xp_ref, gate_ref, run_ref, runt_ref, hidden_ref):
    length = x_ref.shape[0]

    def norm(rows):
        normed, _ = norm_parts(x_ref[rows, :].astype(f32))
        hidden_ref[rows, :] = (normed * (1.0 + mod_ref[1:2, :]) + mod_ref[0:1, :]).astype(bf16)

    row_loop(length, norm)
    for cols in spans(x_ref.shape[1]):
        xp_ref[:, cols] = dot(hidden_ref[...], perm_ref[:, cols]).astype(bf16)

    gate = dot(xp_ref[...], wf_ref[...]) + bf_ref[...]
    gate_ref[...] = gate
    decay = -(jnp.maximum(gate, 0.0) + jnp.log1p(jnp.exp(-jnp.abs(gate))))
    row = lax.broadcasted_iota(jnp.int32, (length, length), 0)
    col = lax.broadcasted_iota(jnp.int32, (length, length), 1)
    tri = (row >= col).astype(bf16)
    high, rest = halves(decay)
    rest32 = decay - high.astype(f32)
    low = (rest32 - rest.astype(f32)).astype(bf16)
    inclusive = dot(tri, high) + dot(tri, rest) + dot(tri, low)
    exclusive = inclusive - decay
    run_ref[0] = inclusive
    run_ref[1] = exclusive
    runt_ref[0] = inclusive.T
    runt_ref[1] = exclusive.T


def project_part(slot, xp_ref, main_ref, left_ref, write):
    pick = pick_left(None, slot)
    main_rows = rows_in(main_ref)

    for cols in spans(xp_ref.shape[1]):
        main = main_ref[..., cols].reshape(main_rows, -1)
        left = dot(pick, left_ref[..., cols].reshape(16 * GROUPS, -1)).astype(bf16)
        write(cols, dot(xp_ref[:, :main_rows], main) + dot(xp_ref[:, main_rows:], left))


def two_terms(scale):
    return jnp.concatenate(halves(scale), axis=1)


def spread_heads(terms, cols, head_width):
    spread = head_lanes(LANES, cols.stop - cols.start, cols.start, head_width).astype(bf16)
    return dot(terms, jnp.concatenate([spread, spread], axis=0))


def head_sums(values, cols, head_width):
    return dot_bt(values, head_lanes(LANES, cols.stop - cols.start, cols.start, head_width).astype(bf16))


def own_block(shape, row_start, lane_start, head_width):
    row = lax.broadcasted_iota(jnp.int32, (shape[0], 1), 0) + row_start
    lane = lax.broadcasted_iota(jnp.int32, (1, shape[1]), 1) + lane_start
    same = None
    for head in range(
        max(row_start, lane_start) // head_width,
        min(row_start + shape[0] - 1, lane_start + shape[1] - 1) // head_width + 1,
    ):
        low, high = head * head_width, (head + 1) * head_width
        both = ((row >= low) & (row < high)) & ((lane >= low) & (lane < high))
        same = both if same is None else same | both
    if same is None:
        return jnp.broadcast_to(row < 0, shape)
    return same


def group_rows(ref, cols):
    per = rows_in(ref) // ref.shape[0]
    return ref[cols.start // per : cols.stop // per].reshape(-1, ref.shape[-1])


def rows_in(ref):
    return int(np.prod(ref.shape[:-1]))


def near_lanes(cols, width, head_width):
    low = cols.start // head_width * head_width // LANES * LANES
    last = (cols.stop - 1) // head_width
    return slice(low, min(width, -(-(last + 1) * head_width // LANES) * LANES))


def unfolded(ref, way, near, cols, head_width):
    folded = ref[way, near, :]
    return jnp.concatenate([
        jnp.where(own_block(folded.shape, near.start, at, head_width), folded, 0)
        for at in range(cols.start, cols.stop, LANES)
    ], axis=1)


def state_part(head_width, ways, left, right_ref, scale_ref, out_ref):
    width = right_ref.shape[1]
    terms = [two_terms(scale_ref[way]) for way in range(ways)]
    for cols in spans(width, 2 * LANES):
        near = near_lanes(cols, width, head_width)
        mask = own_block((cols.stop - cols.start, near.stop - near.start), cols.start, near.start, head_width)
        for way in range(ways):
            scaled = left(cols).astype(f32) * spread_heads(terms[way], cols, head_width)
            product = jnp.where(mask, dot_at(scaled.astype(bf16), right_ref[:, near]), 0.0)
            total = product[:, :LANES]
            for at in range(LANES, near.stop - near.start, LANES):
                total = total + product[:, at : at + LANES]
            out_ref[way, cols, :] = total.astype(bf16)


def edge_part(source, out):
    for t in range(source.shape[1] // LANES):
        out(t, source[:, t * LANES : (t + 1) * LANES])


def pair_weights(run_ref, runt_ref, head, rows, length):
    count = rows.size
    own = lax.broadcasted_iota(jnp.int32, (count, LANES), 1) == head
    inc_t = jnp.sum(jnp.where(own, run_ref[0, rows, :], 0.0), axis=1, keepdims=True)
    exc_t = jnp.sum(jnp.where(own, run_ref[1, rows, :], 0.0), axis=1, keepdims=True)
    inc_s = runt_ref[0, pl.ds(head, 1), :]
    exc_s = runt_ref[1, pl.ds(head, 1), :]
    weight = jnp.exp(jnp.minimum(inc_t - inc_s, exc_s - exc_t))
    row = lax.broadcasted_iota(jnp.int32, (count, length), 0) + rows.start
    col = lax.broadcasted_iota(jnp.int32, (count, length), 1)
    return jnp.where(row == col, 2.0, weight)


def window_of(head, heads, head_width):
    start = pl.multiple_of(((head * head_width) // LANES - head // (heads - 1)) * LANES, LANES)
    return pl.ds(start, 2 * LANES), start


def own_lanes(rows, start, head, head_width):
    lane = lax.broadcasted_iota(jnp.int32, (rows, 2 * LANES), 1) + start
    return (lane >= head * head_width) & (lane < (head + 1) * head_width)


def row_blocks(length, size):
    size = min(length, size)
    return [pl.ds(start, size) for start in range(0, length, size)]


def mix_part(head_width, heads, low, high, qkv_ref, run_ref, runt_ref, mix_ref):
    length, width = mix_ref.shape

    @pl.loop(low // 2, high // 2)
    def _(pair):
        for odd in range(2):
            head = pair * 2 + odd
            win, start = window_of(head, heads, head_width)
            mask = own_lanes(length, start, head, head_width)
            keys = jnp.where(mask, qkv_ref[1, :, win], 0)
            vals = jnp.where(mask, qkv_ref[2, :, win], 0)
            for rows in row_blocks(length, 2 * LANES):
                weight = pair_weights(run_ref, runt_ref, head, rows, length)
                score = dot_bt(qkv_ref[0, rows, win], keys)
                mix_ref[rows, win] += dot((score * weight).astype(bf16), vals)


def fill_padded(pad_ref, rims_ref, middle):
    length = pad_ref.shape[0] - 2 * GRID
    pad_ref[:GRID, :] = rims_ref[0]
    pad_ref[GRID : GRID + length, :] = middle
    pad_ref[GRID + length :, :] = rims_ref[1]


def mixed_part(head_width, ways, qkv_ref, taken_ref, state_ref, taps_ref, vpad, mix_ref, mixed):
    length, width = mix_ref.shape
    place = lax.broadcasted_iota(jnp.int32, (length, LANES), 0) % GRID
    sums = jnp.zeros((length, LANES), f32)
    terms = [two_terms(taken_ref[way]) for way in range(ways)]
    for cols in spans(width, 2 * LANES):
        gained = mix_ref[:, cols]
        near = near_lanes(cols, width, head_width)
        for way in range(ways):
            block = unfolded(state_ref, way, near, cols, head_width)
            gained = gained + spread_heads(terms[way], cols, head_width) * dot(qkv_ref[0, :, near], block)
        mix_ref[:, cols] = gained
        sums = sums + head_sums((gained * gained).astype(bf16), cols, head_width)
    inverse = two_terms(lax.rsqrt(sums * (1.0 / head_width) + epsilon))
    for span in spans(width, 2 * LANES):
        normed = mix_ref[:, span] * spread_heads(inverse, span, head_width)
        for start in range(span.start, span.stop, LANES):
            cols = slice(start, start + LANES)
            conv = jnp.zeros((length, LANES), f32)
            for lateral in range(3):
                column = jnp.zeros((length, LANES), f32)
                for vertical in range(3):
                    tap = taps_ref[3 * vertical + lateral : 3 * vertical + lateral + 1, cols]
                    column = column + tap * vpad[vertical * GRID : vertical * GRID + length, cols].astype(f32)
                if lateral == 0:
                    column = jnp.where(place > 0, pltpu.roll(column, 1, 0), 0.0)
                if lateral == 2:
                    column = jnp.where(place < GRID - 1, pltpu.roll(column, length - 1, 0), 0.0)
                conv = conv + column
            own = normed[:, start - span.start : start - span.start + LANES]
            mixed[:, cols] = (own + (conv + taps_ref[9:10, cols])).astype(bf16)


def permute_part(source, perm_ref, out_ref):
    for cols in spans(perm_ref.shape[1]):
        out_ref[:, cols] = dot(source[...], perm_ref[:, cols]).astype(bf16)


def branch_part(x_ref, mod_ref, mixedp_ref, main_ref, left_ref, branch_ref, middle_ref):
    def write(cols, branch):
        branch_ref[:, cols] = branch.astype(bf16)
        middle_ref[:, cols] = x_ref[:, cols].astype(f32) + mod_ref[2:3, cols] * branch

    project_part(3, mixedp_ref, main_ref, left_ref, write)


def second_hidden(mod_ref, middle_ref, mixed):
    def norm(rows):
        normed, _ = norm_parts(middle_ref[rows, :])
        mixed[rows, :] = (normed * (1.0 + mod_ref[4:5, :]) + mod_ref[3:4, :]).astype(bf16)

    row_loop(mixed.shape[0], norm)


def project_kernel(xp_ref, main_ref, left_ref, out_ref):
    def write(cols, value):
        out_ref[0, :, cols] = value.astype(bf16)

    project_part(pl.program_id(0), xp_ref, main_ref, left_ref, write)


def state_kernel(head_width, ways, left_ref, right_ref, scale_ref, edge_ref, out_ref):
    width = right_ref.shape[1]
    state_part(head_width, ways, lambda cols: left_ref[:, cols], right_ref, scale_ref, out_ref)
    for way in range(ways):

        def write(t, value, way=way):
            out_ref[way, width + t * GRID : width + (t + 1) * GRID, :] = value

        edge_part(edge_ref[way], write)


def mix_kernel(head_width, heads, qkv_ref, run_ref, runt_ref, mix_ref):
    mix_ref[...] = jnp.zeros_like(mix_ref)
    mix_part(head_width, heads, 0, heads, qkv_ref, run_ref, runt_ref, mix_ref)


def after_kernel(
    head_width, ways, x_ref, mod_ref, perm_ref, qkv_ref, mix_in_ref, taken_ref, state_ref, rims_ref, taps_ref,
    main_ref, left_ref, mix_ref, mixedp_ref, branch_ref, middle_ref, h2p_ref, vpad, mixed,
):
    mix_ref[...] = mix_in_ref[...]
    fill_padded(vpad, rims_ref, qkv_ref[2])
    mixed_part(head_width, ways, qkv_ref, taken_ref, state_ref, taps_ref, vpad, mix_ref, mixed)
    permute_part(mixed, perm_ref, mixedp_ref)
    branch_part(x_ref, mod_ref, mixedp_ref, main_ref, left_ref, branch_ref, middle_ref)
    second_hidden(mod_ref, middle_ref, mixed)
    permute_part(mixed, perm_ref, h2p_ref)


def gelu_both(v):
    c = np.float32(np.sqrt(2.0 / np.pi))
    square = v * v
    th = jnp.tanh(c * (v + np.float32(0.044715) * (square * v)))
    half = 0.5 * (1.0 + th)
    slope = half + 0.5 * v * (1.0 - th * th) * (c * (1.0 + np.float32(3 * 0.044715) * square))
    return v * half, slope


def feed_kernel(
    h2p_ref, cot_ref, mod_ref, middle_ref, main_ref, left_ref, down_ref,
    out_ref, gh_ref, gup_ref, gleft_ref, gdown_ref, ggate_ref, down_acc, gdi, h2pt, act, actt, gup, left,
):
    j = pl.program_id(0)
    main_rows = main_ref.shape[0] * main_ref.shape[1]
    length, width = h2p_ref.shape

    @pl.when(j == 0)
    def _():
        gdi[...] = (cot_ref[...].astype(f32) * mod_ref[5:6, :]).astype(bf16)
        h2pt[...] = h2p_ref[...].T
        down_acc[...] = jnp.zeros_like(down_acc)
        gh_ref[...] = jnp.zeros_like(gh_ref)
        gleft_ref[...] = jnp.zeros_like(gleft_ref)

    pick = pick_left(None, j)
    left[...] = dot(pick, left_ref[...].reshape(16 * GROUPS, width)).astype(bf16)
    for cols in spans(width):
        main = main_ref[:, :, cols].reshape(main_rows, -1)
        up = dot(h2p_ref[:, :main_rows], main) + dot(h2p_ref[:, main_rows:], left[:, cols])
        value, slope = gelu_both(up)
        value = value.astype(bf16)
        act[:, cols] = value
        actt[cols, :] = value.T
        gup[:, cols] = (dot_bt(gdi[...], down_ref[cols, :]) * slope).astype(bf16)
    for cols in spans(width):
        down_acc[:, cols] += dot(act[...], down_ref[:, cols])
        gdown_ref[:, cols] = dot(actt[...], gdi[:, cols]).astype(bf16)
        gup_ref[:, :, cols] = dot(h2pt[:main_rows, :], gup[:, cols]).astype(bf16).reshape(GROUPS, 32, -1)
        part = dot(h2pt[main_rows:, :], gup[:, cols]).astype(bf16)
        gleft_ref[:, :, cols] += dot_at(pick, part).astype(bf16).reshape(GROUPS, 16, -1)
    gh_ref[:, main_rows:] += dot_bt(gup[...], left[...])
    for cols in spans(main_rows):
        gh_ref[:, cols] += dot_bt(gup[...], group_rows(main_ref, cols))

    @pl.when(j == pl.num_programs(0) - 1)
    def _():
        out_ref[...] = (middle_ref[...] + mod_ref[5:6, :] * down_acc[...]).astype(bf16)
        ggate_ref[...] = jnp.sum(cot_ref[...].astype(f32) * down_acc[...], axis=0, keepdims=True)


def unpermute(perm_ref, source_ref, out_ref):
    source = source_ref[...].astype(bf16)
    for cols in spans(perm_ref.shape[0]):
        out_ref[:, cols] = dot_bt(source, perm_ref[cols, :])


def norm_back(normed, rstd, factor, grad):
    scaled = grad * (1.0 + factor)
    mean = jnp.mean(scaled, axis=-1, keepdims=True)
    along = jnp.mean(scaled * normed, axis=-1, keepdims=True)
    return (scaled - mean - normed * along) * rstd


def second_part(
    head_width, ghp_ref, perm_ref, middle_ref, mod_ref, cot_ref, branch_ref, mixedp_ref, mix_ref, main_ref, left_ref,
    gmid_ref, gmixed_ref, gmix_ref, gout_ref, gleft_ref, sums_ref, gh, gb, partial,
):
    length, width = middle_ref.shape
    main_rows = rows_in(main_ref)
    unpermute(perm_ref, ghp_ref, gh)
    yield
    partial[...] = jnp.zeros_like(partial)

    def norm(rows):
        normed, rstd = norm_parts(middle_ref[rows, :])
        grad = gh[rows, :]
        partial[0] += eight_rows(grad)
        partial[1] += eight_rows(grad * normed)
        grad_middle = cot_ref[rows, :].astype(f32) + norm_back(normed, rstd, mod_ref[4:5, :], grad)
        gmid_ref[rows, :] = grad_middle
        partial[2] += eight_rows(grad_middle * branch_ref[rows, :].astype(f32))
        gb[rows, :] = (grad_middle * mod_ref[2:3, :]).astype(bf16)

    row_loop(length, norm)
    for k in range(3):
        sums_ref[k : k + 1, :] = jnp.sum(partial[k], axis=0, keepdims=True)
    sums_ref[3:8, :] = jnp.zeros((5, width), f32)
    pick = pick_left(None, 3)
    yield
    left = dot(pick, left_ref[...].reshape(16 * GROUPS, width)).astype(bf16)
    for cols in spans(width):
        gout = dot_at(mixedp_ref[:, :main_rows], gb[:, cols]).astype(bf16)
        gout_ref[..., cols] = gout.reshape(gout_ref.shape[:-1] + (-1,))
        part = dot_at(mixedp_ref[:, main_rows:], gb[:, cols]).astype(bf16)
        gleft_ref[..., cols] = dot_at(pick, part).astype(bf16).reshape(gleft_ref.shape[:-1] + (-1,))
    gh[:, main_rows:] = dot_bt(gb[...], left)
    for cols in spans(main_rows):
        gh[:, cols] = dot_bt(gb[...], group_rows(main_ref, cols))
    gb[...] = gh[...].astype(bf16)
    yield
    for cols in spans(width):
        gmixed_ref[:, cols] = dot_bt(gb[...], perm_ref[cols, :]).astype(bf16)

    sums = jnp.zeros((length, LANES), f32)
    dots = jnp.zeros((length, LANES), f32)
    for cols in spans(width, 2 * LANES):
        mix = mix_ref[:, cols]
        sums = sums + head_sums((mix * mix).astype(bf16), cols, head_width)
        for term in halves(mix * gmixed_ref[:, cols].astype(f32)):
            dots = dots + head_sums(term, cols, head_width)
    inverse = lax.rsqrt(sums * (1.0 / head_width) + epsilon)
    along = two_terms(dots * (1.0 / head_width) * inverse * inverse * inverse)
    inverse = two_terms(inverse)
    for cols in spans(width, 2 * LANES):
        gmix_ref[:, cols] = (
            gmixed_ref[:, cols].astype(f32) * spread_heads(inverse, cols, head_width)
            - mix_ref[:, cols] * spread_heads(along, cols, head_width)
        ).astype(bf16)
    yield


def second_kernel(head_width, *refs):
    for _ in second_part(head_width, *refs):
        pass


def pairs_part(head_width, heads, low, high, qkv_ref, gmix_ref, run_ref, runt_ref, gq_ref, gk_ref, gv_ref, rows_ref, cols_ref, held):
    length, width = gmix_ref.shape

    @pl.loop(low, high)
    def _(head):
        win, start = window_of(head, heads, head_width)
        mask = own_lanes(length, start, head, head_width)
        queries = jnp.where(mask, qkv_ref[0, :, win], 0)
        keys = jnp.where(mask, qkv_ref[1, :, win], 0)
        vals = jnp.where(mask, qkv_ref[2, :, win], 0)
        grads = jnp.where(mask, gmix_ref[:, win], 0)
        own = lax.broadcasted_iota(jnp.int32, (LANES, LANES), 1) == head
        row = lax.broadcasted_iota(jnp.int32, (LANES, LANES), 0)
        col = lax.broadcasted_iota(jnp.int32, (LANES, LANES), 1)
        columns = [None, None]
        for rows in row_blocks(length, 2 * LANES):
            weight = pair_weights(run_ref, runt_ref, head, rows, length)
            at = slice(rows.start, rows.start + rows.size)
            score = dot_bt(queries[at], keys) * weight
            grad = dot_bt(grads[at], vals)
            both = score * grad
            held[0, rows, :] = score.astype(bf16)
            held[1, rows, :] = (grad * weight).astype(bf16)
            for step in range(rows.size // LANES):
                first = rows.start + step * LANES
                strip = both[step * LANES : (step + 1) * LANES]
                middle = strip[:, first : first + LANES]
                pieces = [
                    (0, strip[:, :first], jnp.where(row > col, middle, 0.0)),
                    (1, strip[:, first + LANES :], jnp.where(row < col, middle, 0.0)),
                ]
                for way, part, corner in pieces:
                    total = jnp.sum(corner, axis=1, keepdims=True)
                    lines = [jnp.sum(corner, axis=0, keepdims=True)]
                    if first if way == 0 else length - first - LANES:
                        total = total + jnp.sum(part, axis=1, keepdims=True)
                        lines.insert(0 if way == 0 else 1, jnp.sum(part, axis=0, keepdims=True))
                    blank = jnp.zeros((1, length - sum(line.shape[1] for line in lines)), f32)
                    if blank.shape[1]:
                        lines.insert(len(lines) if way == 0 else 0, blank)
                    line = jnp.concatenate(lines, axis=1)
                    columns[way] = line if columns[way] is None else columns[way] + line
                    rows_ref[way, first : first + LANES, :] += jnp.where(own, total, 0.0)
        for way in range(2):
            cols_ref[way, pl.ds(head, 1), :] = columns[way]
        gq_ref[:, win] += dot(held[1], keys)
        gk_ref[:, win] += dot_at(held[1], queries)
        gv_ref[:, win] += dot_at(held[0], grads)


def pairs_kernel(head_width, heads, qkv_ref, gmix_ref, run_ref, runt_ref, gq_ref, gk_ref, gv_ref, rows_ref, cols_ref, held):
    for ref in (gq_ref, gk_ref, gv_ref, rows_ref, cols_ref):
        ref[...] = jnp.zeros_like(ref)
    pairs_part(
        head_width, heads, 0, heads, qkv_ref, gmix_ref, run_ref, runt_ref, gq_ref, gk_ref, gv_ref, rows_ref, cols_ref, held
    )


def carry_part(
    head_width, ways, early, qkv_ref, gmix_ref, gq_in, gk_in, gv_in, rows_ref, cols_ref, taken_ref, given_ref, gate_ref,
    state_ref, leave_ref, through, vpad, gpad, taps_ref, gqkv_ref, ggate_ref, conv_ref, bias_ref,
):
    length, width = gmix_ref.shape
    place = lax.broadcasted_iota(jnp.int32, (length, LANES), 0) % GRID
    taken_sums = [jnp.zeros((length, LANES), f32) for _ in range(ways)]
    given_sums = [jnp.zeros((length, LANES), f32) for _ in range(ways)]
    take_terms = [two_terms(taken_ref[way]) for way in range(ways)]
    give_terms = [two_terms(given_ref[way]) for way in range(ways)]
    for span in spans(width, 2 * LANES):
        near = near_lanes(span, width, head_width)
        gq, gk, gv = gq_in[:, span], gk_in[:, span], gv_in[:, span]
        for way in range(ways):
            take = spread_heads(take_terms[way], span, head_width)
            give = spread_heads(give_terms[way], span, head_width)
            back_q = take * dot_bt(gmix_ref[:, near], unfolded(state_ref, way, span, near, head_width))
            gq = gq + back_q
            for term in halves(qkv_ref[0, :, span].astype(f32) * back_q):
                taken_sums[way] = taken_sums[way] + head_sums(term, span, head_width)
            back_k = give * dot_bt(qkv_ref[2, :, near], unfolded(leave_ref, way, span, near, head_width))
            gk = gk + back_k
            for term in halves(qkv_ref[1, :, span].astype(f32) * back_k):
                given_sums[way] = given_sums[way] + head_sums(term, span, head_width)
            gv = gv + give * dot(qkv_ref[1, :, near], unfolded(leave_ref, way, near, span, head_width))
        gqkv_ref[0, :, span] = gq.astype(bf16)
        gqkv_ref[1, :, span] = gk.astype(bf16)
        for first in range(span.start, span.stop, LANES):
            cols = slice(first, first + LANES)
            grad = gpad[GRID : GRID + length, cols].astype(f32)
            total = gv[:, first - span.start : first - span.start + LANES]
            for lateral in range(3):
                b = lateral - 1
                column = jnp.zeros((length, LANES), f32)
                for vertical in range(3):
                    tap = taps_ref[3 * vertical + lateral : 3 * vertical + lateral + 1, cols]
                    start = (2 - vertical) * GRID
                    column = column + tap * gpad[start : start + length, cols].astype(f32)
                shifted = grad
                if b == -1:
                    column = jnp.where(place < GRID - 1, pltpu.roll(column, length - 1, 0), 0.0)
                    shifted = jnp.where(place < GRID - 1, pltpu.roll(grad, length - 1, 0), 0.0)
                if b == 1:
                    column = jnp.where(place > 0, pltpu.roll(column, 1, 0), 0.0)
                    shifted = jnp.where(place > 0, pltpu.roll(grad, 1, 0), 0.0)
                total = total + column
                for vertical in range(3):
                    window = vpad[vertical * GRID : vertical * GRID + length, cols].astype(f32)
                    conv_ref[3 * vertical + lateral : 3 * vertical + lateral + 1, cols] = jnp.sum(
                        window * shifted, axis=0, keepdims=True
                    )
            conv_ref[9:10, cols] = jnp.sum(grad, axis=0, keepdims=True)
            gqkv_ref[2, :, cols] = total.astype(bf16)
        if span.start // (2 * LANES) in (1, 3) or span.stop == width:
            yield
    conv_ref[10:16, :] = jnp.zeros((6, width), f32)

    row = lax.broadcasted_iota(jnp.int32, (length, length), 0)
    col = lax.broadcasted_iota(jnp.int32, (length, length), 1)
    before = (col < row).astype(bf16)
    upto = (col <= row).astype(bf16)

    def summed(product, matrix, value):
        high, rest = halves(value)
        low = (value - high.astype(f32) - rest.astype(f32)).astype(bf16)
        return product(matrix, high) + product(matrix, rest) + product(matrix, low)

    def columns(way):
        lines = cols_ref[way]
        if lines.shape[0] < LANES:
            lines = jnp.concatenate([lines, jnp.zeros((LANES - lines.shape[0], length), f32)], axis=0)
        return lines.T

    ahead = rows_ref[0] - columns(0)
    behind = rows_ref[1] - columns(1)
    if ways == 2:
        ahead, behind = ahead + taken_sums[0], behind + taken_sums[1]
        given_ahead, given_behind = given_sums
    else:
        ahead = ahead + taken_sums[0] * (1.0 - early)
        behind = behind + taken_sums[0] * early
        given_ahead, given_behind = given_sums[0] * early, given_sums[0] * (1.0 - early)
    grad_decay = (
        summed(dot_at, upto, ahead)
        + summed(dot, before, given_ahead)
        + summed(dot, upto, behind)
        + summed(dot_at, before, given_behind)
        + through
    )
    gate = gate_ref[...]
    small = jnp.exp(-jnp.abs(gate))
    sigmoid = jnp.where(gate >= 0, 1.0, small) / (1.0 + small)
    grad_gate = (-grad_decay * sigmoid).astype(bf16)
    lane = lax.broadcasted_iota(jnp.int32, grad_gate.shape, 1)
    grad_gate = jnp.where(lane < width // head_width, grad_gate.astype(f32), 0.0)
    ggate_ref[...] = grad_gate.astype(bf16)
    bias_ref[...] = jnp.sum(grad_gate, axis=0, keepdims=True)
    yield


def carry_kernel(
    head_width, ways, qkv_ref, gmix_ref, gq_in, gk_in, gv_in, rows_ref, cols_ref, taken_ref, given_ref, gate_ref,
    state_ref, leave_ref, through_ref, early_ref, gmixed_ref, grims_ref, vrims_ref, taps_ref,
    gqkv_ref, ggate_ref, conv_ref, bias_ref, vpad, gpad,
):
    fill_padded(vpad, vrims_ref, qkv_ref[2])
    fill_padded(gpad, grims_ref, gmixed_ref[...])
    for _ in carry_part(
        head_width, ways, early_ref[...], qkv_ref, gmix_ref, gq_in, gk_in, gv_in, rows_ref, cols_ref, taken_ref,
        given_ref, gate_ref, state_ref, leave_ref, through_ref[...], vpad, gpad, taps_ref, gqkv_ref, ggate_ref, conv_ref,
        bias_ref,
    ):
        pass


def projection_grads(slot, turned, grad_ref, gmain_ref, gleft_ref):
    pick = pick_left(None, slot)
    main_rows = rows_in(gmain_ref)
    for cols in spans(grad_ref.shape[1]):
        grad = grad_ref[:, cols]
        gmain_ref[..., cols] = dot(turned[:main_rows, :], grad).astype(bf16).reshape(gmain_ref.shape[:-1] + (-1,))
        part = dot(turned[main_rows:, :], grad).astype(bf16)
        gleft_ref[..., cols] += dot_at(pick, part).astype(bf16).reshape(gleft_ref.shape[:-1] + (-1,))


def projection_back(slot, grad_ref, main_ref, left_ref, gh_ref):
    width = grad_ref.shape[1]
    main_rows = rows_in(main_ref)
    left = dot(pick_left(None, slot), left_ref[...].reshape(16 * GROUPS, width)).astype(bf16)
    gh_ref[:, main_rows:] += dot_bt(grad_ref[...], left)
    for cols in spans(main_rows):
        gh_ref[:, cols] += dot_bt(grad_ref[...], group_rows(main_ref, cols))


def weights_kernel(
    xp_ref, gqkv_ref, ggate_ref, wf_ref, main_ref, left_ref, gout_left_ref, gmain_ref, gleft_ref, gforget_ref, gh_ref, turned
):
    slot = pl.program_id(0)

    @pl.when(slot == 0)
    def _():
        turned[...] = xp_ref[...].T
        gleft_ref[...] = gout_left_ref[...]
        gh_ref[...] = dot_bt(ggate_ref[...], wf_ref[...])
        gforget_ref[...] = dot(turned[...], ggate_ref[...])

    projection_grads(slot, turned, gqkv_ref.at[0], gmain_ref, gleft_ref)
    projection_back(slot, gqkv_ref.at[0], main_ref, left_ref, gh_ref)


def last_part(ghp_ref, perm_ref, x_ref, mod_ref, gmid_ref, gin_ref, sums_ref, gh, partial):
    unpermute(perm_ref, ghp_ref, gh)
    partial[...] = jnp.zeros_like(partial)

    def norm(rows):
        normed, rstd = norm_parts(x_ref[rows, :].astype(f32))
        grad = gh[rows, :]
        partial[0] += eight_rows(grad)
        partial[1] += eight_rows(grad * normed)
        gin_ref[rows, :] = gmid_ref[rows, :] + norm_back(normed, rstd, mod_ref[1:2, :], grad)

    row_loop(x_ref.shape[0], norm)
    for k in range(2):
        sums_ref[k : k + 1, :] = jnp.sum(partial[k], axis=0, keepdims=True)


def ring_place(z):
    return z + lax.div(z, 2) * (5 - 2 * z)


class Here:
    def __init__(self):
        row, x = lax.axis_index("dp"), lax.axis_index("seq")
        z, y, core = lax.div(row, 4), lax.rem(lax.div(row, 2), 2), lax.rem(row, 2)
        self.x, self.y, self.z, self.core = x, y, z, core
        self.p = ring_place(z)
        place = lambda z, y, core, x: ((z * 2 + y) * 2 + core, x)
        self.back = [ring_place(lax.rem(self.p + 4 - back, 4)) for back in range(4)]
        self.along = [place(self.back[4 - o], y, core, x) for o in (1, 2, 3)]
        self.next, self.prev = self.along[0], self.along[2]
        self.over_y = place(z, 1 - y, core, x)
        self.over_x = place(z, y, core, 1 - x)
        self.sibling = place(z, y, 1 - core, x)
        self.around = [self.over_y, self.over_x, place(z, 1 - y, core, 1 - x)]

    def ring_z(self, back):
        return self.back[back % 4]

    def partners(self, wide):
        devices = [self.next, self.prev, self.over_y, self.over_x, self.sibling]
        return devices + [self.along[1], self.around[2]] if wide else devices

    def greet(self, wide=False):
        barrier = pltpu.get_barrier_semaphore()
        for device in self.partners(wide):
            pl.semaphore_signal(barrier, inc=1, device_id=device, device_id_type=pl.DeviceIdType.MESH)

    def meet(self, wide=False):
        pl.semaphore_wait(pltpu.get_barrier_semaphore(), len(self.partners(wide)))


def push(source, target, send, recv, device):
    copy = pltpu.make_async_remote_copy(
        src_ref=source, dst_ref=target, send_sem=send, recv_sem=recv, device_id=device,
        device_id_type=pl.DeviceIdType.MESH,
    )
    copy.start()
    return copy


def routes(rows, ways=3):
    tiles = rows // 16
    third = 2 if tiles >= 7 and ways == 3 else 0
    first = tiles if ways == 1 else -(-(tiles - third) // 2)
    cuts = [0, 16 * first, 16 * (tiles - third), rows]
    return [pl.ds(low, high - low) for low, high in zip(cuts, cuts[1:])]


class Gather:
    def __init__(self, tag, here, ins, outs, sems, ways=3):
        self.here, self.ins, self.outs, self.sems, self.ways = here, ins, outs, sems, ways
        self.flights, self.todo, self.own = {}, {}, {}
        for i in range(len(ins)):
            a, b, c = routes(ins[i].shape[0], ways)
            self.todo[tag, 0, i, 0] = (), functools.partial(self.along_z, i, 0)
            for s in range(4):
                if s:
                    self.todo[tag, 0, i, s] = (("z", i, s - 1),), functools.partial(self.along_z, i, s)
                self.todo[tag, 1, i, s] = (("a1", i, s),), functools.partial(self.second, i, s, 0)
                waits = [("a2", i, s)]
                if b.size:
                    self.todo[tag, 2, i, s] = (("b1", i, s),), functools.partial(self.second, i, s, 1)
                    waits.append(("b2", i, s))
                if c.size:
                    waits.append(("cy", i, 0) if s == 0 else ("cz", i, s - 1))
                    self.todo[tag, 4, i, s] = (waits[-1],), functools.partial(self.third, i, s)
                    waits[-1] = ("c", i, s)
                self.todo[tag, 5, i, s] = tuple(waits), functools.partial(self.across, i, s)
            if c.size:
                self.todo[tag, 3, i, 0] = (("cx", i, 0),), functools.partial(self.third_over_y, i)

    def send(self, key, number, source, target, device):
        i, s = key[1:]
        self.flights[key] = push(source, target, self.sems[0].at[number, i, s], self.sems[1].at[number, i, s], device)

    def start(self):
        here = self.here
        for i, block in enumerate(self.ins):
            target = self.outs[i].at[here.z, here.y, here.core, here.x]
            self.own[i] = pltpu.make_async_copy(block, target, self.sems[2].at[i])
            self.own[i].start()

    def run(self, name):
        waits, action = self.todo.pop(name)
        for key in waits:
            if key[0] != "c":
                self.flights[key].wait_recv()
        action()

    def settle(self, i):
        if i in self.own:
            self.own.pop(i).wait()

    def along_z(self, i, s):
        here = self.here
        a, b, c = routes(self.ins[i].shape[0], self.ways)
        slot = self.outs[i].at[here.ring_z(s), here.y, here.core, here.x]
        held = self.ins[i] if s == 0 else slot
        if s < 3:
            both = pl.ds(0, a.size + b.size)
            self.send(("z", i, s), 0, held.at[both], slot.at[both], here.next)
        self.send(("a1", i, s), 1, held.at[a], slot.at[a], here.over_y)
        if b.size:
            self.send(("b1", i, s), 2, held.at[b], slot.at[b], here.over_x)
        if s == 0 and c.size:
            self.send(("cx", i, 0), 5, held.at[c], slot.at[c], here.over_x)

    def second(self, i, s, half):
        here, out = self.here, self.outs[i]
        a, b, c = routes(self.ins[i].shape[0], self.ways)
        z = here.ring_z(s)
        if s == 0:
            self.settle(i)
        if half:
            block = out.at[z, here.y, here.core, :, b]
            self.send(("b2", i, s), 4, block, block, here.over_y)
        else:
            block = out.at[z, :, here.core, here.x, a]
            self.send(("a2", i, s), 3, block, block, here.over_x)

    def third_over_y(self, i):
        here = self.here
        c = routes(self.ins[i].shape[0], self.ways)[2]
        self.settle(i)
        block = self.outs[i].at[here.z, here.y, here.core, :, c]
        self.send(("cy", i, 0), 6, block, block, here.over_y)

    def third(self, i, s):
        here = self.here
        c = routes(self.ins[i].shape[0], self.ways)[2]
        if s < 3:
            block = self.outs[i].at[here.ring_z(s), :, here.core, :, c]
            self.send(("cz", i, s), 7, block, block, here.next)

    def across(self, i, s):
        here = self.here
        block = self.outs[i].at[here.ring_z(s), :, here.core]
        self.send(("core", i, s), 8, block, block, here.sibling)

    def arrived(self, i, places=range(4)):
        for s in places:
            self.flights["core", i, s].wait_recv()

    def finish(self):
        for copy in self.flights.values():
            copy.wait_send()


def gather_sems(count):
    dma = pltpu.SemaphoreType.DMA
    return [dma((9, count, 4)), dma((9, count, 4)), dma((count,))]


class ShortGather:
    def __init__(self, tag, here, own, out, sems):
        self.here, self.own, self.out, self.sems = here, own, out, sems
        self.flights = {}
        self.todo = {
            (tag, 0, 0, 0): ((), self.along),
            (tag, 1, 0, 0): (tuple(("z", o) for o in range(3)), self.around),
            (tag, 2, 0, 0): (tuple(("xy", o) for o in range(3)), self.across),
        }

    def send(self, key, number, source, target, device):
        self.flights[key] = push(source, target, self.sems[0].at[number], self.sems[1].at[number], device)

    def start(self):
        here = self.here
        target = self.out.at[here.z, here.y, here.core, here.x]
        self.copy = pltpu.make_async_copy(self.own, target, self.sems[0].at[7])
        self.copy.start()

    def run(self, name):
        waits, action = self.todo.pop(name)
        for key in waits:
            self.flights[key].wait_recv()
        action()

    def along(self):
        here = self.here
        slot = self.out.at[here.z, here.y, here.core, here.x]
        for o, device in enumerate(here.along):
            self.send(("z", o), o, self.own, slot, device)

    def around(self):
        here = self.here
        self.copy.wait()
        block = self.out.at[:, here.y, here.core, here.x]
        for o, device in enumerate(here.around):
            self.send(("xy", o), 3 + o, block, block, device)

    def across(self):
        block = self.out.at[:, :, self.here.core]
        self.send(("core", 0), 6, block, block, self.here.sibling)

    def arrived(self):
        self.flights["core", 0].wait_recv()

    def finish(self):
        for copy in self.flights.values():
            copy.wait_send()


def short_gather_sems():
    return [pltpu.SemaphoreType.DMA((8,)), pltpu.SemaphoreType.DMA((8,))]


class ShortScatter:
    def __init__(self, tag, here, partial, final, scratch):
        self.acc, self.mate, self.xy_rows, self.z_rows, self.send_sem, self.recv_sem = scratch
        self.here, self.partial, self.final = here, partial, final
        self.flights = {}
        self.todo = {
            (tag, 0, 0, 0): (tuple(("core", n) for n in range(8)), self.from_sibling),
            (tag, 1, 0, 0): (tuple(("xy", o) for o in range(3)), self.around),
            (tag, 2, 0, 0): (tuple(("z", o) for o in range(3)), self.last),
        }

    def send(self, key, number, source, target, device):
        self.flights[key] = push(source, target, self.send_sem.at[number], self.recv_sem.at[number], device)

    def start(self):
        here = self.here
        for z in range(4):
            for y in range(2):
                rows = pl.ds(8 * z + 4 * y + 2 * (1 - here.core), 2)
                self.send(
                    ("core", 2 * z + y), 2 * z + y, self.partial.at[rows], self.mate.at[z, y], here.sibling
                )

    def run(self, name):
        waits, action = self.todo.pop(name)
        for key in waits:
            self.flights[key].wait_recv()
        action()

    def from_sibling(self):
        here = self.here
        for z in range(4):
            for y in range(2):
                rows = pl.ds(8 * z + 4 * y + 2 * here.core, 2)
                self.acc[z, y] = self.partial[rows] + self.mate[z, y]
        places = [(1 - here.y, here.x), (here.y, 1 - here.x), (1 - here.y, 1 - here.x)]
        for o, (y, x) in enumerate(places):
            self.send(("xy", o), 8 + o, self.acc.at[:, y, x], self.xy_rows.at[o], here.around[o])

    def around(self):
        here = self.here
        mine = self.acc.at[:, here.y, here.x]
        mine[...] = mine[...] + self.xy_rows[0] + self.xy_rows[1] + self.xy_rows[2]
        for o, device in enumerate(here.along):
            z = here.ring_z(3 - o)
            self.send(("z", o), 11 + o, mine.at[z], self.z_rows.at[o], device)

    def last(self):
        here = self.here
        self.final(self.acc[here.z, here.y, here.x] + self.z_rows[0] + self.z_rows[1] + self.z_rows[2])

    def finish(self):
        for copy in self.flights.values():
            copy.wait_send()


def short_scatter_scratch(block):
    rows, lanes = block.shape[-2:]
    dma = pltpu.SemaphoreType.DMA
    return [
        pltpu.VMEM((4, 2, 2, rows, lanes), f32), pltpu.VMEM((4, 2, 2, rows, lanes), f32),
        pltpu.VMEM((3, 4, rows, lanes), f32), pltpu.VMEM((3, rows, lanes), f32), dma((14,)), dma((14,)),
    ]


def gathered_shape(block):
    return sds((4, 2, 2, 2) + block.shape, block.dtype)


def add_rows(target, source, lead, low, size):
    chunk = 16

    @pl.loop(0, size // chunk)
    def _(r):
        start = pl.multiple_of(r * chunk, chunk)
        here, there = pl.ds(low + start, chunk), pl.ds(start, chunk)
        for at in lead:
            target[at + (here,)] = target[at + (here,)] + source[at + (there,)]


class Scatter:
    def __init__(self, tag, here, ins, final, scratch, ways=3):
        (
            self.acc, self.mate, self.one_a, self.one_b, self.two_rows, self.ring_rows, self.ring_c, self.c_y, self.c_x,
            self.send_sem, self.recv_sem, self.load_sem,
        ) = scratch
        self.here, self.ins, self.final = here, ins, final
        self.rows = self.acc.shape[3]
        self.a, self.b, self.c = routes(self.rows, ways)
        self.flights, self.loads, self.todo, self.released = {}, {}, {}, set()
        for k in range(4):
            self.todo[tag, 0, 0, k] = (("core", k),), functools.partial(self.from_sibling, k)
            self.todo[tag, 1, 0, k] = (("a1", k),), functools.partial(self.first_sum, k, 0)
            waits = [("a2", k)]
            if self.b.size:
                self.todo[tag, 2, 0, k] = (("b1", k),), functools.partial(self.first_sum, k, 1)
                waits.append(("b2", k))
            if k:
                waits.append(("z", k - 1))
            self.todo[tag, 3, 0, k] = tuple(waits), functools.partial(self.second_sum, k)
            if self.c.size:
                waits = (("c", k), ("cz", k - 1)) if k else (("c", k),)
                self.todo[tag, 4, 0, k] = waits, functools.partial(self.third_sum, k)
        if self.c.size:
            self.todo[tag, 5, 0, 0] = (("cy", 0),), self.third_over_y
            self.todo[tag, 5, 0, 1] = (("cx", 0), ("own", 0)), self.third_over_x

    def send(self, key, number, source, target, device, piece=0):
        at = (number + piece, key[1])
        self.flights[key] = push(source, target, self.send_sem.at[at], self.recv_sem.at[at], device)

    def pieces(self, k):
        z, low = self.here.ring_z(k + 1), 0
        for number, ref in enumerate(self.ins):
            if len(ref.shape) == 3:
                for y in range(2):
                    yield (
                        number + y, lambda core, y=y: ref.at[pl.ds(8 * z + 4 * y + 2 * core, 2)], lambda slot, y=y: slot.at[y]
                    )
            elif len(ref.shape) == 5:
                yield number, lambda core, ref=ref: ref.at[:, core], lambda slot: slot
            else:
                span = pl.ds(low, ref.shape[4])
                low += ref.shape[4]
                yield (
                    number, lambda core, ref=ref: ref.at[z, :, core], lambda slot, span=span: slot.at[:, :, span]
                )

    def load(self, k, numbers=None):
        for number, source, target in self.pieces(k):
            if numbers is not None and number not in numbers:
                continue
            self.loads[k, number] = pltpu.make_async_copy(
                source(self.here.core), target(self.acc.at[k]), self.load_sem.at[k, number]
            )
            self.loads[k, number].start()

    def to_sibling(self, k, numbers=None):
        for number, source, target in self.pieces(k):
            if numbers is not None and number not in numbers:
                continue
            self.send(
                ("core", k, number), 8, source(1 - self.here.core), target(self.mate.at[k]), self.here.sibling, number
            )

    def offer(self, k):
        self.load(k)
        self.to_sibling(k)

    def release(self, k):
        for number, _, _ in self.pieces(k):
            self.flights["core", k, number].wait_send()
        self.released.add(k)

    def prepare(self, numbers=None):
        for k in range(4):
            self.load(k, numbers)

    def start(self, numbers=None):
        for k in range(4):
            self.to_sibling(k, numbers)

    def run(self, name):
        waits, action = self.todo.pop(name)
        for key in waits:
            if key[0] == "core":
                for number, _, _ in self.pieces(key[1]):
                    self.loads[key[1], number].wait()
                    self.flights["core", key[1], number].wait_recv()
            elif key[0] not in ("c", "own"):
                self.flights[key].wait_recv()
        action()

    def from_sibling(self, k):
        here, acc = self.here, self.acc.at[k]
        add_rows(acc, self.mate.at[k], [(a, b) for a in range(2) for b in range(2)], 0, self.rows)
        self.send(("a1", k), 0, acc.at[:, 1 - here.x, self.a], self.one_a.at[k], here.over_x)
        if self.b.size:
            self.send(("b1", k), 1, acc.at[1 - here.y, :, self.b], self.one_b.at[k], here.over_y)

    def first_sum(self, k, half):
        here, acc = self.here, self.acc.at[k]
        if half:
            add_rows(acc.at[here.y], self.one_b.at[k], [(0,), (1,)], self.b.start, self.b.size)
            self.send(
                ("b2", k), 3, acc.at[here.y, 1 - here.x, self.b], self.two_rows.at[k, self.b], here.over_x
            )
        else:
            add_rows(acc.at[:, here.x], self.one_a.at[k], [(0,), (1,)], self.a.start, self.a.size)
            self.send(
                ("a2", k), 2, acc.at[1 - here.y, here.x, self.a], self.two_rows.at[k, self.a], here.over_y
            )

    def second_sum(self, k):
        here = self.here
        size = self.a.size + self.b.size
        mine = self.acc.at[k, here.y, here.x]
        add_rows(mine, self.two_rows.at[k], [()], 0, size)
        if k:
            add_rows(mine, self.ring_rows.at[k - 1], [()], 0, size)
        if k < 3:
            self.send(("z", k), 4, mine.at[pl.ds(0, size)], self.ring_rows.at[k], here.next)
        elif not self.c.size:
            self.final(mine)

    def third_sum(self, k):
        here, acc = self.here, self.acc.at[k]
        if k:
            add_rows(acc, self.ring_c.at[k - 1], [(a, b) for a in range(2) for b in range(2)], self.c.start, self.c.size)
        if k < 3:
            self.send(("cz", k), 5, acc.at[:, :, self.c], self.ring_c.at[k], here.next)
        else:
            self.send(("cy", 0), 6, acc.at[1 - here.y, :, self.c], self.c_y, here.over_y)

    def third_over_y(self):
        here, acc = self.here, self.acc.at[3]
        add_rows(acc.at[here.y], self.c_y, [(0,), (1,)], self.c.start, self.c.size)
        self.send(("cx", 0), 7, acc.at[here.y, 1 - here.x, self.c], self.c_x, here.over_x)

    def third_over_x(self):
        mine = self.acc.at[3, self.here.y, self.here.x]
        add_rows(mine, self.c_x, [()], self.c.start, self.c.size)
        self.final(mine)

    def finish(self):
        for key, copy in self.flights.items():
            if key[0] != "core" or key[1] not in self.released:
                copy.wait_send()


def scatter_scratch(block, ways=3):
    dma = pltpu.SemaphoreType.DMA
    rows, lanes, kind = sum(b.shape[-2] for b in block), block[0].shape[-1], block[0].dtype
    a, b, c = (max(span.size, 16) for span in routes(rows, ways))
    both = sum(span.size for span in routes(rows, ways)[:2])
    return [
        pltpu.VMEM((4, 2, 2, rows, lanes), kind), pltpu.VMEM((4, 2, 2, rows, lanes), kind),
        pltpu.VMEM((4, 2, a, lanes), kind), pltpu.VMEM((4, 2, b, lanes), kind),
        pltpu.VMEM((4, both, lanes), kind), pltpu.VMEM((3, both, lanes), kind),
        pltpu.VMEM((3, 2, 2, c, lanes), kind), pltpu.VMEM((2, c, lanes), kind), pltpu.VMEM((c, lanes), kind),
        dma((11, 4)), dma((11, 4)), dma((4, 3)),
    ]


def in_order(plan, chain, networks):
    pieces = iter(chain)
    for item in plan:
        if item == -1:
            next(pieces)()
        else:
            networks[item[0]].run(item)
    assert next(pieces, None) is None and not any(net.todo for net in networks.values())


def small_rows(cond, forget, taps, place):
    at = lax.rem(place * taps.shape[0], LANES)
    taps = lax.dynamic_update_slice(jnp.zeros((4 * LANES,), bf16), taps, (at,)).reshape(4, LANES)
    cond = cond.reshape(-1, LANES)
    forget = forget.reshape(36, -1)
    return jnp.concatenate([
        jnp.pad(cond, ((0, 16 - cond.shape[0]), (0, 0))), jnp.pad(taps, ((0, 12), (0, 0))),
        jnp.pad(forget, ((0, 12), (0, LANES - forget.shape[1]))),
    ])


def unpack_small(small, taps_share, wf_ref, taps_ref, flat):
    wf_ref[: 32 * GROUPS, :] = small[:, 32:64, :].reshape(32 * GROUPS, LANES)
    wf_ref[32 * GROUPS :, :] = dot(pick_left(None, 0), small[:, 64:80, :].reshape(16 * GROUPS, LANES)).astype(bf16)
    flat[...] = jnp.zeros_like(flat)
    for d in range(GROUPS):
        row = d * taps_share // LANES
        flat[row : row + 4, :] += small[d, 16:32, :].astype(f32)[:4]
    tiles = taps_ref.shape[1] // LANES
    taps_ref[...] = jnp.zeros_like(taps_ref)
    for k in range(10):
        for t in range(tiles):
            taps_ref[k : k + 1, t * LANES : (t + 1) * LANES] = flat[k * tiles + t : k * tiles + t + 1, :]


def pack_rows(sources, wide, left, out, other=None):
    for j, (source, first, per_row) in enumerate(sources):
        target = other if other is not None and j == 3 else out.at[pl.ds(32 * j, 32)]
        if first == 0:
            wide[: source.shape[0], :] = source[...].astype(f32)
        for t in range(out.shape[1] // LANES):
            cols = slice(t * LANES, (t + 1) * LANES)
            rows = wide[pl.ds(first + t, 36, stride=per_row), :]
            target[:, cols] = rows[:32].astype(bf16)
            left[4 * j : 4 * j + 4, cols] = rows[32:]
    out[(128 if other is None else 96) : (144 if other is None else 112), :] = left[...].astype(bf16)


def fill_permutation(perm_ref):
    width = perm_ref.shape[0]
    at = lax.broadcasted_iota(jnp.int32, (1, width), 1)
    late = at - 32 * GROUPS
    order = jnp.where(late < 0, (at >> 5) * 36 + (at & 31), (late >> 2) * 36 + 32 + (late & 3))
    for rows in spans(width, 2 * LANES):
        row = lax.broadcasted_iota(jnp.int32, (rows.stop - rows.start, width), 0) + rows.start
        perm_ref[rows, :] = (row == order).astype(bf16)


def forward_kernel(
    head_width, heads, taps_share, x_ref, ada_ref, bias_ref, bf_ref, own_s, query_ref, key_ref, value_ref, out_ref, up_ref,
    all_s, all_a, all_u, xp_out, qkv_out, mix_out, mixedp_out, branch_out, middle_out, h2p_out, perm_out,
    mod_ref, wf_ref, taps_ref, gate_ref, run_ref, runt_ref, state_ref, rims_ref, given_ref, taken_ref, cond_ref,
    xp_ref, qkv_ref, mix_ref, mixedp_ref, branch_ref, middle_ref, h2p_ref, perm_ref,
    own_a, own_u, wide, ada_wide, rows_left, small, flat, partial, main, left, outbox, inbox, vpad, mixed, load_sem, swap_sem, *rest,
):
    length, width = x_ref.shape
    tiles = width // LANES
    here = Here()
    here.greet(True)
    lower = here.x == 0
    squares = [(ref, 0, tiles) for ref in (query_ref, key_ref, value_ref, out_ref)]
    pack_rows(squares, wide, rows_left, own_a, own_u.at[pl.ds(144, 32)])
    pack_rows([(up_ref, j * tiles, 4 * tiles) for j in range(4)], wide, rows_left, own_u)
    first = ShortGather("f", here, own_s, all_s, rest[:2])
    gather = Gather("g", here, (own_a, own_u), (all_a, all_u), rest[2:5])

    def to_mod(total):
        for k in range(6):
            for t in range(tiles):
                mod_ref[k : k + 1, t * LANES : (t + 1) * LANES] = total[k * tiles + t : k * tiles + t + 1, :]
        mod_ref[6:8, :] = jnp.zeros((2, width), f32)

    scatter = ShortScatter("s", here, partial, to_mod, rest[5:])
    stores, loads = [], []

    def fetch(number, source, target):
        copy = pltpu.make_async_copy(source, target, load_sem.at[number])
        copy.start()
        return copy

    def modulation():
        first.arrived()
        fetch(5, all_s, small).wait()
        me = ((here.z * 2 + here.y) * 2 + here.core) * 2 + here.x
        row = lax.broadcasted_iota(jnp.int32, (width, LANES), 0)
        lane = lax.broadcasted_iota(jnp.int32, (width, LANES), 1)
        pick = ((row == lane + me * 36) & (lane < 36)).astype(bf16)
        lines = small[...].reshape(GROUPS, 80, LANES)[:, :16, :].astype(f32)
        mine = jnp.zeros((GROUPS, LANES), f32)
        for t in range(tiles):
            cond = lines[:, t, :]
            cond = (cond / (1.0 + jnp.exp(-cond))).astype(bf16)
            mine = mine + dot(cond, pick[t * LANES : (t + 1) * LANES])
        cond_ref[...] = mine.astype(bf16)
        mine = mine[:, :36].astype(bf16)
        for t in range(6 * tiles):
            rows = ada_wide[pl.ds(t, 36, stride=6 * tiles), :].astype(bf16)
            partial[:, t, :] = dot(mine, rows) + bias_ref[t : t + 1, :].astype(f32)
        scatter.start()

    def small_arrays():
        unpack_small(small[...].reshape(GROUPS, 80, LANES), taps_share, wf_ref, taps_ref, flat)

    def norm_one():
        first_part(x_ref, mod_ref, perm_ref, wf_ref, bf_ref, xp_ref, gate_ref, run_ref, runt_ref, mixed)
        stores.extend([fetch(6, xp_ref, xp_out), fetch(13, perm_ref, perm_out)])
        total = run_ref[0, length - 1 : length, :]
        given_ref[0] = jnp.where(lower, jnp.exp(total - run_ref[0]), jnp.exp(run_ref[1]))
        taken_ref[0] = jnp.where(lower, jnp.exp(total - run_ref[1]), jnp.exp(run_ref[0]))
        mix_ref[...] = jnp.zeros_like(mix_ref)

    def load(slot):
        source = all_a.at[:, :, :, :, pl.ds(32 * slot, 32)] if slot < 3 else all_u.at[:, :, :, :, pl.ds(144, 32)]
        loads.append(fetch(slot, source, main.at[slot % 2]))

    def project(slot):
        if slot == 0:
            gather.arrived(0)
            others = fetch(4, all_a.at[:, :, :, :, pl.ds(96, 16)], left)
            load(0)
            load(1)
            others.wait()
        loads[slot].wait()

        def write(cols, value):
            qkv_ref[slot, :, cols] = value.astype(bf16)

        project_part(slot, xp_ref, main.at[slot % 2], left, write)
        if slot == 0:
            load(2)
        if slot == 2:
            stores.append(fetch(7, qkv_ref, qkv_out))

    def states():
        state_part(head_width, 1, lambda cols: qkv_ref[1, :, cols], qkv_ref.at[2], given_ref, outbox)
        edge = pl.multiple_of((1 - here.x) * (length - GRID), GRID)

        def write_edge(t, value):
            outbox[0, width + t * GRID : width + (t + 1) * GRID, :] = value

        edge_part(qkv_ref[2, pl.ds(edge, GRID), :], write_edge)
        stores.append(push(outbox, inbox, swap_sem.at[0], swap_sem.at[1], here.over_x))

    def mix(part):
        mix_part(head_width, heads, part * heads // 4, (part + 1) * heads // 4, qkv_ref, run_ref, runt_ref, mix_ref)

    def mixing():
        swap = stores.pop()
        swap.wait_recv()
        state_ref[0] = inbox[0, :width, :]
        for t in range(tiles):
            cols = slice(t * LANES, (t + 1) * LANES)
            rows = inbox[0, width + t * GRID : width + (t + 1) * GRID, :]
            rims_ref[0, :, cols] = jnp.where(lower, 0, rows).astype(bf16)
            rims_ref[1, :, cols] = jnp.where(lower, rows, 0).astype(bf16)
        fill_padded(vpad, rims_ref, qkv_ref[2])
        mixed_part(head_width, 1, qkv_ref, taken_ref, state_ref, taps_ref, vpad, mix_ref, mixed)
        stores.append(fetch(8, mix_ref, mix_out))
        swap.wait_send()

    def turn():
        gather.arrived(1)
        load(3)
        permute_part(mixed, perm_ref, mixedp_ref)
        stores.append(fetch(9, mixedp_ref, mixedp_out))

    def branch():
        loads[3].wait()
        branch_part(x_ref, mod_ref, mixedp_ref, main.at[1], left, branch_ref, middle_ref)
        stores.extend([fetch(10, branch_ref, branch_out), fetch(11, middle_ref, middle_out)])

    def norm_two():
        second_hidden(mod_ref, middle_ref, mixed)
        permute_part(mixed, perm_ref, h2p_ref)
        stores.append(fetch(12, h2p_ref, h2p_out))

    def prepare():
        fill_permutation(perm_ref)
        ada_wide[...] = ada_ref[...].astype(f32)
        partial[:, 6 * tiles :, :] = jnp.zeros((GROUPS, 64 - 6 * tiles, LANES), f32)

    chain = [prepare, modulation, small_arrays, norm_one]
    chain += [functools.partial(project, slot) for slot in range(3)] + [states]
    chain += [functools.partial(mix, part) for part in range(4)] + [mixing, turn, branch, norm_two]
    first.start()
    gather.start()
    here.meet(True)
    in_order(FORWARD_PLAN, chain, {"f": first, "g": gather, "s": scatter})
    for network in (first, gather, scatter):
        network.finish()
    for copy in stores:
        copy.wait()


def forward_fused(x, ada, bias, bf, small, shards, heads, taps_share):
    length, width = x.shape
    head_width = width // heads
    message = width + width // LANES * GRID
    anywhere, vm = pl.BlockSpec(memory_space=pl.ANY), pl.BlockSpec(memory_space=pltpu.VMEM)
    rows, wide = (length, width), (length, LANES)
    bulk = (
        sds(rows, bf16), sds((3,) + rows, bf16), sds(rows), sds(rows, bf16), sds(rows, bf16), sds(rows), sds(rows, bf16),
        sds((width, width), bf16),
    )
    kept = (
        sds((8, width)), sds((width, LANES), bf16), sds((16, width)), sds(wide), sds((2,) + wide), sds((2, LANES, length)),
        sds((1, width, LANES), bf16), sds((2, GRID, width), bf16), sds((1,) + wide), sds((1,) + wide),
        sds((GROUPS, LANES), bf16),
    )
    partial = sds((GROUPS, 64, LANES))
    own, own_up = sds((112, width), bf16), sds((176, width), bf16)
    dma = pltpu.SemaphoreType.DMA
    out = pl.pallas_call(
        functools.partial(forward_kernel, head_width, heads, taps_share),
        out_shape=tuple(gathered_shape(b) for b in (small, own, own_up)) + bulk + kept,
        in_specs=[vm] * 10,
        out_specs=(anywhere,) * (3 + len(bulk)) + (vm,) * len(kept),
        scratch_shapes=[pltpu.VMEM(b.shape, b.dtype) for b in bulk] + [
            pltpu.VMEM(own.shape, bf16), pltpu.VMEM(own_up.shape, bf16), pltpu.VMEM(shards[4].shape, f32),
            pltpu.VMEM(ada.shape, f32), pltpu.VMEM((16, width), f32),
            pltpu.VMEM((4, 2, 2, 2) + small.shape, bf16), pltpu.VMEM((96, LANES), f32),
            pltpu.VMEM(partial.shape, f32), pltpu.VMEM((2, 4, 2, 2, 2, 32, width), bf16),
            pltpu.VMEM((4, 2, 2, 2, 16, width), bf16), pltpu.VMEM((1, message, LANES), bf16),
            pltpu.VMEM((1, message, LANES), bf16), pltpu.VMEM((length + 2 * GRID, width), bf16), pltpu.VMEM(rows, bf16),
            dma((14,)), dma((2,)),
        ] + short_gather_sems() + gather_sems(2) + short_scatter_scratch(partial),
        compiler_params=pltpu.CompilerParams(collective_id=0, has_side_effects=True, vmem_limit_bytes=VMEM_LIMIT),
        name="forward",
    )(x, ada, bias, bf, small, *shards)
    gathered = [g.reshape((GROUPS,) + g.shape[4:]) for g in out[:3]]
    return gathered, out[3 : 3 + len(bulk)], out[3 + len(bulk) :]


def feed_fused_kernel(
    h2p, cot, mod_ref, flat_d, up_in, middle_in,
    all_d, out_out, gh_out, gup_out, gleft_ref, ggate_ref, down_own,
    gdi, h2pt, act, slope, actt, gup, main, left, left_own, down, down_acc, gh, middle, stage_d, stage_u, own_d, wide, load_sem, *rest,
):
    length, width = h2p.shape
    main_rows = GROUPS * 32
    here = Here()
    here.greet()
    gather = Gather("g", here, (own_d,), (all_d,), rest[:3], FEED_WAYS[0])
    scatter = Scatter("d", here, [stage_d], plain_final(down_own), rest[3:], FEED_WAYS[1])
    order = [here.ring_z(k + 1) for k in range(4)]

    def fetch(number, source, target):
        copy = pltpu.make_async_copy(source, target, load_sem.at[number])
        copy.start()
        return copy

    def load_up(k, number):
        rows = pl.ds(pl.multiple_of(32 * order[k], 32), 32)
        return fetch(number, up_in.at[:, rows], main.at[k % 2])

    def load_down(k):
        gather.arrived(0, [(k + 1) % 4])
        return fetch(8 + k, all_d.at[order[k]], down.at[k % 2])

    def left_rows(k):
        return dot(pick_left(None, order[k]), left[...].reshape(16 * GROUPS, width)).astype(bf16)

    def start():
        gdi[...] = (cot[...].astype(f32) * mod_ref[5:6, :]).astype(bf16)
        h2pt[...] = h2p[...].T
        gleft_ref[...] = jnp.zeros_like(gleft_ref)
        others.wait()

    def up_step(k):
        loads[k].wait()
        left_own[...] = left_rows(k)
        for cols in spans(width):
            up = dot(h2p[:, :main_rows], main[k % 2, :, :, cols].reshape(main_rows, -1))
            up = up + dot(h2p[:, main_rows:], left_own[:, cols])
            value, rate = gelu_both(up)
            value = value.astype(bf16)
            act[k, :, cols] = value
            actt[cols, :] = value.T
            slope[k, :, cols] = rate.astype(bf16)
        loads.append(load_up(k + 2, k + 2) if k < 2 else load_up(k - 2, k + 2))

    def down_grad(k):
        if k > 0:
            scatter.release(k - 1)
        for cols in spans(width):
            stage_d[:, :, :, :, cols] = dot(actt[...], gdi[:, cols]).astype(bf16).reshape(2, 2, 2, width // 8, -1)
        scatter.offer(k)

    def back_act(k):
        load_down(k).wait()
        rows_of = down[k % 2].reshape(width, width)
        for cols in spans(width):
            gup[:, cols] = (dot_bt(gdi[...], rows_of[cols]) * slope[k, :, cols].astype(f32)).astype(bf16)

    def down_step(k):
        rows_of = down[k % 2].reshape(width, width)
        for cols in spans(width):
            part = dot(act[k], rows_of[:, cols])
            if k == 0:
                down_acc[:, cols] = part
            else:
                down_acc[:, cols] += part
    def back_hidden(k):
        loads[4 + k].wait()
        for cols in spans(main_rows):
            part = dot_bt(gup[...], main[k % 2, cols.start // 32 : cols.stop // 32].reshape(-1, width))
            if k == 0:
                gh[:, cols] = part
            else:
                gh[:, cols] += part
        part = dot_bt(gup[...], left_rows(k))
        if k == 0:
            gh[:, main_rows:] = part
        else:
            gh[:, main_rows:] += part
        if k < 2:
            loads.append(load_up(k + 2, 6 + k))

    def up_grad(k):
        if k > 0:
            stores[k - 1].wait()
        projection_grads(order[k], h2pt, gup, stage_u, gleft_ref)
        rows = pl.ds(pl.multiple_of(32 * order[k], 32), 32)
        stores.append(fetch(13 + k, stage_u, gup_out.at[:, rows]))

    def end():
        keep = fetch(17, gh, gh_out)
        ggate_ref[...] = jnp.sum(cot[...].astype(f32) * down_acc[...], axis=0, keepdims=True)
        keep_middle.wait()
        for cols in spans(width):
            act[0, :, cols] = (middle[:, cols] + mod_ref[5:6, cols] * down_acc[:, cols]).astype(bf16)
        stores.extend([fetch(19, act.at[0], out_out), keep])

    chain = [start]
    for k in range(4):
        chain += [functools.partial(up_step, k), functools.partial(down_grad, k)]
    for k in range(4):
        chain += [functools.partial(step, k) for step in (back_act, down_step, back_hidden, up_grad)]
    others = fetch(12, up_in.at[:, pl.ds(128, 16)], left)
    loads = [load_up(0, 0), load_up(1, 1)]
    keep_middle = fetch(18, middle_in, middle)
    stores = []
    wide[...] = flat_d[...].astype(f32)
    for t in range(width // LANES):
        rows = wide[pl.ds(t, own_d.shape[0], stride=width // LANES), :]
        own_d[:, t * LANES : (t + 1) * LANES] = rows.astype(bf16)
    gather.start()
    here.meet()
    in_order(FEED_PLAN, chain + [end], {"d": scatter, "g": gather})
    scatter.finish()
    gather.finish()
    for copy in stores[3:]:
        copy.wait()


def feed_fused(h2p, cot, mod, flat_d, up_w, middle):
    length, width = h2p.shape
    anywhere, vm = pl.BlockSpec(memory_space=pl.ANY), pl.BlockSpec(memory_space=pltpu.VMEM)
    rows = (length, width)
    dma = pltpu.SemaphoreType.DMA
    stage = (2, 2, 2, width // 8, width)
    own = sds((width // 8, width), bf16)
    return pl.pallas_call(
        feed_fused_kernel,
        out_shape=(
            gathered_shape(own), sds(rows, bf16), sds(rows), sds((GROUPS, 128, width), bf16),
            sds((GROUPS, 16, width), bf16), sds((1, width)), sds(flat_d.shape),
        ),
        in_specs=[vm] * 4 + [anywhere] * 2,
        out_specs=(anywhere,) * 4 + (vm,) * 3,
        scratch_shapes=[
            pltpu.VMEM(rows, bf16), pltpu.VMEM((width, length), bf16), pltpu.VMEM((4,) + rows, bf16),
            pltpu.VMEM((4,) + rows, bf16), pltpu.VMEM((width, length), bf16), pltpu.VMEM(rows, bf16),
            pltpu.VMEM((2, GROUPS, 32, width), bf16), pltpu.VMEM((GROUPS, 16, width), bf16), pltpu.VMEM((128, width), bf16),
            pltpu.VMEM((2,) + stage, bf16), pltpu.VMEM(rows, f32), pltpu.VMEM(rows, f32), pltpu.VMEM(rows, f32),
            pltpu.VMEM(stage, bf16),
            pltpu.VMEM((GROUPS, 32, width), bf16), pltpu.VMEM(own.shape, bf16), pltpu.VMEM(flat_d.shape, f32), dma((20,)),
        ] + gather_sems(1) + scatter_scratch([sds(stage, bf16)], FEED_WAYS[1]),
        compiler_params=pltpu.CompilerParams(
            collective_id=1, has_side_effects=True, vmem_limit_bytes=62 * 1024 * 1024
        ),
        name="feed",
    )(h2p, cot, mod, flat_d, up_w, middle)[1:]


def six(array):
    return array.reshape((4, 2, 2, 2) + array.shape[1:])


def flat_rows(out, first, value, per_row):
    for t in range(value.shape[1] // LANES):
        out[pl.ds(first + t, value.shape[0], stride=per_row), :] = value[:, t * LANES : (t + 1) * LANES]


def square_final(outs):
    def final(total):
        value = total[...].astype(f32)
        per_row = value.shape[1] // LANES
        for j, out in enumerate(outs):
            flat_rows(out, 0, value[32 * j : 32 * j + 32], per_row)
            flat_rows(out, 32 * per_row, value[128 + 4 * j : 132 + 4 * j], per_row)

    return final


def columns_final(out):
    def final(total):
        value = total[...].astype(f32)
        tiles = value.shape[1] // LANES
        for j in range(4):
            flat_rows(out, j * tiles, value[32 * j : 32 * j + 32], 4 * tiles)
            flat_rows(out, 32 * 4 * tiles + j * tiles, value[128 + 4 * j : 132 + 4 * j], 4 * tiles)

    return final


def plain_final(out):
    def final(total):
        value = total[...].astype(f32)
        flat_rows(out, 0, value, value.shape[1] // LANES)

    return final


def small_final(out):
    def final(total):
        out[...] = total[...]

    return final


def fill_small(block, gforget, conv, bias, flat, taps_share):
    tiles = conv.shape[1] // LANES
    for k in range(10):
        for t in range(tiles):
            flat[k * tiles + t : k * tiles + t + 1, :] = conv[k : k + 1, t * LANES : (t + 1) * LANES]
    flat[10 * tiles :, :] = jnp.zeros_like(flat[10 * tiles :, :])
    block[:, :32, :] = gforget[: 32 * GROUPS, :].reshape(GROUPS, 32, LANES)
    block[:, 40:, :] = jnp.broadcast_to(bias[...].reshape(1, 1, LANES), (GROUPS, 8, LANES))
    for d in range(GROUPS):
        at = 32 * GROUPS + 4 * d
        block[d, 32:36, :] = gforget[at : at + 4, :]
        row = d * taps_share // LANES
        block[d, 36:40, :] = flat[row : row + 4, :]


def backward_kernel(
    head_width, heads, taps_share,
    mod_ref, run_ref, runt_ref, taken_ref, given_ref, gate_ref, state_ref, vrims_ref, taps_ref,
    ghp_in, perm_in, middle_in, cot_in, branch_in, mixedp_in, mix_in, weight_in, up_in, qkv_in, xp_in, gup_in, gupl_in,
    gmid_out, gqkv_out, gmain_out, gout_out, small_out, gleft_ref, ggate_ref, sums_ref, up_ref,
    pool, perm, gmix, gb, main, qkv, gqkv, held, vpad, gpad, pair_rows, pair_cols,
    outbox, inbox, rims, leave, conv_ref, bias_ref, gforget_ref, flat, small, partial, fetch_sem, swap_sem, *scratch,
):
    length, width = gmix.shape
    here = Here()
    here.greet()
    lower = here.x == 0
    gmixed = gpad.at[pl.ds(GRID, length)]
    turned = perm.at[:, pl.ds(0, length)]
    scatter = Scatter("u", here, [gup_in, gupl_in], columns_final(up_ref), scratch, BACKWARD_WAYS)
    scatter.prepare()

    def fetch(number, source, target):
        copy = pltpu.make_async_copy(source, target, fetch_sem.at[number])
        copy.start()
        return copy

    first = [
        fetch(0, ghp_in, pool.at[0]), fetch(1, perm_in, perm), fetch(2, middle_in, pool.at[1]), fetch(3, cot_in, qkv.at[0]),
        fetch(4, branch_in, qkv.at[1]), fetch(5, mixedp_in, qkv.at[2]),
        fetch(6, up_in.at[:, :, :, :, pl.ds(144, 32)], main.at[0]),
        fetch(7, weight_in.at[:, pl.ds(96, 16)], gleft_ref),
        fetch(8, mix_in, pool.at[2]),
    ]
    second = second_part(
        head_width, pool.at[0], perm, pool.at[1], mod_ref, qkv.at[0], qkv.at[1], qkv.at[2], pool.at[2], main.at[0], gleft_ref,
        pool.at[1], gmixed, gmix, main.at[1], gleft_ref, sums_ref, pool.at[3], gb, partial,
    )
    gq, gk, gv = pool.at[0], pool.at[2], pool.at[3]
    early = jnp.where(lower, jnp.ones((1, LANES), f32), 0.0)
    carry = carry_part(
        head_width, 1, early, qkv, gmix, gq, gk, gv, pair_rows, pair_cols, taken_ref, given_ref, gate_ref, state_ref,
        leave, jnp.zeros((1, LANES), f32), vpad, gpad, taps_ref, gqkv, ggate_ref, conv_ref, bias_ref,
    )
    stores = []

    def begin():
        first[0].wait()
        first[1].wait()
        next(second)
        for copy in first[2:]:
            copy.wait()

    def out_grad():
        next(second)
        stores.append(fetch(11, main.at[1], gout_out))
        next(second)
        stores.pop().wait()

    def states():
        again = fetch(9, qkv_in, qkv)
        stores.extend([fetch(10, pool.at[1], gmid_out), fetch(12, xp_in, gb)])
        for ref in (gq, gk, gv, pair_rows, pair_cols):
            ref[...] = jnp.zeros_like(ref)
        again.wait()
        state_part(head_width, 1, lambda cols: qkv[0, :, cols], gmix, taken_ref, outbox)
        edge = pl.multiple_of((1 - here.x) * (length - GRID), GRID)

        def write_edge(t, value):
            outbox[0, width + t * GRID : width + (t + 1) * GRID, :] = value

        edge_part(gmixed[pl.ds(edge, GRID), :], write_edge)
        stores.append(push(outbox, inbox, swap_sem.at[0], swap_sem.at[1], here.over_x))

    def pairs(part):
        pairs_part(
            head_width, heads, part * heads // 4, (part + 1) * heads // 4, qkv, gmix, run_ref, runt_ref, gq, gk, gv,
            pair_rows, pair_cols, held,
        )

    def carry_first():
        swap = stores.pop()
        swap.wait_recv()
        leave[0] = inbox[0, :width, :]
        for t in range(width // LANES):
            cols = slice(t * LANES, (t + 1) * LANES)
            edge_rows = inbox[0, width + t * GRID : width + (t + 1) * GRID, :]
            rims[0, :, cols] = jnp.where(lower, 0, edge_rows).astype(bf16)
            rims[1, :, cols] = jnp.where(lower, edge_rows, 0).astype(bf16)
        fill_padded(vpad, vrims_ref, qkv[2])
        gpad[:GRID, :] = rims[0]
        gpad[GRID + length :, :] = rims[1]
        next(carry)
        swap.wait_send()

    def turn():
        stores.append(fetch(13, gqkv, gqkv_out))
        stores[1].wait()
        turned[...] = gb[...].T
        gforget_ref[...] = dot(turned[...], ggate_ref[...])
        fill_small(small, gforget_ref, conv_ref, bias_ref, flat, taps_share)
        fetch(17, small, small_out).wait()

    def weight(slot):
        buffer = main.at[slot % 2]
        if slot == 2:
            stores[3].wait()
        projection_grads(slot, turned, gqkv.at[slot], buffer, gleft_ref)
        stores.append(fetch(14 + slot, buffer, gmain_out.at[:, :, :, :, pl.ds(32 * slot, 32)]))

    chain = [begin, functools.partial(next, second), out_grad, states]
    chain += [functools.partial(pairs, part) for part in range(4)] + [carry_first]
    chain += [functools.partial(next, carry)] * 3 + [turn] + [functools.partial(weight, slot) for slot in range(3)]
    here.meet()
    scatter.start()
    in_order(BACKWARD_PLAN, chain, {"u": scatter})
    scatter.finish()
    for number in (0, 2, 4, 5):
        stores[number].wait()


def backward_fused(heads, taps_share, small, arrays, grads):
    length, width = arrays[0].shape
    head_width = width // heads
    message = width + width // LANES * GRID
    anywhere, vm = pl.BlockSpec(memory_space=pl.ANY), pl.BlockSpec(memory_space=pltpu.VMEM)
    rows, wide = (length, width), (length, LANES)
    dma = pltpu.SemaphoreType.DMA
    return pl.pallas_call(
        functools.partial(backward_kernel, head_width, heads, taps_share),
        out_shape=(
            sds(rows), sds((3,) + rows, bf16), sds((4, 2, 2, 2, 96, width), bf16), sds((4, 2, 2, 2, 32, width), bf16),
            sds((GROUPS, 48, LANES)), sds((GROUPS, 16, width), bf16), sds(wide, bf16), sds((8, width)),
            sds((144 * width // LANES, LANES)),
        ),
        in_specs=[vm] * len(small) + [anywhere] * (len(arrays) + len(grads)),
        out_specs=(anywhere,) * 5 + (vm,) * 4,
        scratch_shapes=[
            pltpu.VMEM((4,) + rows, f32), pltpu.VMEM((width, width), bf16), pltpu.VMEM(rows, bf16), pltpu.VMEM(rows, bf16),
            pltpu.VMEM((2, 4, 2, 2, 2, 32, width), bf16), pltpu.VMEM((3,) + rows, bf16), pltpu.VMEM((3,) + rows, bf16), pltpu.VMEM((2, length, length), bf16),
            pltpu.VMEM((length + 2 * GRID, width), bf16), pltpu.VMEM((length + 2 * GRID, width), bf16),
            pltpu.VMEM((2,) + wide, f32), pltpu.VMEM((2, heads, length), f32),
            pltpu.VMEM((1, message, LANES), bf16), pltpu.VMEM((1, message, LANES), bf16),
            pltpu.VMEM((2, GRID, width), bf16), pltpu.VMEM((1, width, LANES), bf16), pltpu.VMEM((16, width), f32),
            pltpu.VMEM((1, LANES), f32), pltpu.VMEM((width, LANES), f32), pltpu.VMEM((96, LANES), f32),
            pltpu.VMEM((GROUPS, 48, LANES), f32), pltpu.VMEM((3, 8, width), f32), dma((18,)), dma((2,)),
        ] + scatter_scratch(grads, BACKWARD_WAYS),
        compiler_params=pltpu.CompilerParams(
            collective_id=3, has_side_effects=True, vmem_limit_bytes=62 * 1024 * 1024
        ),
        name="backward",
    )(*small, *arrays, *[six(g) for g in grads])


def finish_kernel(
    mod_ref, sums_two, gate_two, ggate_ref, wf_ref,
    weight_in, gqkv_in, perm_in, x_in, gmid_in, gmain_in, gout_in, gleft_in, small_in,
    gin_out, all_mod, query_out, key_out, value_out, out_out, small_ref,
    gin_ref, query_ref, key_ref, value_ref, out_ref, main, left, gqkv, perm, x, gmid, ghp, gh, sums_one, own_mod, partial, load_sem, *rest,
):
    width = perm.shape[0]
    here = Here()
    here.greet(True)
    scatter = Scatter(
        "a", here, [gmain_in, gout_in, gleft_in], square_final((query_ref, key_ref, value_ref, out_ref)), rest[:12]
    )
    small = Scatter("s", here, [small_in], small_final(small_ref), rest[12:24])
    gather = ShortGather("g", here, own_mod, all_mod, rest[24:])
    scatter.prepare()
    small.prepare()

    def fetch(number, source, target):
        copy = pltpu.make_async_copy(source, target, load_sem.at[number])
        copy.start()
        return copy

    def load(slot):
        return fetch(slot, weight_in.at[:, pl.ds(32 * slot, 32)], main.at[slot % 2])

    grads = fetch(3, gqkv_in, gqkv)
    rest_rows = fetch(4, weight_in.at[:, pl.ds(96, 16)], left)
    loads = [load(0), load(1)]
    others = [fetch(5, perm_in, perm), fetch(6, x_in, x), fetch(7, gmid_in, gmid)]
    stores = []

    def back(slot):
        if slot == 0:
            ghp[...] = dot_bt(ggate_ref[...], wf_ref[...])
            grads.wait()
            rest_rows.wait()
        loads[slot].wait()
        projection_back(slot, gqkv.at[slot], main.at[slot % 2], left, ghp)
        if slot == 0:
            loads.append(load(2))

    def last():
        for copy in others:
            copy.wait()
        last_part(ghp, perm, x, mod_ref, gmid, gin_ref, sums_one, gh, partial)
        lines = [sums_one[0:1, :], sums_one[1:2, :], sums_two[2:3, :], sums_two[0:1, :], sums_two[1:2, :], gate_two[...]]
        tiles = width // LANES
        for k, line in enumerate(lines):
            for t in range(tiles):
                own_mod[k * tiles + t : k * tiles + t + 1, :] = line[:, t * LANES : (t + 1) * LANES]
        own_mod[len(lines) * tiles :, :] = jnp.zeros_like(own_mod[len(lines) * tiles :, :])
        gather.start()
        stores.append(fetch(8, gin_ref, gin_out))

    here.meet(True)
    scatter.start()
    small.start()
    chain = [functools.partial(back, slot) for slot in range(3)] + [last]
    in_order(FINISH_PLAN, chain, {"a": scatter, "s": small, "g": gather})
    results = [(query_ref, query_out), (key_ref, key_out), (value_ref, value_out), (out_ref, out_out)]
    stores.extend(fetch(9 + number, *pair) for number, pair in enumerate(results))
    gather.arrived()
    for network in (scatter, small, gather):
        network.finish()
    for copy in stores:
        copy.wait()


def results_kernel(sources, cond_ref, mod_in, *refs):
    ins, outs = refs[: len(sources)], refs[len(sources) : -4]
    all_mod, ada, sems, own_sem = refs[-4:]
    ada_out, total_ref = outs[-2:]
    copies = []
    for number, (ref, (target, low)) in enumerate(zip(ins, sources)):
        place = outs[target] if low is None else outs[target].at[pl.ds(low, ref.shape[0])]
        copies.append(pltpu.make_async_copy(ref, place, sems.at[number]))
    fetch = pltpu.make_async_copy(mod_in, all_mod, own_sem.at[0])
    for copy in [fetch] + copies:
        copy.start()
    cond = cond_ref[...]
    cond = jnp.concatenate([cond, cond, cond], axis=0)
    fetch.wait()
    tiles = ada.shape[0] // 36
    for t in range(tiles):
        rows = all_mod[:, t, :]
        high, middle = halves(rows)
        low = (rows - high.astype(f32) - middle.astype(f32)).astype(bf16)
        product = dot_at(cond, jnp.concatenate([high, middle, low], axis=0))
        ada[pl.ds(t, 36, stride=tiles), :] = product[:36]
        total_ref[t : t + 1, :] = jnp.sum(rows, axis=0, keepdims=True)
    last = pltpu.make_async_copy(ada, ada_out, own_sem.at[1])
    last.start()
    for copy in copies + [last]:
        copy.wait()


def results(pieces, cond, all_mod, ada_rows):
    flat, sources, shapes = [], [], []
    for target, arrays in enumerate(pieces):
        rows = 0
        for array in arrays:
            sources.append((target, None if len(arrays) == 1 else rows))
            flat.append(array)
            rows += array.shape[0]
        shapes.append(sds((rows,) + arrays[0].shape[1:], arrays[0].dtype))
    anywhere, vm = pl.BlockSpec(memory_space=pl.ANY), pl.BlockSpec(memory_space=pltpu.VMEM)
    dma = pltpu.SemaphoreType.DMA
    return pl.pallas_call(
        functools.partial(results_kernel, tuple(sources)),
        out_shape=tuple(shapes) + (sds((ada_rows, LANES)), sds((ada_rows // 36, LANES))),
        in_specs=[vm, anywhere] + [anywhere] * len(flat),
        out_specs=(anywhere,) * (len(shapes) + 1) + (vm,),
        scratch_shapes=[
            pltpu.VMEM(all_mod.shape, f32), pltpu.VMEM((ada_rows, LANES), f32), dma((len(flat),)), dma((2,)),
        ],
        compiler_params=pltpu.CompilerParams(vmem_limit_bytes=20 * 1024 * 1024),
        name="results",
    )(cond, all_mod, *flat)


def finish_fused(small, arrays, grads, grad_small):
    length, width = arrays[3].shape
    anywhere, vm = pl.BlockSpec(memory_space=pl.ANY), pl.BlockSpec(memory_space=pltpu.VMEM)
    rows = (length, width)
    dma = pltpu.SemaphoreType.DMA
    own = sds((64, LANES))
    return pl.pallas_call(
        finish_kernel,
        out_shape=(sds(rows), gathered_shape(own)) + (sds((36 * width // LANES, LANES)),) * 4
        + (sds(grad_small.shape[1:]),),
        in_specs=[vm] * len(small) + [anywhere] * (len(arrays) + len(grads) + 1),
        out_specs=(anywhere,) * 6 + (vm,),
        scratch_shapes=[pltpu.VMEM(rows, f32)] + [pltpu.VMEM((36 * width // LANES, LANES), f32)] * 4 + [
            pltpu.VMEM((2, GROUPS, 32, width), bf16), pltpu.VMEM((GROUPS, 16, width), bf16), pltpu.VMEM((3,) + rows, bf16),
            pltpu.VMEM((width, width), bf16), pltpu.VMEM(rows, bf16), pltpu.VMEM(rows, f32), pltpu.VMEM(rows, f32),
            pltpu.VMEM(rows, f32), pltpu.VMEM((8, width), f32), pltpu.VMEM(own.shape, f32),
            pltpu.VMEM((2, 8, width), f32), dma((13,)),
        ] + scatter_scratch(grads) + scatter_scratch([grad_small]) + short_gather_sems(),
        compiler_params=pltpu.CompilerParams(
            collective_id=4, has_side_effects=True, vmem_limit_bytes=VMEM_LIMIT
        ),
        name="finish",
    )(*small, *arrays, *grads, six(grad_small))


def joined_states(messages, totals, width, head_width):
    count = lax.axis_size("seq")
    place = lax.axis_index("seq")

    def grid_rows(message):
        rows = message[width:].reshape(width // LANES, GRID, LANES)
        return rows.transpose(1, 0, 2).reshape(GRID, width)

    if count == 1:
        return jnp.zeros_like(messages[:, :width]), jnp.zeros((2, GRID, width), bf16)
    if count == 2:
        got = lax.ppermute(messages[0], "seq", [(0, 1), (1, 0)])
        rows = grid_rows(got)
        return got[None, :width], jnp.stack([jnp.where(place == 1, rows, 0), jnp.where(place == 0, rows, 0)])
    forward = [(i, i + 1) for i in range(count - 1)]
    backward = [(i + 1, i) for i in range(count - 1)]
    rims = jnp.stack([
        grid_rows(lax.ppermute(messages[0], "seq", forward)), grid_rows(lax.ppermute(messages[1], "seq", backward))
    ])
    states = lax.all_gather(messages[:, :width, :], "seq").astype(f32)
    passed = lax.all_gather(totals, "seq")
    heads_of_rows = np.arange(width) // head_width
    order = jnp.arange(count)
    ahead = jnp.zeros(states.shape[2:], f32)
    behind = jnp.zeros(states.shape[2:], f32)
    for source in range(count):
        between_up = jnp.where((order > source) & (order < place), 1.0, 0.0) @ passed
        between_down = jnp.where((order < source) & (order > place), 1.0, 0.0) @ passed
        ahead = ahead + jnp.where(source < place, jnp.exp(between_up), 0.0)[heads_of_rows, None] * states[source, 0]
        behind = behind + jnp.where(source > place, jnp.exp(between_down), 0.0)[heads_of_rows, None] * states[source, 1]
    return jnp.stack([ahead, behind]).astype(bf16), rims


def split_rows(matrix):
    grouped = matrix.reshape(GROUPS, -1, matrix.shape[1])
    return grouped[:, :32], grouped[:, 32:]


def pack_whole(parts, width):
    query, key, value, out, up, down = parts
    square = [piece.reshape(GROUPS, -1, width) for piece in (query, key, value, out)]
    up = up.reshape(GROUPS, square[0].shape[1], -1, width)
    columns = [up[:, :, j] for j in range(up.shape[2])]
    blocks = []
    for group in (square, columns):
        blocks.append(
            jnp.concatenate([piece[:, :32] for piece in group] + [piece[:, 32:] for piece in group], axis=1)
        )
    return blocks + [down.reshape(GROUPS, -1, width)]


def unpack_squares(block):
    return [
        jnp.concatenate([block[..., 32 * j : 32 * j + 32, :], block[..., 128 + 4 * j : 132 + 4 * j, :]], axis=-2)
        for j in range(4)
    ]


def unpack_blocks(blocks):
    squares = unpack_squares(blocks[0])
    columns = unpack_squares(blocks[1])
    lead = blocks[0].shape[:-2]
    up = jnp.stack(columns, axis=-2)
    return [piece.reshape(lead + (-1,)) for piece in squares] + [up.reshape(lead + (-1,)), blocks[2].reshape(lead + (-1,))]


def on_device(
    activations, conditioning, cotangent, w_ada, b_ada, w_query, w_key, w_value, w_forget, b_forget, conv_taps, w_out,
    w_up, w_down,
):
    _, length, width = activations.shape
    heads = b_forget.shape[0]
    head_width = width // heads
    data_count, seq_count = lax.axis_size("dp"), lax.axis_size("seq")
    devices = data_count * seq_count
    me = lax.axis_index("dp") * seq_count + lax.axis_index("seq")
    packed_here = (data_count, seq_count) == (16, 2)
    everywhere = ("dp", "seq")

    mod_width = 6 * width
    share = w_ada.shape[0]
    if share % mod_width == 0:
        ada_rows = share // mod_width
        first_row, inset = me * ada_rows, None
        ada_part = w_ada.reshape(ada_rows, mod_width)
    else:
        ada_rows = -(-share // mod_width) + 1
        first_row = (me * share) // mod_width
        inset = me * share - first_row * mod_width
        ada_part = lax.dynamic_update_slice(jnp.zeros((ada_rows * mod_width,), bf16), w_ada, (inset,))
        ada_part = ada_part.reshape(ada_rows, mod_width)

    def own_columns(cond_all):
        cond_act = jax.nn.silu(cond_all.astype(f32)).astype(bf16)
        cond_wide = jnp.pad(cond_act, ((0, 0), (0, ada_rows)))
        return lax.dynamic_slice_in_dim(cond_wide, first_row, ada_rows, axis=1)

    main_rows = 32 * GROUPS
    forget_b = jnp.pad(b_forget.astype(f32), (0, LANES - heads)).reshape(1, LANES)
    x = activations[0]
    cot = cotangent[0]
    rows = (length, width)

    def main_spec(block, columns=width):
        return pl.BlockSpec((GROUPS, 32, columns), block)

    def left_spec(block, columns=width):
        return pl.BlockSpec((GROUPS, 16, columns), block)

    def whole(shape):
        return pl.BlockSpec(shape, lambda *_: (0,) * len(shape))

    ways = 1 if seq_count == 2 else 2
    message_rows = width + width // LANES * GRID
    state_call = call(
        functools.partial(state_kernel, head_width, ways), sds((ways, message_rows, LANES), bf16), "states"
    )
    place = lax.axis_index("seq")

    def edges(values):
        low, high = values[:GRID], values[-GRID:]
        if ways == 1:
            return jnp.where(place == 0, high, low)[None]
        return jnp.stack([high, low])

    shards = (w_query, w_key, w_value, w_out, w_up, w_down)
    if packed_here:
        small = small_rows(conditioning[0], w_forget, conv_taps, me)
        bias = lax.dynamic_update_slice(jnp.zeros((mod_width,), bf16), b_ada, (me * b_ada.shape[0],)).reshape(-1, LANES)
        (small, attention_w, up_w), bulk, kept = forward_fused(
            x, w_ada.reshape(-1, LANES), bias, forget_b, small, [piece.reshape(-1, LANES) for piece in shards[:5]], heads, conv_taps.shape[0]
        )
        xp, qkv, mix, mixed_p, branch, middle, hidden_two_p, perm = bulk
        mod, forget_p, taps, gate_pre, run, runt, states, value_rims, given, taken, cond_mine = kept
        output, ghp_two, gup_main, gup_left, ggate_two, g_down = feed_fused(
            hidden_two_p, cot, mod, w_down.reshape(-1, LANES), up_w, middle
        )
    else:
        lanes_at = np.arange(width)
        per_group = width // GROUPS
        order = np.where(
            lanes_at < main_rows,
            lanes_at // 32 * per_group + lanes_at % 32,
            (lanes_at - main_rows) // 4 * per_group + 32 + (lanes_at - main_rows) % 4,
        )
        perm = (jnp.arange(width, dtype=jnp.int32)[:, None] == jnp.asarray(order, jnp.int32)[None, :]).astype(bf16)
        small = [w_forget, conv_taps, b_ada]
        sizes = np.cumsum([0] + [piece.shape[0] for piece in small])
        small = lax.all_gather(jnp.concatenate(small), everywhere)
        forget_w = small[:, : sizes[1]].reshape(width, heads)
        taps = small[:, sizes[1] : sizes[2]].reshape(10, width).astype(f32)
        taps = jnp.pad(taps, ((0, 6), (0, 0)))
        ada_bias = small[:, sizes[2] :].reshape(6, width).astype(f32)
        forget_main, forget_left = split_rows(forget_w)
        forget_p = jnp.concatenate([forget_main.reshape(-1, heads), forget_left.reshape(-1, heads)])
        forget_p = jnp.pad(forget_p, ((0, 0), (0, LANES - heads)))
        cond_part = own_columns(lax.all_gather(conditioning, "dp", axis=0, tiled=True))
        partial_mod = jnp.dot(cond_part, ada_part, preferred_element_type=f32)
        mod = lax.psum(lax.psum_scatter(partial_mod, "dp", scatter_dimension=0, tiled=True), "seq")
        mod = jnp.pad(mod.reshape(6, width) + ada_bias, ((0, 2), (0, 0)))
        blocks = pack_whole([lax.all_gather(s, everywhere, axis=0, tiled=True) for s in shards], width)
        attention_w, up_w, down_w = blocks
        down_w = down_w.reshape(-1, width)
        xp, gate_pre, run, runt = call(
            first_part,
            (sds(rows, bf16), sds((length, LANES)), sds((2, length, LANES)), sds((2, LANES, length))),
            "first_norm",
            scratch_shapes=[pltpu.VMEM(rows, bf16)],
        )(x, mod, perm, forget_p, forget_b)
        qkv = call(
            project_kernel,
            sds((3,) + rows, bf16),
            "project",
            grid=(3,),
            in_specs=[whole(rows), main_spec(lambda j: (0, j, 0)), left_spec(lambda j: (0, 8, 0))],
            out_specs=pl.BlockSpec((1,) + rows, lambda j: (j, 0, 0)),
        )(xp, attention_w, attention_w)
        total = run[0, -1]
        given = jnp.stack([jnp.exp(total - run[0]), jnp.exp(run[1])])
        taken = jnp.stack([jnp.exp(run[0]), jnp.exp(total - run[1])])
        if ways == 1:
            given = jnp.where(place == 0, given[0], given[1])[None]
            taken = jnp.where(place == 0, taken[1], taken[0])[None]
        messages = state_call(qkv[1], qkv[2], given, edges(qkv[2]))
        states, value_rims = joined_states(messages, total, width, head_width)
        mix_local = call(
            functools.partial(mix_kernel, head_width, heads), sds(rows), "mix"
        )(qkv, run, runt)
        mix, mixed_p, branch, middle, hidden_two_p = call(
            functools.partial(after_kernel, head_width, ways),
            (sds(rows), sds(rows, bf16), sds(rows, bf16), sds(rows), sds(rows, bf16)),
            "after",
            grid=(1,),
            in_specs=[
                whole(rows), whole((8, width)), whole((width, width)), whole((3,) + rows), whole(rows),
                whole((ways, length, LANES)), whole((ways, width, LANES)), whole((2, GRID, width)), whole((16, width)),
                main_spec(lambda i: (0, 3, 0)), left_spec(lambda i: (0, 8, 0)),
            ],
            out_specs=[whole(rows)] * 5,
            scratch_shapes=[pltpu.VMEM((length + 2 * GRID, width), bf16), pltpu.VMEM(rows, bf16)],
        )(x, mod, perm, qkv, mix_local, taken, states, value_rims, taps, attention_w, attention_w)
        output, ghp_two, gup_main, gup_left, gdown, ggate_two = call(
            feed_kernel,
            (
                sds(rows, bf16), sds(rows), sds((GROUPS, 128, width), bf16), sds((GROUPS, 16, width), bf16),
                sds(down_w.shape, bf16), sds((1, width)),
            ),
            "feed",
            grid=(4,),
            in_specs=[
                whole(rows), whole(rows), whole((8, width)), whole(rows), main_spec(lambda j: (0, j, 0)),
                left_spec(lambda j: (0, 8, 0)), pl.BlockSpec((width, width), lambda j: (j, 0)),
            ],
            out_specs=[
                whole(rows), whole(rows), main_spec(lambda j: (0, j, 0)), left_spec(lambda j: (0, 0, 0)),
                pl.BlockSpec((width, width), lambda j: (j, 0)), whole((1, width)),
            ],
            scratch_shapes=[
                pltpu.VMEM(rows, f32), pltpu.VMEM(rows, bf16), pltpu.VMEM((width, length), bf16), pltpu.VMEM(rows, bf16),
                pltpu.VMEM((width, length), bf16), pltpu.VMEM(rows, bf16), pltpu.VMEM((width - main_rows, width), bf16),
            ],
        )(hidden_two_p, cot, mod, middle, up_w, up_w, down_w)

    share_forget, share_taps, share_bias = w_forget.shape[0], conv_taps.shape[0], b_ada.shape[0]

    if packed_here:
        grad_middle, gqkv, gmain, gout_main, grad_small, gleft, grad_gate, sums_two, g_up = backward_fused(
            heads,
            share_taps,
            (mod, run, runt, taken, given, gate_pre, states, value_rims, taps),
            (ghp_two, perm, middle, cot, branch, mixed_p, mix, attention_w, six(up_w), qkv, xp),
            (gup_main, gup_left),
        )
        grad_input, mod_all, g_query, g_key, g_value, g_out, grad_small = finish_fused(
            (mod, sums_two, ggate_two, grad_gate, forget_p), (attention_w, gqkv, perm, x, grad_middle),
            (gmain, gout_main, six(gleft)), grad_small,
        )
        g_forget = grad_small[:36, :heads].reshape(-1)
        g_taps = lax.dynamic_slice(grad_small[36:40].reshape(-1), (lax.rem(me * share_taps, LANES),), (share_taps,))
        grad_bias = grad_small[40, :heads]
        *shares, grad_ada, mod_sum = results(
            [[output], [grad_input], [g_query], [g_key], [g_value], [g_out], [g_up], [g_down]], cond_mine,
            mod_all.reshape(devices, 64, LANES), share // LANES,
        )
        output, grad_input, *shares = shares
        shares = [piece.reshape(-1) for piece in shares]
        grad_ada, mod_sum = grad_ada.reshape(-1), mod_sum.reshape(-1)
    else:
        grad_middle, grad_mixed, grad_mix, gout_main, gout_left, sums_two = call(
            functools.partial(second_kernel, head_width),
            (
                sds(rows), sds(rows, bf16), sds(rows, bf16), sds((GROUPS, 32, width), bf16),
                sds((GROUPS, 16, width), bf16), sds((8, width)),
            ),
            "second_norm",
            grid=(1,),
            in_specs=[
                whole(rows), whole((width, width)), whole(rows), whole((8, width)), whole(rows), whole(rows), whole(rows),
                whole(rows), main_spec(lambda i: (0, 3, 0)), left_spec(lambda i: (0, 8, 0)),
            ],
            out_specs=[
                whole(rows), whole(rows), whole(rows), whole((GROUPS, 32, width)), whole((GROUPS, 16, width)),
                whole((8, width)),
            ],
            scratch_shapes=[
                pltpu.VMEM(rows, f32), pltpu.VMEM(rows, bf16), pltpu.VMEM((3, 8, width), f32),
            ],
        )(ghp_two, perm, middle, mod, cot, branch, mixed_p, mix, attention_w, attention_w)

        back = state_call(qkv[0], grad_mix, taken, edges(grad_mixed))
        if ways == 2:
            back = jnp.stack([
                jnp.concatenate([back[1, :width], back[0, width:]]), jnp.concatenate([back[0, :width], back[1, width:]])
            ])
        leaving, grad_rims = joined_states(back, total, width, head_width)
        if ways == 2:
            leaving = leaving[::-1]

        gq_local, gk_local, gv_local, pair_rows, pair_cols = call(
            functools.partial(pairs_kernel, head_width, heads),
            (sds(rows), sds(rows), sds(rows), sds((2, length, LANES)), sds((2, heads, length))),
            "pairs",
            scratch_shapes=[pltpu.VMEM((2, length, length), bf16)],
        )(qkv, grad_mix, run, runt)
        if seq_count > 2:
            rows_through = jnp.sum(states.astype(f32) * leaving.astype(f32), axis=(0, 2))
            through = jnp.exp(total[:heads]) * jnp.sum(rows_through.reshape(heads, head_width), axis=1)
            through = jnp.pad(through, (0, LANES - heads)).reshape(1, LANES)
        else:
            through = jnp.zeros((1, LANES), f32)
        early = jnp.where(place == 0, jnp.ones((1, LANES), f32), 0.0)

        pad_scratch = pltpu.VMEM((length + 2 * GRID, width), bf16)
        gqkv, grad_gate, grad_conv, grad_bias = call(
            functools.partial(carry_kernel, head_width, ways),
            (sds((3,) + rows, bf16), sds((length, LANES), bf16), sds((16, width)), sds((1, LANES))),
            "carry",
            scratch_shapes=[pad_scratch, pad_scratch],
        )(
            qkv, grad_mix, gq_local, gk_local, gv_local, pair_rows, pair_cols, taken, given, gate_pre, states, leaving,
            through, early, grad_mixed, grad_rims, value_rims, taps,
        )
        gmain, gleft, gforget, ghp_one = call(
            weights_kernel,
            (sds((GROUPS, 96, width), bf16), sds((GROUPS, 16, width), bf16), sds((width, LANES)), sds(rows)),
            "weights",
            grid=(3,),
            in_specs=[
                whole(rows), pl.BlockSpec((1,) + rows, lambda j: (j, 0, 0)), whole((length, LANES)),
                whole((width, LANES)), main_spec(lambda j: (0, j, 0)), left_spec(lambda j: (0, 8, 0)),
                left_spec(lambda j: (0, 0, 0)),
            ],
            out_specs=[
                main_spec(lambda j: (0, j, 0)), left_spec(lambda j: (0, 0, 0)), whole((width, LANES)), whole(rows),
            ],
            scratch_shapes=[pltpu.VMEM((width, length), bf16)],
        )(xp, gqkv, grad_gate, forget_p, attention_w, attention_w, gout_left)
        grad_input, sums_one = call(
            last_part, (sds(rows), sds((8, width))), "last_norm",
            scratch_shapes=[pltpu.VMEM(rows, f32), pltpu.VMEM((2, 8, width), f32)],
        )(ghp_one, perm, x, mod, grad_middle)

        gforget = gforget[:, :heads]
        gforget = jnp.concatenate(
            [gforget[:main_rows].reshape(GROUPS, 32, heads), gforget[main_rows:].reshape(GROUPS, 4, heads)], axis=1
        )
        grad_small = jnp.concatenate([gforget.reshape(devices, -1), grad_conv[:10].reshape(devices, -1)], axis=1)
        grad_small = lax.psum_scatter(grad_small, everywhere, scatter_dimension=0, tiled=True).reshape(-1)
        g_forget, g_taps = grad_small[:share_forget], grad_small[share_forget:]
        grad_bias = lax.psum(grad_bias[0, :heads], everywhere)
        grads = [
            jnp.concatenate([gmain, gout_main, gleft], axis=1), jnp.concatenate([gup_main, gup_left], axis=1),
            gdown.reshape(GROUPS, -1, width),
        ]
        shares = [
            lax.psum_scatter(g.reshape(-1), everywhere, scatter_dimension=0, tiled=True).astype(f32)
            for g in unpack_blocks(grads)
        ]
        grad_mod = jnp.concatenate([sums_one[:2], sums_two[2:3], sums_two[:2], ggate_two])
        mod_all = lax.all_gather(grad_mod.reshape(1, mod_width), everywhere, axis=0, tiled=True)

        mod_all = jnp.sum(mod_all.reshape(data_count, seq_count, mod_width), axis=1)
        mod_sum = jnp.sum(mod_all, axis=0)
        grad_ada = jnp.dot(cond_part.astype(f32).T, mod_all, precision=lax.Precision.HIGHEST).reshape(-1)
        if inset is not None:
            grad_ada = lax.dynamic_slice(grad_ada, (inset,), (share,))
    grad_ada_bias = lax.dynamic_slice(mod_sum, (me * share_bias,), (share_bias,))
    g_query, g_key, g_value, g_out, g_up, g_down = shares
    return (
        output[None], grad_input[None], grad_ada, grad_ada_bias, g_query, g_key, g_value, g_forget,
        grad_bias, g_taps, g_out, g_up, g_down,
    )


def solution(mesh):
    rows = P("dp", "seq", None)
    shard = P(("dp", "seq"))
    return jax.shard_map(
        on_device,
        mesh=mesh,
        in_specs=(
            rows, P("dp", None), rows, shard, shard, shard, shard, shard, shard, P(), shard, shard, shard, shard,
        ),
        out_specs=(
            rows, rows, shard, shard, shard, shard, shard, shard, P(), shard, shard, shard, shard,
        ),
        check_vma=False,
    )
```
